32 devices in a mesh: dp: 4 (over y, x), grid: 8 (over z, core).
Axes of the slice: x: 2, y: 2, z: 4, core: 2. Of those that a mesh axis runs over, the one named last changes fastest.
Arguments:
- embeddings: bfloat16 [10240, 768], P(('dp', 'grid')), may hold values from -6 to 6
- cluster: int32 [10240, 1], P(('dp', 'grid')), may hold values from 0 to 3; in each aligned block of 320 rows (0 to 319, 320 to 639, ...) at most 160 rows name the same one
- order_key: int32 [10240], P(('dp', 'grid')), may hold values from 0 to 10239, each once
Outputs:
- best: float32 [10240], P(('dp', 'grid'))
The draws below stay inside these ranges and needn't reach their ends.
Inputs may be any that keep to these rules, and one draw needn't show every extreme that they name: In the rows of one device at most 160 rows name one cluster, and on some device one cluster is named by exactly 160 rows; every cluster is named. `order_key`: each number of 0 to 10239 appears once.
All inputs are finite; a program needn't handle non-finite values.
Results may differ from the reference program's by a relative error of at most 0.0012.
Values may be sent and summed in bfloat16 or wider, within the bound.
No kernel may reach another device: no remote copies, remote signals or barrier semaphores. Data moves between devices by JAX's collectives and lax.ppermute only.
A program may use at most 128 MiB of HBM per device.

```python
import math
import jax
import jax.numpy as jnp
import numpy as np
from jax import lax

E = 768
R_DEV = 320
MOST = 160
CLUSTERS = 4
ROWS = 10240


def shard_levels(own_key, dims, cuts, smallest, high):
    def one(axis_at, shards_of):
        draws = jax.random.uniform(jax.random.fold_in(jax.random.fold_in(own_key, 6), axis_at), (shards_of,), jnp.float32, smallest / len(cuts), high / len(cuts))
        return jnp.repeat(jnp.exp(draws), dims[axis_at] // shards_of).reshape((-1,) + (1,) * (len(dims) - axis_at - 1))

    gain = one(*cuts[0])
    for cut in cuts[1:]:
        gain = gain * one(*cut)
    return gain


def shared_out(stream_key, own, number, rows, amount, top, most, skew):
    order = jax.random.permutation(stream_key, amount)
    packed, usual = load_shares(amount, rows * top, most, skew, True), load_shares(amount, rows * top, most, skew, False)
    places = jnp.arange(amount)

    def named(tallies, rotation):
        used = int((tallies > 0).sum())
        fixed = max(1, used // 4)
        passed = fixed + (places - fixed + rotation * (used - fixed)) % max(1, amount - fixed)
        return jnp.zeros((amount,), jnp.int32).at[order[jnp.where(places < fixed, places, passed)]].set(jnp.asarray(tallies, jnp.int32))

    tallies = jnp.where(number % 4 == 0, named(packed, number // 4), named(usual, number - number // 4 - 1))
    mixed = jax.random.permutation(jax.random.fold_in(own, 3), amount)
    donor, sink = mixed[0:amount // 2 * 2:2], mixed[1:amount // 2 * 2:2]
    slack = jnp.minimum(tallies[donor] - 1, most - tallies[sink]) // 2
    slack = jnp.where((donor == order[0]) | (sink == order[0]) | (tallies[sink] == 0), 0, jnp.maximum(slack, 0))
    passed = jax.random.randint(jax.random.fold_in(own, 4), (amount // 2,), 0, 1 << 20) % (slack + 1)
    tallies = tallies.at[donor].add(-passed).at[sink].add(passed)
    items = jnp.searchsorted(jnp.cumsum(tallies), jnp.arange(rows * top), side="right").astype(jnp.int32)
    listing = items.reshape(top, rows).T
    listing = listing[jax.random.permutation(jax.random.fold_in(own, 1), rows)]
    rotation = jax.random.randint(jax.random.fold_in(own, 2), (rows, 1), 0, top)
    return jnp.take_along_axis(listing, (jnp.arange(top)[None, :] + rotation) % top, axis=1)


def load_shares(number_of, total, most, skew, full):
    weights = [(1 << 20) // math.isqrt(grade ** skew) + 1 for grade in range(1, number_of + 1)]
    largest = most if full else min(most, max(-(-total // number_of), total * weights[0] // sum(weights)))
    least = 1 if total - largest >= number_of - 1 else 0
    given, spare = [largest] + [least] * (number_of - 1), total - largest - least * (number_of - 1)
    while spare > 0:
        candidates = [i for i in range(1, number_of) if given[i] < largest] or [i for i in range(1, number_of) if given[i] < most]
        mass, remaining = sum([weights[i] for i in candidates]), spare
        for i in candidates:
            addition = min(most - given[i], max(1, remaining * weights[i] // mass), spare)
            given[i] = given[i] + addition
            spare = spare - addition
    return np.array(given)


def bell_draw(stream_key, dims, spread, reach, shards=(), kind=jnp.bfloat16):
    values = jax.random.normal(stream_key, dims, jnp.float32) * spread
    if len(shards) > 0:
        values = shard_levels(stream_key, dims, shards, -0.22, 0.18) * values
    return jnp.clip(values, min=-reach, max=reach).astype(kind)


def setup_inputs(seed: int = 0) -> dict:
    streams_of = jax.random.split(jax.random.key(seed), 4)
    embeddings = bell_draw(streams_of[0], (ROWS, E), 1.0, 6.0, ((0, 32),))
    cluster_keys = jax.random.split(jax.random.fold_in(streams_of[1], 1), ROWS // R_DEV)
    cluster_turns = jax.random.permutation(jax.random.fold_in(streams_of[1], 3), ROWS // R_DEV)
    cluster = jax.vmap(lambda own, number: shared_out(jax.random.fold_in(streams_of[1], 2), own, number, R_DEV, CLUSTERS, 1, MOST, 1))(cluster_keys, cluster_turns).reshape((ROWS, 1))
    order_key = jax.random.permutation(streams_of[2], ROWS).astype(jnp.int32)
    return {"embeddings": embeddings, "cluster": cluster, "order_key": order_key}


def reference(embeddings, cluster, order_key):
    values = embeddings.astype(jnp.float32)
    scaled = values * lax.rsqrt(lax.optimization_barrier(jnp.sum(values * values, axis=1, keepdims=True)) + 1e-06)
    units = lax.optimization_barrier(scaled.astype(jnp.bfloat16)).astype(jnp.float32)
    labels = cluster[:, 0]
    blocks = units.shape[0] // R_DEV

    def one_block(index):
        start = (index * R_DEV).astype(jnp.int32)
        queries = lax.dynamic_slice_in_dim(units, start, R_DEV, 0)
        query_labels = lax.dynamic_slice_in_dim(labels, start, R_DEV, 0)
        query_keys = lax.dynamic_slice_in_dim(order_key, start, R_DEV, 0)
        sims = jnp.dot(queries, units.T, precision=lax.Precision.HIGHEST, preferred_element_type=jnp.float32)
        allowed = (labels[None, :] == query_labels[:, None]) & (order_key[None, :] < query_keys[:, None])
        return lax.optimization_barrier(jnp.max(jnp.where(allowed, sims, jnp.float32(-1.0)), axis=1))
    return lax.map(one_block, jnp.arange(blocks, dtype=jnp.int32)).reshape(-1)
```

```python
import functools

import jax
import jax.numpy as jnp
from jax import lax
from jax.experimental import pallas as pl
from jax.experimental.pallas import tpu as pltpu
from jax.sharding import PartitionSpec as P

EPSILON = 1e-06
EXTRA = 16
LANES = 128
BOTH = ("dp", "grid")


def up(value, multiple):
    return -(-value // multiple) * multiple


def turned_to_row(column, rows):
    padded = up(rows, LANES)
    if padded != rows:
        column = jnp.concatenate([column, jnp.zeros((padded - rows, LANES), column.dtype)], axis=0)
    return column.T[0:1, :rows]


def turned_to_column(row, rows):
    return jnp.broadcast_to(row, (LANES, row.shape[1])).T[:rows]


def codes(block, rows, span):
    parts = block[rows : rows + EXTRA, : up(rows, LANES)].astype(jnp.float32)
    return parts[2:3] * (4.0 * span) + parts[0:1] * 256.0 + parts[1:2]


def prepare_kernel(embeddings, cluster, order_key, block):
    rows, width = embeddings.shape
    values = embeddings[...].astype(jnp.float32)
    scale = lax.rsqrt(jnp.sum(values * values, axis=1, keepdims=True) + EPSILON)
    block[0:rows, :] = (values * scale).astype(jnp.bfloat16)
    labels = turned_to_row(
        jnp.broadcast_to(cluster[...].astype(jnp.float32), (rows, LANES)), rows
    )
    keys = order_key[...]
    high = (keys >> 8).astype(jnp.float32)
    low = (keys & 255).astype(jnp.float32)
    parts = jnp.concatenate(
        [high, low, labels + 1.0, jnp.zeros((EXTRA - 3, rows), jnp.float32)], axis=0
    )
    parts = jnp.concatenate([parts, jnp.zeros((EXTRA, width - rows), jnp.float32)], axis=1)
    block[rows : rows + EXTRA, :] = parts.astype(jnp.bfloat16)


def prepare(embeddings, cluster, order_key):
    rows, width = embeddings.shape
    return pl.pallas_call(
        prepare_kernel,
        out_shape=jax.ShapeDtypeStruct((rows + EXTRA, width), jnp.bfloat16),
        compiler_params=pltpu.CompilerParams(vmem_limit_bytes=16 << 20),
        cost_estimate=pl.CostEstimate(
            flops=4 * rows * width, bytes_accessed=4 * rows * width, transcendentals=rows
        ),
    )(embeddings, cluster, order_key.reshape(1, rows))


def similarities(ours, held):
    return lax.dot_general(
        ours, held, (((1,), (1,)), ((), ())), preferred_element_type=jnp.float32
    )


def lane_tiles_max(values):
    best = values[:, :LANES]
    for at in range(LANES, values.shape[1], LANES):
        best = jnp.maximum(best, values[:, at : at + LANES])
    return best


def row_from_partial(partial, rows):
    padded = up(rows, LANES)
    if padded != rows:
        partial = jnp.concatenate(
            [partial, jnp.zeros((padded - rows, LANES), partial.dtype)], axis=0
        )
    return jnp.max(partial.T, axis=0, keepdims=True)[:, :rows]


def meet(block, rows, span, held, held_codes, to_block, to_held):
    total = held.shape[0]
    step = 64
    column = turned_to_column(codes(block, rows, span), rows)
    partials = []
    best_held = jnp.full((8, total), -1.0, jnp.float32)
    for at in range(0, rows, step):
        sims = similarities(block[at : at + step, :], held[...])
        wide = jnp.concatenate([column[at : at + step]] * (total // LANES), axis=1)
        gap = wide - held_codes
        if to_block and to_held:
            sims = jnp.where(jnp.abs(gap) < span, sims, -1.0)
            later = gap > 0.0
            partials.append(lane_tiles_max(jnp.where(later, sims, -1.0)))
            other = jnp.where(later, -1.0, sims)
        elif to_block:
            partials.append(
                lane_tiles_max(jnp.where((gap > 0.0) & (gap < span), sims, -1.0))
            )
        else:
            other = jnp.where((gap < 0.0) & (gap > -span), sims, -1.0)
        if to_held:
            for row in range(0, step, 8):
                best_held = jnp.maximum(best_held, other[row : row + 8])
    mine = row_from_partial(jnp.concatenate(partials, axis=0), rows) if to_block else None
    return mine, jnp.max(best_held, axis=0, keepdims=True) if to_held else None


def plane_kernel(rows, span, *refs):
    blocks, partner, held, held_codes, best = refs[:-4], refs[-4], refs[-3], refs[-2], refs[-1]
    for at, block in enumerate(blocks):
        held[at * rows : (at + 1) * rows, :] = block[0:rows, :]
    row = jnp.concatenate([codes(block, rows, span)[:, :rows] for block in blocks], axis=1)
    held_codes[...] = row
    mine, _ = meet(blocks[0], rows, span, held, row, True, False)
    _, theirs = meet(partner, rows, span, held, row, False, True)
    best[...] = jnp.concatenate(
        [jnp.maximum(theirs[:, :rows], mine), theirs[:, rows:]], axis=1
    )


def plane(blocks, partner, rows, span):
    width = partner.shape[1]
    total = len(blocks) * rows
    row = jax.ShapeDtypeStruct((1, total), jnp.float32)
    return pl.pallas_call(
        functools.partial(plane_kernel, rows, span),
        out_shape=(jax.ShapeDtypeStruct((total, width), jnp.bfloat16), row, row),
        compiler_params=pltpu.CompilerParams(vmem_limit_bytes=32 << 20),
        cost_estimate=pl.CostEstimate(
            flops=4 * rows * total * width, bytes_accessed=4 * total * width, transcendentals=0
        ),
    )(*blocks, partner)


def line_kernel(rows, span, held, held_codes, best, block, new_best, block_best):
    mine, theirs = meet(block, rows, span, held, held_codes[...], True, True)
    new_best[...] = jnp.maximum(best[...], theirs)
    block_best[...] = mine


def line(held, held_codes, best, block, rows, span):
    total, width = held.shape
    return pl.pallas_call(
        functools.partial(line_kernel, rows, span),
        out_shape=(
            jax.ShapeDtypeStruct((1, total), jnp.float32),
            jax.ShapeDtypeStruct((1, rows), jnp.float32),
        ),
        compiler_params=pltpu.CompilerParams(vmem_limit_bytes=32 << 20),
        cost_estimate=pl.CostEstimate(
            flops=2 * rows * total * width, bytes_accessed=2 * total * width, transcendentals=0
        ),
    )(held, held_codes, best, block)


def line_rounds(chips):
    if chips == 4:
        return [[(0, 2), (3, 1), (1, 0)], [(0, 3), (3, 2), (2, 1)]]
    rounds = []
    for shift in range(1, chips // 2 + 1):
        senders = chips // 2 if 2 * shift == chips else chips
        rounds.append([(s, (s + shift) % chips) for s in range(senders)])
    return rounds


def solution(mesh):
    groups, members = mesh.shape["dp"], mesh.shape["grid"]
    chips = members // 2

    def moves(pairs):
        return [(a * members + b, c * members + d) for (a, b), (c, d) in pairs]

    def back(pairs):
        return [(target, source) for source, target in pairs]

    everyone = [(p, g) for p in range(groups) for g in range(members)]
    other_core = moves([((p, g), (p, g ^ 1)) for p, g in everyone])

    def other_group(p, shift):
        return p ^ shift if groups & (groups - 1) == 0 else (p + shift) % groups

    across = [
        moves([((p, g), (other_group(p, shift), g)) for p, g in everyone])
        for shift in range(1, groups)
    ]
    rounds = line_rounds(chips)

    def along(pairs, cross):
        return moves(
            [
                ((p, 2 * s + c), (p, 2 * t + (c ^ cross)))
                for p in range(groups)
                for s, t in pairs
                for c in range(2)
            ]
        )

    def shards(embeddings, cluster, order_key):
        rows = embeddings.shape[0]
        span = 256
        while span < rows * groups * members:
            span *= 2
        chip = lax.axis_index("grid") // 2
        block = prepare(embeddings, cluster, order_key)
        partner = lax.ppermute(block, BOTH, other_core)
        from_line = [lax.ppermute(block, BOTH, along(pairs, 0)) for pairs in rounds]
        from_plane = [lax.ppermute(block, BOTH, pairs) for pairs in across]
        held, held_codes, best = plane([block] + from_plane, partner, rows, span)
        results = []
        for pairs, near in zip(rounds, from_line):
            far = lax.ppermute(near, BOTH, other_core)
            senders = functools.reduce(jnp.logical_or, [chip == s for s, _ in pairs])
            for cross, arrived in ((0, near), (1, far)):
                best, found = line(held, held_codes, best, arrived, rows, span)
                found = lax.ppermute(found, BOTH, back(along(pairs, cross)))
                results.append(jnp.where(senders, found, -1.0))
        for at, pairs in enumerate(across):
            part = best[:, (at + 1) * rows : (at + 2) * rows]
            results.append(lax.ppermute(part, BOTH, back(pairs)))
        return functools.reduce(jnp.maximum, results, best[:, :rows]).reshape(rows)

    placed = (P(BOTH, None), P(BOTH, None), P(BOTH))
    return jax.shard_map(
        shards, mesh=mesh, in_specs=placed, out_specs=P(BOTH), check_vma=False
    )
```

```python
import functools

import jax
import jax.numpy as jnp
from jax import lax
from jax.experimental import pallas as pl
from jax.experimental.pallas import tpu as pltpu
from jax.sharding import PartitionSpec as P

EPSILON = 1e-06
EXTRA = 16
LANES = 128
TILE = 256
BOTH = ("dp", "grid")


def up(value, multiple):
    return -(-value // multiple) * multiple


def turned_to_column(row, rows):
    return jnp.broadcast_to(row, (LANES, row.shape[1])).T[:rows]


def codes(block, rows, span):
    parts = block[rows : rows + EXTRA, : up(rows, LANES)].astype(jnp.float32)
    return parts[2:3] * (4.0 * span) + parts[0:1] * 256.0 + parts[1:2]


def prepare_kernel(embeddings, cluster, order_key, block):
    rows, width = embeddings.shape
    values = embeddings[...].astype(jnp.float32)
    scale = lax.rsqrt(jnp.sum(values * values, axis=1, keepdims=True) + EPSILON)
    block[0:rows, :] = (values * scale).astype(jnp.bfloat16)
    keys = order_key[...].reshape(1, rows)
    parts = [keys >> 8, keys & 255, cluster[...] + 1]
    parts = [part.astype(jnp.float32) for part in parts]
    parts = jnp.concatenate(parts + [jnp.zeros((EXTRA - 3, rows), jnp.float32)], axis=0)
    parts = jnp.concatenate([parts, jnp.zeros((EXTRA, width - rows), jnp.float32)], axis=1)
    block[rows : rows + EXTRA, :] = parts.astype(jnp.bfloat16)


def prepare(embeddings, cluster, order_key):
    rows, width = embeddings.shape
    return pl.pallas_call(
        prepare_kernel,
        out_shape=jax.ShapeDtypeStruct((rows + EXTRA, width), jnp.bfloat16),
        compiler_params=pltpu.CompilerParams(vmem_limit_bytes=16 << 20),
        cost_estimate=pl.CostEstimate(
            flops=4 * rows * width, bytes_accessed=4 * rows * width, transcendentals=rows
        ),
    )(embeddings, cluster.reshape(1, rows), order_key)


def row_from_partial(partial, rows):
    padded = up(rows, LANES)
    if padded != rows:
        partial = jnp.concatenate(
            [partial, jnp.zeros((padded - rows, LANES), partial.dtype)], axis=0
        )
    return jnp.max(partial.T, axis=0, keepdims=True)[:, :rows]


def meet(block, rows, span, held, held_codes, to_block, to_held):
    column = turned_to_column(codes(block, rows, span), rows)
    partial = jnp.full((rows, LANES), -1.0, jnp.float32)
    best_held = []
    for at in range(0, held.shape[0], TILE):
        sims = lax.dot_general(
            block[0:rows, :],
            held[at : at + TILE, :],
            (((1,), (1,)), ((), ())),
            preferred_element_type=jnp.float32,
        )
        for lane in range(0, TILE, LANES):
            part = sims[:, lane : lane + LANES]
            gap = column - held_codes[:, at + lane : at + lane + LANES]
            if to_block and to_held:
                part = jnp.where(jnp.abs(gap) < span, part, -1.0)
                later = gap > 0.0
                partial = jnp.maximum(partial, jnp.where(later, part, -1.0))
                other = jnp.where(later, -1.0, part)
            elif to_block:
                partial = jnp.maximum(
                    partial, jnp.where((gap > 0.0) & (gap < span), part, -1.0)
                )
            else:
                other = jnp.where((gap < 0.0) & (gap > -span), part, -1.0)
            if to_held:
                best_held.append(jnp.max(other, axis=0, keepdims=True))
    return (
        row_from_partial(partial, rows) if to_block else None,
        jnp.concatenate(best_held, axis=1) if to_held else None,
    )


def meet_kernel(rows, span, count, modes, holders, earlier, split, *refs):
    blocks, refs = refs[:count], refs[count:]
    holds, refs = refs[:holders], refs[holders:]
    bests, refs = refs[: holders * earlier], refs[holders * earlier :]
    outs, found, held = refs[:holders], refs[holders:-1], refs[-1]
    if split:
        found, joined = found[:-1], found[-1]
        top = 0
        for piece in blocks[-split:]:
            joined[top : top + piece.shape[0], :] = piece[...]
            top += piece.shape[0]
        blocks = blocks[:-split] + (joined,)
    total = held.shape[0]
    row = []
    for at, block in enumerate(holds):
        held[at * rows : (at + 1) * rows, :] = block[0:rows, :]
        row.append(codes(block, rows, span)[:, :rows])
    if total > holders * rows:
        held[holders * rows :, :] = jnp.zeros((total - holders * rows, held.shape[1]), held.dtype)
        row.append(jnp.zeros((1, total - holders * rows), jnp.float32))
    row = jnp.concatenate(row, axis=1)
    best = None
    at = 0
    for block, (to_block, to_held) in zip(blocks, modes):
        mine, theirs = meet(block, rows, span, held, row, to_block, to_held)
        if to_block:
            found[at][...] = mine
            at += 1
        if to_held:
            best = theirs if best is None else jnp.maximum(best, theirs)
    top = 0
    for out in found[at:]:
        out[...] = blocks[-1][top : top + out.shape[0], :]
        top += out.shape[0]
    for at, out in enumerate(outs):
        part = best[:, at * rows : (at + 1) * rows]
        if earlier:
            part = jnp.maximum(part, bests[at][...])
        out[...] = part


def meeting(blocks, modes, holds, bests, rows, span, keep=(), split=0):
    width = blocks[0].shape[1]
    holders = len(holds)
    total = up(holders * rows, TILE)
    row = jax.ShapeDtypeStruct((1, rows), jnp.float32)
    count = holders + sum(to_block for to_block, _ in modes)
    kept = tuple(jax.ShapeDtypeStruct((height, width), jnp.bfloat16) for height in keep)
    joined = [pltpu.VMEM((rows + EXTRA, width), jnp.bfloat16)] if split else []
    results = pl.pallas_call(
        functools.partial(
            meet_kernel, rows, span, len(blocks), modes, holders, 1 if bests else 0, split
        ),
        out_shape=(row,) * count + kept,
        scratch_shapes=joined + [pltpu.VMEM((total, width), jnp.bfloat16)],
        compiler_params=pltpu.CompilerParams(vmem_limit_bytes=32 << 20),
        cost_estimate=pl.CostEstimate(flops=rows, bytes_accessed=rows, transcendentals=0),
    )(*blocks, *holds, *bests)
    return list(results[:holders]), list(results[holders:count]), list(results[count:])


OWN = (True, False)
HELD = (False, True)
TWO = (True, True)


def line_rounds(chips):
    if chips == 4:
        return [[(0, 2), (3, 1), (1, 0)], [(0, 3), (3, 2), (2, 1)]]
    rounds = []
    for shift in range(1, chips // 2 + 1):
        senders = chips // 2 if 2 * shift == chips else chips
        rounds.append([(s, (s + shift) % chips) for s in range(senders)])
    return rounds


def solution(mesh):
    groups, members = mesh.shape["dp"], mesh.shape["grid"]
    assert groups == 4 and members % 2 == 0
    chips = members // 2
    rounds = line_rounds(chips)

    def everywhere(target):
        return [
            (p * members + g, a * members + b)
            for p in range(groups)
            for g in range(members)
            for a, b in [target(p, g)]
        ]

    other_core = everywhere(lambda p, g: (p, g ^ 1))
    first = everywhere(lambda p, g: (p ^ (1 + g % 2), g))
    second = everywhere(lambda p, g: (p ^ (2 - g % 2), g))
    corner = everywhere(lambda p, g: (p ^ 3, g))

    def along(pairs, cross):
        return [
            (p * members + 2 * s + c, p * members + 2 * t + (c ^ cross))
            for p in range(groups)
            for s, t in pairs
            for c in range(2)
        ]

    def back(pairs):
        return [(target, source) for source, target in pairs]

    def shards(embeddings, cluster, order_key):
        rows = embeddings.shape[0]
        span = 256
        while span < rows * groups * members:
            span *= 2
        chip = lax.axis_index("grid") // 2
        block = prepare(embeddings, cluster, order_key)
        near = [lax.ppermute(block, BOTH, along(rounds[0], 0))]
        from_first = lax.ppermute(block, BOTH, first)
        near += [lax.ppermute(block, BOTH, along(pairs, 0)) for pairs in rounds[1:]]
        from_second = lax.ppermute(block, BOTH, second)
        from_corner = lax.ppermute(from_first, BOTH, second)
        partner = lax.optimization_barrier((block, from_first))[0]
        partner = lax.ppermute(partner, BOTH, other_core)

        results = []

        def give_back(found, pairs):
            senders = functools.reduce(jnp.logical_or, [chip == s for s, _ in pairs])
            for cross, part in enumerate(found):
                part = lax.ppermute(part, BOTH, back(along(pairs, cross)))
                results.append(jnp.where(senders, part, -1.0))

        three = [block, from_first, from_second]
        bests, (mine, one), pieces = meeting(
            [block, near[0]], [OWN, TWO], three, [], rows, span, keep=(rows // 2, rows // 2 + EXTRA)
        )
        results.append(mine)
        pieces = [lax.ppermute(piece, BOTH, other_core) for piece in pieces]
        corner_best, (mine, one_more), _ = meeting(
            [block, near[0]], [OWN, TWO], [from_corner], [], rows, span
        )
        results.append(mine)
        bests, (other,), _ = meeting(
            [partner] + pieces,
            [HELD, TWO],
            three + [from_corner],
            bests + corner_best,
            rows,
            span,
            split=len(pieces),
        )
        give_back([jnp.maximum(one, one_more), other], rounds[0])
        for pairs, one in zip(rounds[1:], near[1:]):
            found = []
            one, bests = lax.optimization_barrier((one, bests))
            for part in (one, lax.ppermute(one, BOTH, other_core)):
                bests, mine, _ = meeting([part], [TWO], three + [from_corner], bests, rows, span)
                found += mine
            give_back(found, pairs)
        results += [
            lax.ppermute(part, BOTH, pairs)
            for part, pairs in zip(bests[1:], (first, second, corner))
        ]
        return functools.reduce(jnp.maximum, results, bests[0]).reshape(rows)

    placed = (P(BOTH, None), P(BOTH, None), P(BOTH))
    return jax.shard_map(
        shards, mesh=mesh, in_specs=placed, out_specs=P(BOTH), check_vma=False
    )
```

```python
import functools

import jax
import jax.numpy as jnp
from jax import lax
from jax.experimental import pallas as pl
from jax.experimental.pallas import tpu as pltpu
from jax.sharding import PartitionSpec as P

EPSILON = 1e-06
EXTRA = 16
LANES = 128
TILE = 256
BOTH = ("dp", "grid")


def up(value, multiple):
    return -(-value // multiple) * multiple


def turned_to_column(row, rows):
    return jnp.broadcast_to(row, (LANES, row.shape[1])).T[:rows]


def codes(block, rows, span):
    parts = block[rows : rows + EXTRA, : up(rows, LANES)].astype(jnp.float32)
    return parts[2:3] * (4.0 * span) + parts[0:1] * 256.0 + parts[1:2]


def prepare_kernel(
    embeddings_hbm, cluster_hbm, order_key_hbm, block, embeddings, cluster, order_key, arrived
):
    copies = [
        pltpu.make_async_copy(source, target, arrived.at[at])
        for at, (source, target) in enumerate(
            (
                (embeddings_hbm, embeddings),
                (cluster_hbm, cluster),
                (order_key_hbm, order_key),
            )
        )
    ]
    for copy in copies:
        copy.start()
    for copy in copies:
        copy.wait()
    rows, width = embeddings.shape
    values = embeddings[...].astype(jnp.float32)
    scale = lax.rsqrt(jnp.sum(values * values, axis=1, keepdims=True) + EPSILON)
    block[0:rows, :] = (values * scale).astype(jnp.bfloat16)
    keys = order_key[...].reshape(1, rows)
    parts = [keys >> 8, keys & 255, cluster[...] + 1]
    parts = [part.astype(jnp.float32) for part in parts]
    parts = jnp.concatenate(parts + [jnp.zeros((EXTRA - 3, rows), jnp.float32)], axis=0)
    parts = jnp.concatenate([parts, jnp.zeros((EXTRA, width - rows), jnp.float32)], axis=1)
    block[rows : rows + EXTRA, :] = parts.astype(jnp.bfloat16)


def prepare(embeddings, cluster, order_key):
    rows, width = embeddings.shape
    inputs = (embeddings, cluster.reshape(1, rows), order_key)
    return pl.pallas_call(
        prepare_kernel,
        in_specs=[pl.BlockSpec(memory_space=pltpu.HBM)] * 3,
        out_shape=jax.ShapeDtypeStruct((rows + EXTRA, width), jnp.bfloat16),
        scratch_shapes=[pltpu.VMEM(array.shape, array.dtype) for array in inputs]
        + [pltpu.SemaphoreType.DMA((3,))],
        compiler_params=pltpu.CompilerParams(vmem_limit_bytes=56 << 20),
        cost_estimate=pl.CostEstimate(flops=rows, bytes_accessed=rows, transcendentals=0),
    )(*inputs)


def row_from_partial(partial, rows):
    padded = up(rows, LANES)
    if padded != rows:
        partial = jnp.concatenate(
            [partial, jnp.zeros((padded - rows, LANES), partial.dtype)], axis=0
        )
    return jnp.max(partial.T, axis=0, keepdims=True)[:, :rows]


def meet(block, rows, span, held, held_codes, to_block, to_held):
    column = turned_to_column(codes(block, rows, span), rows)
    partial = jnp.full((rows, LANES), -1.0, jnp.float32)
    best_held = []
    for at in range(0, held.shape[0], TILE):
        tile = min(TILE, held.shape[0] - at)
        sims = lax.dot_general(
            block[0:rows, :],
            held[at : at + tile, :],
            (((1,), (1,)), ((), ())),
            preferred_element_type=jnp.float32,
        )
        for lane in range(0, tile, LANES):
            part = sims[:, lane : lane + LANES]
            gap = column - held_codes[:, at + lane : at + lane + LANES]
            if to_block and to_held:
                part = jnp.where(jnp.abs(gap) < span, part, -1.0)
                later = gap > 0.0
                partial = jnp.maximum(partial, jnp.where(later, part, -1.0))
                other = jnp.where(later, -1.0, part)
            elif to_block:
                partial = jnp.maximum(
                    partial, jnp.where((gap > 0.0) & (gap < span), part, -1.0)
                )
            else:
                other = jnp.where((gap < 0.0) & (gap > -span), part, -1.0)
            if to_held:
                best_held.append(jnp.max(other, axis=0, keepdims=True))
    return (
        row_from_partial(partial, rows) if to_block else None,
        jnp.concatenate(best_held, axis=1) if to_held else None,
    )


def assemble(whole, pieces):
    top = 0
    for piece in pieces:
        whole[top : top + piece.shape[0], :] = piece[...]
        top += piece.shape[0]


def meet_kernel(rows, span, sizes, modes, groups, *refs):
    kinds = []
    for size in sizes:
        kinds.append(refs[:size])
        refs = refs[size:]
    blocks, holds, bests, outs, found, kept, scratch = kinds
    held, scratch = scratch[0], iter(scratch[1:])

    def whole(block):
        if len(block) == 1:
            return block[0]
        joined = next(scratch)
        assemble(joined, block)
        return joined

    blocks = [whole(block) for block in regrouped(blocks, groups[0])]
    holds = [whole(block) for block in regrouped(holds, groups[1])]
    total = held.shape[0]
    row = []
    for at, block in enumerate(holds):
        held[at * rows : (at + 1) * rows, :] = block[0:rows, :]
        row.append(codes(block, rows, span)[:, :rows])
    rest = total - len(holds) * rows
    if rest:
        held[total - rest :, :] = jnp.zeros((rest, held.shape[1]), held.dtype)
        row.append(jnp.zeros((1, rest), jnp.float32))
    row = jnp.concatenate(row, axis=1)
    best = None
    found = iter(found)
    for block, (to_block, to_held) in zip(blocks, modes):
        mine, theirs = meet(block, rows, span, held, row, to_block, to_held)
        if to_block:
            next(found)[...] = mine
        if to_held:
            best = theirs if best is None else jnp.maximum(best, theirs)
    if kept:
        top = 0
        for out in kept:
            out[...] = blocks[-1][top : top + out.shape[0], :]
            top += out.shape[0]
    parts = [best[:, at * rows : (at + 1) * rows] for at in range(len(holds))]
    if bests:
        parts = [jnp.maximum(part, earlier[...]) for part, earlier in zip(parts, bests)]
    for out, places in zip(outs, groups[2]):
        if len(places) == 1:
            out[...] = parts[places[0]]
        else:
            out[...] = jnp.concatenate([parts[place] for place in places], axis=1)


def regrouped(flat, lengths):
    flat = iter(flat)
    return [[next(flat) for _ in range(length)] for length in lengths]


def meeting(blocks, modes, holds, bests, rows, span, keep=(), together=None):
    width = blocks[0][0].shape[1]
    together = together or [(at,) for at in range(len(holds))]
    lengths = [[len(block) for block in some] for some in (blocks, holds)]
    flat = [[piece for block in some for piece in block] for some in (blocks, holds)]
    outs = [jax.ShapeDtypeStruct((1, rows * len(some)), jnp.float32) for some in together]
    found = [jax.ShapeDtypeStruct((1, rows), jnp.float32)] * sum(mode[0] for mode in modes)
    kept = [jax.ShapeDtypeStruct((height, width), jnp.bfloat16) for height in keep]
    split = sum(length > 1 for some in lengths for length in some)
    scratch = [pltpu.VMEM((up(len(holds) * rows, LANES), width), jnp.bfloat16)]
    scratch += [pltpu.VMEM((rows + EXTRA, width), jnp.bfloat16)] * split
    kinds = flat + [bests, outs, found, kept, scratch]
    results = pl.pallas_call(
        functools.partial(
            meet_kernel, rows, span, [len(kind) for kind in kinds], modes, lengths + [together]
        ),
        out_shape=outs + found + kept,
        scratch_shapes=scratch,
        compiler_params=pltpu.CompilerParams(vmem_limit_bytes=32 << 20),
        cost_estimate=pl.CostEstimate(flops=rows, bytes_accessed=rows, transcendentals=0),
    )(*flat[0], *flat[1], *bests)
    return regrouped(results, [len(outs), len(found), len(kept)])


OWN = (True, False)
HELD = (False, True)
TWO = (True, True)


def line_rounds(chips):
    if chips == 4:
        return [[(0, 2), (3, 1), (1, 0)], [(0, 3), (3, 2), (2, 1)]]
    rounds = []
    for shift in range(1, chips // 2 + 1):
        senders = chips // 2 if 2 * shift == chips else chips
        rounds.append([(s, (s + shift) % chips) for s in range(senders)])
    return rounds


def solution(mesh):
    groups, members = mesh.shape["dp"], mesh.shape["grid"]
    assert groups == 4 and members % 2 == 0
    chips = members // 2
    rounds = line_rounds(chips)

    def everywhere(target):
        return [
            (p * members + g, a * members + b)
            for p in range(groups)
            for g in range(members)
            for a, b in [target(p, g)]
        ]

    other_core = everywhere(lambda p, g: (p, g ^ 1))
    first = everywhere(lambda p, g: (p ^ (1 + g % 2), g))
    second = everywhere(lambda p, g: (p ^ (2 - g % 2), g))

    def along(pairs):
        return [
            (p * members + 2 * s + c, p * members + 2 * t + c)
            for p in range(groups)
            for s, t in pairs
            for c in range(2)
        ]

    def back(pairs):
        return [(target, source) for source, target in pairs]

    def shards(embeddings, cluster, order_key):
        rows = embeddings.shape[0]
        span = 256
        while span < rows * groups * members:
            span *= 2
        chip = lax.axis_index("grid") // 2
        block = prepare(embeddings, cluster, order_key)
        halves = (rows // 2, rows // 2 + EXTRA)
        own = [block]
        near = [[lax.ppermute(block, BOTH, along(pairs))] for pairs in rounds]
        from_first = [lax.ppermute(block, BOTH, first)]
        from_second = [lax.ppermute(block, BOTH, second)]
        from_corner = [
            lax.ppermute(piece, BOTH, second)
            for piece in (from_first[0][: halves[0]], from_first[0][halves[0] :])
        ]
        partner = lax.optimization_barrier((block, from_first[0]))[0]
        partner = [lax.ppermute(partner, BOTH, other_core)]

        results = []

        def give_back(mine, theirs, pairs):
            mine = jnp.maximum(mine, lax.ppermute(theirs, BOTH, other_core))
            mine = lax.ppermute(mine, BOTH, back(along(pairs)))
            senders = functools.reduce(jnp.logical_or, [chip == s for s, _ in pairs])
            results.append(jnp.where(senders, mine, -1.0))

        bests, (mine, one), pieces = meeting(
            [own, near[0]], [OWN, TWO], [own, from_first], [], rows, span, keep=halves
        )
        results.append(mine)
        pieces = [lax.ppermute(piece, BOTH, other_core) for piece in pieces]
        more_bests, (mine, one_more), _ = meeting(
            [own, near[0]], [OWN, TWO], [from_second, from_corner], [], rows, span
        )
        results.append(mine)
        held = [own, from_first, from_second, from_corner]
        bests, (other,), _ = meeting(
            [partner, pieces], [HELD, TWO], held, bests + more_bests, rows, span
        )
        give_back(jnp.maximum(one, one_more), other, rounds[0])
        for at, (pairs, one) in enumerate(zip(rounds[1:], near[1:])):
            one, bests = lax.optimization_barrier((one, bests))
            far = [lax.ppermute(piece, BOTH, other_core) for piece in one]
            bests, (mine,), _ = meeting([one], [TWO], held, bests, rows, span)
            last = at == len(rounds) - 2
            bests, (theirs,), _ = meeting(
                [far], [TWO], held, bests, rows, span, together=[(0,), (1, 3), (2,)] if last else None
            )
            give_back(mine, theirs, pairs)
        from_x = lax.ppermute(bests[1], BOTH, first)
        results.append(from_x[:, :rows])
        onward = jnp.maximum(bests[2], from_x[:, rows:])
        results.append(lax.ppermute(onward, BOTH, second))
        return functools.reduce(jnp.maximum, results, bests[0]).reshape(rows)

    placed = (P(BOTH, None), P(BOTH, None), P(BOTH))
    return jax.shard_map(
        shards, mesh=mesh, in_specs=placed, out_specs=P(BOTH), check_vma=False
    )
```

```python
import functools

import jax
import jax.numpy as jnp
from jax import lax
from jax.experimental import pallas as pl
from jax.experimental.pallas import tpu as pltpu
from jax.sharding import PartitionSpec as P

EPSILON = 1e-06
EXTRA = 16
LANES = 128
TILE = 256
BOTH = ("dp", "grid")


def up(value, multiple):
    return -(-value // multiple) * multiple


def turned_to_column(row, rows):
    return jnp.broadcast_to(row, (LANES, row.shape[1])).T[:rows]


def codes(block, rows, span):
    parts = block[rows : rows + EXTRA, : up(rows, LANES)].astype(jnp.float32)
    return parts[2:3] * (4.0 * span) + parts[0:1] * 256.0 + parts[1:2]


def prepare_kernel(
    embeddings_hbm, cluster_hbm, order_key_hbm, block, embeddings, cluster, order_key, arrived
):
    copies = [
        pltpu.make_async_copy(source, target, arrived.at[at])
        for at, (source, target) in enumerate(
            (
                (embeddings_hbm, embeddings),
                (cluster_hbm, cluster),
                (order_key_hbm, order_key),
            )
        )
    ]
    for copy in copies:
        copy.start()
    for copy in copies:
        copy.wait()
    rows, width = embeddings.shape
    values = embeddings[...].astype(jnp.float32)
    scale = lax.rsqrt(jnp.sum(values * values, axis=1, keepdims=True) + EPSILON)
    block[0:rows, :] = (values * scale).astype(jnp.bfloat16)
    keys = order_key[...].reshape(1, rows)
    parts = [keys >> 8, keys & 255, cluster[...] + 1]
    parts = [part.astype(jnp.float32) for part in parts]
    parts = jnp.concatenate(parts + [jnp.zeros((EXTRA - 3, rows), jnp.float32)], axis=0)
    parts = jnp.concatenate([parts, jnp.zeros((EXTRA, width - rows), jnp.float32)], axis=1)
    block[rows : rows + EXTRA, :] = parts.astype(jnp.bfloat16)


def prepare(embeddings, cluster, order_key):
    rows, width = embeddings.shape
    inputs = (embeddings, cluster.reshape(1, rows), order_key)
    return pl.pallas_call(
        prepare_kernel,
        in_specs=[pl.BlockSpec(memory_space=pltpu.HBM)] * 3,
        out_shape=jax.ShapeDtypeStruct((rows + EXTRA, width), jnp.bfloat16),
        scratch_shapes=[pltpu.VMEM(array.shape, array.dtype) for array in inputs]
        + [pltpu.SemaphoreType.DMA((3,))],
        compiler_params=pltpu.CompilerParams(vmem_limit_bytes=56 << 20),
        cost_estimate=pl.CostEstimate(flops=rows, bytes_accessed=rows, transcendentals=0),
    )(*inputs)


def row_from_partial(partial, rows):
    padded = up(rows, LANES)
    if padded != rows:
        partial = jnp.concatenate(
            [partial, jnp.zeros((padded - rows, LANES), partial.dtype)], axis=0
        )
    return jnp.max(partial.T, axis=0, keepdims=True)[:, :rows]


def meet(block, rows, span, held, held_codes, to_block, to_held):
    column = turned_to_column(codes(block, rows, span), rows)
    partial = jnp.full((rows, LANES), -1.0, jnp.float32)
    best_held = []
    for at in range(0, held.shape[0], TILE):
        tile = min(TILE, held.shape[0] - at)
        sims = lax.dot_general(
            block[0:rows, :],
            held[at : at + tile, :],
            (((1,), (1,)), ((), ())),
            preferred_element_type=jnp.float32,
        )
        for lane in range(0, tile, LANES):
            part = sims[:, lane : lane + LANES]
            gap = column - held_codes[:, at + lane : at + lane + LANES]
            if to_block and to_held:
                part = jnp.where(jnp.abs(gap) < span, part, -1.0)
                later = gap > 0.0
                partial = jnp.maximum(partial, jnp.where(later, part, -1.0))
                other = jnp.where(later, -1.0, part)
            elif to_block:
                partial = jnp.maximum(
                    partial, jnp.where((gap > 0.0) & (gap < span), part, -1.0)
                )
            else:
                other = jnp.where((gap < 0.0) & (gap > -span), part, -1.0)
            if to_held:
                best_held.append(jnp.max(other, axis=0, keepdims=True))
    return (
        row_from_partial(partial, rows) if to_block else None,
        jnp.concatenate(best_held, axis=1) if to_held else None,
    )


def assemble(whole, pieces):
    top = 0
    for piece in pieces:
        whole[top : top + piece.shape[0], :] = piece[...]
        top += piece.shape[0]


def meet_kernel(rows, span, sizes, modes, groups, *refs):
    kinds = []
    for size in sizes:
        kinds.append(refs[:size])
        refs = refs[size:]
    blocks, holds, bests, outs, found, kept, scratch = kinds
    held, scratch = scratch[0], iter(scratch[1:])

    def whole(block):
        if len(block) == 1:
            return block[0]
        joined = next(scratch)
        assemble(joined, block)
        return joined

    blocks = [whole(block) for block in regrouped(blocks, groups[0])]
    holds = [whole(block) for block in regrouped(holds, groups[1])]
    total = held.shape[0]
    row = []
    for at, block in enumerate(holds):
        held[at * rows : (at + 1) * rows, :] = block[0:rows, :]
        row.append(codes(block, rows, span)[:, :rows])
    rest = total - len(holds) * rows
    if rest:
        held[total - rest :, :] = jnp.zeros((rest, held.shape[1]), held.dtype)
        row.append(jnp.zeros((1, rest), jnp.float32))
    row = jnp.concatenate(row, axis=1)
    best = None
    found = iter(found)
    for block, (to_block, to_held) in zip(blocks, modes):
        mine, theirs = meet(block, rows, span, held, row, to_block, to_held)
        if to_block:
            next(found)[...] = mine
        if to_held:
            best = theirs if best is None else jnp.maximum(best, theirs)
    if kept:
        top = 0
        for out in kept:
            out[...] = blocks[-1][top : top + out.shape[0], :]
            top += out.shape[0]
    parts = [best[:, at * rows : (at + 1) * rows] for at in range(len(holds))]
    if bests:
        parts = [jnp.maximum(part, earlier[...]) for part, earlier in zip(parts, bests)]
    for out, places in zip(outs, groups[2]):
        if len(places) == 1:
            out[...] = parts[places[0]]
        else:
            out[...] = jnp.concatenate([parts[place] for place in places], axis=1)


def regrouped(flat, lengths):
    flat = iter(flat)
    return [[next(flat) for _ in range(length)] for length in lengths]


def meeting(blocks, modes, holds, bests, rows, span, keep=(), together=None):
    width = blocks[0][0].shape[1]
    together = together or [(at,) for at in range(len(holds))]
    lengths = [[len(block) for block in some] for some in (blocks, holds)]
    flat = [[piece for block in some for piece in block] for some in (blocks, holds)]
    outs = [jax.ShapeDtypeStruct((1, rows * len(some)), jnp.float32) for some in together]
    found = [jax.ShapeDtypeStruct((1, rows), jnp.float32)] * sum(mode[0] for mode in modes)
    kept = [jax.ShapeDtypeStruct((height, width), jnp.bfloat16) for height in keep]
    split = sum(length > 1 for some in lengths for length in some)
    scratch = [pltpu.VMEM((up(len(holds) * rows, LANES), width), jnp.bfloat16)]
    scratch += [pltpu.VMEM((rows + EXTRA, width), jnp.bfloat16)] * split
    kinds = flat + [bests, outs, found, kept, scratch]
    results = pl.pallas_call(
        functools.partial(
            meet_kernel, rows, span, [len(kind) for kind in kinds], modes, lengths + [together]
        ),
        out_shape=outs + found + kept,
        scratch_shapes=scratch,
        compiler_params=pltpu.CompilerParams(vmem_limit_bytes=32 << 20),
        cost_estimate=pl.CostEstimate(flops=rows, bytes_accessed=rows, transcendentals=0),
    )(*flat[0], *flat[1], *bests)
    return regrouped(results, [len(outs), len(found), len(kept)])


OWN = (True, False)
HELD = (False, True)
TWO = (True, True)


def line_rounds(chips):
    if chips == 4:
        return [[(0, 2), (3, 1), (1, 0)], [(0, 3), (3, 2), (2, 1)]]
    rounds = []
    for shift in range(1, chips // 2 + 1):
        senders = chips // 2 if 2 * shift == chips else chips
        rounds.append([(s, (s + shift) % chips) for s in range(senders)])
    return rounds


def solution(mesh):
    groups, members = mesh.shape["dp"], mesh.shape["grid"]
    assert groups == 4 and members % 2 == 0
    chips = members // 2
    rounds = line_rounds(chips)
    rounds += [[]] * (len(rounds) % 2)

    def everywhere(target):
        return [
            (p * members + g, a * members + b)
            for p in range(groups)
            for g in range(members)
            for a, b in [target(p, g)]
        ]

    other_core = everywhere(lambda p, g: (p, g ^ 1))
    first = everywhere(lambda p, g: (p ^ (1 + g % 2), g))
    second = everywhere(lambda p, g: (p ^ (2 - g % 2), g))

    def along(pairs, *cores):
        return [
            (p * members + 2 * s + c, p * members + 2 * t + c)
            for p in range(groups)
            for s, t in pairs
            for c in cores
        ]

    def back(pairs):
        return [(target, source) for source, target in pairs]

    def shards(embeddings, cluster, order_key):
        rows = embeddings.shape[0]
        span = 256
        while span < rows * groups * members:
            span *= 2
        chip, core = lax.axis_index("grid") // 2, lax.axis_index("grid") % 2
        block = prepare(embeddings, cluster, order_key)
        halves = (rows // 2, rows // 2 + EXTRA)
        own = [block]
        near = [[lax.ppermute(block, BOTH, along(pairs, 0, 1))] for pairs in rounds]
        from_first = [lax.ppermute(block, BOTH, first)]
        from_corner = [lax.ppermute(from_first[0], BOTH, second)]
        later = lax.optimization_barrier((block, from_first[0]))[0]
        from_second = [lax.ppermute(later, BOTH, second)]
        partner = [lax.ppermute(later, BOTH, other_core)]

        results = []
        turned = []

        bests, (mine, one), pieces = meeting(
            [own, near[0]], [OWN, TWO], [own, from_first], [], rows, span, keep=halves
        )
        results.append(mine)
        pieces = [lax.ppermute(piece, BOTH, other_core) for piece in pieces]
        more_bests, (mine, one_more), _ = meeting(
            [own, near[0]], [OWN, TWO], [from_second, from_corner], [], rows, span
        )
        results.append(mine)
        held = [own, from_first, from_second, from_corner]
        bests, (other,), _ = meeting(
            [partner, pieces], [HELD, TWO], held, bests + more_bests, rows, span
        )
        turned.append(jnp.concatenate([jnp.maximum(one, one_more), other], axis=1))
        for at, (pairs, one) in enumerate(zip(rounds[1:], near[1:])):
            one, bests = lax.optimization_barrier((one, bests))
            far = [lax.ppermute(piece, BOTH, other_core) for piece in one]
            bests, (mine,), _ = meeting([one], [TWO], held, bests, rows, span)
            last = at == len(rounds) - 2
            bests, (theirs,), _ = meeting(
                [far], [TWO], held, bests, rows, span, together=[(0,), (1, 3), (2,)] if last else None
            )
            turned.append(jnp.concatenate([mine, theirs], axis=1))
        for at in range(0, len(rounds), 2):
            even, odd = turned[at], turned[at + 1]
            sent = lax.ppermute(jnp.where(core == 0, odd, even), BOTH, other_core)
            kept = jnp.where(core == 0, even, odd)
            kept = jnp.maximum(kept, jnp.concatenate([sent[:, rows:], sent[:, :rows]], axis=1))
            pairs = along(rounds[at], 0) + along(rounds[at + 1], 1)
            kept = lax.ppermute(kept, BOTH, back(pairs))
            sender = functools.reduce(
                jnp.logical_or,
                [(chip == s) & (core == c) for c in range(2) for s, _ in rounds[at + c]],
            )
            kept = jnp.where(sender, kept, -1.0)
            results += [kept[:, :rows], lax.ppermute(kept[:, rows:], BOTH, other_core)]
        from_x = lax.ppermute(bests[1], BOTH, first)
        results.append(from_x[:, :rows])
        onward = jnp.maximum(bests[2], from_x[:, rows:])
        results.append(lax.ppermute(onward, BOTH, second))
        return functools.reduce(jnp.maximum, results, bests[0]).reshape(rows)

    placed = (P(BOTH, None), P(BOTH, None), P(BOTH))
    return jax.shard_map(
        shards, mesh=mesh, in_specs=placed, out_specs=P(BOTH), check_vma=False
    )
```

```python
import functools

import jax
import jax.numpy as jnp
from jax import lax
from jax.experimental import pallas as pl
from jax.experimental.pallas import tpu as pltpu
from jax.sharding import PartitionSpec as P

EPSILON = 1e-06
EXTRA = 16
LANES = 128
TILE = 256
BOTH = ("dp", "grid")


def up(value, multiple):
    return -(-value // multiple) * multiple


def turned_to_column(row, rows):
    return jnp.broadcast_to(row, (LANES, row.shape[1])).T[:rows]


def codes(block, rows, span):
    parts = block[block.shape[0] - EXTRA :, : up(rows, LANES)].astype(jnp.float32)
    return parts[2:3] * (4.0 * span) + parts[0:1] * 256.0 + parts[1:2]


def prepare_kernel(
    embeddings_hbm, cluster_hbm, order_key_hbm, block, embeddings, cluster, order_key, arrived
):
    copies = [
        pltpu.make_async_copy(source, target, arrived.at[at])
        for at, (source, target) in enumerate(
            (
                (embeddings_hbm, embeddings),
                (cluster_hbm, cluster),
                (order_key_hbm, order_key),
            )
        )
    ]
    for copy in copies:
        copy.start()
    for copy in copies:
        copy.wait()
    rows, width = embeddings.shape
    values = embeddings[...].astype(jnp.float32)
    scale = lax.rsqrt(jnp.sum(values * values, axis=1, keepdims=True) + EPSILON)
    block[0:rows, :] = (values * scale).astype(jnp.bfloat16)
    keys = order_key[...].reshape(1, rows)
    parts = [keys >> 8, keys & 255, cluster[...] + 1]
    parts = [part.astype(jnp.float32) for part in parts]
    parts = jnp.concatenate(parts + [jnp.zeros((EXTRA - 3, rows), jnp.float32)], axis=0)
    parts = jnp.concatenate([parts, jnp.zeros((EXTRA, width - rows), jnp.float32)], axis=1)
    block[rows : rows + EXTRA, :] = parts.astype(jnp.bfloat16)


def prepare(embeddings, cluster, order_key):
    rows, width = embeddings.shape
    inputs = (embeddings, cluster.reshape(1, rows), order_key)
    return pl.pallas_call(
        prepare_kernel,
        in_specs=[pl.BlockSpec(memory_space=pltpu.HBM)] * 3,
        out_shape=jax.ShapeDtypeStruct((rows + EXTRA, width), jnp.bfloat16),
        scratch_shapes=[pltpu.VMEM(array.shape, array.dtype) for array in inputs]
        + [pltpu.SemaphoreType.DMA((3,))],
        compiler_params=pltpu.CompilerParams(vmem_limit_bytes=56 << 20),
        cost_estimate=pl.CostEstimate(flops=rows, bytes_accessed=rows, transcendentals=0),
    )(*inputs)


def row_from_partial(partial, rows):
    padded = up(rows, LANES)
    if padded != rows:
        partial = jnp.concatenate(
            [partial, jnp.zeros((padded - rows, LANES), partial.dtype)], axis=0
        )
    return jnp.max(partial.T, axis=0, keepdims=True)[:, :rows]


def meet(block, rows, span, held, held_codes, to_block, to_held):
    column = turned_to_column(codes(block, rows, span), rows)
    partial = jnp.full((rows, LANES), -1.0, jnp.float32)
    best_held = []
    for at in range(0, held.shape[0], TILE):
        tile = min(TILE, held.shape[0] - at)
        sims = lax.dot_general(
            block[0:rows, :],
            held[at : at + tile, :],
            (((1,), (1,)), ((), ())),
            preferred_element_type=jnp.float32,
        )
        for lane in range(0, tile, LANES):
            part = sims[:, lane : lane + LANES]
            gap = column - held_codes[:, at + lane : at + lane + LANES]
            if to_block and to_held:
                part = jnp.where(jnp.abs(gap) < span, part, -1.0)
                later = gap > 0.0
                partial = jnp.maximum(partial, jnp.where(later, part, -1.0))
                other = jnp.where(later, -1.0, part)
            elif to_block:
                partial = jnp.maximum(
                    partial, jnp.where((gap > 0.0) & (gap < span), part, -1.0)
                )
            else:
                other = jnp.where((gap < 0.0) & (gap > -span), part, -1.0)
            if to_held:
                best_held.append(jnp.max(other, axis=0, keepdims=True))
    return (
        row_from_partial(partial, rows) if to_block else None,
        jnp.concatenate(best_held, axis=1) if to_held else None,
    )


def assemble(whole, top, end, pieces):
    for piece in pieces:
        height = min(piece.shape[0], end - top)
        whole[top : top + height, :] = piece[0:height, :]
        top += height


def meet_kernel(rows, span, sizes, modes, groups, *refs):
    kinds = []
    for size in sizes:
        kinds.append(refs[:size])
        refs = refs[size:]
    blocks, holds, bests, outs, found, kept, scratch = kinds
    held, scratch = scratch[0], iter(scratch[1:])

    def whole(block):
        if len(block) == 1:
            return block[0]
        joined = next(scratch)
        assemble(joined, 0, joined.shape[0], block)
        return joined

    blocks = [whole(block) for block in regrouped(blocks, groups[0])]
    holds = regrouped(holds, groups[1])
    total = held.shape[0]
    row = []
    for at, block in enumerate(holds):
        assemble(held, at * rows, (at + 1) * rows, block)
        row.append(codes(block[-1], rows, span)[:, :rows])
    rest = total - len(holds) * rows
    if rest:
        held[total - rest :, :] = jnp.zeros((rest, held.shape[1]), held.dtype)
        row.append(jnp.zeros((1, rest), jnp.float32))
    row = jnp.concatenate(row, axis=1)
    best = None
    found = iter(found)
    for block, (to_block, to_held) in zip(blocks, modes):
        mine, theirs = meet(block, rows, span, held, row, to_block, to_held)
        if to_block:
            next(found)[...] = mine
        if to_held:
            best = theirs if best is None else jnp.maximum(best, theirs)
    if kept:
        top = 0
        for out in kept:
            out[...] = blocks[-1][top : top + out.shape[0], :]
            top += out.shape[0]
    parts = [best[:, at * rows : (at + 1) * rows] for at in range(len(holds))]
    if bests:
        parts = [jnp.maximum(part, earlier[...]) for part, earlier in zip(parts, bests)]
    for out, places in zip(outs, groups[2]):
        if len(places) == 1:
            out[...] = parts[places[0]]
        else:
            out[...] = jnp.concatenate([parts[place] for place in places], axis=1)


def regrouped(flat, lengths):
    flat = iter(flat)
    return [[next(flat) for _ in range(length)] for length in lengths]


def meeting(blocks, modes, holds, bests, rows, span, keep=(), together=None):
    width = blocks[0][0].shape[1]
    together = together or [(at,) for at in range(len(holds))]
    lengths = [[len(block) for block in some] for some in (blocks, holds)]
    flat = [[piece for block in some for piece in block] for some in (blocks, holds)]
    outs = [jax.ShapeDtypeStruct((1, rows * len(some)), jnp.float32) for some in together]
    found = [jax.ShapeDtypeStruct((1, rows), jnp.float32)] * sum(mode[0] for mode in modes)
    kept = [jax.ShapeDtypeStruct((height, width), jnp.bfloat16) for height in keep]
    split = sum(length > 1 for length in lengths[0])
    scratch = [pltpu.VMEM((up(len(holds) * rows, LANES), width), jnp.bfloat16)]
    scratch += [pltpu.VMEM((rows + EXTRA, width), jnp.bfloat16)] * split
    kinds = flat + [bests, outs, found, kept, scratch]
    results = pl.pallas_call(
        functools.partial(
            meet_kernel, rows, span, [len(kind) for kind in kinds], modes, lengths + [together]
        ),
        out_shape=outs + found + kept,
        scratch_shapes=scratch,
        compiler_params=pltpu.CompilerParams(vmem_limit_bytes=32 << 20),
        cost_estimate=pl.CostEstimate(flops=rows, bytes_accessed=rows, transcendentals=0),
    )(*flat[0], *flat[1], *bests)
    return regrouped(results, [len(outs), len(found), len(kept)])


OWN = (True, False)
HELD = (False, True)
TWO = (True, True)


def line_rounds(chips):
    if chips == 4:
        return [[(0, 2), (3, 1), (1, 0)], [(0, 3), (3, 2), (2, 1)]]
    rounds = []
    for shift in range(1, chips // 2 + 1):
        senders = chips // 2 if 2 * shift == chips else chips
        rounds.append([(s, (s + shift) % chips) for s in range(senders)])
    return rounds


def solution(mesh):
    groups, members = mesh.shape["dp"], mesh.shape["grid"]
    assert groups == 4 and members % 2 == 0
    chips = members // 2

    def everywhere(target):
        return [
            (p * members + g, a * members + b)
            for p in range(groups)
            for g in range(members)
            for a, b in [target(p, g)]
        ]

    other_core = everywhere(lambda p, g: (p, g ^ 1))
    first = everywhere(lambda p, g: (p ^ (1 + g % 2), g))
    second = everywhere(lambda p, g: (p ^ (2 - g % 2), g))

    rounds = line_rounds(chips)
    rounds += [[]] * (len(rounds) % 2)
    rounds = [
        [
            (p * members + 2 * s + c, p * members + 2 * t + c)
            for p in range(groups)
            for c in range(2)
            for s, t in rounds[at + c]
        ]
        for at in range(0, len(rounds), 2)
    ]

    def back(pairs):
        return [(target, source) for source, target in pairs]

    def shards(embeddings, cluster, order_key):
        rows = embeddings.shape[0]
        span = 256
        while span < rows * groups * members:
            span *= 2
        block = prepare(embeddings, cluster, order_key)
        halves = (rows // 2, rows // 2 + EXTRA)
        own = [block]
        parts = (block[: halves[0]], block[halves[0] :])
        partner = lax.ppermute(block, BOTH, other_core)
        near = [[lax.ppermute(block, BOTH, pairs)] for pairs in rounds]
        from_first = [lax.ppermute(part, BOTH, first) for part in parts]
        near_other = [[lax.ppermute(partner, BOTH, pairs)] for pairs in rounds]
        from_corner = [lax.ppermute(part, BOTH, second) for part in from_first]
        later = lax.optimization_barrier((block, *from_first))[0]
        from_second = [lax.ppermute(later, BOTH, second)]
        held = [own, from_first, from_second, from_corner]

        results, kept, sent = [], [], []
        bests, (mine, one), pieces = meeting(
            [own, near[0]], [OWN, TWO], held[:2], [], rows, span, keep=halves
        )
        results.append(mine)
        pieces = [lax.ppermute(piece, BOTH, other_core) for piece in pieces]
        more_bests, (mine, one_more), _ = meeting(
            [own, near[0]], [OWN, TWO], held[2:], [], rows, span
        )
        results.append(mine)
        kept.append(jnp.maximum(one, one_more))
        bests, found, _ = meeting(
            [[partner], pieces], [HELD, TWO], held, bests + more_bests, rows, span
        )
        sent += found
        rest = [blocks for both in zip(near, near_other) for blocks in both][1:]
        for at, one in enumerate(rest):
            (one,), bests = lax.optimization_barrier((one, bests))
            far = [lax.ppermute(one, BOTH, other_core)]
            bests, found, _ = meeting([[one]], [TWO], held, bests, rows, span)
            kept += found
            last = at == len(rest) - 1
            bests, found, _ = meeting(
                [far], [TWO], held, bests, rows, span, together=[(0,), (1, 3), (2,)] if last else None
            )
            sent += found
        sent = lax.ppermute(jnp.concatenate(sent, axis=1), BOTH, other_core)
        kept = jnp.maximum(jnp.concatenate(kept, axis=1), sent)
        for at, pairs in enumerate(rounds):
            found = lax.ppermute(kept[:, 2 * at * rows : 2 * (at + 1) * rows], BOTH, back(pairs))
            me = lax.axis_index(BOTH)
            sender = functools.reduce(jnp.logical_or, [me == source for source, _ in pairs])
            found = jnp.where(sender, found, -1.0)
            results += [found[:, :rows], lax.ppermute(found[:, rows:], BOTH, other_core)]
        from_x = lax.ppermute(bests[1], BOTH, first)
        results.append(from_x[:, :rows])
        onward = jnp.maximum(bests[2], from_x[:, rows:])
        results.append(lax.ppermute(onward, BOTH, second))
        return functools.reduce(jnp.maximum, results, bests[0]).reshape(rows)

    placed = (P(BOTH, None), P(BOTH, None), P(BOTH))
    return jax.shard_map(
        shards, mesh=mesh, in_specs=placed, out_specs=P(BOTH), check_vma=False
    )
```

```python
import functools

import jax
import jax.numpy as jnp
from jax import lax
from jax.experimental import pallas as pl
from jax.experimental.pallas import tpu as pltpu
from jax.sharding import PartitionSpec as P

EPSILON = 1e-06
EXTRA = 16
LANES = 128
TILE = 256
BOTH = ("dp", "grid")


def up(value, multiple):
    return -(-value // multiple) * multiple


def turned_to_column(row, rows):
    return jnp.broadcast_to(row, (LANES, row.shape[1])).T[:rows]


def codes(block, rows, span):
    parts = block[block.shape[0] - EXTRA :, : up(rows, LANES)].astype(jnp.float32)
    return parts[2:3] * (4.0 * span) + parts[0:1] * 256.0 + parts[1:2]


def prepare_kernel(
    embeddings_hbm,
    cluster_hbm,
    order_key_hbm,
    block,
    *refs,
):
    *parts_out, embeddings, cluster, order_key, arrived = refs
    copies = [
        pltpu.make_async_copy(source, target, arrived.at[at])
        for at, (source, target) in enumerate(
            (
                (embeddings_hbm, embeddings),
                (cluster_hbm, cluster),
                (order_key_hbm, order_key),
            )
        )
    ]
    for copy in copies:
        copy.start()
    for copy in copies:
        copy.wait()
    rows, width = embeddings.shape
    values = embeddings[...].astype(jnp.float32)
    scale = lax.rsqrt(jnp.sum(values * values, axis=1, keepdims=True) + EPSILON)
    block[0:rows, :] = (values * scale).astype(jnp.bfloat16)
    keys = order_key[...].reshape(1, rows)
    parts = [keys >> 8, keys & 255, cluster[...] + 1]
    parts = [part.astype(jnp.float32) for part in parts]
    parts = jnp.concatenate(parts + [jnp.zeros((EXTRA - 3, rows), jnp.float32)], axis=0)
    parts = jnp.concatenate([parts, jnp.zeros((EXTRA, width - rows), jnp.float32)], axis=1)
    block[rows : rows + EXTRA, :] = parts.astype(jnp.bfloat16)
    top = 0
    for out in parts_out:
        out[...] = block[top : top + out.shape[0], :]
        top += out.shape[0]


def prepare(embeddings, cluster, order_key, heights):
    rows, width = embeddings.shape
    inputs = (embeddings, cluster.reshape(1, rows), order_key)
    return pl.pallas_call(
        prepare_kernel,
        in_specs=[pl.BlockSpec(memory_space=pltpu.HBM)] * 3,
        out_shape=[
            jax.ShapeDtypeStruct((height, width), jnp.bfloat16)
            for height in (rows + EXTRA, *heights)
        ],
        scratch_shapes=[pltpu.VMEM(array.shape, array.dtype) for array in inputs]
        + [pltpu.SemaphoreType.DMA((3,))],
        compiler_params=pltpu.CompilerParams(vmem_limit_bytes=56 << 20),
        cost_estimate=pl.CostEstimate(flops=rows, bytes_accessed=rows, transcendentals=0),
    )(*inputs)


def row_from_partial(partial, rows):
    padded = up(rows, LANES)
    if padded != rows:
        partial = jnp.concatenate(
            [partial, jnp.zeros((padded - rows, LANES), partial.dtype)], axis=0
        )
    return jnp.max(partial.T, axis=0, keepdims=True)[:, :rows]


def meet(block, rows, span, held, held_codes, to_block, to_held):
    column = turned_to_column(codes(block, rows, span), rows)
    partial = jnp.full((rows, LANES), -1.0, jnp.float32)
    best_held = []
    for at in range(0, held.shape[0], TILE):
        tile = min(TILE, held.shape[0] - at)
        sims = lax.dot_general(
            block[0:rows, :],
            held[at : at + tile, :],
            (((1,), (1,)), ((), ())),
            preferred_element_type=jnp.float32,
        )
        for lane in range(0, tile, LANES):
            part = sims[:, lane : lane + LANES]
            gap = column - held_codes[:, at + lane : at + lane + LANES]
            if to_block and to_held:
                part = jnp.where(jnp.abs(gap) < span, part, -1.0)
                later = gap > 0.0
                partial = jnp.maximum(partial, jnp.where(later, part, -1.0))
                other = jnp.where(later, -1.0, part)
            elif to_block:
                partial = jnp.maximum(
                    partial, jnp.where((gap > 0.0) & (gap < span), part, -1.0)
                )
            else:
                other = jnp.where((gap < 0.0) & (gap > -span), part, -1.0)
            if to_held:
                best_held.append(jnp.max(other, axis=0, keepdims=True))
    return (
        row_from_partial(partial, rows) if to_block else None,
        jnp.concatenate(best_held, axis=1) if to_held else None,
    )


def assemble(whole, top, end, pieces):
    for piece in pieces:
        height = min(piece.shape[0], end - top)
        whole[top : top + height, :] = piece[0:height, :]
        top += height


def meet_kernel(rows, span, sizes, modes, groups, *refs):
    kinds = []
    for size in sizes:
        kinds.append(refs[:size])
        refs = refs[size:]
    blocks, holds, bests, outs, found, kept, scratch = kinds
    held, scratch = scratch[0], iter(scratch[1:])

    def whole(block):
        if len(block) == 1:
            return block[0]
        joined = next(scratch)
        assemble(joined, 0, joined.shape[0], block)
        return joined

    blocks = [whole(block) for block in regrouped(blocks, groups[0])]
    holds = regrouped(holds, groups[1])
    total = held.shape[0]
    row = []
    for at, block in enumerate(holds):
        assemble(held, at * rows, (at + 1) * rows, block)
        row.append(codes(block[-1], rows, span)[:, :rows])
    rest = total - len(holds) * rows
    if rest:
        held[total - rest :, :] = jnp.zeros((rest, held.shape[1]), held.dtype)
        row.append(jnp.zeros((1, rest), jnp.float32))
    row = jnp.concatenate(row, axis=1)
    best = None
    found = iter(found)
    for block, (to_block, to_held) in zip(blocks, modes):
        mine, theirs = meet(block, rows, span, held, row, to_block, to_held)
        if to_block:
            next(found)[...] = mine
        if to_held:
            best = theirs if best is None else jnp.maximum(best, theirs)
    if kept:
        top = 0
        for out in kept:
            out[...] = blocks[-1][top : top + out.shape[0], :]
            top += out.shape[0]
    parts = [best[:, at * rows : (at + 1) * rows] for at in range(len(holds))]
    if bests:
        parts = [jnp.maximum(part, earlier[...]) for part, earlier in zip(parts, bests)]
    for out, places in zip(outs, groups[2]):
        if len(places) == 1:
            out[...] = parts[places[0]]
        else:
            out[...] = jnp.concatenate([parts[place] for place in places], axis=1)


def regrouped(flat, lengths):
    flat = iter(flat)
    return [[next(flat) for _ in range(length)] for length in lengths]


def meeting(blocks, modes, holds, bests, rows, span, keep=(), together=None):
    width = blocks[0][0].shape[1]
    together = together or [(at,) for at in range(len(holds))]
    lengths = [[len(block) for block in some] for some in (blocks, holds)]
    flat = [[piece for block in some for piece in block] for some in (blocks, holds)]
    outs = [jax.ShapeDtypeStruct((1, rows * len(some)), jnp.float32) for some in together]
    found = [jax.ShapeDtypeStruct((1, rows), jnp.float32)] * sum(mode[0] for mode in modes)
    kept = [jax.ShapeDtypeStruct((height, width), jnp.bfloat16) for height in keep]
    split = sum(length > 1 for length in lengths[0])
    scratch = [pltpu.VMEM((up(len(holds) * rows, LANES), width), jnp.bfloat16)]
    scratch += [pltpu.VMEM((rows + EXTRA, width), jnp.bfloat16)] * split
    kinds = flat + [bests, outs, found, kept, scratch]
    results = pl.pallas_call(
        functools.partial(
            meet_kernel, rows, span, [len(kind) for kind in kinds], modes, lengths + [together]
        ),
        out_shape=outs + found + kept,
        scratch_shapes=scratch,
        compiler_params=pltpu.CompilerParams(vmem_limit_bytes=32 << 20),
        cost_estimate=pl.CostEstimate(flops=rows, bytes_accessed=rows, transcendentals=0),
    )(*flat[0], *flat[1], *bests)
    return regrouped(results, [len(outs), len(found), len(kept)])


OWN = (True, False)
HELD = (False, True)
TWO = (True, True)


def line_rounds(chips):
    if chips == 4:
        return [[(0, 2), (3, 1), (1, 0)], [(0, 3), (3, 2), (2, 1)]]
    rounds = []
    for shift in range(1, chips // 2 + 1):
        senders = chips // 2 if 2 * shift == chips else chips
        rounds.append([(s, (s + shift) % chips) for s in range(senders)])
    return rounds


def solution(mesh):
    groups, members = mesh.shape["dp"], mesh.shape["grid"]
    assert groups == 4 and members % 2 == 0
    chips = members // 2

    def everywhere(target):
        return [
            (p * members + g, a * members + b)
            for p in range(groups)
            for g in range(members)
            for a, b in [target(p, g)]
        ]

    other_core = everywhere(lambda p, g: (p, g ^ 1))
    first = everywhere(lambda p, g: (p ^ (1 + g % 2), g))
    second = everywhere(lambda p, g: (p ^ (2 - g % 2), g))

    rounds = line_rounds(chips)
    rounds += [[]] * (len(rounds) % 2)
    rounds = [
        [
            (p * members + 2 * s + c, p * members + 2 * t + c)
            for p in range(groups)
            for c in range(2)
            for s, t in rounds[at + c]
        ]
        for at in range(0, len(rounds), 2)
    ]

    def back(pairs):
        return [(target, source) for source, target in pairs]

    def shards(embeddings, cluster, order_key):
        rows = embeddings.shape[0]
        span = 256
        while span < rows * groups * members:
            span *= 2
        halves = (rows // 2, rows // 2 + EXTRA)
        block, *parts = prepare(embeddings, cluster, order_key, halves)
        own = [block]
        partner = lax.ppermute(block, BOTH, other_core)
        near = [[lax.ppermute(block, BOTH, pairs)] for pairs in rounds]
        from_first = [lax.ppermute(part, BOTH, first) for part in parts]
        near_other = [[lax.ppermute(partner, BOTH, pairs)] for pairs in rounds]
        from_corner = [lax.ppermute(part, BOTH, second) for part in from_first]
        from_second = [lax.ppermute(block, BOTH, second)]
        held = [own, from_first, from_second, from_corner]

        results, kept, sent = [], [], []
        bests, (mine, one), pieces = meeting(
            [own, near[0]], [OWN, TWO], held[:2], [], rows, span, keep=halves
        )
        results.append(mine)
        pieces = [lax.ppermute(piece, BOTH, other_core) for piece in pieces]
        more_bests, (mine, one_more), _ = meeting(
            [own, near[0]], [OWN, TWO], held[2:], [], rows, span
        )
        results.append(mine)
        kept.append(jnp.maximum(one, one_more))
        bests, found, _ = meeting(
            [[partner], pieces], [HELD, TWO], held, bests + more_bests, rows, span
        )
        sent += found
        rest = [blocks for both in zip(near, near_other) for blocks in both][1:]
        for at, one in enumerate(rest):
            (one,), bests = lax.optimization_barrier((one, bests))
            far = [lax.ppermute(one, BOTH, other_core)]
            bests, found, _ = meeting([[one]], [TWO], held, bests, rows, span)
            kept += found
            last = at == len(rest) - 1
            bests, found, _ = meeting(
                [far], [TWO], held, bests, rows, span, together=[(0,), (1, 3), (2,)] if last else None
            )
            sent += found
        sent = lax.ppermute(jnp.concatenate(sent, axis=1), BOTH, other_core)
        kept = jnp.maximum(jnp.concatenate(kept, axis=1), sent)
        for at, pairs in enumerate(rounds):
            found = lax.ppermute(kept[:, 2 * at * rows : 2 * (at + 1) * rows], BOTH, back(pairs))
            me = lax.axis_index(BOTH)
            sender = functools.reduce(jnp.logical_or, [me == source for source, _ in pairs])
            found = jnp.where(sender, found, -1.0)
            results += [found[:, :rows], lax.ppermute(found[:, rows:], BOTH, other_core)]
        from_x = lax.ppermute(bests[1], BOTH, first)
        results.append(from_x[:, :rows])
        onward = jnp.maximum(bests[2], from_x[:, rows:])
        results.append(lax.ppermute(onward, BOTH, second))
        return functools.reduce(jnp.maximum, results, bests[0]).reshape(rows)

    placed = (P(BOTH, None), P(BOTH, None), P(BOTH))
    return jax.shard_map(
        shards, mesh=mesh, in_specs=placed, out_specs=P(BOTH), check_vma=False
    )
```

```python
import functools

import jax
import jax.numpy as jnp
from jax import lax
from jax.experimental import pallas as pl
from jax.experimental.pallas import tpu as pltpu
from jax.sharding import PartitionSpec as P

EPSILON = 1e-06
EXTRA = 16
LANES = 128
TILE = 256
BOTH = ("dp", "grid")


def up(value, multiple):
    return -(-value // multiple) * multiple


def turned_to_column(row, rows):
    return jnp.broadcast_to(row, (LANES, row.shape[1])).T[:rows]


def codes(block, rows, span):
    parts = block[block.shape[0] - EXTRA :, : up(rows, LANES)].astype(jnp.float32)
    return parts[2:3] * (4.0 * span) + parts[0:1] * 256.0 + parts[1:2]


def prepare_kernel(span, embeddings, named, block, *parts_out):
    rows, width = embeddings.shape
    values = embeddings[...].astype(jnp.float32)
    scale = lax.rsqrt(jnp.sum(values * values, axis=1, keepdims=True) + EPSILON)
    block[0:rows, :] = (values * scale).astype(jnp.bfloat16)
    names = named[...].reshape(1, rows)
    keys = names & (span - 1)
    parts = [keys >> 8, keys & 255, (names >> (span.bit_length() - 1)) + 1]
    parts = [part.astype(jnp.float32) for part in parts]
    parts = jnp.concatenate(parts + [jnp.zeros((EXTRA - 3, rows), jnp.float32)], axis=0)
    parts = jnp.concatenate([parts, jnp.zeros((EXTRA, width - rows), jnp.float32)], axis=1)
    block[rows : rows + EXTRA, :] = parts.astype(jnp.bfloat16)
    top = 0
    for out in parts_out:
        out[...] = block[top : top + out.shape[0], :]
        top += out.shape[0]


def prepare(embeddings, cluster, order_key, span, heights):
    rows, width = embeddings.shape
    named = cluster[:, 0] * span + order_key
    return pl.pallas_call(
        functools.partial(prepare_kernel, span),
        out_shape=[
            jax.ShapeDtypeStruct((height, width), jnp.bfloat16)
            for height in (rows + EXTRA, *heights)
        ],
        compiler_params=pltpu.CompilerParams(vmem_limit_bytes=16 << 20),
        cost_estimate=pl.CostEstimate(flops=rows, bytes_accessed=rows, transcendentals=0),
    )(embeddings, named)


def row_from_partial(partial, rows):
    padded = up(rows, LANES)
    if padded != rows:
        partial = jnp.concatenate(
            [partial, jnp.zeros((padded - rows, LANES), partial.dtype)], axis=0
        )
    return jnp.max(partial.T, axis=0, keepdims=True)[:, :rows]


def meet(block, rows, span, held, held_codes, to_block, to_held):
    column = turned_to_column(codes(block, rows, span), rows)
    partial = jnp.full((rows, LANES), -1.0, jnp.float32)
    best_held = []
    for at in range(0, held.shape[0], TILE):
        tile = min(TILE, held.shape[0] - at)
        sims = lax.dot_general(
            block[0:rows, :],
            held[at : at + tile, :],
            (((1,), (1,)), ((), ())),
            preferred_element_type=jnp.float32,
        )
        for lane in range(0, tile, LANES):
            part = sims[:, lane : lane + LANES]
            gap = column - held_codes[:, at + lane : at + lane + LANES]
            if to_block and to_held:
                part = jnp.where(jnp.abs(gap) < span, part, -1.0)
                later = gap > 0.0
                partial = jnp.maximum(partial, jnp.where(later, part, -1.0))
                other = jnp.where(later, -1.0, part)
            elif to_block:
                partial = jnp.maximum(
                    partial, jnp.where((gap > 0.0) & (gap < span), part, -1.0)
                )
            else:
                other = jnp.where((gap < 0.0) & (gap > -span), part, -1.0)
            if to_held:
                best_held.append(jnp.max(other, axis=0, keepdims=True))
    return (
        row_from_partial(partial, rows) if to_block else None,
        jnp.concatenate(best_held, axis=1) if to_held else None,
    )


def assemble(whole, top, end, pieces):
    for piece in pieces:
        height = min(piece.shape[0], end - top)
        whole[top : top + height, :] = piece[0:height, :]
        top += height


def meet_kernel(rows, span, sizes, modes, groups, *refs):
    kinds = []
    for size in sizes:
        kinds.append(refs[:size])
        refs = refs[size:]
    blocks, holds, bests, outs, found, kept, scratch = kinds
    held, scratch = scratch[0], iter(scratch[1:])

    def whole(block):
        if len(block) == 1:
            return block[0]
        joined = next(scratch)
        assemble(joined, 0, joined.shape[0], block)
        return joined

    blocks = [whole(block) for block in regrouped(blocks, groups[0])]
    holds = regrouped(holds, groups[1])
    total = held.shape[0]
    row = []
    for at, block in enumerate(holds):
        assemble(held, at * rows, (at + 1) * rows, block)
        row.append(codes(block[-1], rows, span)[:, :rows])
    rest = total - len(holds) * rows
    if rest:
        held[total - rest :, :] = jnp.zeros((rest, held.shape[1]), held.dtype)
        row.append(jnp.zeros((1, rest), jnp.float32))
    row = jnp.concatenate(row, axis=1)
    best = None
    found = iter(found)
    for block, (to_block, to_held) in zip(blocks, modes):
        mine, theirs = meet(block, rows, span, held, row, to_block, to_held)
        if to_block:
            next(found)[...] = mine
        if to_held:
            best = theirs if best is None else jnp.maximum(best, theirs)
    if kept:
        top = 0
        for out in kept:
            out[...] = blocks[-1][top : top + out.shape[0], :]
            top += out.shape[0]
    parts = [best[:, at * rows : (at + 1) * rows] for at in range(len(holds))]
    if bests:
        parts = [jnp.maximum(part, earlier[...]) for part, earlier in zip(parts, bests)]
    for out, places in zip(outs, groups[2]):
        if len(places) == 1:
            out[...] = parts[places[0]]
        else:
            out[...] = jnp.concatenate([parts[place] for place in places], axis=1)


def regrouped(flat, lengths):
    flat = iter(flat)
    return [[next(flat) for _ in range(length)] for length in lengths]


def meeting(blocks, modes, holds, bests, rows, span, keep=(), together=None):
    width = blocks[0][0].shape[1]
    together = together or [(at,) for at in range(len(holds))]
    lengths = [[len(block) for block in some] for some in (blocks, holds)]
    flat = [[piece for block in some for piece in block] for some in (blocks, holds)]
    outs = [jax.ShapeDtypeStruct((1, rows * len(some)), jnp.float32) for some in together]
    found = [jax.ShapeDtypeStruct((1, rows), jnp.float32)] * sum(mode[0] for mode in modes)
    kept = [jax.ShapeDtypeStruct((height, width), jnp.bfloat16) for height in keep]
    split = sum(length > 1 for length in lengths[0])
    scratch = [pltpu.VMEM((up(len(holds) * rows, LANES), width), jnp.bfloat16)]
    scratch += [pltpu.VMEM((rows + EXTRA, width), jnp.bfloat16)] * split
    kinds = flat + [bests, outs, found, kept, scratch]
    results = pl.pallas_call(
        functools.partial(
            meet_kernel, rows, span, [len(kind) for kind in kinds], modes, lengths + [together]
        ),
        out_shape=outs + found + kept,
        scratch_shapes=scratch,
        compiler_params=pltpu.CompilerParams(vmem_limit_bytes=32 << 20),
        cost_estimate=pl.CostEstimate(flops=rows, bytes_accessed=rows, transcendentals=0),
    )(*flat[0], *flat[1], *bests)
    return regrouped(results, [len(outs), len(found), len(kept)])


OWN = (True, False)
HELD = (False, True)
TWO = (True, True)


def line_rounds(chips):
    if chips == 4:
        return [[(0, 2), (3, 1), (1, 0)], [(0, 3), (3, 2), (2, 1)]]
    rounds = []
    for shift in range(1, chips // 2 + 1):
        senders = chips // 2 if 2 * shift == chips else chips
        rounds.append([(s, (s + shift) % chips) for s in range(senders)])
    return rounds


def solution(mesh):
    groups, members = mesh.shape["dp"], mesh.shape["grid"]
    assert groups == 4 and members % 2 == 0
    chips = members // 2

    def everywhere(target):
        return [
            (p * members + g, a * members + b)
            for p in range(groups)
            for g in range(members)
            for a, b in [target(p, g)]
        ]

    other_core = everywhere(lambda p, g: (p, g ^ 1))
    first = everywhere(lambda p, g: (p ^ (1 + g % 2), g))
    second = everywhere(lambda p, g: (p ^ (2 - g % 2), g))

    rounds = line_rounds(chips)
    rounds += [[]] * (len(rounds) % 2)
    rounds = [
        [
            (p * members + 2 * s + c, p * members + 2 * t + c)
            for p in range(groups)
            for c in range(2)
            for s, t in rounds[at + c]
        ]
        for at in range(0, len(rounds), 2)
    ]

    def back(pairs):
        return [(target, source) for source, target in pairs]

    def shards(embeddings, cluster, order_key):
        rows = embeddings.shape[0]
        span = 256
        while span < rows * groups * members:
            span *= 2
        halves = (rows // 2, rows // 2 + EXTRA)
        block, *parts = prepare(embeddings, cluster, order_key, span, halves)
        own = [block]
        partner = lax.ppermute(block, BOTH, other_core)
        near = [[lax.ppermute(block, BOTH, pairs)] for pairs in rounds]
        from_first = [lax.ppermute(part, BOTH, first) for part in parts]
        near_other = [[lax.ppermute(partner, BOTH, pairs)] for pairs in rounds]
        from_corner = [lax.ppermute(part, BOTH, second) for part in from_first]
        from_second = [lax.ppermute(block, BOTH, second)]
        held = [own, from_first, from_second, from_corner]

        results, kept, sent = [], [], []
        bests, (mine, one), pieces = meeting(
            [own, near[0]], [OWN, TWO], held[:2], [], rows, span, keep=halves
        )
        results.append(mine)
        pieces = [lax.ppermute(piece, BOTH, other_core) for piece in pieces]
        more_bests, (mine, one_more), _ = meeting(
            [own, near[0]], [OWN, TWO], held[2:], [], rows, span
        )
        results.append(mine)
        kept.append(jnp.maximum(one, one_more))
        bests, found, _ = meeting(
            [[partner], pieces], [HELD, TWO], held, bests + more_bests, rows, span
        )
        sent += found
        rest = [blocks for both in zip(near, near_other) for blocks in both][1:]
        for at, one in enumerate(rest):
            (one,), bests = lax.optimization_barrier((one, bests))
            far = [lax.ppermute(one, BOTH, other_core)]
            bests, found, _ = meeting([[one]], [TWO], held, bests, rows, span)
            kept += found
            last = at == len(rest) - 1
            bests, found, _ = meeting(
                [far], [TWO], held, bests, rows, span, together=[(0,), (1, 3), (2,)] if last else None
            )
            sent += found
        sent = lax.ppermute(jnp.concatenate(sent, axis=1), BOTH, other_core)
        kept = jnp.maximum(jnp.concatenate(kept, axis=1), sent)
        for at, pairs in enumerate(rounds):
            found = lax.ppermute(kept[:, 2 * at * rows : 2 * (at + 1) * rows], BOTH, back(pairs))
            me = lax.axis_index(BOTH)
            sender = functools.reduce(jnp.logical_or, [me == source for source, _ in pairs])
            found = jnp.where(sender, found, -1.0)
            results += [found[:, :rows], lax.ppermute(found[:, rows:], BOTH, other_core)]
        from_x = lax.ppermute(bests[1], BOTH, first)
        results.append(from_x[:, :rows])
        onward = jnp.maximum(bests[2], from_x[:, rows:])
        results.append(lax.ppermute(onward, BOTH, second))
        return functools.reduce(jnp.maximum, results, bests[0]).reshape(rows)

    placed = (P(BOTH, None), P(BOTH, None), P(BOTH))
    return jax.shard_map(
        shards, mesh=mesh, in_specs=placed, out_specs=P(BOTH), check_vma=False
    )
```

```python
import functools

import jax
import jax.numpy as jnp
from jax import lax
from jax.experimental import pallas as pl
from jax.experimental.pallas import tpu as pltpu
from jax.sharding import PartitionSpec as P

EPSILON = 1e-06
EXTRA = 16
LANES = 128
TILE = 256
BOTH = ("dp", "grid")


def up(value, multiple):
    return -(-value // multiple) * multiple


def turned_to_column(row, rows):
    return jnp.broadcast_to(row, (LANES, row.shape[1])).T[:rows]


def codes(block, rows, span):
    parts = block[block.shape[0] - EXTRA :, : up(rows, LANES)].astype(jnp.float32)
    return parts[2:3] * (4.0 * span) + parts[0:1] * 256.0 + parts[1:2]


def prepare_kernel(span, embeddings, named, block, *parts_out):
    rows, width = embeddings.shape
    values = embeddings[...].astype(jnp.float32)
    scale = lax.rsqrt(jnp.sum(values * values, axis=1, keepdims=True) + EPSILON)
    block[0:rows, :] = (values * scale).astype(jnp.bfloat16)
    names = named[...].reshape(1, rows)
    keys = names & (span - 1)
    parts = [keys >> 8, keys & 255, names >> (span.bit_length() - 1)]
    parts = [part.astype(jnp.float32) for part in parts]
    parts = jnp.concatenate(parts + [jnp.zeros((EXTRA - 3, rows), jnp.float32)], axis=0)
    parts = jnp.concatenate([parts, jnp.zeros((EXTRA, width - rows), jnp.float32)], axis=1)
    block[rows : rows + EXTRA, :] = parts.astype(jnp.bfloat16)
    top = 0
    for out in parts_out:
        out[...] = block[top : top + out.shape[0], :]
        top += out.shape[0]


def prepare(embeddings, named, span, heights=()):
    rows, width = embeddings.shape
    return pl.pallas_call(
        functools.partial(prepare_kernel, span),
        out_shape=[
            jax.ShapeDtypeStruct((height, width), jnp.bfloat16)
            for height in (rows + EXTRA, *heights)
        ],
        compiler_params=pltpu.CompilerParams(vmem_limit_bytes=16 << 20),
        cost_estimate=pl.CostEstimate(flops=rows, bytes_accessed=rows, transcendentals=0),
    )(embeddings, named)


def row_from_partial(partial, rows):
    padded = up(rows, LANES)
    if padded != rows:
        partial = jnp.concatenate(
            [partial, jnp.zeros((padded - rows, LANES), partial.dtype)], axis=0
        )
    return jnp.max(partial.T, axis=0, keepdims=True)[:, :rows]


def meet(block, rows, span, held, held_codes, to_block, to_held):
    column = turned_to_column(codes(block, rows, span), rows)
    partial = jnp.full((rows, LANES), -1.0, jnp.float32)
    best_held = []
    for at in range(0, held.shape[0], TILE):
        tile = min(TILE, held.shape[0] - at)
        sims = lax.dot_general(
            block[0:rows, :],
            held[at : at + tile, :],
            (((1,), (1,)), ((), ())),
            preferred_element_type=jnp.float32,
        )
        for lane in range(0, tile, LANES):
            part = sims[:, lane : lane + LANES]
            gap = column - held_codes[:, at + lane : at + lane + LANES]
            if to_block and to_held:
                part = jnp.where(jnp.abs(gap) < span, part, -1.0)
                later = gap > 0.0
                partial = jnp.maximum(partial, jnp.where(later, part, -1.0))
                other = jnp.where(later, -1.0, part)
            elif to_block:
                partial = jnp.maximum(
                    partial, jnp.where((gap > 0.0) & (gap < span), part, -1.0)
                )
            else:
                other = jnp.where((gap < 0.0) & (gap > -span), part, -1.0)
            if to_held:
                best_held.append(jnp.max(other, axis=0, keepdims=True))
    return (
        row_from_partial(partial, rows) if to_block else None,
        jnp.concatenate(best_held, axis=1) if to_held else None,
    )


def assemble(whole, top, end, pieces):
    for piece in pieces:
        height = min(piece.shape[0], end - top)
        whole[top : top + height, :] = piece[0:height, :]
        top += height


def meet_kernel(rows, span, sizes, modes, groups, *refs):
    kinds = []
    for size in sizes:
        kinds.append(refs[:size])
        refs = refs[size:]
    blocks, holds, bests, outs, found, kept, scratch = kinds
    held, scratch = scratch[0], iter(scratch[1:])

    def whole(block):
        if len(block) == 1:
            return block[0]
        joined = next(scratch)
        assemble(joined, 0, joined.shape[0], block)
        return joined

    blocks = [whole(block) for block in regrouped(blocks, groups[0])]
    holds = regrouped(holds, groups[1])
    total = held.shape[0]
    row = []
    for at, block in enumerate(holds):
        assemble(held, at * rows, (at + 1) * rows, block)
        row.append(codes(block[-1], rows, span)[:, :rows])
    rest = total - len(holds) * rows
    if rest:
        held[total - rest :, :] = jnp.zeros((rest, held.shape[1]), held.dtype)
        row.append(jnp.zeros((1, rest), jnp.float32))
    row = jnp.concatenate(row, axis=1)
    best = None
    found = iter(found)
    for block, (to_block, to_held) in zip(blocks, modes):
        mine, theirs = meet(block, rows, span, held, row, to_block, to_held)
        if to_block:
            next(found)[...] = mine
        if to_held:
            best = theirs if best is None else jnp.maximum(best, theirs)
    if kept:
        top = 0
        for out in kept:
            out[...] = blocks[-1][top : top + out.shape[0], :]
            top += out.shape[0]
    parts = [best[:, at * rows : (at + 1) * rows] for at in range(len(holds))]
    if bests:
        parts = [jnp.maximum(part, earlier[...]) for part, earlier in zip(parts, bests)]
    for out, places in zip(outs, groups[2]):
        if len(places) == 1:
            out[...] = parts[places[0]]
        else:
            out[...] = jnp.concatenate([parts[place] for place in places], axis=1)


def regrouped(flat, lengths):
    flat = iter(flat)
    return [[next(flat) for _ in range(length)] for length in lengths]


def meeting(blocks, modes, holds, bests, rows, span, keep=(), together=None):
    width = blocks[0][0].shape[1]
    together = together or [(at,) for at in range(len(holds))]
    lengths = [[len(block) for block in some] for some in (blocks, holds)]
    flat = [[piece for block in some for piece in block] for some in (blocks, holds)]
    outs = [jax.ShapeDtypeStruct((1, rows * len(some)), jnp.float32) for some in together]
    found = [jax.ShapeDtypeStruct((1, rows), jnp.float32)] * sum(mode[0] for mode in modes)
    kept = [jax.ShapeDtypeStruct((height, width), jnp.bfloat16) for height in keep]
    split = sum(length > 1 for length in lengths[0])
    scratch = [pltpu.VMEM((up(len(holds) * rows, LANES), width), jnp.bfloat16)]
    scratch += [pltpu.VMEM((rows + EXTRA, width), jnp.bfloat16)] * split
    kinds = flat + [bests, outs, found, kept, scratch]
    results = pl.pallas_call(
        functools.partial(
            meet_kernel, rows, span, [len(kind) for kind in kinds], modes, lengths + [together]
        ),
        out_shape=outs + found + kept,
        scratch_shapes=scratch,
        compiler_params=pltpu.CompilerParams(vmem_limit_bytes=32 << 20),
        cost_estimate=pl.CostEstimate(flops=rows, bytes_accessed=rows, transcendentals=0),
    )(*flat[0], *flat[1], *bests)
    return regrouped(results, [len(outs), len(found), len(kept)])


OWN = (True, False)
HELD = (False, True)
TWO = (True, True)


def line_rounds(chips):
    if chips == 4:
        return [[(0, 2), (3, 1), (1, 0)], [(0, 3), (3, 2), (2, 1)]]
    rounds = []
    for shift in range(1, chips // 2 + 1):
        senders = chips // 2 if 2 * shift == chips else chips
        rounds.append([(s, (s + shift) % chips) for s in range(senders)])
    return rounds


def solution(mesh):
    groups, members = mesh.shape["dp"], mesh.shape["grid"]
    assert groups == 4 and members % 2 == 0
    chips = members // 2

    def everywhere(target):
        return [
            (p * members + g, a * members + b)
            for p in range(groups)
            for g in range(members)
            for a, b in [target(p, g)]
        ]

    other_core = everywhere(lambda p, g: (p, g ^ 1))
    first = everywhere(lambda p, g: (p ^ (1 + g % 2), g))
    second = everywhere(lambda p, g: (p ^ (2 - g % 2), g))

    rounds = line_rounds(chips)
    rounds += [[]] * (len(rounds) % 2)
    rounds = [
        [
            (p * members + 2 * s + c, p * members + 2 * t + c)
            for p in range(groups)
            for c in range(2)
            for s, t in rounds[at + c]
        ]
        for at in range(0, len(rounds), 2)
    ]

    def back(pairs):
        return [(target, source) for source, target in pairs]

    def shards(embeddings, cluster, order_key):
        rows = embeddings.shape[0]
        span = 256
        while span < rows * groups * members:
            span *= 2
        heights = (rows // 5 * 4, rows // 5 + EXTRA)
        named = (cluster[:, 0] + 1) * span + order_key
        partner = lax.ppermute(embeddings, BOTH, other_core)
        raw = [lax.ppermute(embeddings, BOTH, pairs) for pairs in rounds]
        block, *parts = prepare(embeddings, named, span, heights)
        own = [block]
        from_first = [lax.ppermute(part, BOTH, first) for part in parts]
        from_second = [lax.ppermute(block, BOTH, second)]
        (partner,) = prepare(partner, lax.ppermute(named, BOTH, other_core), span)
        near_other = [[lax.ppermute(partner, BOTH, pairs)] for pairs in rounds]
        from_corner = [lax.ppermute(part, BOTH, second) for part in from_first]
        near = [
            prepare(rows_of, lax.ppermute(named, BOTH, pairs), span, heights)
            for rows_of, pairs in zip(raw, rounds)
        ]
        pieces = [lax.ppermute(piece, BOTH, other_core) for piece in near[0][1:]]
        near = [blocks[:1] for blocks in near]
        held = [own, from_first, from_second, from_corner]

        results, kept, sent = [], [], []
        bests, (mine, one), _ = meeting(
            [own, near[0]], [OWN, TWO], held[:3], [], rows, span
        )
        results.append(mine)
        bests, (other,), _ = meeting(
            [[partner], pieces], [HELD, TWO], held[:3], bests, rows, span
        )
        corner_best, (mine, one_more, other_more), _ = meeting(
            [own, near[0], [partner], pieces], [OWN, TWO, HELD, TWO], held[3:], [], rows, span
        )
        results.append(mine)
        bests += corner_best
        kept.append(jnp.maximum(one, one_more))
        sent.append(jnp.maximum(other, other_more))
        rest = [blocks for both in zip(near, near_other) for blocks in both][1:]
        for at, one in enumerate(rest):
            (one,), bests = lax.optimization_barrier((one, bests))
            far = [lax.ppermute(one, BOTH, other_core)]
            bests, found, _ = meeting([[one]], [TWO], held, bests, rows, span)
            kept += found
            last = at == len(rest) - 1
            bests, found, _ = meeting(
                [far], [TWO], held, bests, rows, span, together=[(0,), (1, 3), (2,)] if last else None
            )
            sent += found
        sent = lax.ppermute(jnp.concatenate(sent, axis=1), BOTH, other_core)
        kept = jnp.maximum(jnp.concatenate(kept, axis=1), sent)
        for at, pairs in enumerate(rounds):
            found = lax.ppermute(kept[:, 2 * at * rows : 2 * (at + 1) * rows], BOTH, back(pairs))
            me = lax.axis_index(BOTH)
            sender = functools.reduce(jnp.logical_or, [me == source for source, _ in pairs])
            found = jnp.where(sender, found, -1.0)
            results += [found[:, :rows], lax.ppermute(found[:, rows:], BOTH, other_core)]
        from_x = lax.ppermute(bests[1], BOTH, first)
        results.append(from_x[:, :rows])
        onward = jnp.maximum(bests[2], from_x[:, rows:])
        results.append(lax.ppermute(onward, BOTH, second))
        return functools.reduce(jnp.maximum, results, bests[0]).reshape(rows)

    placed = (P(BOTH, None), P(BOTH, None), P(BOTH))
    return jax.shard_map(
        shards, mesh=mesh, in_specs=placed, out_specs=P(BOTH), check_vma=False
    )
```

```python
import functools

import jax
import jax.numpy as jnp
from jax import lax
from jax.experimental import pallas as pl
from jax.experimental.pallas import tpu as pltpu
from jax.sharding import PartitionSpec as P

EPSILON = 1e-06
EXTRA = 16
LANES = 128
TILE = 256
BOTH = ("dp", "grid")


def up(value, multiple):
    return -(-value // multiple) * multiple


def turned_to_column(row, rows):
    return jnp.broadcast_to(row, (LANES, row.shape[1])).T[:rows]


def codes(block, rows, span):
    parts = block[block.shape[0] - EXTRA :, : up(rows, LANES)].astype(jnp.float32)
    return parts[2:3] * (4.0 * span) + parts[0:1] * 256.0 + parts[1:2]


def unit_rows(rows, out):
    values = rows[...].astype(jnp.float32)
    scale = lax.rsqrt(jnp.sum(values * values, axis=1, keepdims=True) + EPSILON)
    out[0 : rows.shape[0], :] = (values * scale).astype(jnp.bfloat16)


def give_parts(block, outs):
    top = 0
    for out in outs:
        out[...] = block[top : top + out.shape[0], :]
        top += out.shape[0]


def prepare_kernel(span, embeddings, named, block, *parts_out):
    rows, width = embeddings.shape
    unit_rows(embeddings, block)
    names = named[...].reshape(1, rows)
    keys = names & (span - 1)
    parts = [keys >> 8, keys & 255, names >> (span.bit_length() - 1)]
    parts = [part.astype(jnp.float32) for part in parts]
    parts = jnp.concatenate(parts + [jnp.zeros((EXTRA - 3, rows), jnp.float32)], axis=0)
    parts = jnp.concatenate([parts, jnp.zeros((EXTRA, width - rows), jnp.float32)], axis=1)
    block[rows : rows + EXTRA, :] = parts.astype(jnp.bfloat16)
    codes_out, *parts_out = parts_out
    codes_out[0:EXTRA, :] = block[rows : rows + EXTRA, :]
    give_parts(block, parts_out)


def complete_kernel(rows_of, named, block, *parts_out):
    unit_rows(rows_of, block)
    block[rows_of.shape[0] :, :] = named[0:EXTRA, :]
    give_parts(block, parts_out)


def with_units(kernel, rows_of, named, heights=()):
    rows, width = rows_of.shape
    return pl.pallas_call(
        kernel,
        out_shape=[
            jax.ShapeDtypeStruct((height, width), jnp.bfloat16)
            for height in (rows + EXTRA, *heights)
        ],
        compiler_params=pltpu.CompilerParams(vmem_limit_bytes=16 << 20),
        cost_estimate=pl.CostEstimate(flops=rows, bytes_accessed=rows, transcendentals=0),
    )(rows_of, named)


def row_from_partial(partial, rows):
    padded = up(rows, LANES)
    if padded != rows:
        partial = jnp.concatenate(
            [partial, jnp.zeros((padded - rows, LANES), partial.dtype)], axis=0
        )
    return jnp.max(partial.T, axis=0, keepdims=True)[:, :rows]


def meet(block, rows, span, held, held_codes, to_block, to_held):
    column = turned_to_column(codes(block, rows, span), rows)
    partial = jnp.full((rows, LANES), -1.0, jnp.float32)
    best_held = []
    for at in range(0, held.shape[0], TILE):
        tile = min(TILE, held.shape[0] - at)
        sims = lax.dot_general(
            block[0:rows, :],
            held[at : at + tile, :],
            (((1,), (1,)), ((), ())),
            preferred_element_type=jnp.float32,
        )
        for lane in range(0, tile, LANES):
            part = sims[:, lane : lane + LANES]
            gap = column - held_codes[:, at + lane : at + lane + LANES]
            if to_block and to_held:
                part = jnp.where(jnp.abs(gap) < span, part, -1.0)
                later = gap > 0.0
                partial = jnp.maximum(partial, jnp.where(later, part, -1.0))
                other = jnp.where(later, -1.0, part)
            elif to_block:
                partial = jnp.maximum(
                    partial, jnp.where((gap > 0.0) & (gap < span), part, -1.0)
                )
            else:
                other = jnp.where((gap < 0.0) & (gap > -span), part, -1.0)
            if to_held:
                best_held.append(jnp.max(other, axis=0, keepdims=True))
    return (
        row_from_partial(partial, rows) if to_block else None,
        jnp.concatenate(best_held, axis=1) if to_held else None,
    )


def assemble(whole, top, end, pieces):
    for piece in pieces:
        height = min(piece.shape[0], end - top)
        if height == 0:
            break
        whole[top : top + height, :] = piece[0:height, :]
        top += height


def meet_kernel(rows, span, sizes, modes, groups, *refs):
    kinds = []
    for size in sizes:
        kinds.append(refs[:size])
        refs = refs[size:]
    blocks, holds, bests, outs, found, kept, scratch = kinds
    held, scratch = scratch[0], iter(scratch[1:])

    def whole(block):
        if len(block) == 1:
            return block[0]
        joined = next(scratch)
        assemble(joined, 0, joined.shape[0], block)
        return joined

    blocks = [whole(block) for block in regrouped(blocks, groups[0])]
    holds = regrouped(holds, groups[1])
    total = held.shape[0]
    row = []
    for at, block in enumerate(holds):
        assemble(held, at * rows, (at + 1) * rows, block)
        row.append(codes(block[-1], rows, span)[:, :rows])
    rest = total - len(holds) * rows
    if rest:
        held[total - rest :, :] = jnp.zeros((rest, held.shape[1]), held.dtype)
        row.append(jnp.zeros((1, rest), jnp.float32))
    row = jnp.concatenate(row, axis=1)
    best = None
    found = iter(found)
    for block, (to_block, to_held) in zip(blocks, modes):
        mine, theirs = meet(block, rows, span, held, row, to_block, to_held)
        if to_block:
            next(found)[...] = mine
        if to_held:
            best = theirs if best is None else jnp.maximum(best, theirs)
    if kept:
        top = 0
        for out in kept:
            out[...] = blocks[-1][top : top + out.shape[0], :]
            top += out.shape[0]
    parts = [best[:, at * rows : (at + 1) * rows] for at in range(len(holds))]
    if bests:
        parts = [jnp.maximum(part, earlier[...]) for part, earlier in zip(parts, bests)]
    for out, places in zip(outs, groups[2]):
        if len(places) == 1:
            out[...] = parts[places[0]]
        else:
            out[...] = jnp.concatenate([parts[place] for place in places], axis=1)


def regrouped(flat, lengths):
    flat = iter(flat)
    return [[next(flat) for _ in range(length)] for length in lengths]


def meeting(blocks, modes, holds, bests, rows, span, keep=(), together=None):
    width = blocks[0][0].shape[1]
    together = together or [(at,) for at in range(len(holds))]
    lengths = [[len(block) for block in some] for some in (blocks, holds)]
    flat = [[piece for block in some for piece in block] for some in (blocks, holds)]
    outs = [jax.ShapeDtypeStruct((1, rows * len(some)), jnp.float32) for some in together]
    found = [jax.ShapeDtypeStruct((1, rows), jnp.float32)] * sum(mode[0] for mode in modes)
    kept = [jax.ShapeDtypeStruct((height, width), jnp.bfloat16) for height in keep]
    split = sum(length > 1 for length in lengths[0])
    scratch = [pltpu.VMEM((up(len(holds) * rows, LANES), width), jnp.bfloat16)]
    scratch += [pltpu.VMEM((rows + EXTRA, width), jnp.bfloat16)] * split
    kinds = flat + [bests, outs, found, kept, scratch]
    results = pl.pallas_call(
        functools.partial(
            meet_kernel, rows, span, [len(kind) for kind in kinds], modes, lengths + [together]
        ),
        out_shape=outs + found + kept,
        scratch_shapes=scratch,
        compiler_params=pltpu.CompilerParams(vmem_limit_bytes=32 << 20),
        cost_estimate=pl.CostEstimate(flops=rows, bytes_accessed=rows, transcendentals=0),
    )(*flat[0], *flat[1], *bests)
    return regrouped(results, [len(outs), len(found), len(kept)])


OWN = (True, False)
HELD = (False, True)
TWO = (True, True)


def line_rounds(chips):
    if chips == 4:
        return [[(0, 2), (3, 1), (1, 0)], [(0, 3), (3, 2), (2, 1)]]
    rounds = []
    for shift in range(1, chips // 2 + 1):
        senders = chips // 2 if 2 * shift == chips else chips
        rounds.append([(s, (s + shift) % chips) for s in range(senders)])
    return rounds


def solution(mesh):
    groups, members = mesh.shape["dp"], mesh.shape["grid"]
    assert groups == 4 and members % 2 == 0
    chips = members // 2

    def everywhere(target):
        return [
            (p * members + g, a * members + b)
            for p in range(groups)
            for g in range(members)
            for a, b in [target(p, g)]
        ]

    other_core = everywhere(lambda p, g: (p, g ^ 1))
    first = everywhere(lambda p, g: (p ^ (1 + g % 2), g))
    second = everywhere(lambda p, g: (p ^ (2 - g % 2), g))

    rounds = line_rounds(chips)
    rounds += [[]] * (len(rounds) % 2)
    rounds = [
        [
            (p * members + 2 * s + c, p * members + 2 * t + c)
            for p in range(groups)
            for c in range(2)
            for s, t in rounds[at + c]
        ]
        for at in range(0, len(rounds), 2)
    ]

    def back(pairs):
        return [(target, source) for source, target in pairs]

    def shards(embeddings, cluster, order_key):
        rows = embeddings.shape[0]
        span = 256
        while span < rows * groups * members:
            span *= 2
        heights = (rows - 16, 16 + EXTRA)
        named = (cluster[:, 0] + 1) * span + order_key
        partner = lax.ppermute(embeddings, BOTH, other_core)
        raw = [lax.ppermute(embeddings, BOTH, pairs) for pairs in rounds]
        block, codes_of, *parts = with_units(
            functools.partial(prepare_kernel, span), embeddings, named, (EXTRA,) + heights
        )
        own = [block]
        from_first = [lax.ppermute(part, BOTH, first) for part in parts]
        from_second = [lax.ppermute(block, BOTH, second)]
        (partner,) = with_units(complete_kernel, partner, lax.ppermute(codes_of, BOTH, other_core))
        near_other = [[lax.ppermute(partner, BOTH, pairs)] for pairs in rounds]
        from_corner = [lax.ppermute(part, BOTH, second) for part in from_first]
        near = [
            with_units(complete_kernel, rows_of, lax.ppermute(codes_of, BOTH, pairs), (rows, EXTRA))
            for rows_of, pairs in zip(raw, rounds)
        ]
        pieces = [lax.ppermute(piece, BOTH, other_core) for piece in near[0][1:]]
        near = [blocks[:1] for blocks in near]
        held = [own, from_first, from_second, from_corner]

        results, kept, sent = [], [], []
        bests, (mine, one), _ = meeting(
            [own, near[0]], [OWN, TWO], held[:3], [], rows, span
        )
        results.append(mine)
        bests, (other,), _ = meeting(
            [[partner], pieces], [HELD, TWO], held[:3], bests, rows, span
        )
        corner_best, (mine, one_more, other_more), _ = meeting(
            [own, near[0], [partner], pieces], [OWN, TWO, HELD, TWO], held[3:], [], rows, span
        )
        results.append(mine)
        bests += corner_best
        kept.append(jnp.maximum(one, one_more))
        sent.append(jnp.maximum(other, other_more))
        rest = [blocks for both in zip(near, near_other) for blocks in both][1:]
        for at, one in enumerate(rest):
            (one,), bests = lax.optimization_barrier((one, bests))
            far = [lax.ppermute(one, BOTH, other_core)]
            bests, found, _ = meeting([[one]], [TWO], held, bests, rows, span)
            kept += found
            last = at == len(rest) - 1
            bests, found, _ = meeting(
                [far], [TWO], held, bests, rows, span, together=[(0,), (1, 3), (2,)] if last else None
            )
            sent += found
        sent = lax.ppermute(jnp.concatenate(sent, axis=1), BOTH, other_core)
        kept = jnp.maximum(jnp.concatenate(kept, axis=1), sent)
        for at, pairs in enumerate(rounds):
            found = lax.ppermute(kept[:, 2 * at * rows : 2 * (at + 1) * rows], BOTH, back(pairs))
            me = lax.axis_index(BOTH)
            sender = functools.reduce(jnp.logical_or, [me == source for source, _ in pairs])
            found = jnp.where(sender, found, -1.0)
            results += [found[:, :rows], lax.ppermute(found[:, rows:], BOTH, other_core)]
        from_x = lax.ppermute(bests[1], BOTH, first)
        results.append(from_x[:, :rows])
        onward = jnp.maximum(bests[2], from_x[:, rows:])
        results.append(lax.ppermute(onward, BOTH, second))
        return functools.reduce(jnp.maximum, results, bests[0]).reshape(rows)

    placed = (P(BOTH, None), P(BOTH, None), P(BOTH))
    return jax.shard_map(
        shards, mesh=mesh, in_specs=placed, out_specs=P(BOTH), check_vma=False
    )
```

```python
import functools

import jax
import jax.numpy as jnp
from jax import lax
from jax.experimental import pallas as pl
from jax.experimental.pallas import tpu as pltpu
from jax.sharding import PartitionSpec as P

EPSILON = 1e-06
EXTRA = 16
LANES = 128
TILE = 256
BOTH = ("dp", "grid")


def up(value, multiple):
    return -(-value // multiple) * multiple


def turned_to_column(row, rows):
    return jnp.broadcast_to(row, (LANES, row.shape[1])).T[:rows]


def codes(block, rows, span):
    parts = block[block.shape[0] - EXTRA :, : up(rows, LANES)].astype(jnp.float32)
    return parts[2:3] * (4.0 * span) + parts[0:1] * 256.0 + parts[1:2]


def unit_rows(rows, out):
    values = rows[...].astype(jnp.float32)
    scale = lax.rsqrt(jnp.sum(values * values, axis=1, keepdims=True) + EPSILON)
    out[0 : rows.shape[0], :] = (values * scale).astype(jnp.bfloat16)


def give_parts(block, outs):
    top = 0
    for out in outs:
        out[...] = block[top : top + out.shape[0], :]
        top += out.shape[0]


def prepare_kernel(span, embeddings, named, block, *parts_out):
    rows, width = embeddings.shape
    unit_rows(embeddings, block)
    names = named[...].reshape(1, rows)
    keys = names & (span - 1)
    parts = [keys >> 8, keys & 255, names >> (span.bit_length() - 1)]
    parts = [part.astype(jnp.float32) for part in parts]
    parts = jnp.concatenate(parts + [jnp.zeros((EXTRA - 3, rows), jnp.float32)], axis=0)
    parts = jnp.concatenate([parts, jnp.zeros((EXTRA, width - rows), jnp.float32)], axis=1)
    block[rows : rows + EXTRA, :] = parts.astype(jnp.bfloat16)
    codes_out, *parts_out = parts_out
    codes_out[0:EXTRA, :] = block[rows : rows + EXTRA, :]
    give_parts(block, parts_out)


def complete_kernel(rows_of, named, block, *parts_out):
    unit_rows(rows_of, block)
    block[rows_of.shape[0] :, :] = named[0:EXTRA, :]
    give_parts(block, parts_out)


def with_units(kernel, rows_of, named, heights=()):
    rows, width = rows_of.shape
    return pl.pallas_call(
        kernel,
        out_shape=[
            jax.ShapeDtypeStruct((height, width), jnp.bfloat16)
            for height in (rows + EXTRA, *heights)
        ],
        compiler_params=pltpu.CompilerParams(vmem_limit_bytes=16 << 20),
        cost_estimate=pl.CostEstimate(flops=rows, bytes_accessed=rows, transcendentals=0),
    )(rows_of, named)


def row_from_partial(partial, rows):
    padded = up(rows, LANES)
    if padded != rows:
        partial = jnp.concatenate(
            [partial, jnp.zeros((padded - rows, LANES), partial.dtype)], axis=0
        )
    return jnp.max(partial.T, axis=0, keepdims=True)[:, :rows]


def meet(block, rows, span, held, held_codes, to_block, to_held):
    column = turned_to_column(codes(block, rows, span), rows)
    partial = jnp.full((rows, LANES), -1.0, jnp.float32)
    best_held = []
    for at in range(0, held.shape[0], TILE):
        tile = min(TILE, held.shape[0] - at)
        sims = lax.dot_general(
            block[0:rows, :],
            held[at : at + tile, :],
            (((1,), (1,)), ((), ())),
            preferred_element_type=jnp.float32,
        )
        for lane in range(0, tile, LANES):
            part = sims[:, lane : lane + LANES]
            gap = column - held_codes[:, at + lane : at + lane + LANES]
            if to_block and to_held:
                part = jnp.where(jnp.abs(gap) < span, part, -1.0)
                later = gap > 0.0
                partial = jnp.maximum(partial, jnp.where(later, part, -1.0))
                other = jnp.where(later, -1.0, part)
            elif to_block:
                partial = jnp.maximum(
                    partial, jnp.where((gap > 0.0) & (gap < span), part, -1.0)
                )
            else:
                other = jnp.where((gap < 0.0) & (gap > -span), part, -1.0)
            if to_held:
                best_held.append(jnp.max(other, axis=0, keepdims=True))
    return (
        row_from_partial(partial, rows) if to_block else None,
        jnp.concatenate(best_held, axis=1) if to_held else None,
    )


def assemble(whole, top, end, pieces):
    for piece in pieces:
        height = min(piece.shape[0], end - top)
        if height == 0:
            break
        whole[top : top + height, :] = piece[0:height, :]
        top += height


def meet_kernel(rows, span, sizes, modes, groups, *refs):
    kinds = []
    for size in sizes:
        kinds.append(refs[:size])
        refs = refs[size:]
    blocks, holds, bests, outs, found, kept, scratch = kinds
    held, scratch = scratch[0], iter(scratch[1:])

    def whole(block):
        if len(block) == 1:
            return block[0]
        joined = next(scratch)
        assemble(joined, 0, joined.shape[0], block)
        return joined

    blocks = [whole(block) for block in regrouped(blocks, groups[0])]
    holds = regrouped(holds, groups[1])
    total = held.shape[0]
    row = []
    for at, block in enumerate(holds):
        assemble(held, at * rows, (at + 1) * rows, block)
        row.append(codes(block[-1], rows, span)[:, :rows])
    rest = total - len(holds) * rows
    if rest:
        held[total - rest :, :] = jnp.zeros((rest, held.shape[1]), held.dtype)
        row.append(jnp.zeros((1, rest), jnp.float32))
    row = jnp.concatenate(row, axis=1)
    best = None
    found = iter(found)
    for block, (to_block, to_held) in zip(blocks, modes):
        mine, theirs = meet(block, rows, span, held, row, to_block, to_held)
        if to_block:
            next(found)[...] = mine
        if to_held:
            best = theirs if best is None else jnp.maximum(best, theirs)
    if kept:
        top = 0
        for out in kept:
            out[...] = blocks[-1][top : top + out.shape[0], :]
            top += out.shape[0]
    parts = [best[:, at * rows : (at + 1) * rows] for at in range(len(holds))]
    if bests:
        parts = [jnp.maximum(part, earlier[...]) for part, earlier in zip(parts, bests)]
    for out, places in zip(outs, groups[2]):
        if len(places) == 1:
            out[...] = parts[places[0]]
        else:
            out[...] = jnp.concatenate([parts[place] for place in places], axis=1)


def regrouped(flat, lengths):
    flat = iter(flat)
    return [[next(flat) for _ in range(length)] for length in lengths]


def meeting(blocks, modes, holds, bests, rows, span, keep=(), together=None):
    width = blocks[0][0].shape[1]
    together = together or [(at,) for at in range(len(holds))]
    lengths = [[len(block) for block in some] for some in (blocks, holds)]
    flat = [[piece for block in some for piece in block] for some in (blocks, holds)]
    outs = [jax.ShapeDtypeStruct((1, rows * len(some)), jnp.float32) for some in together]
    found = [jax.ShapeDtypeStruct((1, rows), jnp.float32)] * sum(mode[0] for mode in modes)
    kept = [jax.ShapeDtypeStruct((height, width), jnp.bfloat16) for height in keep]
    split = sum(length > 1 for length in lengths[0])
    scratch = [pltpu.VMEM((up(len(holds) * rows, LANES), width), jnp.bfloat16)]
    scratch += [pltpu.VMEM((rows + EXTRA, width), jnp.bfloat16)] * split
    kinds = flat + [bests, outs, found, kept, scratch]
    results = pl.pallas_call(
        functools.partial(
            meet_kernel, rows, span, [len(kind) for kind in kinds], modes, lengths + [together]
        ),
        out_shape=outs + found + kept,
        scratch_shapes=scratch,
        compiler_params=pltpu.CompilerParams(vmem_limit_bytes=32 << 20),
        cost_estimate=pl.CostEstimate(flops=rows, bytes_accessed=rows, transcendentals=0),
    )(*flat[0], *flat[1], *bests)
    return regrouped(results, [len(outs), len(found), len(kept)])


OWN = (True, False)
HELD = (False, True)
TWO = (True, True)


def line_rounds(chips):
    if chips == 4:
        return [[(0, 2), (3, 1), (1, 0)], [(0, 3), (3, 2), (2, 1)]]
    rounds = []
    for shift in range(1, chips // 2 + 1):
        senders = chips // 2 if 2 * shift == chips else chips
        rounds.append([(s, (s + shift) % chips) for s in range(senders)])
    return rounds


def solution(mesh):
    groups, members = mesh.shape["dp"], mesh.shape["grid"]
    assert groups == 4 and members % 2 == 0
    chips = members // 2

    def everywhere(target):
        return [
            (p * members + g, a * members + b)
            for p in range(groups)
            for g in range(members)
            for a, b in [target(p, g)]
        ]

    other_core = everywhere(lambda p, g: (p, g ^ 1))
    first = everywhere(lambda p, g: (p ^ (1 + g % 2), g))
    second = everywhere(lambda p, g: (p ^ (2 - g % 2), g))

    rounds = line_rounds(chips)
    rounds += [[]] * (len(rounds) % 2)
    rounds = [
        [
            (p * members + 2 * s + c, p * members + 2 * t + c)
            for p in range(groups)
            for c in range(2)
            for s, t in rounds[at + c]
        ]
        for at in range(0, len(rounds), 2)
    ]

    def back(pairs):
        return [(target, source) for source, target in pairs]

    def shards(embeddings, cluster, order_key):
        rows = embeddings.shape[0]
        span = 256
        while span < rows * groups * members:
            span *= 2
        halves = rows // 2
        named = (cluster[:, 0] + 1) * span + order_key
        partner = lax.ppermute(embeddings, BOTH, other_core)
        raw = [lax.ppermute(embeddings, BOTH, pairs) for pairs in rounds]
        block, codes_of = with_units(
            functools.partial(prepare_kernel, span), embeddings, named, (EXTRA,)
        )
        own = [block]
        from_first = [lax.ppermute(block, BOTH, first)]
        from_second = [lax.ppermute(block, BOTH, second)]
        (partner,) = with_units(complete_kernel, partner, lax.ppermute(codes_of, BOTH, other_core))
        near_other = [[lax.ppermute(partner, BOTH, pairs)] for pairs in rounds]
        from_corner = [
            lax.ppermute(part, BOTH, second)
            for part in (from_first[0][:halves], from_first[0][halves:])
        ]
        near = [
            with_units(complete_kernel, rows_of, lax.ppermute(codes_of, BOTH, pairs), (rows, EXTRA))
            for rows_of, pairs in zip(raw, rounds)
        ]
        pieces = [lax.ppermute(piece, BOTH, other_core) for piece in near[0][1:]]
        near = [blocks[:1] for blocks in near]
        held = [own, from_first, from_second, from_corner]

        results, kept, sent = [], [], []
        bests, (mine, one), _ = meeting(
            [own, near[0]], [OWN, TWO], held[:3], [], rows, span
        )
        results.append(mine)
        bests, (other,), _ = meeting(
            [[partner], pieces], [HELD, TWO], held[:3], bests, rows, span
        )
        *from_corner, bests = lax.optimization_barrier((*from_corner, bests))
        held[3] = from_corner
        corner_best, (mine, one_more, other_more), _ = meeting(
            [own, near[0], [partner], pieces], [OWN, TWO, HELD, TWO], held[3:], [], rows, span
        )
        results.append(mine)
        bests += corner_best
        kept.append(jnp.maximum(one, one_more))
        sent.append(jnp.maximum(other, other_more))
        rest = [blocks for both in zip(near, near_other) for blocks in both][1:]
        for at, one in enumerate(rest):
            (one,), bests = lax.optimization_barrier((one, bests))
            far = [lax.ppermute(one, BOTH, other_core)]
            bests, found, _ = meeting([[one]], [TWO], held, bests, rows, span)
            kept += found
            last = at == len(rest) - 1
            bests, found, _ = meeting(
                [far], [TWO], held, bests, rows, span, together=[(0,), (1, 3), (2,)] if last else None
            )
            sent += found
        sent = lax.ppermute(jnp.concatenate(sent, axis=1), BOTH, other_core)
        kept = jnp.maximum(jnp.concatenate(kept, axis=1), sent)
        for at, pairs in enumerate(rounds):
            found = lax.ppermute(kept[:, 2 * at * rows : 2 * (at + 1) * rows], BOTH, back(pairs))
            me = lax.axis_index(BOTH)
            sender = functools.reduce(jnp.logical_or, [me == source for source, _ in pairs])
            found = jnp.where(sender, found, -1.0)
            results += [found[:, :rows], lax.ppermute(found[:, rows:], BOTH, other_core)]
        from_x = lax.ppermute(bests[1], BOTH, first)
        results.append(from_x[:, :rows])
        onward = jnp.maximum(bests[2], from_x[:, rows:])
        results.append(lax.ppermute(onward, BOTH, second))
        return functools.reduce(jnp.maximum, results, bests[0]).reshape(rows)

    placed = (P(BOTH, None), P(BOTH, None), P(BOTH))
    return jax.shard_map(
        shards, mesh=mesh, in_specs=placed, out_specs=P(BOTH), check_vma=False
    )
```

```python
import functools

import jax
import jax.numpy as jnp
from jax import lax
from jax.experimental import pallas as pl
from jax.experimental.pallas import tpu as pltpu
from jax.sharding import PartitionSpec as P

EPSILON = 1e-06
EXTRA = 16
CODES = 3
LANES = 128
TILE = 256
BOTH = ("dp", "grid")


def up(value, multiple):
    return -(-value // multiple) * multiple


def turned_to_column(row, rows):
    return jnp.broadcast_to(row, (LANES, row.shape[1])).T[:rows]


def codes(block, rows, span, first=0):
    parts = block[block.shape[0] - EXTRA :, : up(rows, LANES)].astype(jnp.float32)
    parts = parts[first : first + CODES]
    return parts[2:3] * (4.0 * span) + parts[0:1] * 256.0 + parts[1:2]


def unit_rows(rows, out):
    values = rows[...].astype(jnp.float32)
    scale = lax.rsqrt(jnp.sum(values * values, axis=1, keepdims=True) + EPSILON)
    out[0 : rows.shape[0], :] = (values * scale).astype(jnp.bfloat16)


def give_parts(block, outs):
    top = 0
    for out in outs:
        out[...] = block[top : top + out.shape[0], :]
        top += out.shape[0]


def prepare_kernel(span, embeddings, named, block, *parts_out):
    rows, width = embeddings.shape
    unit_rows(embeddings, block)
    names = named[...].reshape(1, rows)
    keys = names & (span - 1)
    parts = [keys >> 8, keys & 255, names >> (span.bit_length() - 1)]
    parts = [part.astype(jnp.float32) for part in parts]
    parts = jnp.concatenate(parts + [jnp.zeros((EXTRA - 3, rows), jnp.float32)], axis=0)
    parts = jnp.concatenate([parts, jnp.zeros((EXTRA, width - rows), jnp.float32)], axis=1)
    block[rows : rows + EXTRA, :] = parts.astype(jnp.bfloat16)
    codes_out, *parts_out = parts_out
    codes_out[0:EXTRA, :] = block[rows : rows + EXTRA, :]
    give_parts(block, parts_out)


def complete_kernel(rows_of, codes_of, other_codes, block):
    rows, width = rows_of.shape
    unit_rows(rows_of, block)
    named = [part[...].astype(jnp.float32)[0:CODES] for part in (codes_of, other_codes)]
    named = jnp.concatenate(named + [jnp.zeros((EXTRA - 2 * CODES, width), jnp.float32)], axis=0)
    block[rows:, :] = named.astype(jnp.bfloat16)


def unit_kernel(rows_of, block, *parts_out):
    unit_rows(rows_of, block)
    give_parts(block, parts_out)


def with_units(kernel, heights, rows_of, *others):
    rows, width = rows_of.shape
    return pl.pallas_call(
        kernel,
        out_shape=[jax.ShapeDtypeStruct((height, width), jnp.bfloat16) for height in heights],
        compiler_params=pltpu.CompilerParams(vmem_limit_bytes=16 << 20),
        cost_estimate=pl.CostEstimate(flops=rows, bytes_accessed=rows, transcendentals=0),
    )(rows_of, *others)


def row_from_partial(partial, rows):
    padded = up(rows, LANES)
    if padded != rows:
        partial = jnp.concatenate(
            [partial, jnp.zeros((padded - rows, LANES), partial.dtype)], axis=0
        )
    return jnp.max(partial.T, axis=0, keepdims=True)[:, :rows]


def products(block, rows, held, at, tile):
    return lax.dot_general(
        block[0:rows, :],
        held[at : at + tile, :],
        (((1,), (1,)), ((), ())),
        preferred_element_type=jnp.float32,
    )


def meet(sims_of, row, rows, span, held_codes, to_block, to_held):
    column = turned_to_column(row, rows)
    partial = jnp.full((rows, LANES), -1.0, jnp.float32)
    best_held = []
    for at in range(0, held_codes.shape[1], TILE):
        tile = min(TILE, held_codes.shape[1] - at)
        sims = sims_of(at, tile)
        for lane in range(0, tile, LANES):
            part = sims[:, lane : lane + LANES]
            gap = column - held_codes[:, at + lane : at + lane + LANES]
            if to_block and to_held:
                part = jnp.where(jnp.abs(gap) < span, part, -1.0)
                later = gap > 0.0
                partial = jnp.maximum(partial, jnp.where(later, part, -1.0))
                other = jnp.where(later, -1.0, part)
            elif to_block:
                partial = jnp.maximum(
                    partial, jnp.where((gap > 0.0) & (gap < span), part, -1.0)
                )
            else:
                other = jnp.where((gap < 0.0) & (gap > -span), part, -1.0)
            if to_held:
                best_held.append(jnp.max(other, axis=0, keepdims=True))
    return (
        row_from_partial(partial, rows) if to_block else None,
        jnp.concatenate(best_held, axis=1) if to_held else None,
    )


def assemble(whole, top, end, pieces):
    for piece in pieces:
        height = min(piece.shape[0], end - top)
        if height == 0:
            break
        whole[top : top + height, :] = piece[0:height, :]
        top += height


def hold(held, holds, rows):
    for at, block in enumerate(holds):
        assemble(held, at * rows, (at + 1) * rows, block)
    rest = held.shape[0] - len(holds) * rows
    if rest:
        held[len(holds) * rows :, :] = jnp.zeros((rest, held.shape[1]), held.dtype)


def products_kernel(rows, lengths, *refs):
    *refs, out, held = refs
    block, *holds = regrouped(refs, lengths)
    hold(held, holds, rows)
    for at in range(0, held.shape[0], TILE):
        tile = min(TILE, held.shape[0] - at)
        top = 0
        for piece in block:
            height = piece.shape[0]
            out[top : top + height, at : at + tile] = products(piece, height, held, at, tile)
            top += height


def all_products(block, holds, rows):
    width = block[0].shape[1]
    total = up(len(holds) * rows, LANES)
    parts = [block, *holds]
    return pl.pallas_call(
        functools.partial(products_kernel, rows, [len(part) for part in parts]),
        out_shape=jax.ShapeDtypeStruct((rows, total), jnp.float32),
        scratch_shapes=[pltpu.VMEM((total, width), jnp.bfloat16)],
        compiler_params=pltpu.CompilerParams(vmem_limit_bytes=32 << 20),
        cost_estimate=pl.CostEstimate(flops=5 * rows * total * width // 4, bytes_accessed=rows, transcendentals=0),
    )(*[piece for part in parts for piece in part])


def meet_kernel(rows, span, sizes, modes, lengths, together, *refs):
    blocks, holds, bests, given, outs, found, scratch = regrouped(refs, sizes)
    (held,) = scratch
    holds = regrouped(holds, lengths)
    hold(held, holds, rows)
    row = [codes(block[-1], rows, span)[:, :rows] for block in holds]
    rest = held.shape[0] - len(holds) * rows
    if rest:
        row.append(jnp.zeros((1, rest), jnp.float32))
    row = jnp.concatenate(row, axis=1)
    best = None
    found = iter(found)

    def join(sims_of, own_row, to_block, to_held):
        nonlocal best
        mine, theirs = meet(sims_of, own_row, rows, span, row, to_block, to_held)
        if to_block:
            next(found)[...] = mine
        if to_held:
            best = theirs if best is None else jnp.maximum(best, theirs)

    for block, mode in zip(blocks, modes):
        join(
            lambda at, tile, block=block: products(block, rows, held, at, tile),
            codes(block, rows, span),
            *mode,
        )
    for sims, block in zip(given, blocks):
        join(
            lambda at, tile, sims=sims: sims[:, at : at + tile],
            codes(block, rows, span, first=CODES),
            *TWO,
        )
    parts = [best[:, at * rows : (at + 1) * rows] for at in range(len(holds))]
    if bests:
        parts = [jnp.maximum(part, earlier[...]) for part, earlier in zip(parts, bests)]
    for out, places in zip(outs, together):
        if len(places) == 1:
            out[...] = parts[places[0]]
        else:
            out[...] = jnp.concatenate([parts[place] for place in places], axis=1)


def regrouped(flat, lengths):
    flat = iter(flat)
    return [[next(flat) for _ in range(length)] for length in lengths]


def meeting(blocks, modes, holds, bests, rows, span, given=(), together=None):
    width = blocks[0].shape[1]
    together = together or [(at,) for at in range(len(holds))]
    flat = [piece for block in holds for piece in block]
    outs = [jax.ShapeDtypeStruct((1, rows * len(some)), jnp.float32) for some in together]
    count = sum(mode[0] for mode in modes) + len(given)
    found = [jax.ShapeDtypeStruct((1, rows), jnp.float32)] * count
    scratch = [pltpu.VMEM((up(len(holds) * rows, LANES), width), jnp.bfloat16)]
    kinds = [blocks, flat, bests, given, outs, found, scratch]
    results = pl.pallas_call(
        functools.partial(
            meet_kernel,
            rows,
            span,
            [len(kind) for kind in kinds],
            modes,
            [len(block) for block in holds],
            together,
        ),
        out_shape=outs + found,
        scratch_shapes=scratch,
        compiler_params=pltpu.CompilerParams(vmem_limit_bytes=32 << 20),
        cost_estimate=pl.CostEstimate(flops=rows, bytes_accessed=rows, transcendentals=0),
    )(*blocks, *flat, *bests, *given)
    return regrouped(results, [len(outs), len(found)])


OWN = (True, False)
HELD = (False, True)
TWO = (True, True)


def line_rounds(chips):
    if chips == 4:
        return [[(0, 2), (3, 1), (1, 0)], [(0, 3), (3, 2), (2, 1)]]
    rounds = []
    for shift in range(1, chips // 2 + 1):
        senders = chips // 2 if 2 * shift == chips else chips
        rounds.append([(s, (s + shift) % chips) for s in range(senders)])
    return rounds


def solution(mesh):
    groups, members = mesh.shape["dp"], mesh.shape["grid"]
    assert groups == 4 and members % 2 == 0
    chips = members // 2

    def everywhere(target):
        return [
            (p * members + g, a * members + b)
            for p in range(groups)
            for g in range(members)
            for a, b in [target(p, g)]
        ]

    other_core = everywhere(lambda p, g: (p, g ^ 1))
    first = everywhere(lambda p, g: (p ^ (1 + g % 2), g))
    second = everywhere(lambda p, g: (p ^ (2 - g % 2), g))

    rounds = line_rounds(chips)
    rounds += [[]] * (len(rounds) % 2)
    rounds = [
        [
            (p * members + 2 * s + c, p * members + 2 * t + c)
            for p in range(groups)
            for c in range(2)
            for s, t in rounds[at + c]
        ]
        for at in range(0, len(rounds), 2)
    ]

    def back(pairs):
        return [(target, source) for source, target in pairs]

    def shards(embeddings, cluster, order_key):
        rows = embeddings.shape[0]
        span = 256
        while span < rows * groups * members:
            span *= 2
        halves = (rows // 2, rows // 2 + EXTRA)
        uneven = (rows // 2 + EXTRA, rows // 2 - EXTRA)
        named = (cluster[:, 0] + 1) * span + order_key
        partner = lax.ppermute(embeddings, BOTH, other_core)
        raw = [lax.ppermute(embeddings, BOTH, pairs) for pairs in rounds]
        block, codes_of, *parts = with_units(
            functools.partial(prepare_kernel, span),
            (rows + EXTRA, EXTRA, *halves),
            embeddings,
            named,
        )
        own = [block]
        from_first = [lax.ppermute(part, BOTH, first) for part in parts]
        from_second = [lax.ppermute(block, BOTH, second)]
        other_codes = lax.ppermute(codes_of, BOTH, other_core)
        (partner,) = with_units(complete_kernel, (rows + EXTRA,), partner, other_codes, codes_of)
        near_other = [lax.ppermute(partner, BOTH, pairs) for pairs in rounds]
        from_corner = [lax.ppermute(part, BOTH, second) for part in from_first]
        near = [with_units(unit_kernel, (rows, *uneven), rows_of) for rows_of in raw]
        far = [[lax.ppermute(piece, BOTH, other_core) for piece in blocks[1:]] for blocks in near]

        results, kept, sent = [], [], []
        bests, found = meeting(
            [block, partner], [OWN, HELD], [own, from_first, from_second], [], rows, span
        )
        results += found
        *from_corner, bests = lax.optimization_barrier((*from_corner, bests))
        corner_best, found = meeting([block, partner], [OWN, HELD], [from_corner], [], rows, span)
        results += found
        bests += corner_best
        held = [own, from_first, from_second, from_corner]
        for at, one in enumerate(near_other):
            sims_near = all_products(near[at][:1], held, rows)
            *far[at], sims_near = lax.optimization_barrier((*far[at], sims_near))
            sims_far = all_products(far[at], held, rows)
            one, bests, sims_near, sims_far = lax.optimization_barrier(
                (one, bests, sims_near, sims_far)
            )
            far_other = lax.ppermute(one, BOTH, other_core)
            bests, found = meeting([one], [TWO], held, bests, rows, span, given=[sims_near])
            kept += found
            last = at == len(rounds) - 1
            bests, found = meeting(
                [far_other],
                [TWO],
                held,
                bests,
                rows,
                span,
                given=[sims_far],
                together=[(0,), (1, 3), (2,)] if last else None,
            )
            sent += found
        sent = lax.ppermute(jnp.concatenate(sent, axis=1), BOTH, other_core)
        kept = jnp.maximum(jnp.concatenate(kept, axis=1), sent)
        for at, pairs in enumerate(rounds):
            found = lax.ppermute(kept[:, 2 * at * rows : 2 * (at + 1) * rows], BOTH, back(pairs))
            me = lax.axis_index(BOTH)
            sender = functools.reduce(jnp.logical_or, [me == source for source, _ in pairs])
            found = jnp.where(sender, found, -1.0)
            results += [found[:, rows:], lax.ppermute(found[:, :rows], BOTH, other_core)]
        from_x = lax.ppermute(bests[1], BOTH, first)
        results.append(from_x[:, :rows])
        onward = jnp.maximum(bests[2], from_x[:, rows:])
        results.append(lax.ppermute(onward, BOTH, second))
        return functools.reduce(jnp.maximum, results, bests[0]).reshape(rows)

    placed = (P(BOTH, None), P(BOTH, None), P(BOTH))
    return jax.shard_map(
        shards, mesh=mesh, in_specs=placed, out_specs=P(BOTH), check_vma=False
    )
```

```python
import functools

import jax
import jax.numpy as jnp
from jax import lax
from jax.experimental import pallas as pl
from jax.experimental.pallas import tpu as pltpu
from jax.sharding import PartitionSpec as P

EPSILON = 1e-06
EXTRA = 16
CODES = 3
LANES = 128
TILE = 256
CHUNK = 32
BOTH = ("dp", "grid")


def up(value, multiple):
    return -(-value // multiple) * multiple


def turned_to_column(row, rows):
    return jnp.broadcast_to(row, (LANES, row.shape[1])).T[:rows]


def codes(block, rows, span, first=0):
    parts = block[block.shape[0] - EXTRA :, : up(rows, LANES)].astype(jnp.float32)
    parts = parts[first : first + CODES]
    return parts[2:3] * (4.0 * span) + parts[0:1] * 256.0 + parts[1:2]


def unit_rows(rows, out):
    values = rows[...].astype(jnp.float32)
    scale = lax.rsqrt(jnp.sum(values * values, axis=1, keepdims=True) + EPSILON)
    out[0 : rows.shape[0], :] = (values * scale).astype(jnp.bfloat16)


def give_parts(block, outs):
    for out, top in zip(outs, (0, block.shape[0] - outs[-1].shape[0])):
        out[...] = block[top : top + out.shape[0], :]


def prepare_kernel(span, embeddings, named, block, *parts_out):
    rows, width = embeddings.shape
    unit_rows(embeddings, block)
    names = named[...].reshape(1, rows)
    keys = names & (span - 1)
    parts = [keys >> 8, keys & 255, names >> (span.bit_length() - 1)]
    parts = [part.astype(jnp.float32) for part in parts]
    parts = jnp.concatenate(parts + [jnp.zeros((EXTRA - 3, rows), jnp.float32)], axis=0)
    parts = jnp.concatenate([parts, jnp.zeros((EXTRA, width - rows), jnp.float32)], axis=1)
    block[rows : rows + EXTRA, :] = parts.astype(jnp.bfloat16)
    codes_out, *parts_out = parts_out
    codes_out[0:EXTRA, :] = block[rows : rows + EXTRA, :]
    give_parts(block, parts_out)


def complete_kernel(rows_of, codes_of, other_codes, block):
    rows, width = rows_of.shape
    unit_rows(rows_of, block)
    named = [part[...].astype(jnp.float32)[0:CODES] for part in (codes_of, other_codes)]
    named = jnp.concatenate(named + [jnp.zeros((EXTRA - 2 * CODES, width), jnp.float32)], axis=0)
    block[rows:, :] = named.astype(jnp.bfloat16)


def unit_kernel(rows_of, block, *parts_out):
    unit_rows(rows_of, block)
    give_parts(block, parts_out)


def with_units(kernel, heights, rows_of, *others):
    rows, width = rows_of.shape
    return pl.pallas_call(
        kernel,
        out_shape=[jax.ShapeDtypeStruct((height, width), jnp.bfloat16) for height in heights],
        compiler_params=pltpu.CompilerParams(vmem_limit_bytes=16 << 20),
        cost_estimate=pl.CostEstimate(flops=rows, bytes_accessed=rows, transcendentals=0),
    )(rows_of, *others)


def row_from_partial(partial, rows):
    padded = up(rows, LANES)
    if padded != rows:
        partial = jnp.concatenate(
            [partial, jnp.zeros((padded - rows, LANES), partial.dtype)], axis=0
        )
    return jnp.max(partial.T, axis=0, keepdims=True)[:, :rows]


def meet(units, row, rows, span, held, held_codes, to_block, to_held):
    column = turned_to_column(row, rows)
    starts = range(0, rows, CHUNK)
    partial = [jnp.full((CHUNK, LANES), -1.0, jnp.float32) for _ in starts]
    best_held = []
    for at in range(0, held.shape[0], TILE):
        sims = lax.dot_general(
            units,
            held[at : at + TILE, :],
            (((1,), (1,)), ((), ())),
            preferred_element_type=jnp.float32,
        )
        best = [jnp.full((CHUNK, LANES), -1.0, jnp.float32) for _ in range(0, TILE, LANES)]
        for place, top in enumerate(starts):
            mine = column[top : top + CHUNK]
            for lane in range(0, TILE, LANES):
                part = sims[top : top + CHUNK, lane : lane + LANES]
                gap = mine - held_codes[:, at + lane : at + lane + LANES]
                if to_block and to_held:
                    part = jnp.where(jnp.abs(gap) < span, part, -1.0)
                    later = gap > 0.0
                    ours, theirs = jnp.where(later, part, -1.0), jnp.where(later, -1.0, part)
                elif to_block:
                    ours = jnp.where((gap > 0.0) & (gap < span), part, -1.0)
                else:
                    theirs = jnp.where((gap < 0.0) & (gap > -span), part, -1.0)
                if to_block:
                    partial[place] = jnp.maximum(partial[place], ours)
                if to_held:
                    best[lane // LANES] = jnp.maximum(best[lane // LANES], theirs)
        best_held += [jnp.max(some, axis=0, keepdims=True) for some in best]
    return (
        row_from_partial(jnp.concatenate(partial, axis=0), rows) if to_block else None,
        jnp.concatenate(best_held, axis=1) if to_held else None,
    )


def assemble(whole, top, rows, pieces, extra):
    first, *others = pieces
    height = min(first.shape[0], rows)
    whole[top : top + height, :] = first[0:height, :]
    for last in others:
        height = last.shape[0] - extra
        whole[top + rows - height : top + rows, :] = last[0:height, :]


def gather_kernel(rows, span, lengths, *refs):
    *pieces, held, row = refs
    holds = regrouped(pieces, lengths)
    for at, block in enumerate(holds):
        assemble(held, at * rows, rows, block, EXTRA)
    row[...] = jnp.concatenate(
        [codes(block[-1], rows, span)[:, :rows] for block in holds], axis=1
    )


def gather(holds, rows, span):
    width = holds[0][0].shape[1]
    total = len(holds) * rows
    return pl.pallas_call(
        functools.partial(gather_kernel, rows, span, [len(block) for block in holds]),
        out_shape=[
            jax.ShapeDtypeStruct((total, width), jnp.bfloat16),
            jax.ShapeDtypeStruct((1, total), jnp.float32),
        ],
        compiler_params=pltpu.CompilerParams(vmem_limit_bytes=16 << 20),
        cost_estimate=pl.CostEstimate(flops=rows, bytes_accessed=rows, transcendentals=0),
    )(*[piece for block in holds for piece in block])


def regrouped(flat, lengths):
    flat = iter(flat)
    return [[next(flat) for _ in range(length)] for length in lengths]


def plane_kernel(rows, span, block, partner, held, row, best, mine):
    mine[...], _ = meet(
        block[0:rows, :], codes(block, rows, span), rows, span, held, row[...], *OWN
    )
    _, best[...] = meet(
        partner[0:rows, :], codes(partner, rows, span), rows, span, held, row[...], *HELD
    )


def line_kernel(rows, span, count, together, *refs):
    pieces, (second, held, row, best, *outs, found, joined) = refs[:count], refs[count:]
    if count > 1:
        assemble(joined, 0, rows, pieces, 0)
    units = joined if count > 1 else pieces[0]
    results = [
        meet(
            block[0:rows, :],
            codes(second, rows, span, first=place),
            rows,
            span,
            held,
            row[...],
            *TWO,
        )
        for block, place in ((units, CODES), (second, 0))
    ]
    found[...] = jnp.concatenate([mine for mine, _ in results], axis=1)
    best = jnp.maximum(best[...], jnp.maximum(results[0][1], results[1][1]))
    for out, places in zip(outs, together):
        out[...] = jnp.concatenate(
            [best[:, place * rows : (place + 1) * rows] for place in places], axis=1
        )


def plane(block, partner, held, row, rows, span):
    total, width = held.shape
    return pl.pallas_call(
        functools.partial(plane_kernel, rows, span),
        out_shape=[
            jax.ShapeDtypeStruct((1, total), jnp.float32),
            jax.ShapeDtypeStruct((1, rows), jnp.float32),
        ],
        compiler_params=pltpu.CompilerParams(vmem_limit_bytes=32 << 20),
        cost_estimate=pl.CostEstimate(flops=8 * rows * total * width, bytes_accessed=rows, transcendentals=0),
    )(block, partner, held, row)


def line(pieces, second, held, row, best, rows, span, together):
    total, width = held.shape
    outs = [jax.ShapeDtypeStruct((1, rows * len(some)), jnp.float32) for some in together]
    *bests, found = pl.pallas_call(
        functools.partial(line_kernel, rows, span, len(pieces), together),
        out_shape=outs + [jax.ShapeDtypeStruct((1, 2 * rows), jnp.float32)],
        scratch_shapes=[pltpu.VMEM((rows, width), jnp.bfloat16)],
        compiler_params=pltpu.CompilerParams(vmem_limit_bytes=32 << 20),
        cost_estimate=pl.CostEstimate(flops=rows, bytes_accessed=rows, transcendentals=0),
    )(*pieces, second, held, row, best)
    return bests, found


OWN = (True, False)
HELD = (False, True)
TWO = (True, True)


def line_rounds(chips):
    if chips == 4:
        return [[(0, 2), (3, 1), (1, 0)], [(0, 3), (3, 2), (2, 1)]]
    rounds = []
    for shift in range(1, chips // 2 + 1):
        senders = chips // 2 if 2 * shift == chips else chips
        rounds.append([(s, (s + shift) % chips) for s in range(senders)])
    return rounds


def solution(mesh):
    groups, members = mesh.shape["dp"], mesh.shape["grid"]
    assert groups == 4 and members % 2 == 0
    chips = members // 2

    def everywhere(target):
        return [
            (p * members + g, a * members + b)
            for p in range(groups)
            for g in range(members)
            for a, b in [target(p, g)]
        ]

    other_core = everywhere(lambda p, g: (p, g ^ 1))
    first = everywhere(lambda p, g: (p ^ (1 + g % 2), g))
    second = everywhere(lambda p, g: (p ^ (2 - g % 2), g))

    rounds = line_rounds(chips)
    rounds += [[]] * (len(rounds) % 2)
    rounds = [
        [
            (p * members + 2 * s + c, p * members + 2 * t + c)
            for p in range(groups)
            for c in range(2)
            for s, t in rounds[at + c]
        ]
        for at in range(0, len(rounds), 2)
    ]

    def back(pairs):
        return [(target, source) for source, target in pairs]

    def shards(embeddings, cluster, order_key):
        rows = embeddings.shape[0]
        span = 256
        while span < rows * groups * members:
            span *= 2
        halves = (rows // 2, rows // 2 + EXTRA)
        named = (cluster[:, 0] + 1) * span + order_key
        partner = lax.ppermute(embeddings, BOTH, other_core)
        raw = [lax.ppermute(embeddings, BOTH, pairs) for pairs in rounds]
        block, codes_of, *parts = with_units(
            functools.partial(prepare_kernel, span),
            (rows + EXTRA, EXTRA, *halves),
            embeddings,
            named,
        )
        from_first = [lax.ppermute(part, BOTH, first) for part in parts]
        from_second = [lax.ppermute(block, BOTH, second)]
        other_codes = lax.ppermute(codes_of, BOTH, other_core)
        (partner,) = with_units(complete_kernel, (rows + EXTRA,), partner, other_codes, codes_of)
        near_other = [lax.ppermute(partner, BOTH, pairs) for pairs in rounds]
        from_corner = [lax.ppermute(part, BOTH, second) for part in from_first]
        near = [
            list(with_units(unit_kernel, (rows, rows // 2, rows // 2), rows_of))
            for rows_of in raw
        ]
        far = [[lax.ppermute(piece, BOTH, other_core) for piece in blocks[1:]] for blocks in near]

        results, kept, sent = [], [], []
        held, row = gather([[block], from_first, from_second, from_corner], rows, span)
        held, *far[0] = lax.optimization_barrier((held, *far[0]))
        best, mine = plane(block, partner, held, row, rows, span)
        results.append(mine)
        whole, last = [tuple(range(groups))], [(0,), (1, 3), (2,)]
        for at, second_near in enumerate(near_other):
            second_near, best = lax.optimization_barrier((second_near, best))
            second_far = lax.ppermute(second_near, BOTH, other_core)
            (best,), found = line(near[at][:1], second_near, held, row, best, rows, span, whole)
            kept.append(found)
            bests, found = line(
                far[at],
                second_far,
                held,
                row,
                best,
                rows,
                span,
                last if at == len(rounds) - 1 else whole,
            )
            best = bests[0]
            sent.append(found)
        sent = lax.ppermute(jnp.concatenate(sent, axis=1), BOTH, other_core)
        kept = jnp.maximum(jnp.concatenate(kept, axis=1), sent)
        for at, pairs in enumerate(rounds):
            found = lax.ppermute(kept[:, 2 * at * rows : 2 * (at + 1) * rows], BOTH, back(pairs))
            me = lax.axis_index(BOTH)
            sender = functools.reduce(jnp.logical_or, [me == source for source, _ in pairs])
            found = jnp.where(sender, found, -1.0)
            results += [found[:, :rows], lax.ppermute(found[:, rows:], BOTH, other_core)]
        from_x = lax.ppermute(bests[1], BOTH, first)
        results.append(from_x[:, :rows])
        onward = jnp.maximum(bests[2], from_x[:, rows:])
        results.append(lax.ppermute(onward, BOTH, second))
        return functools.reduce(jnp.maximum, results, bests[0]).reshape(rows)

    placed = (P(BOTH, None), P(BOTH, None), P(BOTH))
    return jax.shard_map(
        shards, mesh=mesh, in_specs=placed, out_specs=P(BOTH), check_vma=False
    )
```

```python
import functools

import jax
import jax.numpy as jnp
from jax import lax
from jax.experimental import pallas as pl
from jax.experimental.pallas import tpu as pltpu
from jax.sharding import PartitionSpec as P

EPSILON = 1e-06
EXTRA = 16
CODES = 3
LANES = 128
TILE = 256
CHUNK = 32
BOTH = ("dp", "grid")


def up(value, multiple):
    return -(-value // multiple) * multiple


def turned_to_column(row, rows):
    return jnp.broadcast_to(row, (LANES, row.shape[1])).T[:rows]


def codes(block, rows, span, first=0):
    parts = block[block.shape[0] - EXTRA :, : up(rows, LANES)].astype(jnp.float32)
    parts = parts[first : first + CODES]
    return parts[2:3] * (4.0 * span) + parts[0:1] * 256.0 + parts[1:2]


def unit_rows(rows, out):
    values = rows[...].astype(jnp.float32)
    scale = lax.rsqrt(jnp.sum(values * values, axis=1, keepdims=True) + EPSILON)
    out[0 : rows.shape[0], :] = (values * scale).astype(jnp.bfloat16)


def give_parts(block, outs):
    for out, top in zip(outs, (0, block.shape[0] - outs[-1].shape[0])):
        out[...] = block[top : top + out.shape[0], :]


def prepare_kernel(span, embeddings, named, block, *parts_out):
    rows, width = embeddings.shape
    unit_rows(embeddings, block)
    names = named[...].reshape(1, rows)
    keys = names & (span - 1)
    parts = [keys >> 8, keys & 255, names >> (span.bit_length() - 1)]
    parts = [part.astype(jnp.float32) for part in parts]
    parts = jnp.concatenate(parts + [jnp.zeros((EXTRA - 3, rows), jnp.float32)], axis=0)
    parts = jnp.concatenate([parts, jnp.zeros((EXTRA, width - rows), jnp.float32)], axis=1)
    block[rows : rows + EXTRA, :] = parts.astype(jnp.bfloat16)
    codes_out, *parts_out = parts_out
    codes_out[0:EXTRA, :] = block[rows : rows + EXTRA, :]
    give_parts(block, parts_out)


def complete_kernel(rows_of, codes_of, other_codes, block):
    rows, width = rows_of.shape
    unit_rows(rows_of, block)
    named = [part[...].astype(jnp.float32)[0:CODES] for part in (codes_of, other_codes)]
    named = jnp.concatenate(named + [jnp.zeros((EXTRA - 2 * CODES, width), jnp.float32)], axis=0)
    block[rows:, :] = named.astype(jnp.bfloat16)


def unit_kernel(rows_of, block, *parts_out):
    unit_rows(rows_of, block)
    give_parts(block, parts_out)


def with_units(kernel, heights, rows_of, *others):
    rows, width = rows_of.shape
    return pl.pallas_call(
        kernel,
        out_shape=[jax.ShapeDtypeStruct((height, width), jnp.bfloat16) for height in heights],
        compiler_params=pltpu.CompilerParams(vmem_limit_bytes=8 << 20),
        cost_estimate=pl.CostEstimate(flops=rows, bytes_accessed=rows, transcendentals=0),
    )(rows_of, *others)


def row_from_partial(partial, rows):
    padded = up(rows, LANES)
    if padded != rows:
        partial = jnp.concatenate(
            [partial, jnp.zeros((padded - rows, LANES), partial.dtype)], axis=0
        )
    return jnp.max(partial.T, axis=0, keepdims=True)[:, :rows]


def meet(units, row, rows, span, held, held_codes, to_block, to_held):
    column = turned_to_column(row, rows)
    starts = range(0, rows, CHUNK)
    partial = [jnp.full((CHUNK, LANES), -1.0, jnp.float32) for _ in starts]
    best_held = []
    for at in range(0, held.shape[0], TILE):
        sims = lax.dot_general(
            units,
            held[at : at + TILE, :],
            (((1,), (1,)), ((), ())),
            preferred_element_type=jnp.float32,
        )
        best = [jnp.full((CHUNK, LANES), -1.0, jnp.float32) for _ in range(0, TILE, LANES)]
        for place, top in enumerate(starts):
            mine = column[top : top + CHUNK]
            for lane in range(0, TILE, LANES):
                part = sims[top : top + CHUNK, lane : lane + LANES]
                gap = mine - held_codes[:, at + lane : at + lane + LANES]
                if to_block and to_held:
                    part = jnp.where(jnp.abs(gap) < span, part, -1.0)
                    later = gap > 0.0
                    ours, theirs = jnp.where(later, part, -1.0), jnp.where(later, -1.0, part)
                elif to_block:
                    ours = jnp.where((gap > 0.0) & (gap < span), part, -1.0)
                else:
                    theirs = jnp.where((gap < 0.0) & (gap > -span), part, -1.0)
                if to_block:
                    partial[place] = jnp.maximum(partial[place], ours)
                if to_held:
                    best[lane // LANES] = jnp.maximum(best[lane // LANES], theirs)
        best_held += [jnp.max(some, axis=0, keepdims=True) for some in best]
    return (
        row_from_partial(jnp.concatenate(partial, axis=0), rows) if to_block else None,
        jnp.concatenate(best_held, axis=1) if to_held else None,
    )


def assemble(whole, top, rows, pieces, extra):
    first, *others = pieces
    height = min(first.shape[0], rows)
    whole[top : top + height, :] = first[0:height, :]
    for last in others:
        height = last.shape[0] - extra
        whole[top + rows - height : top + rows, :] = last[0:height, :]


def gather_kernel(rows, span, lengths, *refs):
    *pieces, held, row = refs
    holds = regrouped(pieces, lengths)
    for at, block in enumerate(holds):
        assemble(held, at * rows, rows, block, EXTRA)
    row[...] = jnp.concatenate(
        [codes(block[-1], rows, span)[:, :rows] for block in holds], axis=1
    )


def gather(holds, rows, span):
    width = holds[0][0].shape[1]
    total = len(holds) * rows
    return pl.pallas_call(
        functools.partial(gather_kernel, rows, span, [len(block) for block in holds]),
        out_shape=[
            jax.ShapeDtypeStruct((total, width), jnp.bfloat16),
            jax.ShapeDtypeStruct((1, total), jnp.float32),
        ],
        compiler_params=pltpu.CompilerParams(vmem_limit_bytes=8 << 20),
        cost_estimate=pl.CostEstimate(flops=rows, bytes_accessed=rows, transcendentals=0),
    )(*[piece for block in holds for piece in block])


def regrouped(flat, lengths):
    flat = iter(flat)
    return [[next(flat) for _ in range(length)] for length in lengths]


def plane_kernel(rows, span, block, partner, held, row, best, mine):
    mine[...], _ = meet(
        block[0:rows, :], codes(block, rows, span), rows, span, held, row[...], *OWN
    )
    _, best[...] = meet(
        partner[0:rows, :], codes(partner, rows, span), rows, span, held, row[...], *HELD
    )


def line_kernel(rows, span, count, together, *refs):
    pieces, (second, held, row, best, *outs, found, joined) = refs[:count], refs[count:]
    if count > 1:
        assemble(joined, 0, rows, pieces, 0)
    units = joined if count > 1 else pieces[0]
    results = [
        meet(
            block[0:rows, :],
            codes(second, rows, span, first=place),
            rows,
            span,
            held,
            row[...],
            *TWO,
        )
        for block, place in ((units, CODES), (second, 0))
    ]
    found[...] = jnp.concatenate([mine for mine, _ in results], axis=1)
    best = jnp.maximum(best[...], jnp.maximum(results[0][1], results[1][1]))
    for out, places in zip(outs, together):
        out[...] = jnp.concatenate(
            [best[:, place * rows : (place + 1) * rows] for place in places], axis=1
        )


def plane(block, partner, held, row, rows, span):
    total, width = held.shape
    return pl.pallas_call(
        functools.partial(plane_kernel, rows, span),
        out_shape=[
            jax.ShapeDtypeStruct((1, total), jnp.float32),
            jax.ShapeDtypeStruct((1, rows), jnp.float32),
        ],
        compiler_params=pltpu.CompilerParams(vmem_limit_bytes=12 << 20),
        cost_estimate=pl.CostEstimate(flops=rows * total * width // 2, bytes_accessed=rows, transcendentals=0),
    )(block, partner, held, row)


def line(pieces, second, held, row, best, rows, span, together):
    total, width = held.shape
    outs = [jax.ShapeDtypeStruct((1, rows * len(some)), jnp.float32) for some in together]
    *bests, found = pl.pallas_call(
        functools.partial(line_kernel, rows, span, len(pieces), together),
        out_shape=outs + [jax.ShapeDtypeStruct((1, 2 * rows), jnp.float32)],
        scratch_shapes=[pltpu.VMEM((rows, width), jnp.bfloat16)],
        compiler_params=pltpu.CompilerParams(vmem_limit_bytes=12 << 20),
        cost_estimate=pl.CostEstimate(flops=rows, bytes_accessed=rows, transcendentals=0),
    )(*pieces, second, held, row, best)
    return bests, found


OWN = (True, False)
HELD = (False, True)
TWO = (True, True)


def line_rounds(chips):
    if chips == 4:
        return [[(0, 2), (3, 1), (1, 0)], [(0, 3), (3, 2), (2, 1)]]
    rounds = []
    for shift in range(1, chips // 2 + 1):
        senders = chips // 2 if 2 * shift == chips else chips
        rounds.append([(s, (s + shift) % chips) for s in range(senders)])
    return rounds


def solution(mesh):
    groups, members = mesh.shape["dp"], mesh.shape["grid"]
    assert groups == 4 and members % 2 == 0
    chips = members // 2

    def everywhere(target):
        return [
            (p * members + g, a * members + b)
            for p in range(groups)
            for g in range(members)
            for a, b in [target(p, g)]
        ]

    other_core = everywhere(lambda p, g: (p, g ^ 1))
    first = everywhere(lambda p, g: (p ^ (1 + g % 2), g))
    second = everywhere(lambda p, g: (p ^ (2 - g % 2), g))

    rounds = line_rounds(chips)
    rounds += [[]] * (len(rounds) % 2)
    rounds = [
        [
            (p * members + 2 * s + c, p * members + 2 * t + c)
            for p in range(groups)
            for c in range(2)
            for s, t in rounds[at + c]
        ]
        for at in range(0, len(rounds), 2)
    ]

    def back(pairs):
        return [(target, source) for source, target in pairs]

    def shards(embeddings, cluster, order_key):
        rows = embeddings.shape[0]
        span = 256
        while span < rows * groups * members:
            span *= 2
        halves = (rows // 2, rows // 2 + EXTRA)
        named = (cluster[:, 0] + 1) * span + order_key
        partner = lax.ppermute(embeddings, BOTH, other_core)
        raw = [lax.ppermute(embeddings, BOTH, pairs) for pairs in rounds]
        block, codes_of, *parts = with_units(
            functools.partial(prepare_kernel, span),
            (rows + EXTRA, EXTRA, *halves),
            embeddings,
            named,
        )
        from_first = [lax.ppermute(part, BOTH, first) for part in parts]
        from_second = [lax.ppermute(block, BOTH, second)]
        other_codes = lax.ppermute(codes_of, BOTH, other_core)
        (partner,) = with_units(complete_kernel, (rows + EXTRA,), partner, other_codes, codes_of)
        near_other = [lax.ppermute(partner, BOTH, pairs) for pairs in rounds]
        from_corner = [lax.ppermute(part, BOTH, second) for part in from_first]
        near = [
            list(with_units(unit_kernel, (rows, rows // 2, rows // 2), rows_of))
            for rows_of in raw
        ]
        far = [[lax.ppermute(piece, BOTH, other_core) for piece in blocks[1:]] for blocks in near]

        results, kept, sent = [], [], []
        held, row = gather([[block], from_first, from_second, from_corner], rows, span)
        held, *far[0] = lax.optimization_barrier((held, *far[0]))
        best, mine = plane(block, partner, held, row, rows, span)
        results.append(mine)
        whole, last = [tuple(range(groups))], [(0,), (1, 3), (2,)]
        for at, second_near in enumerate(near_other):
            second_near, best = lax.optimization_barrier((second_near, best))
            second_far = lax.ppermute(second_near, BOTH, other_core)
            (best,), found = line(near[at][:1], second_near, held, row, best, rows, span, whole)
            kept.append(found)
            bests, found = line(
                far[at],
                second_far,
                held,
                row,
                best,
                rows,
                span,
                last if at == len(rounds) - 1 else whole,
            )
            best = bests[0]
            sent.append(found)
        sent = lax.ppermute(jnp.concatenate(sent, axis=1), BOTH, other_core)
        kept = jnp.maximum(jnp.concatenate(kept, axis=1), sent)
        for at, pairs in enumerate(rounds):
            found = lax.ppermute(kept[:, 2 * at * rows : 2 * (at + 1) * rows], BOTH, back(pairs))
            me = lax.axis_index(BOTH)
            sender = functools.reduce(jnp.logical_or, [me == source for source, _ in pairs])
            found = jnp.where(sender, found, -1.0)
            results += [found[:, :rows], lax.ppermute(found[:, rows:], BOTH, other_core)]
        from_x = lax.ppermute(bests[1], BOTH, first)
        results.append(from_x[:, :rows])
        onward = jnp.maximum(bests[2], from_x[:, rows:])
        results.append(lax.ppermute(onward, BOTH, second))
        return functools.reduce(jnp.maximum, results, bests[0]).reshape(rows)

    placed = (P(BOTH, None), P(BOTH, None), P(BOTH))
    return jax.shard_map(
        shards, mesh=mesh, in_specs=placed, out_specs=P(BOTH), check_vma=False
    )
```

```python
import functools

import jax
import jax.numpy as jnp
from jax import lax
from jax.experimental import pallas as pl
from jax.experimental.pallas import tpu as pltpu
from jax.sharding import PartitionSpec as P

EPSILON = 1e-06
EXTRA = 16
CODES = 3
LANES = 128
TILE = 256
CHUNK = 32
BOTH = ("dp", "grid")


def up(value, multiple):
    return -(-value // multiple) * multiple


def turned_to_column(row, rows):
    return jnp.broadcast_to(row, (LANES, row.shape[1])).T[:rows]


def codes(block, rows, span, first=0):
    parts = block[block.shape[0] - EXTRA :, : up(rows, LANES)].astype(jnp.float32)
    parts = parts[first : first + CODES]
    return parts[2:3] * (4.0 * span) + parts[0:1] * 256.0 + parts[1:2]


def unit_rows(rows, out):
    values = rows[...].astype(jnp.float32)
    scale = lax.rsqrt(jnp.sum(values * values, axis=1, keepdims=True) + EPSILON)
    out[0 : rows.shape[0], :] = (values * scale).astype(jnp.bfloat16)


def give_parts(block, outs):
    for out, top in zip(outs, (0, block.shape[0] - outs[-1].shape[0])):
        out[...] = block[top : top + out.shape[0], :]


def prepare_kernel(span, embeddings, named, block, codes_out, *parts_out):
    rows, width = embeddings.shape
    unit_rows(embeddings, block)
    names = named[...].reshape(1, rows)
    keys = names & (span - 1)
    parts = [keys >> 8, keys & 255, names >> (span.bit_length() - 1)]
    parts = [part.astype(jnp.float32) for part in parts]
    parts = jnp.concatenate(parts + [jnp.zeros((EXTRA - CODES, rows), jnp.float32)], axis=0)
    parts = jnp.concatenate([parts, jnp.zeros((EXTRA, width - rows), jnp.float32)], axis=1)
    block[rows : rows + EXTRA, :] = parts.astype(jnp.bfloat16)
    codes_out[...] = block[rows : rows + EXTRA, :]
    give_parts(block, parts_out)


def complete_kernel(rows_of, codes_of, other_codes, block):
    rows, width = rows_of.shape
    unit_rows(rows_of, block)
    named = [part[...].astype(jnp.float32)[0:CODES] for part in (codes_of, other_codes)]
    named = jnp.concatenate(named + [jnp.zeros((EXTRA - 2 * CODES, width), jnp.float32)], axis=0)
    block[rows:, :] = named.astype(jnp.bfloat16)


def unit_kernel(rows_of, block, *parts_out):
    unit_rows(rows_of, block)
    give_parts(block, parts_out)


def with_units(kernel, heights, rows_of, *others):
    rows, width = rows_of.shape
    return pl.pallas_call(
        kernel,
        out_shape=[jax.ShapeDtypeStruct((height, width), jnp.bfloat16) for height in heights],
        compiler_params=pltpu.CompilerParams(vmem_limit_bytes=8 << 20),
        cost_estimate=pl.CostEstimate(flops=rows, bytes_accessed=rows, transcendentals=0),
    )(rows_of, *others)


def row_from_partial(partial, rows):
    padded = up(rows, LANES)
    if padded != rows:
        partial = jnp.concatenate(
            [partial, jnp.zeros((padded - rows, LANES), partial.dtype)], axis=0
        )
    return jnp.max(partial.T, axis=0, keepdims=True)[:, :rows]


def meet(units, row, rows, span, held, held_codes, to_block, to_held):
    column = turned_to_column(row, rows)
    starts = range(0, rows, CHUNK)
    partial = [jnp.full((CHUNK, LANES), -1.0, jnp.float32) for _ in starts]
    best_held = []
    for at in range(0, held.shape[0], TILE):
        tile = min(TILE, held.shape[0] - at)
        sims = lax.dot_general(
            units,
            held[at : at + tile, :],
            (((1,), (1,)), ((), ())),
            preferred_element_type=jnp.float32,
        )
        best = [jnp.full((CHUNK, LANES), -1.0, jnp.float32) for _ in range(0, tile, LANES)]
        for place, top in enumerate(starts):
            mine = column[top : top + CHUNK]
            for lane in range(0, tile, LANES):
                part = sims[top : top + CHUNK, lane : lane + LANES]
                gap = mine - held_codes[:, at + lane : at + lane + LANES]
                if to_block and to_held:
                    part = jnp.where(jnp.abs(gap) < span, part, -1.0)
                    later = gap > 0.0
                    ours, theirs = jnp.where(later, part, -1.0), jnp.where(later, -1.0, part)
                elif to_block:
                    ours = jnp.where((gap > 0.0) & (gap < span), part, -1.0)
                else:
                    theirs = jnp.where((gap < 0.0) & (gap > -span), part, -1.0)
                if to_block:
                    partial[place] = jnp.maximum(partial[place], ours)
                if to_held:
                    best[lane // LANES] = jnp.maximum(best[lane // LANES], theirs)
        best_held += [jnp.max(some, axis=0, keepdims=True) for some in best]
    return (
        row_from_partial(jnp.concatenate(partial, axis=0), rows) if to_block else None,
        jnp.concatenate(best_held, axis=1) if to_held else None,
    )


def assemble(whole, top, rows, pieces, extra):
    first, *others = pieces
    height = min(first.shape[0], rows)
    whole[top : top + height, :] = first[0:height, :]
    for last in others:
        height = last.shape[0] - extra
        whole[top + rows - height : top + rows, :] = last[0:height, :]


def hold(holds, held, rows, span):
    for at, block in enumerate(holds):
        assemble(held, at * rows, rows, block, EXTRA)
    row = [codes(block[-1], rows, span)[:, :rows] for block in holds]
    rest = held.shape[0] - len(holds) * rows
    if rest:
        held[len(holds) * rows :, :] = jnp.zeros((rest, held.shape[1]), held.dtype)
        row.append(jnp.zeros((1, rest), jnp.float32))
    return jnp.concatenate(row, axis=1)


def gather_kernel(rows, span, lengths, *refs):
    *pieces, held, row, joined = refs
    *holds, far = regrouped(pieces, lengths)
    row[...] = hold(holds, held, rows, span)
    assemble(joined, 0, rows, far, 0)


def gather(holds, far, rows, span):
    width = far[0].shape[1]
    total = len(holds) * rows
    parts = [*holds, far]
    return pl.pallas_call(
        functools.partial(gather_kernel, rows, span, [len(part) for part in parts]),
        out_shape=[
            jax.ShapeDtypeStruct((total, width), jnp.bfloat16),
            jax.ShapeDtypeStruct((1, total), jnp.float32),
            jax.ShapeDtypeStruct((rows, width), jnp.bfloat16),
        ],
        compiler_params=pltpu.CompilerParams(vmem_limit_bytes=8 << 20),
        cost_estimate=pl.CostEstimate(
            flops=rows * total * width // 4, bytes_accessed=rows, transcendentals=0
        ),
    )(*[piece for part in parts for piece in part])


def regrouped(flat, lengths):
    flat = iter(flat)
    return [[next(flat) for _ in range(length)] for length in lengths]


def plane_kernel(rows, span, lengths, block, partner, *refs):
    *pieces, best, mine, held = refs
    row = hold(regrouped(pieces, lengths), held, rows, span)
    mine[...], _ = meet(block[0:rows, :], codes(block, rows, span), rows, span, held, row, *OWN)
    _, theirs = meet(partner[0:rows, :], codes(partner, rows, span), rows, span, held, row, *HELD)
    best[...] = theirs[:, : best.shape[1]]


def rest_kernel(rows, span, block, partner, held, row, best, mine):
    count = best.shape[1]
    start = held.shape[0] - up(count, LANES)
    held, row = held.at[start:, :], row[:, start:]
    mine[...], _ = meet(block[0:rows, :], codes(block, rows, span), rows, span, held, row, *OWN)
    _, theirs = meet(partner[0:rows, :], codes(partner, rows, span), rows, span, held, row, *HELD)
    best[...] = theirs[:, row.shape[1] - count :]


def line_kernel(rows, span, together, count, units, second, held, row, *refs):
    bests, outs, found = refs[:count], refs[count:-1], refs[-1]
    results = [
        meet(
            block[0:rows, :],
            codes(second, rows, span, first=place),
            rows,
            span,
            held,
            row[...],
            *TWO,
        )
        for block, place in ((units, CODES), (second, 0))
    ]
    found[...] = jnp.concatenate([mine for mine, _ in results], axis=1)
    best = jnp.concatenate([best[...] for best in bests], axis=1)
    best = jnp.maximum(best, jnp.maximum(results[0][1], results[1][1]))
    for out, places in zip(outs, together):
        out[...] = jnp.concatenate(
            [best[:, place * rows : (place + 1) * rows] for place in places], axis=1
        )


def plane(block, partner, holds, rows, span):
    width = block.shape[1]
    total = len(holds) * rows
    return pl.pallas_call(
        functools.partial(plane_kernel, rows, span, [len(part) for part in holds]),
        out_shape=[
            jax.ShapeDtypeStruct((1, total), jnp.float32),
            jax.ShapeDtypeStruct((1, rows), jnp.float32),
        ],
        scratch_shapes=[pltpu.VMEM((up(total, LANES), width), jnp.bfloat16)],
        compiler_params=pltpu.CompilerParams(vmem_limit_bytes=12 << 20),
        cost_estimate=pl.CostEstimate(flops=rows, bytes_accessed=rows, transcendentals=0),
    )(block, partner, *[piece for part in holds for piece in part])


def plane_rest(block, partner, held, row, count, rows, span):
    return pl.pallas_call(
        functools.partial(rest_kernel, rows, span),
        out_shape=[
            jax.ShapeDtypeStruct((1, count), jnp.float32),
            jax.ShapeDtypeStruct((1, rows), jnp.float32),
        ],
        compiler_params=pltpu.CompilerParams(vmem_limit_bytes=12 << 20),
        cost_estimate=pl.CostEstimate(flops=rows, bytes_accessed=rows, transcendentals=0),
    )(block, partner, held, row)


def line(units, second, held, row, bests, rows, span, together):
    outs = [jax.ShapeDtypeStruct((1, rows * len(some)), jnp.float32) for some in together]
    *bests, found = pl.pallas_call(
        functools.partial(line_kernel, rows, span, together, len(bests)),
        out_shape=outs + [jax.ShapeDtypeStruct((1, 2 * rows), jnp.float32)],
        compiler_params=pltpu.CompilerParams(vmem_limit_bytes=12 << 20),
        cost_estimate=pl.CostEstimate(flops=rows, bytes_accessed=rows, transcendentals=0),
    )(units, second, held, row, *bests)
    return bests, found


OWN = (True, False)
HELD = (False, True)
TWO = (True, True)


def line_rounds(chips):
    if chips == 4:
        return [[(0, 2), (3, 1), (1, 0)], [(0, 3), (3, 2), (2, 1)]]
    rounds = []
    for shift in range(1, chips // 2 + 1):
        senders = chips // 2 if 2 * shift == chips else chips
        rounds.append([(s, (s + shift) % chips) for s in range(senders)])
    return rounds


def solution(mesh):
    groups, members = mesh.shape["dp"], mesh.shape["grid"]
    assert groups == 4 and members % 2 == 0
    chips = members // 2

    def everywhere(target):
        return [
            (p * members + g, a * members + b)
            for p in range(groups)
            for g in range(members)
            for a, b in [target(p, g)]
        ]

    other_core = everywhere(lambda p, g: (p, g ^ 1))
    first = everywhere(lambda p, g: (p ^ (1 + g % 2), g))
    second = everywhere(lambda p, g: (p ^ (2 - g % 2), g))
    corner_pairs = everywhere(lambda p, g: (p ^ 3, g))

    rounds = line_rounds(chips)
    rounds += [[]] * (len(rounds) % 2)
    rounds = [
        [
            (p * members + 2 * s + c, p * members + 2 * t + c)
            for p in range(groups)
            for c in range(2)
            for s, t in rounds[at + c]
        ]
        for at in range(0, len(rounds), 2)
    ]

    def back(pairs):
        return [(target, source) for source, target in pairs]

    def shards(embeddings, cluster, order_key):
        rows = embeddings.shape[0]
        span = 256
        while span < rows * groups * members:
            span *= 2
        halves = (rows // 2, rows // 2 + EXTRA)
        partner = lax.ppermute(embeddings, BOTH, other_core)
        raw = [lax.ppermute(embeddings, BOTH, pairs) for pairs in rounds]
        named = (cluster[:, 0] + 1) * span + order_key
        block, codes_of, *parts = with_units(
            functools.partial(prepare_kernel, span),
            (rows + EXTRA, EXTRA, *halves),
            embeddings,
            named,
        )
        from_first = [lax.ppermute(part, BOTH, first) for part in parts]
        from_second = [lax.ppermute(block, BOTH, second)]
        other_codes = lax.ppermute(codes_of, BOTH, other_core)
        (partner,) = with_units(complete_kernel, (rows + EXTRA,), partner, other_codes, codes_of)
        near_other = [lax.ppermute(partner, BOTH, pairs) for pairs in rounds]
        from_corner = [lax.ppermute(part, BOTH, second) for part in from_first]
        near = [
            list(with_units(unit_kernel, (rows, rows // 2, rows // 2), rows_of))
            for rows_of in raw
        ]
        far = [[lax.ppermute(piece, BOTH, other_core) for piece in blocks[1:]] for blocks in near]

        results, kept, sent = [], [], []
        best_two, mine = plane(block, partner, [[block], from_first], rows, span)
        results.append(mine)
        *from_corner, best_two = lax.optimization_barrier((*from_corner, best_two))
        blocks = [[block], from_first, from_second, from_corner]
        held, row, far_units = gather(blocks, far[0], rows, span)
        best_rest, mine = plane_rest(block, partner, held, row, 2 * rows, rows, span)
        results.append(mine)
        bests = [best_two, best_rest]
        far = [far_units] + [jnp.concatenate(pieces, axis=0) for pieces in far[1:]]
        whole, last = [tuple(range(groups))], [(at,) for at in range(groups)]
        for at, second_near in enumerate(near_other):
            second_near, *bests = lax.optimization_barrier((second_near, *bests))
            second_far = lax.ppermute(second_near, BOTH, other_core)
            bests, found = line(near[at][0], second_near, held, row, bests, rows, span, whole)
            kept.append(found)
            bests, found = line(
                far[at],
                second_far,
                held,
                row,
                bests,
                rows,
                span,
                last if at == len(rounds) - 1 else whole,
            )
            sent.append(found)
        sent = lax.ppermute(jnp.concatenate(sent, axis=1), BOTH, other_core)
        kept = jnp.maximum(jnp.concatenate(kept, axis=1), sent)
        kept, *bests = lax.optimization_barrier((kept, *bests))
        for at, pairs in enumerate(rounds):
            found = lax.ppermute(kept[:, 2 * at * rows : 2 * (at + 1) * rows], BOTH, back(pairs))
            me = lax.axis_index(BOTH)
            sender = functools.reduce(jnp.logical_or, [me == source for source, _ in pairs])
            found = jnp.where(sender, found, -1.0)
            results += [found[:, :rows], lax.ppermute(found[:, rows:], BOTH, other_core)]
        results += [
            lax.ppermute(best, BOTH, pairs)
            for best, pairs in zip(bests[1:], (first, second, corner_pairs))
        ]
        return functools.reduce(jnp.maximum, results, bests[0]).reshape(rows)

    placed = (P(BOTH, None), P(BOTH, None), P(BOTH))
    return jax.shard_map(
        shards, mesh=mesh, in_specs=placed, out_specs=P(BOTH), check_vma=False
    )
```

```python
import functools

import jax
import jax.numpy as jnp
from jax import lax
from jax.experimental import pallas as pl
from jax.experimental.pallas import tpu as pltpu
from jax.sharding import PartitionSpec as P

EPSILON = 1e-06
EXTRA = 16
CODES = 3
LANES = 128
TILE = 256
CHUNK = 32
BOTH = ("dp", "grid")


def up(value, multiple):
    return -(-value // multiple) * multiple


def turned_to_column(row, rows):
    return jnp.broadcast_to(row, (LANES, row.shape[1])).T[:rows]


def codes(block, rows, span, first=0):
    parts = block[block.shape[0] - EXTRA :, : up(rows, LANES)].astype(jnp.float32)
    parts = parts[first : first + CODES]
    return parts[2:3] * (4.0 * span) + parts[0:1] * 256.0 + parts[1:2]


def unit_rows(rows, out):
    values = rows[...].astype(jnp.float32)
    scale = lax.rsqrt(jnp.sum(values * values, axis=1, keepdims=True) + EPSILON)
    out[0 : rows.shape[0], :] = (values * scale).astype(jnp.bfloat16)


def give_parts(block, outs):
    for out, top in zip(outs, (0, block.shape[0] - outs[-1].shape[0])):
        out[...] = block[top : top + out.shape[0], :]


def prepare_kernel(span, embeddings, named, block, codes_out, *parts_out):
    rows, width = embeddings.shape
    unit_rows(embeddings, block)
    names = named[...].reshape(1, rows)
    keys = names & (span - 1)
    parts = [keys >> 8, keys & 255, names >> (span.bit_length() - 1)]
    parts = [part.astype(jnp.float32) for part in parts]
    parts = jnp.concatenate(parts + [jnp.zeros((EXTRA - CODES, rows), jnp.float32)], axis=0)
    parts = jnp.concatenate([parts, jnp.zeros((EXTRA, width - rows), jnp.float32)], axis=1)
    block[rows : rows + EXTRA, :] = parts.astype(jnp.bfloat16)
    codes_out[...] = block[rows : rows + EXTRA, :]
    give_parts(block, parts_out)


def complete_kernel(rows_of, codes_of, other_codes, block):
    rows, width = rows_of.shape
    unit_rows(rows_of, block)
    named = [part[...].astype(jnp.float32)[0:CODES] for part in (codes_of, other_codes)]
    named = jnp.concatenate(named + [jnp.zeros((EXTRA - 2 * CODES, width), jnp.float32)], axis=0)
    block[rows:, :] = named.astype(jnp.bfloat16)


def unit_kernel(rows_of, block, *parts_out):
    unit_rows(rows_of, block)
    give_parts(block, parts_out)


def with_units(kernel, heights, rows_of, *others):
    rows, width = rows_of.shape
    return pl.pallas_call(
        kernel,
        out_shape=[jax.ShapeDtypeStruct((height, width), jnp.bfloat16) for height in heights],
        compiler_params=pltpu.CompilerParams(vmem_limit_bytes=8 << 20),
        cost_estimate=pl.CostEstimate(flops=rows, bytes_accessed=rows, transcendentals=0),
    )(rows_of, *others)


def row_from_partial(partial, rows):
    padded = up(rows, LANES)
    if padded != rows:
        partial = jnp.concatenate(
            [partial, jnp.zeros((padded - rows, LANES), partial.dtype)], axis=0
        )
    return jnp.max(partial.T, axis=0, keepdims=True)[:, :rows]


def meet(units, parts, rows, span, held, held_codes):
    columns = [turned_to_column(row, rows) for row, _ in parts]
    starts = [(block, top) for block in range(len(parts)) for top in range(0, rows, CHUNK)]
    partial = {start: jnp.full((CHUNK, LANES), -1.0, jnp.float32) for start in starts}
    best_held = []
    for at in range(0, held.shape[0], TILE):
        tile = min(TILE, held.shape[0] - at)
        sims = lax.dot_general(
            units[...],
            held[at : at + tile, :],
            (((1,), (1,)), ((), ())),
            preferred_element_type=jnp.float32,
        )
        best = [jnp.full((CHUNK, LANES), -1.0, jnp.float32) for _ in range(0, tile, LANES)]
        for block, top in starts:
            to_block, to_held = parts[block][1]
            mine = columns[block][top : top + CHUNK]
            line = block * rows + top
            for lane in range(0, tile, LANES):
                part = sims[line : line + CHUNK, lane : lane + LANES]
                gap = mine - held_codes[:, at + lane : at + lane + LANES]
                if to_block and to_held:
                    part = jnp.where(jnp.abs(gap) < span, part, -1.0)
                    later = gap > 0.0
                    ours, theirs = jnp.where(later, part, -1.0), jnp.where(later, -1.0, part)
                elif to_block:
                    ours = jnp.where((gap > 0.0) & (gap < span), part, -1.0)
                else:
                    theirs = jnp.where((gap < 0.0) & (gap > -span), part, -1.0)
                if to_block:
                    partial[block, top] = jnp.maximum(partial[block, top], ours)
                if to_held:
                    best[lane // LANES] = jnp.maximum(best[lane // LANES], theirs)
        best_held += [jnp.max(some, axis=0, keepdims=True) for some in best]
    found = [
        row_from_partial(
            jnp.concatenate([partial[block, top] for top in range(0, rows, CHUNK)], axis=0), rows
        )
        for block, (_, (to_block, _)) in enumerate(parts)
        if to_block
    ]
    return found, jnp.concatenate(best_held, axis=1)


def assemble(whole, top, rows, pieces, extra):
    first, *others = pieces
    height = min(first.shape[0], rows)
    whole[top : top + height, :] = first[0:height, :]
    for last in others:
        height = last.shape[0] - extra
        whole[top + rows - height : top + rows, :] = last[0:height, :]


def hold(holds, held, rows, span):
    for at, block in enumerate(holds):
        assemble(held, at * rows, rows, block, EXTRA)
    row = [codes(block[-1], rows, span)[:, :rows] for block in holds]
    rest = held.shape[0] - len(holds) * rows
    if rest:
        held[len(holds) * rows :, :] = jnp.zeros((rest, held.shape[1]), held.dtype)
        row.append(jnp.zeros((1, rest), jnp.float32))
    return jnp.concatenate(row, axis=1)


def gather_kernel(rows, span, lengths, *refs):
    *pieces, held, row, joined = refs
    *holds, far = regrouped(pieces, lengths)
    row[...] = hold(holds, held, rows, span)
    assemble(joined, 0, rows, far, 0)


def gather(holds, far, rows, span):
    width = far[0].shape[1]
    total = len(holds) * rows
    parts = [*holds, far]
    return pl.pallas_call(
        functools.partial(gather_kernel, rows, span, [len(part) for part in parts]),
        out_shape=[
            jax.ShapeDtypeStruct((total, width), jnp.bfloat16),
            jax.ShapeDtypeStruct((1, total), jnp.float32),
            jax.ShapeDtypeStruct((rows, width), jnp.bfloat16),
        ],
        compiler_params=pltpu.CompilerParams(vmem_limit_bytes=8 << 20),
        cost_estimate=pl.CostEstimate(
            flops=rows * total * width // 4, bytes_accessed=rows, transcendentals=0
        ),
    )(*[piece for part in parts for piece in part])


def regrouped(flat, lengths):
    flat = iter(flat)
    return [[next(flat) for _ in range(length)] for length in lengths]


def pair(units, first, second, rows):
    units[0:rows, :] = first[0:rows, :]
    units[rows:, :] = second[0:rows, :]


def plane_kernel(rows, span, lengths, block, partner, *refs):
    *pieces, best, mine, held, units = refs
    row = hold(regrouped(pieces, lengths), held, rows, span)
    pair(units, block, partner, rows)
    parts = [(codes(block, rows, span), OWN), (codes(partner, rows, span), HELD)]
    (mine[...],), theirs = meet(units, parts, rows, span, held, row)
    best[...] = theirs[:, : best.shape[1]]


def rest_kernel(rows, span, block, partner, held, row, best, mine, units):
    count = best.shape[1]
    start = held.shape[0] - up(count, LANES)
    held, row = held.at[start:, :], row[:, start:]
    pair(units, block, partner, rows)
    parts = [(codes(block, rows, span), OWN), (codes(partner, rows, span), HELD)]
    (mine[...],), theirs = meet(units, parts, rows, span, held, row)
    best[...] = theirs[:, row.shape[1] - count :]


def line_kernel(rows, span, together, count, first, second, held, row, *refs):
    bests, outs, (found, units) = refs[:count], refs[count:-2], refs[-2:]
    pair(units, first, second, rows)
    parts = [(codes(second, rows, span, first=place), TWO) for place in (CODES, 0)]
    mine, theirs = meet(units, parts, rows, span, held, row[...])
    found[...] = jnp.concatenate(mine, axis=1)
    best = jnp.maximum(jnp.concatenate([best[...] for best in bests], axis=1), theirs)
    for out, places in zip(outs, together):
        out[...] = jnp.concatenate(
            [best[:, place * rows : (place + 1) * rows] for place in places], axis=1
        )


def plane(block, partner, holds, rows, span):
    width = block.shape[1]
    total = len(holds) * rows
    return pl.pallas_call(
        functools.partial(plane_kernel, rows, span, [len(part) for part in holds]),
        out_shape=[
            jax.ShapeDtypeStruct((1, total), jnp.float32),
            jax.ShapeDtypeStruct((1, rows), jnp.float32),
        ],
        scratch_shapes=[
            pltpu.VMEM((up(total, LANES), width), jnp.bfloat16),
            pltpu.VMEM((2 * rows, width), jnp.bfloat16),
        ],
        compiler_params=pltpu.CompilerParams(vmem_limit_bytes=12 << 20),
        cost_estimate=pl.CostEstimate(flops=rows, bytes_accessed=rows, transcendentals=0),
    )(block, partner, *[piece for part in holds for piece in part])


def plane_rest(block, partner, held, row, count, rows, span):
    return pl.pallas_call(
        functools.partial(rest_kernel, rows, span),
        out_shape=[
            jax.ShapeDtypeStruct((1, count), jnp.float32),
            jax.ShapeDtypeStruct((1, rows), jnp.float32),
        ],
        scratch_shapes=[pltpu.VMEM((2 * rows, block.shape[1]), jnp.bfloat16)],
        compiler_params=pltpu.CompilerParams(vmem_limit_bytes=12 << 20),
        cost_estimate=pl.CostEstimate(flops=rows, bytes_accessed=rows, transcendentals=0),
    )(block, partner, held, row)


def line(first, second, held, row, bests, rows, span, together):
    outs = [jax.ShapeDtypeStruct((1, rows * len(some)), jnp.float32) for some in together]
    *bests, found = pl.pallas_call(
        functools.partial(line_kernel, rows, span, together, len(bests)),
        out_shape=outs + [jax.ShapeDtypeStruct((1, 2 * rows), jnp.float32)],
        scratch_shapes=[pltpu.VMEM((2 * rows, second.shape[1]), jnp.bfloat16)],
        compiler_params=pltpu.CompilerParams(vmem_limit_bytes=12 << 20),
        cost_estimate=pl.CostEstimate(flops=rows, bytes_accessed=rows, transcendentals=0),
    )(first, second, held, row, *bests)
    return bests, found


OWN = (True, False)
HELD = (False, True)
TWO = (True, True)


def line_rounds(chips):
    if chips == 4:
        return [[(0, 2), (3, 1), (1, 0)], [(0, 3), (3, 2), (2, 1)]]
    rounds = []
    for shift in range(1, chips // 2 + 1):
        senders = chips // 2 if 2 * shift == chips else chips
        rounds.append([(s, (s + shift) % chips) for s in range(senders)])
    return rounds


def solution(mesh):
    groups, members = mesh.shape["dp"], mesh.shape["grid"]
    assert groups == 4 and members % 2 == 0
    chips = members // 2

    def everywhere(target):
        return [
            (p * members + g, a * members + b)
            for p in range(groups)
            for g in range(members)
            for a, b in [target(p, g)]
        ]

    other_core = everywhere(lambda p, g: (p, g ^ 1))
    first = everywhere(lambda p, g: (p ^ (1 + g % 2), g))
    second = everywhere(lambda p, g: (p ^ (2 - g % 2), g))

    rounds = line_rounds(chips)
    rounds += [[]] * (len(rounds) % 2)
    rounds = [
        [
            (p * members + 2 * s + c, p * members + 2 * t + c)
            for p in range(groups)
            for c in range(2)
            for s, t in rounds[at + c]
        ]
        for at in range(0, len(rounds), 2)
    ]

    def back(pairs):
        return [(target, source) for source, target in pairs]

    def shards(embeddings, cluster, order_key):
        rows = embeddings.shape[0]
        span = 256
        while span < rows * groups * members:
            span *= 2
        halves = (rows // 2, rows // 2 + EXTRA)
        partner = lax.ppermute(embeddings, BOTH, other_core)
        raw = [lax.ppermute(embeddings, BOTH, pairs) for pairs in rounds]
        named = (cluster[:, 0] + 1) * span + order_key
        block, codes_of, *parts = with_units(
            functools.partial(prepare_kernel, span),
            (rows + EXTRA, EXTRA, *halves),
            embeddings,
            named,
        )
        from_first = [lax.ppermute(part, BOTH, first) for part in parts]
        from_second = [lax.ppermute(block, BOTH, second)]
        other_codes = lax.ppermute(codes_of, BOTH, other_core)
        (partner,) = with_units(complete_kernel, (rows + EXTRA,), partner, other_codes, codes_of)
        near_other = [lax.ppermute(partner, BOTH, pairs) for pairs in rounds]
        from_corner = [lax.ppermute(part, BOTH, second) for part in from_first]
        near = [
            list(with_units(unit_kernel, (rows, rows // 2, rows // 2), rows_of))
            for rows_of in raw
        ]
        far = [[lax.ppermute(piece, BOTH, other_core) for piece in blocks[1:]] for blocks in near]

        results, kept, sent = [], [], []
        best_two, mine = plane(block, partner, [[block], from_first], rows, span)
        results.append(mine)
        *from_corner, best_two = lax.optimization_barrier((*from_corner, best_two))
        blocks = [[block], from_first, from_second, from_corner]
        held, row, far_units = gather(blocks, far[0], rows, span)
        best_rest, mine = plane_rest(block, partner, held, row, 2 * rows, rows, span)
        results.append(mine)
        bests = [best_two, best_rest]
        far = [far_units] + [jnp.concatenate(pieces, axis=0) for pieces in far[1:]]
        whole, last = [tuple(range(groups))], [(0,), (1, 3), (2,)]
        for at, second_near in enumerate(near_other):
            second_near, *bests = lax.optimization_barrier((second_near, *bests))
            second_far = lax.ppermute(second_near, BOTH, other_core)
            bests, found = line(near[at][0], second_near, held, row, bests, rows, span, whole)
            kept.append(found)
            bests, found = line(
                far[at],
                second_far,
                held,
                row,
                bests,
                rows,
                span,
                last if at == len(rounds) - 1 else whole,
            )
            sent.append(found)
        sent = lax.ppermute(jnp.concatenate(sent, axis=1), BOTH, other_core)
        kept = jnp.maximum(jnp.concatenate(kept, axis=1), sent)
        for at, pairs in enumerate(rounds):
            found = lax.ppermute(kept[:, 2 * at * rows : 2 * (at + 1) * rows], BOTH, back(pairs))
            me = lax.axis_index(BOTH)
            sender = functools.reduce(jnp.logical_or, [me == source for source, _ in pairs])
            found = jnp.where(sender, found, -1.0)
            results += [found[:, :rows], lax.ppermute(found[:, rows:], BOTH, other_core)]
        from_x = lax.ppermute(bests[1], BOTH, first)
        results.append(from_x[:, :rows])
        onward = jnp.maximum(bests[2], from_x[:, rows:])
        results.append(lax.ppermute(onward, BOTH, second))
        return functools.reduce(jnp.maximum, results, bests[0]).reshape(rows)

    placed = (P(BOTH, None), P(BOTH, None), P(BOTH))
    return jax.shard_map(
        shards, mesh=mesh, in_specs=placed, out_specs=P(BOTH), check_vma=False
    )
```

```python
import functools

import jax
import jax.numpy as jnp
from jax import lax
from jax.experimental import pallas as pl
from jax.experimental.pallas import tpu as pltpu
from jax.sharding import PartitionSpec as P

EPSILON = 1e-06
EXTRA = 16
CODES = 3
LANES = 128
TILE = 256
CHUNK = 32
BOTH = ("dp", "grid")


def up(value, multiple):
    return -(-value // multiple) * multiple


def turned_to_column(row, rows):
    return jnp.broadcast_to(row, (LANES, row.shape[1])).T[:rows]


def codes(block, rows, span, first=0):
    parts = block[block.shape[0] - EXTRA :, : up(rows, LANES)].astype(jnp.float32)
    parts = parts[first : first + CODES]
    return parts[2:3] * (4.0 * span) + parts[0:1] * 256.0 + parts[1:2]


def unit_rows(rows, out):
    values = rows[...].astype(jnp.float32)
    scale = lax.rsqrt(jnp.sum(values * values, axis=1, keepdims=True) + EPSILON)
    out[0 : rows.shape[0], :] = (values * scale).astype(jnp.bfloat16)


def give_parts(block, outs):
    for out, top in zip(outs, (0, block.shape[0] - outs[-1].shape[0])):
        out[...] = block[top : top + out.shape[0], :]


def prepare_kernel(span, embeddings, named, block, codes_out, *parts_out):
    rows, width = embeddings.shape
    unit_rows(embeddings, block)
    names = named[...].reshape(1, rows)
    keys = names & (span - 1)
    parts = [keys >> 8, keys & 255, names >> (span.bit_length() - 1)]
    parts = [part.astype(jnp.float32) for part in parts]
    parts = jnp.concatenate(parts + [jnp.zeros((EXTRA - CODES, rows), jnp.float32)], axis=0)
    parts = jnp.concatenate([parts, jnp.zeros((EXTRA, width - rows), jnp.float32)], axis=1)
    block[rows : rows + EXTRA, :] = parts.astype(jnp.bfloat16)
    codes_out[...] = block[rows : rows + EXTRA, :]
    give_parts(block, parts_out)


def complete_kernel(rows_of, codes_of, other_codes, block):
    rows, width = rows_of.shape
    unit_rows(rows_of, block)
    named = [part[...].astype(jnp.float32)[0:CODES] for part in (codes_of, other_codes)]
    named = jnp.concatenate(named + [jnp.zeros((EXTRA - 2 * CODES, width), jnp.float32)], axis=0)
    block[rows:, :] = named.astype(jnp.bfloat16)


def unit_kernel(rows_of, block, *parts_out):
    unit_rows(rows_of, block)
    give_parts(block, parts_out)


def with_units(kernel, heights, rows_of, *others):
    rows, width = rows_of.shape
    return pl.pallas_call(
        kernel,
        out_shape=[jax.ShapeDtypeStruct((height, width), jnp.bfloat16) for height in heights],
        compiler_params=pltpu.CompilerParams(vmem_limit_bytes=8 << 20),
        cost_estimate=pl.CostEstimate(flops=rows, bytes_accessed=rows, transcendentals=0),
    )(rows_of, *others)


def row_from_partial(partial, rows):
    padded = up(rows, LANES)
    if padded != rows:
        partial = jnp.concatenate(
            [partial, jnp.zeros((padded - rows, LANES), partial.dtype)], axis=0
        )
    return jnp.max(partial.T, axis=0, keepdims=True)[:, :rows]


def meet(units, parts, rows, span, held, held_codes, sims):
    columns = [turned_to_column(row, rows) for row, _ in parts]
    starts = [(block, top) for block in range(len(parts)) for top in range(0, rows, CHUNK)]
    partial = {start: jnp.full((CHUNK, LANES), -1.0, jnp.float32) for start in starts}
    best_held = []

    def form(at):
        end = min(at + TILE, held.shape[0])
        sims[:, at:end] = lax.dot_general(
            units[...],
            held[at:end, :],
            (((1,), (1,)), ((), ())),
            preferred_element_type=jnp.float32,
        )

    total = held.shape[0]
    form(0)
    for at in range(0, total, TILE):
        tile = min(TILE, total - at)
        if at + TILE < total:
            form(at + TILE)
        best = [jnp.full((CHUNK, LANES), -1.0, jnp.float32) for _ in range(0, tile, LANES)]
        for block, top in starts:
            to_block, to_held = parts[block][1]
            mine = columns[block][top : top + CHUNK]
            line = block * rows + top
            for lane in range(0, tile, LANES):
                part = sims[line : line + CHUNK, at + lane : at + lane + LANES]
                gap = mine - held_codes[:, at + lane : at + lane + LANES]
                if to_block and to_held:
                    part = jnp.where(jnp.abs(gap) < span, part, -1.0)
                    later = gap > 0.0
                    ours, theirs = jnp.where(later, part, -1.0), jnp.where(later, -1.0, part)
                elif to_block:
                    ours = jnp.where((gap > 0.0) & (gap < span), part, -1.0)
                else:
                    theirs = jnp.where((gap < 0.0) & (gap > -span), part, -1.0)
                if to_block:
                    partial[block, top] = jnp.maximum(partial[block, top], ours)
                if to_held:
                    best[lane // LANES] = jnp.maximum(best[lane // LANES], theirs)
        best_held += [jnp.max(some, axis=0, keepdims=True) for some in best]
    found = [
        row_from_partial(
            jnp.concatenate([partial[block, top] for top in range(0, rows, CHUNK)], axis=0), rows
        )
        for block, (_, (to_block, _)) in enumerate(parts)
        if to_block
    ]
    return found, jnp.concatenate(best_held, axis=1)


def assemble(whole, top, rows, pieces, extra):
    first, *others = pieces
    height = min(first.shape[0], rows)
    whole[top : top + height, :] = first[0:height, :]
    for last in others:
        height = last.shape[0] - extra
        whole[top + rows - height : top + rows, :] = last[0:height, :]


def hold(holds, held, rows, span):
    for at, block in enumerate(holds):
        assemble(held, at * rows, rows, block, EXTRA)
    row = [codes(block[-1], rows, span)[:, :rows] for block in holds]
    rest = held.shape[0] - len(holds) * rows
    if rest:
        held[len(holds) * rows :, :] = jnp.zeros((rest, held.shape[1]), held.dtype)
        row.append(jnp.zeros((1, rest), jnp.float32))
    return jnp.concatenate(row, axis=1)


def gather_kernel(rows, span, lengths, *refs):
    *pieces, held, row, joined = refs
    *holds, far = regrouped(pieces, lengths)
    row[...] = hold(holds, held, rows, span)
    assemble(joined, 0, rows, far, 0)


def gather(holds, far, rows, span):
    width = far[0].shape[1]
    total = len(holds) * rows
    parts = [*holds, far]
    return pl.pallas_call(
        functools.partial(gather_kernel, rows, span, [len(part) for part in parts]),
        out_shape=[
            jax.ShapeDtypeStruct((total, width), jnp.bfloat16),
            jax.ShapeDtypeStruct((1, total), jnp.float32),
            jax.ShapeDtypeStruct((rows, width), jnp.bfloat16),
        ],
        compiler_params=pltpu.CompilerParams(vmem_limit_bytes=8 << 20),
        cost_estimate=pl.CostEstimate(
            flops=rows * total * width // 4, bytes_accessed=rows, transcendentals=0
        ),
    )(*[piece for part in parts for piece in part])


def regrouped(flat, lengths):
    flat = iter(flat)
    return [[next(flat) for _ in range(length)] for length in lengths]


def pair(units, first, second, rows):
    units[0:rows, :] = first[0:rows, :]
    units[rows:, :] = second[0:rows, :]


def plane_kernel(rows, span, lengths, block, partner, *refs):
    *pieces, best, mine, held, units, sims = refs
    row = hold(regrouped(pieces, lengths), held, rows, span)
    pair(units, block, partner, rows)
    parts = [(codes(block, rows, span), OWN), (codes(partner, rows, span), HELD)]
    (mine[...],), theirs = meet(units, parts, rows, span, held, row, sims)
    best[...] = theirs[:, : best.shape[1]]


def rest_kernel(rows, span, block, partner, held, row, best, mine, units, sims):
    count = best.shape[1]
    start = held.shape[0] - up(count, LANES)
    held, row = held.at[start:, :], row[:, start:]
    pair(units, block, partner, rows)
    parts = [(codes(block, rows, span), OWN), (codes(partner, rows, span), HELD)]
    (mine[...],), theirs = meet(units, parts, rows, span, held, row, sims)
    best[...] = theirs[:, row.shape[1] - count :]


def line_kernel(rows, span, together, count, first, second, held, row, *refs):
    bests, outs, (found, units, sims) = refs[:count], refs[count:-3], refs[-3:]
    pair(units, first, second, rows)
    parts = [(codes(second, rows, span, first=place), TWO) for place in (CODES, 0)]
    mine, theirs = meet(units, parts, rows, span, held, row[...], sims)
    found[...] = jnp.concatenate(mine, axis=1)
    best = jnp.maximum(jnp.concatenate([best[...] for best in bests], axis=1), theirs)
    for out, places in zip(outs, together):
        out[...] = jnp.concatenate(
            [best[:, place * rows : (place + 1) * rows] for place in places], axis=1
        )


def plane(block, partner, holds, rows, span):
    width = block.shape[1]
    total = len(holds) * rows
    return pl.pallas_call(
        functools.partial(plane_kernel, rows, span, [len(part) for part in holds]),
        out_shape=[
            jax.ShapeDtypeStruct((1, total), jnp.float32),
            jax.ShapeDtypeStruct((1, rows), jnp.float32),
        ],
        scratch_shapes=[
            pltpu.VMEM((up(total, LANES), width), jnp.bfloat16),
            pltpu.VMEM((2 * rows, width), jnp.bfloat16),
            pltpu.VMEM((2 * rows, up(total, LANES)), jnp.float32),
        ],
        compiler_params=pltpu.CompilerParams(vmem_limit_bytes=12 << 20),
        cost_estimate=pl.CostEstimate(flops=rows, bytes_accessed=rows, transcendentals=0),
    )(block, partner, *[piece for part in holds for piece in part])


def plane_rest(block, partner, held, row, count, rows, span):
    return pl.pallas_call(
        functools.partial(rest_kernel, rows, span),
        out_shape=[
            jax.ShapeDtypeStruct((1, count), jnp.float32),
            jax.ShapeDtypeStruct((1, rows), jnp.float32),
        ],
        scratch_shapes=[
            pltpu.VMEM((2 * rows, block.shape[1]), jnp.bfloat16),
            pltpu.VMEM((2 * rows, up(count, LANES)), jnp.float32),
        ],
        compiler_params=pltpu.CompilerParams(vmem_limit_bytes=12 << 20),
        cost_estimate=pl.CostEstimate(flops=rows, bytes_accessed=rows, transcendentals=0),
    )(block, partner, held, row)


def line(first, second, held, row, bests, rows, span, together):
    outs = [jax.ShapeDtypeStruct((1, rows * len(some)), jnp.float32) for some in together]
    *bests, found = pl.pallas_call(
        functools.partial(line_kernel, rows, span, together, len(bests)),
        out_shape=outs + [jax.ShapeDtypeStruct((1, 2 * rows), jnp.float32)],
        scratch_shapes=[
            pltpu.VMEM((2 * rows, second.shape[1]), jnp.bfloat16),
            pltpu.VMEM((2 * rows, held.shape[0]), jnp.float32),
        ],
        compiler_params=pltpu.CompilerParams(vmem_limit_bytes=12 << 20),
        cost_estimate=pl.CostEstimate(flops=rows, bytes_accessed=rows, transcendentals=0),
    )(first, second, held, row, *bests)
    return bests, found


OWN = (True, False)
HELD = (False, True)
TWO = (True, True)


def line_rounds(chips):
    if chips == 4:
        return [[(0, 2), (3, 1), (1, 0)], [(0, 3), (3, 2), (2, 1)]]
    rounds = []
    for shift in range(1, chips // 2 + 1):
        senders = chips // 2 if 2 * shift == chips else chips
        rounds.append([(s, (s + shift) % chips) for s in range(senders)])
    return rounds


def solution(mesh):
    groups, members = mesh.shape["dp"], mesh.shape["grid"]
    assert groups == 4 and members % 2 == 0
    chips = members // 2

    def everywhere(target):
        return [
            (p * members + g, a * members + b)
            for p in range(groups)
            for g in range(members)
            for a, b in [target(p, g)]
        ]

    other_core = everywhere(lambda p, g: (p, g ^ 1))
    first = everywhere(lambda p, g: (p ^ (1 + g % 2), g))
    second = everywhere(lambda p, g: (p ^ (2 - g % 2), g))

    rounds = line_rounds(chips)
    rounds += [[]] * (len(rounds) % 2)
    rounds = [
        [
            (p * members + 2 * s + c, p * members + 2 * t + c)
            for p in range(groups)
            for c in range(2)
            for s, t in rounds[at + c]
        ]
        for at in range(0, len(rounds), 2)
    ]

    def back(pairs):
        return [(target, source) for source, target in pairs]

    def shards(embeddings, cluster, order_key):
        rows = embeddings.shape[0]
        span = 256
        while span < rows * groups * members:
            span *= 2
        halves = (rows // 2, rows // 2 + EXTRA)
        partner = lax.ppermute(embeddings, BOTH, other_core)
        raw = [lax.ppermute(embeddings, BOTH, pairs) for pairs in rounds]
        named = (cluster[:, 0] + 1) * span + order_key
        block, codes_of, *parts = with_units(
            functools.partial(prepare_kernel, span),
            (rows + EXTRA, EXTRA, *halves),
            embeddings,
            named,
        )
        from_first = [lax.ppermute(part, BOTH, first) for part in parts]
        from_second = [lax.ppermute(block, BOTH, second)]
        other_codes = lax.ppermute(codes_of, BOTH, other_core)
        (partner,) = with_units(complete_kernel, (rows + EXTRA,), partner, other_codes, codes_of)
        near_other = [lax.ppermute(partner, BOTH, pairs) for pairs in rounds]
        from_corner = [lax.ppermute(part, BOTH, second) for part in from_first]
        near = [
            list(with_units(unit_kernel, (rows, rows // 2, rows // 2), rows_of))
            for rows_of in raw
        ]
        far = [[lax.ppermute(piece, BOTH, other_core) for piece in blocks[1:]] for blocks in near]

        results, kept, sent = [], [], []
        best_two, mine = plane(block, partner, [[block], from_first], rows, span)
        results.append(mine)
        *from_corner, best_two = lax.optimization_barrier((*from_corner, best_two))
        blocks = [[block], from_first, from_second, from_corner]
        held, row, far_units = gather(blocks, far[0], rows, span)
        best_rest, mine = plane_rest(block, partner, held, row, 2 * rows, rows, span)
        results.append(mine)
        bests = [best_two, best_rest]
        far = [far_units] + [jnp.concatenate(pieces, axis=0) for pieces in far[1:]]
        whole, last = [tuple(range(groups))], [(0,), (1, 3), (2,)]
        for at, second_near in enumerate(near_other):
            second_near, *bests = lax.optimization_barrier((second_near, *bests))
            second_far = lax.ppermute(second_near, BOTH, other_core)
            bests, found = line(near[at][0], second_near, held, row, bests, rows, span, whole)
            kept.append(found)
            bests, found = line(
                far[at],
                second_far,
                held,
                row,
                bests,
                rows,
                span,
                last if at == len(rounds) - 1 else whole,
            )
            sent.append(found)
        sent = lax.ppermute(jnp.concatenate(sent, axis=1), BOTH, other_core)
        kept = jnp.maximum(jnp.concatenate(kept, axis=1), sent)
        for at, pairs in enumerate(rounds):
            found = lax.ppermute(kept[:, 2 * at * rows : 2 * (at + 1) * rows], BOTH, back(pairs))
            me = lax.axis_index(BOTH)
            sender = functools.reduce(jnp.logical_or, [me == source for source, _ in pairs])
            found = jnp.where(sender, found, -1.0)
            results += [found[:, :rows], lax.ppermute(found[:, rows:], BOTH, other_core)]
        from_x = lax.ppermute(bests[1], BOTH, first)
        results.append(from_x[:, :rows])
        onward = jnp.maximum(bests[2], from_x[:, rows:])
        results.append(lax.ppermute(onward, BOTH, second))
        return functools.reduce(jnp.maximum, results, bests[0]).reshape(rows)

    placed = (P(BOTH, None), P(BOTH, None), P(BOTH))
    return jax.shard_map(
        shards, mesh=mesh, in_specs=placed, out_specs=P(BOTH), check_vma=False
    )
```

```python
import functools

import jax
import jax.numpy as jnp
from jax import lax
from jax.experimental import pallas as pl
from jax.experimental.pallas import tpu as pltpu
from jax.sharding import PartitionSpec as P

EPSILON = 1e-06
EXTRA = 16
CODES = 3
LANES = 128
TILE = 256
CHUNK = 32
BOTH = ("dp", "grid")


def up(value, multiple):
    return -(-value // multiple) * multiple


def turned_to_column(row, rows):
    return jnp.broadcast_to(row, (LANES, row.shape[1])).T[:rows]


def codes(block, rows, span, first=0):
    parts = block[block.shape[0] - EXTRA :, : up(rows, LANES)].astype(jnp.float32)
    parts = parts[first : first + CODES]
    return parts[2:3] * (4.0 * span) + parts[0:1] * 256.0 + parts[1:2]


def unit_rows(rows, out):
    values = rows[...].astype(jnp.float32)
    scale = lax.rsqrt(jnp.sum(values * values, axis=1, keepdims=True) + EPSILON)
    out[0 : rows.shape[0], :] = (values * scale).astype(jnp.bfloat16)


def give_parts(block, outs):
    for out, top in zip(outs, (0, block.shape[0] - outs[-1].shape[0])):
        out[...] = block[top : top + out.shape[0], :]


def prepare_kernel(embeddings, cluster, order_key, block, codes_out, *parts_out):
    rows, width = embeddings.shape
    unit_rows(embeddings, block)
    keys = order_key[...].reshape(1, rows)
    parts = [keys >> 8, keys & 255, cluster[...] + 1]
    parts = [part.astype(jnp.float32) for part in parts]
    parts = jnp.concatenate(parts + [jnp.zeros((EXTRA - CODES, rows), jnp.float32)], axis=0)
    parts = jnp.concatenate([parts, jnp.zeros((EXTRA, width - rows), jnp.float32)], axis=1)
    block[rows : rows + EXTRA, :] = parts.astype(jnp.bfloat16)
    codes_out[...] = block[rows : rows + EXTRA, :]
    if parts_out:
        give_parts(block, parts_out)


def complete_kernel(block, other_codes, out):
    rows = block.shape[0] - EXTRA
    out[0:rows, :] = block[0:rows, :]
    named = [part[...].astype(jnp.float32)[0:CODES] for part in (block.at[rows:, :], other_codes)]
    rest = jnp.zeros((EXTRA - 2 * CODES, block.shape[1]), jnp.float32)
    out[rows:, :] = jnp.concatenate(named + [rest], axis=0).astype(jnp.bfloat16)


def unit_kernel(rows_of, block, *parts_out):
    unit_rows(rows_of, block)
    give_parts(block, parts_out)


def with_units(kernel, heights, rows_of, *others):
    rows, width = rows_of.shape
    return pl.pallas_call(
        kernel,
        out_shape=[jax.ShapeDtypeStruct((height, width), jnp.bfloat16) for height in heights],
        compiler_params=pltpu.CompilerParams(vmem_limit_bytes=8 << 20),
        cost_estimate=pl.CostEstimate(flops=rows, bytes_accessed=rows, transcendentals=0),
    )(rows_of, *others)


def row_from_partial(partial, rows):
    padded = up(rows, LANES)
    if padded != rows:
        partial = jnp.concatenate(
            [partial, jnp.zeros((padded - rows, LANES), partial.dtype)], axis=0
        )
    return jnp.max(partial.T, axis=0, keepdims=True)[:, :rows]


def meet(units, parts, rows, span, held, held_codes):
    columns = [turned_to_column(row, rows) for row, _ in parts]
    starts = [(block, top) for block in range(len(parts)) for top in range(0, rows, CHUNK)]
    partial = {start: jnp.full((CHUNK, LANES), -1.0, jnp.float32) for start in starts}
    best_held = []
    for at in range(0, held.shape[0], TILE):
        tile = min(TILE, held.shape[0] - at)
        sims = lax.dot_general(
            units[...],
            held[at : at + tile, :],
            (((1,), (1,)), ((), ())),
            preferred_element_type=jnp.float32,
        )
        best = [jnp.full((CHUNK, LANES), -1.0, jnp.float32) for _ in range(0, tile, LANES)]
        for block, top in starts:
            to_block, to_held = parts[block][1]
            mine = columns[block][top : top + CHUNK]
            line = block * rows + top
            for lane in range(0, tile, LANES):
                part = sims[line : line + CHUNK, lane : lane + LANES]
                gap = mine - held_codes[:, at + lane : at + lane + LANES]
                if to_block and to_held:
                    part = jnp.where(jnp.abs(gap) < span, part, -1.0)
                    later = gap > 0.0
                    ours, theirs = jnp.where(later, part, -1.0), jnp.where(later, -1.0, part)
                elif to_block:
                    ours = jnp.where((gap > 0.0) & (gap < span), part, -1.0)
                else:
                    theirs = jnp.where((gap < 0.0) & (gap > -span), part, -1.0)
                if to_block:
                    partial[block, top] = jnp.maximum(partial[block, top], ours)
                if to_held:
                    best[lane // LANES] = jnp.maximum(best[lane // LANES], theirs)
        best_held += [jnp.max(some, axis=0, keepdims=True) for some in best]
    found = [
        row_from_partial(
            jnp.concatenate([partial[block, top] for top in range(0, rows, CHUNK)], axis=0), rows
        )
        for block, (_, (to_block, _)) in enumerate(parts)
        if to_block
    ]
    return found, jnp.concatenate(best_held, axis=1)


def assemble(whole, top, rows, pieces, extra):
    first, *others = pieces
    height = min(first.shape[0], rows)
    whole[top : top + height, :] = first[0:height, :]
    for last in others:
        height = last.shape[0] - extra
        whole[top + rows - height : top + rows, :] = last[0:height, :]


def hold(holds, held, rows, span):
    for at, block in enumerate(holds):
        assemble(held, at * rows, rows, block, EXTRA)
    row = [codes(block[-1], rows, span)[:, :rows] for block in holds]
    rest = held.shape[0] - len(holds) * rows
    if rest:
        held[len(holds) * rows :, :] = jnp.zeros((rest, held.shape[1]), held.dtype)
        row.append(jnp.zeros((1, rest), jnp.float32))
    return jnp.concatenate(row, axis=1)


def gather_kernel(rows, span, lengths, *refs):
    *pieces, held, row, joined = refs
    *holds, far = regrouped(pieces, lengths)
    row[...] = hold(holds, held, rows, span)
    assemble(joined, 0, rows, far, 0)


def gather(holds, far, rows, span):
    width = far[0].shape[1]
    total = len(holds) * rows
    parts = [*holds, far]
    return pl.pallas_call(
        functools.partial(gather_kernel, rows, span, [len(part) for part in parts]),
        out_shape=[
            jax.ShapeDtypeStruct((total, width), jnp.bfloat16),
            jax.ShapeDtypeStruct((1, total), jnp.float32),
            jax.ShapeDtypeStruct((rows, width), jnp.bfloat16),
        ],
        compiler_params=pltpu.CompilerParams(vmem_limit_bytes=8 << 20),
        cost_estimate=pl.CostEstimate(
            flops=rows * total * width // 4, bytes_accessed=rows, transcendentals=0
        ),
    )(*[piece for part in parts for piece in part])


def regrouped(flat, lengths):
    flat = iter(flat)
    return [[next(flat) for _ in range(length)] for length in lengths]


def pair(units, first, second, rows):
    units[0:rows, :] = first[0:rows, :]
    units[rows:, :] = second[0:rows, :]


def plane_kernel(rows, span, lengths, block, partner, *refs):
    *pieces, best, mine, held, units = refs
    row = hold(regrouped(pieces, lengths), held, rows, span)
    pair(units, block, partner, rows)
    parts = [(codes(block, rows, span), OWN), (codes(partner, rows, span), HELD)]
    (mine[...],), theirs = meet(units, parts, rows, span, held, row)
    best[...] = theirs[:, : best.shape[1]]


def rest_kernel(rows, span, block, partner, held, row, best, mine, units):
    count = best.shape[1]
    start = held.shape[0] - up(count, LANES)
    held, row = held.at[start:, :], row[:, start:]
    pair(units, block, partner, rows)
    parts = [(codes(block, rows, span), OWN), (codes(partner, rows, span), HELD)]
    (mine[...],), theirs = meet(units, parts, rows, span, held, row)
    best[...] = theirs[:, row.shape[1] - count :]


def line_kernel(rows, span, together, count, first, second, held, row, *refs):
    bests, outs, (found, units) = refs[:count], refs[count:-2], refs[-2:]
    pair(units, first, second, rows)
    parts = [(codes(second, rows, span, first=place), TWO) for place in (CODES, 0)]
    mine, theirs = meet(units, parts, rows, span, held, row[...])
    found[...] = jnp.concatenate(mine, axis=1)
    best = jnp.maximum(jnp.concatenate([best[...] for best in bests], axis=1), theirs)
    for out, places in zip(outs, together):
        out[...] = jnp.concatenate(
            [best[:, place * rows : (place + 1) * rows] for place in places], axis=1
        )


def plane(block, partner, holds, rows, span):
    width = block.shape[1]
    total = len(holds) * rows
    return pl.pallas_call(
        functools.partial(plane_kernel, rows, span, [len(part) for part in holds]),
        out_shape=[
            jax.ShapeDtypeStruct((1, total), jnp.float32),
            jax.ShapeDtypeStruct((1, rows), jnp.float32),
        ],
        scratch_shapes=[
            pltpu.VMEM((up(total, LANES), width), jnp.bfloat16),
            pltpu.VMEM((2 * rows, width), jnp.bfloat16),
        ],
        compiler_params=pltpu.CompilerParams(vmem_limit_bytes=12 << 20),
        cost_estimate=pl.CostEstimate(flops=rows, bytes_accessed=rows, transcendentals=0),
    )(block, partner, *[piece for part in holds for piece in part])


def plane_rest(block, partner, held, row, count, rows, span):
    return pl.pallas_call(
        functools.partial(rest_kernel, rows, span),
        out_shape=[
            jax.ShapeDtypeStruct((1, count), jnp.float32),
            jax.ShapeDtypeStruct((1, rows), jnp.float32),
        ],
        scratch_shapes=[pltpu.VMEM((2 * rows, block.shape[1]), jnp.bfloat16)],
        compiler_params=pltpu.CompilerParams(vmem_limit_bytes=12 << 20),
        cost_estimate=pl.CostEstimate(flops=rows, bytes_accessed=rows, transcendentals=0),
    )(block, partner, held, row)


def line(first, second, held, row, bests, rows, span, together):
    outs = [jax.ShapeDtypeStruct((1, rows * len(some)), jnp.float32) for some in together]
    *bests, found = pl.pallas_call(
        functools.partial(line_kernel, rows, span, together, len(bests)),
        out_shape=outs + [jax.ShapeDtypeStruct((1, 2 * rows), jnp.float32)],
        scratch_shapes=[pltpu.VMEM((2 * rows, second.shape[1]), jnp.bfloat16)],
        compiler_params=pltpu.CompilerParams(vmem_limit_bytes=12 << 20),
        cost_estimate=pl.CostEstimate(flops=rows, bytes_accessed=rows, transcendentals=0),
    )(first, second, held, row, *bests)
    return bests, found


OWN = (True, False)
HELD = (False, True)
TWO = (True, True)


def line_rounds(chips):
    if chips == 4:
        return [[(0, 2), (3, 1), (1, 0)], [(0, 3), (3, 2), (2, 1)]]
    rounds = []
    for shift in range(1, chips // 2 + 1):
        senders = chips // 2 if 2 * shift == chips else chips
        rounds.append([(s, (s + shift) % chips) for s in range(senders)])
    return rounds


def solution(mesh):
    groups, members = mesh.shape["dp"], mesh.shape["grid"]
    assert groups == 4 and members % 2 == 0
    chips = members // 2

    def everywhere(target):
        return [
            (p * members + g, a * members + b)
            for p in range(groups)
            for g in range(members)
            for a, b in [target(p, g)]
        ]

    other_core = everywhere(lambda p, g: (p, g ^ 1))
    first = everywhere(lambda p, g: (p ^ (1 + g % 2), g))
    second = everywhere(lambda p, g: (p ^ (2 - g % 2), g))
    second_home = everywhere(lambda p, g: (p ^ (2 - g % 2), g ^ 1))

    rounds = line_rounds(chips)
    rounds += [[]] * (len(rounds) % 2)
    rounds = [
        [
            (p * members + 2 * s + c, p * members + 2 * t + c)
            for p in range(groups)
            for c in range(2)
            for s, t in rounds[at + c]
        ]
        for at in range(0, len(rounds), 2)
    ]

    def back(pairs):
        return [(target, source) for source, target in pairs]

    def shards(embeddings, cluster, order_key):
        rows = embeddings.shape[0]
        span = 256
        while span < rows * groups * members:
            span *= 2
        halves = (rows // 2, rows // 2 + EXTRA)
        names = (cluster.reshape(1, rows), order_key)
        raw = [lax.ppermute(embeddings, BOTH, pairs) for pairs in rounds]
        charge = [lax.ppermute(array, BOTH, other_core) for array in (embeddings, *names)]
        block, _, *parts = with_units(prepare_kernel, (rows + EXTRA, EXTRA, *halves), *charge)
        from_first = [lax.ppermute(part, BOTH, first) for part in parts]
        from_second = [lax.ppermute(block, BOTH, second)]
        own, own_codes = with_units(prepare_kernel, (rows + EXTRA, EXTRA), embeddings, *names)
        (both,) = with_units(complete_kernel, (rows + EXTRA,), block, own_codes)
        near_other = [lax.ppermute(both, BOTH, pairs) for pairs in rounds]
        from_corner = [lax.ppermute(part, BOTH, second) for part in from_first]
        near = [
            list(with_units(unit_kernel, (rows, rows // 2, rows // 2), rows_of))
            for rows_of in raw
        ]
        far = [[lax.ppermute(piece, BOTH, other_core) for piece in blocks[1:]] for blocks in near]

        in_charge, results, kept, sent = [], [], [], []
        best_two, mine = plane(block, own, [[block], from_first], rows, span)
        in_charge.append(mine)
        *from_corner, best_two = lax.optimization_barrier((*from_corner, best_two))
        blocks = [[block], from_first, from_second, from_corner]
        held, row, far_units = gather(blocks, far[0], rows, span)
        best_rest, mine = plane_rest(block, own, held, row, 2 * rows, rows, span)
        in_charge.append(mine)
        bests = [best_two, best_rest]
        far = [far_units] + [jnp.concatenate(pieces, axis=0) for pieces in far[1:]]
        whole, last = [tuple(range(groups))], [(0,), (1, 3), (2,)]
        for at, second_near in enumerate(near_other):
            second_near, *bests = lax.optimization_barrier((second_near, *bests))
            second_far = lax.ppermute(second_near, BOTH, other_core)
            bests, found = line(near[at][0], second_near, held, row, bests, rows, span, whole)
            kept.append(found)
            bests, found = line(
                far[at],
                second_far,
                held,
                row,
                bests,
                rows,
                span,
                last if at == len(rounds) - 1 else whole,
            )
            sent.append(found)
        sent = lax.ppermute(jnp.concatenate(sent, axis=1), BOTH, other_core)
        kept = jnp.maximum(jnp.concatenate(kept, axis=1), sent)
        for at, pairs in enumerate(rounds):
            found = lax.ppermute(kept[:, 2 * at * rows : 2 * (at + 1) * rows], BOTH, back(pairs))
            me = lax.axis_index(BOTH)
            sender = functools.reduce(jnp.logical_or, [me == source for source, _ in pairs])
            found = jnp.where(sender, found, -1.0)
            results += [found[:, :rows], lax.ppermute(found[:, rows:], BOTH, other_core)]
        from_x = lax.ppermute(bests[1], BOTH, first)
        in_charge += [bests[0], from_x[:, :rows]]
        onward = jnp.maximum(bests[2], from_x[:, rows:])
        results.append(lax.ppermute(onward, BOTH, second_home))
        home = functools.reduce(jnp.maximum, in_charge)
        results.append(lax.ppermute(home, BOTH, other_core))
        return functools.reduce(jnp.maximum, results).reshape(rows)

    placed = (P(BOTH, None), P(BOTH, None), P(BOTH))
    return jax.shard_map(
        shards, mesh=mesh, in_specs=placed, out_specs=P(BOTH), check_vma=False
    )
```

```python
import functools

import jax
import jax.numpy as jnp
from jax import lax
from jax.experimental import pallas as pl
from jax.experimental.pallas import tpu as pltpu
from jax.sharding import PartitionSpec as P

EPSILON = 1e-06
EXTRA = 16
CODES = 3
LANES = 128
TILE = 256
CHUNK = 32
BOTH = ("dp", "grid")


def up(value, multiple):
    return -(-value // multiple) * multiple


def turned_to_column(row, rows):
    return jnp.broadcast_to(row, (LANES, row.shape[1])).T[:rows]


def codes(block, rows, span, first=0):
    parts = block[block.shape[0] - EXTRA :, : up(rows, LANES)].astype(jnp.float32)
    parts = parts[first : first + CODES]
    return parts[2:3] * (4.0 * span) + parts[0:1] * 256.0 + parts[1:2]


def unit_rows(rows, out):
    values = rows[...].astype(jnp.float32)
    scale = lax.rsqrt(jnp.sum(values * values, axis=1, keepdims=True) + EPSILON)
    out[0 : rows.shape[0], :] = (values * scale).astype(jnp.bfloat16)


def give_parts(block, outs):
    for out, top in zip(outs, (0, block.shape[0] - outs[-1].shape[0])):
        out[...] = block[top : top + out.shape[0], :]


def prepare_kernel(embeddings, cluster, order_key, block, codes_out, *parts_out):
    rows, width = embeddings.shape
    unit_rows(embeddings, block)
    keys = order_key[...].reshape(1, rows)
    parts = [keys >> 8, keys & 255, cluster[...] + 1]
    parts = [part.astype(jnp.float32) for part in parts]
    parts = jnp.concatenate(parts + [jnp.zeros((EXTRA - CODES, rows), jnp.float32)], axis=0)
    parts = jnp.concatenate([parts, jnp.zeros((EXTRA, width - rows), jnp.float32)], axis=1)
    block[rows : rows + EXTRA, :] = parts.astype(jnp.bfloat16)
    codes_out[...] = block[rows : rows + EXTRA, :]
    if parts_out:
        give_parts(block, parts_out)


def complete_kernel(block, other_codes, out):
    rows = block.shape[0] - EXTRA
    out[0:rows, :] = block[0:rows, :]
    named = [part[...].astype(jnp.float32)[0:CODES] for part in (block.at[rows:, :], other_codes)]
    rest = jnp.zeros((EXTRA - 2 * CODES, block.shape[1]), jnp.float32)
    out[rows:, :] = jnp.concatenate(named + [rest], axis=0).astype(jnp.bfloat16)


def unit_kernel(rows_of, block, *parts_out):
    unit_rows(rows_of, block)
    give_parts(block, parts_out)


def with_units(kernel, heights, rows_of, *others):
    rows, width = rows_of.shape
    return pl.pallas_call(
        kernel,
        out_shape=[jax.ShapeDtypeStruct((height, width), jnp.bfloat16) for height in heights],
        compiler_params=pltpu.CompilerParams(vmem_limit_bytes=8 << 20),
        cost_estimate=pl.CostEstimate(flops=rows, bytes_accessed=rows, transcendentals=0),
    )(rows_of, *others)


def row_from_partial(partial, rows):
    padded = up(rows, LANES)
    if padded != rows:
        partial = jnp.concatenate(
            [partial, jnp.zeros((padded - rows, LANES), partial.dtype)], axis=0
        )
    return jnp.max(partial.T, axis=0, keepdims=True)[:, :rows]


def products(units, held, at, tile):
    return lax.dot_general(
        units,
        held[at : at + tile, :],
        (((1,), (1,)), ((), ())),
        preferred_element_type=jnp.float32,
    )


def meet(units, parts, rows, span, held, held_codes):
    columns = [turned_to_column(row, rows) for row, *_ in parts]
    starts = [(block, top) for block in range(len(parts)) for top in range(0, rows, CHUNK)]
    partial = {start: jnp.full((CHUNK, LANES), -1.0, jnp.float32) for start in starts}
    places, count = [], 0
    for part in parts:
        places.append(part[3] if len(part) > 2 else count)
        count += 0 if len(part) > 2 else rows
    best_held = []
    for at in range(0, held.shape[0], TILE):
        tile = min(TILE, held.shape[0] - at)
        sims = products(units[...], held, at, tile)
        best = [jnp.full((CHUNK, LANES), -1.0, jnp.float32) for _ in range(0, tile, LANES)]
        for block, top in starts:
            to_block, to_held = parts[block][1]
            mine = columns[block][top : top + CHUNK]
            line = places[block] + top
            for lane in range(0, tile, LANES):
                if len(parts[block]) > 2:
                    left = at + lane
                    part = parts[block][2][line : line + CHUNK, left : left + LANES]
                else:
                    part = sims[line : line + CHUNK, lane : lane + LANES]
                gap = mine - held_codes[:, at + lane : at + lane + LANES]
                if to_block and to_held:
                    part = jnp.where(jnp.abs(gap) < span, part, -1.0)
                    later = gap > 0.0
                    ours, theirs = jnp.where(later, part, -1.0), jnp.where(later, -1.0, part)
                elif to_block:
                    ours = jnp.where((gap > 0.0) & (gap < span), part, -1.0)
                else:
                    theirs = jnp.where((gap < 0.0) & (gap > -span), part, -1.0)
                if to_block:
                    partial[block, top] = jnp.maximum(partial[block, top], ours)
                if to_held:
                    best[lane // LANES] = jnp.maximum(best[lane // LANES], theirs)
        best_held += [jnp.max(some, axis=0, keepdims=True) for some in best]
    found = [
        row_from_partial(
            jnp.concatenate([partial[block, top] for top in range(0, rows, CHUNK)], axis=0), rows
        )
        for block, (_, (to_block, _), *_) in enumerate(parts)
        if to_block
    ]
    return found, jnp.concatenate(best_held, axis=1)


def assemble(whole, top, rows, pieces, extra):
    first, *others = pieces
    height = min(first.shape[0], rows)
    whole[top : top + height, :] = first[0:height, :]
    for last in others:
        height = last.shape[0] - extra
        whole[top + rows - height : top + rows, :] = last[0:height, :]


def hold(holds, held, rows, span):
    for at, block in enumerate(holds):
        assemble(held, at * rows, rows, block, EXTRA)
    row = [codes(block[-1], rows, span)[:, :rows] for block in holds]
    rest = held.shape[0] - len(holds) * rows
    if rest:
        held[len(holds) * rows :, :] = jnp.zeros((rest, held.shape[1]), held.dtype)
        row.append(jnp.zeros((1, rest), jnp.float32))
    return jnp.concatenate(row, axis=1)


def gather_kernel(rows, span, lengths, *refs):
    *pieces, held, row, joined = refs
    *holds, far = regrouped(pieces, lengths)
    row[...] = hold(holds, held, rows, span)
    assemble(joined, 0, rows, far, 0)


def gather(holds, far, rows, span):
    width = far[0].shape[1]
    total = len(holds) * rows
    parts = [*holds, far]
    return pl.pallas_call(
        functools.partial(gather_kernel, rows, span, [len(part) for part in parts]),
        out_shape=[
            jax.ShapeDtypeStruct((total, width), jnp.bfloat16),
            jax.ShapeDtypeStruct((1, total), jnp.float32),
            jax.ShapeDtypeStruct((rows, width), jnp.bfloat16),
        ],
        compiler_params=pltpu.CompilerParams(vmem_limit_bytes=8 << 20),
        cost_estimate=pl.CostEstimate(
            flops=rows * total * width // 4, bytes_accessed=rows, transcendentals=0
        ),
    )(*[piece for part in parts for piece in part])


def regrouped(flat, lengths):
    flat = iter(flat)
    return [[next(flat) for _ in range(length)] for length in lengths]


def pair(units, first, second, rows):
    units[0:rows, :] = first[0:rows, :]
    units[rows:, :] = second[0:rows, :]


def plane_kernel(rows, span, lengths, block, partner, *refs):
    *pieces, best, mine, held, units = refs
    row = hold(regrouped(pieces, lengths), held, rows, span)
    pair(units, block, partner, rows)
    parts = [(codes(block, rows, span), OWN), (codes(partner, rows, span), HELD)]
    (mine[...],), theirs = meet(units, parts, rows, span, held, row)
    best[...] = theirs[:, : best.shape[1]]


def rest_kernel(rows, span, block, partner, held, row, best, mine, units):
    count = best.shape[1]
    start = held.shape[0] - up(count, LANES)
    held, row = held.at[start:, :], row[:, start:]
    pair(units, block, partner, rows)
    parts = [(codes(block, rows, span), OWN), (codes(partner, rows, span), HELD)]
    (mine[...],), theirs = meet(units, parts, rows, span, held, row)
    best[...] = theirs[:, row.shape[1] - count :]


def products_kernel(rows, first, second, held, sims, units):
    pair(units, first, second, rows)
    for at in range(0, held.shape[0], TILE):
        tile = min(TILE, held.shape[0] - at)
        sims[:, at : at + tile] = products(units[...], held, at, tile)


def all_products(first, second, held, rows):
    total, width = held.shape
    return pl.pallas_call(
        functools.partial(products_kernel, rows),
        out_shape=jax.ShapeDtypeStruct((2 * rows, total), jnp.float32),
        scratch_shapes=[pltpu.VMEM((2 * rows, width), jnp.bfloat16)],
        compiler_params=pltpu.CompilerParams(vmem_limit_bytes=8 << 20),
        cost_estimate=pl.CostEstimate(flops=rows, bytes_accessed=rows, transcendentals=0),
    )(first, second, held)


def line_kernel(rows, span, together, count, start, sims, second, held, row, *refs):
    bests, outs, found = refs[:count], refs[count:-1], refs[-1]
    parts = [
        (codes(second, rows, span, first=CODES), TWO, sims, start),
        (codes(second, rows, span), TWO),
    ]
    mine, theirs = meet(second.at[0:rows, :], parts, rows, span, held, row[...])
    found[...] = jnp.concatenate(mine, axis=1)
    best = jnp.maximum(jnp.concatenate([best[...] for best in bests], axis=1), theirs)
    for out, places in zip(outs, together):
        out[...] = jnp.concatenate(
            [best[:, place * rows : (place + 1) * rows] for place in places], axis=1
        )


def plane(block, partner, holds, rows, span):
    width = block.shape[1]
    total = len(holds) * rows
    return pl.pallas_call(
        functools.partial(plane_kernel, rows, span, [len(part) for part in holds]),
        out_shape=[
            jax.ShapeDtypeStruct((1, total), jnp.float32),
            jax.ShapeDtypeStruct((1, rows), jnp.float32),
        ],
        scratch_shapes=[
            pltpu.VMEM((up(total, LANES), width), jnp.bfloat16),
            pltpu.VMEM((2 * rows, width), jnp.bfloat16),
        ],
        compiler_params=pltpu.CompilerParams(vmem_limit_bytes=12 << 20),
        cost_estimate=pl.CostEstimate(flops=rows, bytes_accessed=rows, transcendentals=0),
    )(block, partner, *[piece for part in holds for piece in part])


def plane_rest(block, partner, held, row, count, rows, span):
    return pl.pallas_call(
        functools.partial(rest_kernel, rows, span),
        out_shape=[
            jax.ShapeDtypeStruct((1, count), jnp.float32),
            jax.ShapeDtypeStruct((1, rows), jnp.float32),
        ],
        scratch_shapes=[pltpu.VMEM((2 * rows, block.shape[1]), jnp.bfloat16)],
        compiler_params=pltpu.CompilerParams(vmem_limit_bytes=12 << 20),
        cost_estimate=pl.CostEstimate(flops=rows, bytes_accessed=rows, transcendentals=0),
    )(block, partner, held, row)


def line(sims, start, second, held, row, bests, rows, span, together):
    outs = [jax.ShapeDtypeStruct((1, rows * len(some)), jnp.float32) for some in together]
    *bests, found = pl.pallas_call(
        functools.partial(line_kernel, rows, span, together, len(bests), start),
        out_shape=outs + [jax.ShapeDtypeStruct((1, 2 * rows), jnp.float32)],
        compiler_params=pltpu.CompilerParams(vmem_limit_bytes=8 << 20),
        cost_estimate=pl.CostEstimate(flops=rows, bytes_accessed=rows, transcendentals=0),
    )(sims, second, held, row, *bests)
    return bests, found


OWN = (True, False)
HELD = (False, True)
TWO = (True, True)


def line_rounds(chips):
    if chips == 4:
        return [[(0, 2), (3, 1), (1, 0)], [(0, 3), (3, 2), (2, 1)]]
    rounds = []
    for shift in range(1, chips // 2 + 1):
        senders = chips // 2 if 2 * shift == chips else chips
        rounds.append([(s, (s + shift) % chips) for s in range(senders)])
    return rounds


def solution(mesh):
    groups, members = mesh.shape["dp"], mesh.shape["grid"]
    assert groups == 4 and members % 2 == 0
    chips = members // 2

    def everywhere(target):
        return [
            (p * members + g, a * members + b)
            for p in range(groups)
            for g in range(members)
            for a, b in [target(p, g)]
        ]

    other_core = everywhere(lambda p, g: (p, g ^ 1))
    first = everywhere(lambda p, g: (p ^ (1 + g % 2), g))
    second = everywhere(lambda p, g: (p ^ (2 - g % 2), g))
    second_home = everywhere(lambda p, g: (p ^ (2 - g % 2), g ^ 1))

    rounds = line_rounds(chips)
    rounds += [[]] * (len(rounds) % 2)
    rounds = [
        [
            (p * members + 2 * s + c, p * members + 2 * t + c)
            for p in range(groups)
            for c in range(2)
            for s, t in rounds[at + c]
        ]
        for at in range(0, len(rounds), 2)
    ]

    def back(pairs):
        return [(target, source) for source, target in pairs]

    def shards(embeddings, cluster, order_key):
        rows = embeddings.shape[0]
        span = 256
        while span < rows * groups * members:
            span *= 2
        halves = (rows // 2, rows // 2 + EXTRA)
        names = (cluster.reshape(1, rows), order_key)
        raw = [lax.ppermute(embeddings, BOTH, pairs) for pairs in rounds]
        charge = [lax.ppermute(array, BOTH, other_core) for array in (embeddings, *names)]
        block, _, *parts = with_units(prepare_kernel, (rows + EXTRA, EXTRA, *halves), *charge)
        from_first = [lax.ppermute(part, BOTH, first) for part in parts]
        from_second = [lax.ppermute(block, BOTH, second)]
        own, own_codes = with_units(prepare_kernel, (rows + EXTRA, EXTRA), embeddings, *names)
        (both,) = with_units(complete_kernel, (rows + EXTRA,), block, own_codes)
        near_other = [lax.ppermute(both, BOTH, pairs) for pairs in rounds]
        from_corner = [lax.ppermute(part, BOTH, second) for part in from_first]
        near = [
            list(with_units(unit_kernel, (rows, rows // 2, rows // 2), rows_of))
            for rows_of in raw
        ]
        far = [[lax.ppermute(piece, BOTH, other_core) for piece in blocks[1:]] for blocks in near]

        in_charge, results, kept, sent = [], [], [], []
        best_two, mine = plane(block, own, [[block], from_first], rows, span)
        in_charge.append(mine)
        *from_corner, best_two = lax.optimization_barrier((*from_corner, best_two))
        blocks = [[block], from_first, from_second, from_corner]
        held, row, far_units = gather(blocks, far[0], rows, span)
        best_rest, mine = plane_rest(block, own, held, row, 2 * rows, rows, span)
        in_charge.append(mine)
        bests = [best_two, best_rest]
        far = [far_units] + [jnp.concatenate(pieces, axis=0) for pieces in far[1:]]
        whole, last = [tuple(range(groups))], [(0,), (1, 3), (2,)]
        for at, second_near in enumerate(near_other):
            sims = all_products(near[at][0], far[at], held, rows)
            second_near, sims, *bests = lax.optimization_barrier((second_near, sims, *bests))
            second_far = lax.ppermute(second_near, BOTH, other_core)
            bests, found = line(sims, 0, second_near, held, row, bests, rows, span, whole)
            kept.append(found)
            bests, found = line(
                sims,
                rows,
                second_far,
                held,
                row,
                bests,
                rows,
                span,
                last if at == len(rounds) - 1 else whole,
            )
            sent.append(found)
        sent = lax.ppermute(jnp.concatenate(sent, axis=1), BOTH, other_core)
        kept = jnp.maximum(jnp.concatenate(kept, axis=1), sent)
        for at, pairs in enumerate(rounds):
            found = lax.ppermute(kept[:, 2 * at * rows : 2 * (at + 1) * rows], BOTH, back(pairs))
            me = lax.axis_index(BOTH)
            sender = functools.reduce(jnp.logical_or, [me == source for source, _ in pairs])
            found = jnp.where(sender, found, -1.0)
            results += [found[:, :rows], lax.ppermute(found[:, rows:], BOTH, other_core)]
        from_x = lax.ppermute(bests[1], BOTH, first)
        in_charge += [bests[0], from_x[:, :rows]]
        onward = jnp.maximum(bests[2], from_x[:, rows:])
        results.append(lax.ppermute(onward, BOTH, second_home))
        home = functools.reduce(jnp.maximum, in_charge)
        results.append(lax.ppermute(home, BOTH, other_core))
        return functools.reduce(jnp.maximum, results).reshape(rows)

    placed = (P(BOTH, None), P(BOTH, None), P(BOTH))
    return jax.shard_map(
        shards, mesh=mesh, in_specs=placed, out_specs=P(BOTH), check_vma=False
    )
```

```python
import functools

import jax
import jax.numpy as jnp
from jax import lax
from jax.experimental import pallas as pl
from jax.experimental.pallas import tpu as pltpu
from jax.sharding import PartitionSpec as P

EPSILON = 1e-06
EXTRA = 16
CODES = 3
LANES = 128
TILE = 256
CHUNK = 32
BOTH = ("dp", "grid")


def up(value, multiple):
    return -(-value // multiple) * multiple


def turned_to_column(row, rows):
    return jnp.broadcast_to(row, (LANES, row.shape[1])).T[:rows]


def codes(block, rows, span, first=0):
    parts = block[block.shape[0] - EXTRA :, : up(rows, LANES)].astype(jnp.float32)
    parts = parts[first : first + CODES]
    return parts[2:3] * (4.0 * span) + parts[0:1] * 256.0 + parts[1:2]


def unit_rows(rows, out):
    values = rows[...].astype(jnp.float32)
    scale = lax.rsqrt(jnp.sum(values * values, axis=1, keepdims=True) + EPSILON)
    out[0 : rows.shape[0], :] = (values * scale).astype(jnp.bfloat16)


def give_parts(block, outs):
    for out, top in zip(outs, (0, block.shape[0] - outs[-1].shape[0])):
        out[...] = block[top : top + out.shape[0], :]


def prepare_kernel(embeddings, cluster, order_key, block, codes_out, *parts_out):
    rows, width = embeddings.shape
    unit_rows(embeddings, block)
    keys = order_key[...].reshape(1, rows)
    parts = [keys >> 8, keys & 255, cluster[...] + 1]
    parts = [part.astype(jnp.float32) for part in parts]
    parts = jnp.concatenate(parts + [jnp.zeros((EXTRA - CODES, rows), jnp.float32)], axis=0)
    parts = jnp.concatenate([parts, jnp.zeros((EXTRA, width - rows), jnp.float32)], axis=1)
    block[rows : rows + EXTRA, :] = parts.astype(jnp.bfloat16)
    codes_out[...] = block[rows : rows + EXTRA, :]
    if parts_out:
        give_parts(block, parts_out)


def complete_kernel(block, other_codes, out):
    rows = block.shape[0] - EXTRA
    out[0:rows, :] = block[0:rows, :]
    named = [part[...].astype(jnp.float32)[0:CODES] for part in (block.at[rows:, :], other_codes)]
    rest = jnp.zeros((EXTRA - 2 * CODES, block.shape[1]), jnp.float32)
    out[rows:, :] = jnp.concatenate(named + [rest], axis=0).astype(jnp.bfloat16)


def unit_kernel(rows_of, block, *parts_out):
    unit_rows(rows_of, block)
    give_parts(block, parts_out)


def with_units(kernel, heights, rows_of, *others):
    rows, width = rows_of.shape
    return pl.pallas_call(
        kernel,
        out_shape=[jax.ShapeDtypeStruct((height, width), jnp.bfloat16) for height in heights],
        compiler_params=pltpu.CompilerParams(vmem_limit_bytes=8 << 20),
        cost_estimate=pl.CostEstimate(flops=rows, bytes_accessed=rows, transcendentals=0),
    )(rows_of, *others)


def row_from_partial(partial, rows):
    padded = up(rows, LANES)
    if padded != rows:
        partial = jnp.concatenate(
            [partial, jnp.zeros((padded - rows, LANES), partial.dtype)], axis=0
        )
    return jnp.max(partial.T, axis=0, keepdims=True)[:, :rows]


def meet(units, parts, rows, span, held, held_codes):
    columns = [turned_to_column(row, rows) for row, _ in parts]
    starts = [(block, top) for block in range(len(parts)) for top in range(0, rows, CHUNK)]
    partial = {start: jnp.full((CHUNK, LANES), -1.0, jnp.float32) for start in starts}
    best_held = []
    for at in range(0, held.shape[0], TILE):
        tile = min(TILE, held.shape[0] - at)
        sims = lax.dot_general(
            units[...],
            held[at : at + tile, :],
            (((1,), (1,)), ((), ())),
            preferred_element_type=jnp.float32,
        )
        best = [jnp.full((CHUNK, LANES), -1.0, jnp.float32) for _ in range(0, tile, LANES)]
        for block, top in starts:
            to_block, to_held = parts[block][1]
            mine = columns[block][top : top + CHUNK]
            line = block * rows + top
            for lane in range(0, tile, LANES):
                part = sims[line : line + CHUNK, lane : lane + LANES]
                gap = mine - held_codes[:, at + lane : at + lane + LANES]
                if to_block and to_held:
                    part = jnp.where(jnp.abs(gap) < span, part, -1.0)
                    later = gap > 0.0
                    ours, theirs = jnp.where(later, part, -1.0), jnp.where(later, -1.0, part)
                elif to_block:
                    ours = jnp.where((gap > 0.0) & (gap < span), part, -1.0)
                else:
                    theirs = jnp.where((gap < 0.0) & (gap > -span), part, -1.0)
                if to_block:
                    partial[block, top] = jnp.maximum(partial[block, top], ours)
                if to_held:
                    best[lane // LANES] = jnp.maximum(best[lane // LANES], theirs)
        best_held += [jnp.max(some, axis=0, keepdims=True) for some in best]
    found = [
        row_from_partial(
            jnp.concatenate([partial[block, top] for top in range(0, rows, CHUNK)], axis=0), rows
        )
        for block, (_, (to_block, _)) in enumerate(parts)
        if to_block
    ]
    return found, jnp.concatenate(best_held, axis=1)


def assemble(whole, top, rows, pieces, extra):
    first, *others = pieces
    height = min(first.shape[0], rows)
    whole[top : top + height, :] = first[0:height, :]
    for last in others:
        height = last.shape[0] - extra
        whole[top + rows - height : top + rows, :] = last[0:height, :]


def hold(holds, held, rows, span):
    for at, block in enumerate(holds):
        assemble(held, at * rows, rows, block, EXTRA)
    row = [codes(block[-1], rows, span)[:, :rows] for block in holds]
    rest = held.shape[0] - len(holds) * rows
    if rest:
        held[len(holds) * rows :, :] = jnp.zeros((rest, held.shape[1]), held.dtype)
        row.append(jnp.zeros((1, rest), jnp.float32))
    return jnp.concatenate(row, axis=1)


def gather_kernel(rows, span, lengths, *refs):
    *pieces, held, row, joined = refs
    *holds, far = regrouped(pieces, lengths)
    row[...] = hold(holds, held, rows, span)
    assemble(joined, 0, rows, far, 0)


def gather(holds, far, rows, span):
    width = far[0].shape[1]
    total = len(holds) * rows
    parts = [*holds, far]
    return pl.pallas_call(
        functools.partial(gather_kernel, rows, span, [len(part) for part in parts]),
        out_shape=[
            jax.ShapeDtypeStruct((total, width), jnp.bfloat16),
            jax.ShapeDtypeStruct((1, total), jnp.float32),
            jax.ShapeDtypeStruct((rows, width), jnp.bfloat16),
        ],
        compiler_params=pltpu.CompilerParams(vmem_limit_bytes=8 << 20),
        cost_estimate=pl.CostEstimate(
            flops=rows * total * width // 4, bytes_accessed=rows, transcendentals=0
        ),
    )(*[piece for part in parts for piece in part])


def regrouped(flat, lengths):
    flat = iter(flat)
    return [[next(flat) for _ in range(length)] for length in lengths]


def pair(units, first, second, rows):
    units[0:rows, :] = first[0:rows, :]
    units[rows:, :] = second[0:rows, :]


def plane_kernel(rows, span, lengths, block, partner, *refs):
    *pieces, best, mine, held, units = refs
    row = hold(regrouped(pieces, lengths), held, rows, span)
    pair(units, block, partner, rows)
    parts = [(codes(block, rows, span), OWN), (codes(partner, rows, span), HELD)]
    (mine[...],), theirs = meet(units, parts, rows, span, held, row)
    best[...] = theirs[:, : best.shape[1]]


def rest_kernel(rows, span, block, partner, held, row, best, mine, units):
    count = best.shape[1]
    start = held.shape[0] - up(count, LANES)
    held, row = held.at[start:, :], row[:, start:]
    pair(units, block, partner, rows)
    parts = [(codes(block, rows, span), OWN), (codes(partner, rows, span), HELD)]
    (mine[...],), theirs = meet(units, parts, rows, span, held, row)
    best[...] = theirs[:, row.shape[1] - count :]


def line_kernel(rows, span, together, count, first, second, held, row, *refs):
    bests, outs, (found, units) = refs[:count], refs[count:-2], refs[-2:]
    pair(units, first, second, rows)
    parts = [(codes(second, rows, span, first=place), TWO) for place in (CODES, 0)]
    mine, theirs = meet(units, parts, rows, span, held, row[...])
    found[...] = jnp.concatenate(mine, axis=1)
    best = jnp.maximum(jnp.concatenate([best[...] for best in bests], axis=1), theirs)
    for out, places in zip(outs, together):
        out[...] = jnp.concatenate(
            [best[:, place * rows : (place + 1) * rows] for place in places], axis=1
        )


def plane(block, partner, holds, rows, span):
    width = block.shape[1]
    total = len(holds) * rows
    return pl.pallas_call(
        functools.partial(plane_kernel, rows, span, [len(part) for part in holds]),
        out_shape=[
            jax.ShapeDtypeStruct((1, total), jnp.float32),
            jax.ShapeDtypeStruct((1, rows), jnp.float32),
        ],
        scratch_shapes=[
            pltpu.VMEM((up(total, LANES), width), jnp.bfloat16),
            pltpu.VMEM((2 * rows, width), jnp.bfloat16),
        ],
        compiler_params=pltpu.CompilerParams(vmem_limit_bytes=12 << 20),
        cost_estimate=pl.CostEstimate(flops=rows, bytes_accessed=rows, transcendentals=0),
    )(block, partner, *[piece for part in holds for piece in part])


def plane_rest(block, partner, held, row, count, rows, span):
    return pl.pallas_call(
        functools.partial(rest_kernel, rows, span),
        out_shape=[
            jax.ShapeDtypeStruct((1, count), jnp.float32),
            jax.ShapeDtypeStruct((1, rows), jnp.float32),
        ],
        scratch_shapes=[pltpu.VMEM((2 * rows, block.shape[1]), jnp.bfloat16)],
        compiler_params=pltpu.CompilerParams(vmem_limit_bytes=12 << 20),
        cost_estimate=pl.CostEstimate(flops=rows, bytes_accessed=rows, transcendentals=0),
    )(block, partner, held, row)


def line(first, second, held, row, bests, rows, span, together):
    outs = [jax.ShapeDtypeStruct((1, rows * len(some)), jnp.float32) for some in together]
    *bests, found = pl.pallas_call(
        functools.partial(line_kernel, rows, span, together, len(bests)),
        out_shape=outs + [jax.ShapeDtypeStruct((1, 2 * rows), jnp.float32)],
        scratch_shapes=[pltpu.VMEM((2 * rows, second.shape[1]), jnp.bfloat16)],
        compiler_params=pltpu.CompilerParams(vmem_limit_bytes=12 << 20),
        cost_estimate=pl.CostEstimate(flops=rows, bytes_accessed=rows, transcendentals=0),
    )(first, second, held, row, *bests)
    return bests, found


OWN = (True, False)
HELD = (False, True)
TWO = (True, True)


def line_rounds(chips):
    if chips == 4:
        return [[(3, 1), (0, 2), (2, 3)], [(3, 0), (0, 1), (1, 2)]]
    rounds = []
    for shift in range(1, chips // 2 + 1):
        senders = chips // 2 if 2 * shift == chips else chips
        rounds.append([(s, (s + shift) % chips) for s in range(senders)])
    return rounds


def solution(mesh):
    groups, members = mesh.shape["dp"], mesh.shape["grid"]
    assert groups == 4 and members % 2 == 0
    chips = members // 2

    def everywhere(target):
        return [
            (p * members + g, a * members + b)
            for p in range(groups)
            for g in range(members)
            for a, b in [target(p, g)]
        ]

    other_core = everywhere(lambda p, g: (p, g ^ 1))
    first = everywhere(lambda p, g: (p ^ (1 + g % 2), g))
    second = everywhere(lambda p, g: (p ^ (2 - g % 2), g))
    second_home = everywhere(lambda p, g: (p ^ (2 - g % 2), g ^ 1))

    rounds = line_rounds(chips)
    rounds += [[]] * (len(rounds) % 2)
    rounds = [
        [
            (p * members + 2 * s + c, p * members + 2 * t + c)
            for p in range(groups)
            for c in range(2)
            for s, t in rounds[at + c]
        ]
        for at in range(0, len(rounds), 2)
    ]

    def back(pairs):
        return [(target, source) for source, target in pairs]

    def shards(embeddings, cluster, order_key):
        rows = embeddings.shape[0]
        span = 256
        while span < rows * groups * members:
            span *= 2
        halves = (rows // 2, rows // 2 + EXTRA)
        names = (cluster.reshape(1, rows), order_key)
        raw = [lax.ppermute(embeddings, BOTH, pairs) for pairs in rounds]
        charge = [lax.ppermute(array, BOTH, other_core) for array in (embeddings, *names)]
        block, _, *parts = with_units(prepare_kernel, (rows + EXTRA, EXTRA, *halves), *charge)
        from_first = [lax.ppermute(part, BOTH, first) for part in parts]
        from_second = [lax.ppermute(block, BOTH, second)]
        own, own_codes = with_units(prepare_kernel, (rows + EXTRA, EXTRA), embeddings, *names)
        (both,) = with_units(complete_kernel, (rows + EXTRA,), block, own_codes)
        near_other = [lax.ppermute(both, BOTH, pairs) for pairs in rounds]
        from_corner = [lax.ppermute(part, BOTH, second) for part in from_first]
        near = [
            list(with_units(unit_kernel, (rows, rows // 2, rows // 2), rows_of))
            for rows_of in raw
        ]
        far = [[lax.ppermute(piece, BOTH, other_core) for piece in blocks[1:]] for blocks in near]

        in_charge, results, kept, sent = [], [], [], []
        best_two, mine = plane(block, own, [[block], from_first], rows, span)
        in_charge.append(mine)
        *from_corner, best_two = lax.optimization_barrier((*from_corner, best_two))
        blocks = [[block], from_first, from_second, from_corner]
        held, row, far_units = gather(blocks, far[0], rows, span)
        best_rest, mine = plane_rest(block, own, held, row, 2 * rows, rows, span)
        in_charge.append(mine)
        bests = [best_two, best_rest]
        far = [far_units] + [jnp.concatenate(pieces, axis=0) for pieces in far[1:]]
        whole, last = [tuple(range(groups))], [(0,), (1, 3), (2,)]
        for at, second_near in enumerate(near_other):
            second_near, *bests = lax.optimization_barrier((second_near, *bests))
            second_far = lax.ppermute(second_near, BOTH, other_core)
            bests, found = line(near[at][0], second_near, held, row, bests, rows, span, whole)
            kept.append(found)
            bests, found = line(
                far[at],
                second_far,
                held,
                row,
                bests,
                rows,
                span,
                last if at == len(rounds) - 1 else whole,
            )
            sent.append(found)
        sent = lax.ppermute(jnp.concatenate(sent, axis=1), BOTH, other_core)
        kept = jnp.maximum(jnp.concatenate(kept, axis=1), sent)
        for at, pairs in enumerate(rounds):
            found = lax.ppermute(kept[:, 2 * at * rows : 2 * (at + 1) * rows], BOTH, back(pairs))
            me = lax.axis_index(BOTH)
            sender = functools.reduce(jnp.logical_or, [me == source for source, _ in pairs])
            found = jnp.where(sender, found, -1.0)
            results += [found[:, :rows], lax.ppermute(found[:, rows:], BOTH, other_core)]
        from_x = lax.ppermute(bests[1], BOTH, first)
        in_charge += [bests[0], from_x[:, :rows]]
        onward = jnp.maximum(bests[2], from_x[:, rows:])
        results.append(lax.ppermute(onward, BOTH, second_home))
        home = functools.reduce(jnp.maximum, in_charge)
        results.append(lax.ppermute(home, BOTH, other_core))
        return functools.reduce(jnp.maximum, results).reshape(rows)

    placed = (P(BOTH, None), P(BOTH, None), P(BOTH))
    return jax.shard_map(
        shards, mesh=mesh, in_specs=placed, out_specs=P(BOTH), check_vma=False
    )
```

```python
import functools

import jax
import jax.numpy as jnp
from jax import lax
from jax.experimental import pallas as pl
from jax.experimental.pallas import tpu as pltpu
from jax.sharding import PartitionSpec as P

EPSILON = 1e-06
EXTRA = 16
CODES = 3
LANES = 128
TILE = 256
CHUNK = 32
BOTH = ("dp", "grid")


def up(value, multiple):
    return -(-value // multiple) * multiple


def turned_to_column(row, rows):
    return jnp.broadcast_to(row, (LANES, row.shape[1])).T[:rows]


def codes(block, rows, span, first=0):
    parts = block[block.shape[0] - EXTRA :, : up(rows, LANES)].astype(jnp.float32)
    parts = parts[first : first + CODES]
    return parts[2:3] * (4.0 * span) + parts[0:1] * 256.0 + parts[1:2]


def unit_rows(rows, out):
    values = rows[...].astype(jnp.float32)
    scale = lax.rsqrt(jnp.sum(values * values, axis=1, keepdims=True) + EPSILON)
    out[0 : rows.shape[0], :] = (values * scale).astype(jnp.bfloat16)


def give_parts(block, outs):
    for out, top in zip(outs, (0, block.shape[0] - outs[-1].shape[0])):
        out[...] = block[top : top + out.shape[0], :]


def prepare_kernel(embeddings, cluster, order_key, block, codes_out, *parts_out):
    rows, width = embeddings.shape
    unit_rows(embeddings, block)
    keys = order_key[...].reshape(1, rows)
    parts = [keys >> 8, keys & 255, cluster[...] + 1]
    parts = [part.astype(jnp.float32) for part in parts]
    parts = jnp.concatenate(parts + [jnp.zeros((EXTRA - CODES, rows), jnp.float32)], axis=0)
    parts = jnp.concatenate([parts, jnp.zeros((EXTRA, width - rows), jnp.float32)], axis=1)
    block[rows : rows + EXTRA, :] = parts.astype(jnp.bfloat16)
    codes_out[...] = block[rows : rows + EXTRA, :]
    if parts_out:
        give_parts(block, parts_out)


def complete_kernel(block, other_codes, out):
    rows = block.shape[0] - EXTRA
    out[0:rows, :] = block[0:rows, :]
    named = [part[...].astype(jnp.float32)[0:CODES] for part in (block.at[rows:, :], other_codes)]
    rest = jnp.zeros((EXTRA - 2 * CODES, block.shape[1]), jnp.float32)
    out[rows:, :] = jnp.concatenate(named + [rest], axis=0).astype(jnp.bfloat16)


def unit_kernel(rows_of, block, *parts_out):
    unit_rows(rows_of, block)
    give_parts(block, parts_out)


def with_units(kernel, heights, rows_of, *others):
    rows, width = rows_of.shape
    return pl.pallas_call(
        kernel,
        out_shape=[jax.ShapeDtypeStruct((height, width), jnp.bfloat16) for height in heights],
        compiler_params=pltpu.CompilerParams(vmem_limit_bytes=8 << 20),
        cost_estimate=pl.CostEstimate(flops=rows, bytes_accessed=rows, transcendentals=0),
    )(rows_of, *others)


def row_from_partial(partial, rows):
    padded = up(rows, LANES)
    if padded != rows:
        partial = jnp.concatenate(
            [partial, jnp.zeros((padded - rows, LANES), partial.dtype)], axis=0
        )
    return jnp.max(partial.T, axis=0, keepdims=True)[:, :rows]


def meet(units, parts, rows, span, held, held_codes):
    columns = [turned_to_column(row, rows) for row, _ in parts]
    starts = [(block, top) for block in range(len(parts)) for top in range(0, rows, CHUNK)]
    partial = {start: jnp.full((CHUNK, LANES), -1.0, jnp.float32) for start in starts}
    best_held = []
    for at in range(0, held.shape[0], TILE):
        tile = min(TILE, held.shape[0] - at)
        sims = lax.dot_general(
            units[...],
            held[at : at + tile, :],
            (((1,), (1,)), ((), ())),
            preferred_element_type=jnp.float32,
        )
        best = [jnp.full((CHUNK, LANES), -1.0, jnp.float32) for _ in range(0, tile, LANES)]
        for block, top in starts:
            to_block, to_held = parts[block][1]
            mine = columns[block][top : top + CHUNK]
            line = block * rows + top
            for lane in range(0, tile, LANES):
                part = sims[line : line + CHUNK, lane : lane + LANES]
                gap = mine - held_codes[:, at + lane : at + lane + LANES]
                if to_block and to_held:
                    part = jnp.where(jnp.abs(gap) < span, part, -1.0)
                    later = gap > 0.0
                    ours, theirs = jnp.where(later, part, -1.0), jnp.where(later, -1.0, part)
                elif to_block:
                    ours = jnp.where((gap > 0.0) & (gap < span), part, -1.0)
                else:
                    theirs = jnp.where((gap < 0.0) & (gap > -span), part, -1.0)
                if to_block:
                    partial[block, top] = jnp.maximum(partial[block, top], ours)
                if to_held:
                    best[lane // LANES] = jnp.maximum(best[lane // LANES], theirs)
        best_held += [jnp.max(some, axis=0, keepdims=True) for some in best]
    found = [
        row_from_partial(
            jnp.concatenate([partial[block, top] for top in range(0, rows, CHUNK)], axis=0), rows
        )
        for block, (_, (to_block, _)) in enumerate(parts)
        if to_block
    ]
    return found, jnp.concatenate(best_held, axis=1)


def assemble(whole, top, rows, pieces, extra):
    first, *others = pieces
    height = min(first.shape[0], rows)
    whole[top : top + height, :] = first[0:height, :]
    for last in others:
        height = last.shape[0] - extra
        whole[top + rows - height : top + rows, :] = last[0:height, :]


def hold(holds, held, rows, span):
    for at, block in enumerate(holds):
        assemble(held, at * rows, rows, block, EXTRA)
    row = [codes(block[-1], rows, span)[:, :rows] for block in holds]
    rest = held.shape[0] - len(holds) * rows
    if rest:
        held[len(holds) * rows :, :] = jnp.zeros((rest, held.shape[1]), held.dtype)
        row.append(jnp.zeros((1, rest), jnp.float32))
    return jnp.concatenate(row, axis=1)


def gather_kernel(rows, span, lengths, *refs):
    *pieces, held, row, joined = refs
    *holds, far = regrouped(pieces, lengths)
    row[...] = hold(holds, held, rows, span)
    assemble(joined, 0, rows, far, 0)


def gather(holds, far, rows, span):
    width = far[0].shape[1]
    total = len(holds) * rows
    parts = [*holds, far]
    return pl.pallas_call(
        functools.partial(gather_kernel, rows, span, [len(part) for part in parts]),
        out_shape=[
            jax.ShapeDtypeStruct((total, width), jnp.bfloat16),
            jax.ShapeDtypeStruct((1, total), jnp.float32),
            jax.ShapeDtypeStruct((rows, width), jnp.bfloat16),
        ],
        compiler_params=pltpu.CompilerParams(vmem_limit_bytes=8 << 20),
        cost_estimate=pl.CostEstimate(
            flops=rows * total * width // 4, bytes_accessed=rows, transcendentals=0
        ),
    )(*[piece for part in parts for piece in part])


def regrouped(flat, lengths):
    flat = iter(flat)
    return [[next(flat) for _ in range(length)] for length in lengths]


def pair(units, first, second, rows):
    units[0:rows, :] = first[0:rows, :]
    units[rows:, :] = second[0:rows, :]


def plane_kernel(rows, span, lengths, block, partner, *refs):
    *pieces, best, mine, held, units = refs
    row = hold(regrouped(pieces, lengths), held, rows, span)
    pair(units, block, partner, rows)
    parts = [(codes(block, rows, span), OWN), (codes(partner, rows, span), HELD)]
    (mine[...],), theirs = meet(units, parts, rows, span, held, row)
    best[...] = theirs[:, : best.shape[1]]


def rest_kernel(rows, span, block, partner, held, row, best, mine, units):
    count = best.shape[1]
    start = held.shape[0] - up(count, LANES)
    held, row = held.at[start:, :], row[:, start:]
    pair(units, block, partner, rows)
    parts = [(codes(block, rows, span), OWN), (codes(partner, rows, span), HELD)]
    (mine[...],), theirs = meet(units, parts, rows, span, held, row)
    best[...] = theirs[:, row.shape[1] - count :]


def line_kernel(rows, span, together, count, first, second, held, row, *refs):
    bests, outs, (found, units) = refs[:count], refs[count:-2], refs[-2:]
    pair(units, first, second, rows)
    parts = [(codes(second, rows, span, first=place), TWO) for place in (CODES, 0)]
    mine, theirs = meet(units, parts, rows, span, held, row[...])
    found[...] = jnp.concatenate(mine, axis=1)
    best = jnp.maximum(jnp.concatenate([best[...] for best in bests], axis=1), theirs)
    for out, places in zip(outs, together):
        out[...] = jnp.concatenate(
            [best[:, place * rows : (place + 1) * rows] for place in places], axis=1
        )


def plane(block, partner, holds, rows, span):
    width = block.shape[1]
    total = len(holds) * rows
    return pl.pallas_call(
        functools.partial(plane_kernel, rows, span, [len(part) for part in holds]),
        out_shape=[
            jax.ShapeDtypeStruct((1, total), jnp.float32),
            jax.ShapeDtypeStruct((1, rows), jnp.float32),
        ],
        scratch_shapes=[
            pltpu.VMEM((up(total, LANES), width), jnp.bfloat16),
            pltpu.VMEM((2 * rows, width), jnp.bfloat16),
        ],
        compiler_params=pltpu.CompilerParams(vmem_limit_bytes=12 << 20),
        cost_estimate=pl.CostEstimate(flops=rows, bytes_accessed=rows, transcendentals=0),
    )(block, partner, *[piece for part in holds for piece in part])


def plane_rest(block, partner, held, row, count, rows, span):
    return pl.pallas_call(
        functools.partial(rest_kernel, rows, span),
        out_shape=[
            jax.ShapeDtypeStruct((1, count), jnp.float32),
            jax.ShapeDtypeStruct((1, rows), jnp.float32),
        ],
        scratch_shapes=[pltpu.VMEM((2 * rows, block.shape[1]), jnp.bfloat16)],
        compiler_params=pltpu.CompilerParams(vmem_limit_bytes=12 << 20),
        cost_estimate=pl.CostEstimate(flops=rows, bytes_accessed=rows, transcendentals=0),
    )(block, partner, held, row)


def line(first, second, held, row, bests, rows, span, together):
    outs = [jax.ShapeDtypeStruct((1, rows * len(some)), jnp.float32) for some in together]
    *bests, found = pl.pallas_call(
        functools.partial(line_kernel, rows, span, together, len(bests)),
        out_shape=outs + [jax.ShapeDtypeStruct((1, 2 * rows), jnp.float32)],
        scratch_shapes=[pltpu.VMEM((2 * rows, second.shape[1]), jnp.bfloat16)],
        compiler_params=pltpu.CompilerParams(vmem_limit_bytes=12 << 20),
        cost_estimate=pl.CostEstimate(flops=rows, bytes_accessed=rows, transcendentals=0),
    )(first, second, held, row, *bests)
    return bests, found


OWN = (True, False)
HELD = (False, True)
TWO = (True, True)


def line_rounds(chips):
    if chips == 4:
        return [[(2, 0), (1, 3), (0, 1), (3, 2)], [(3, 0), (1, 2)]]
    rounds = []
    for shift in range(1, chips // 2 + 1):
        senders = chips // 2 if 2 * shift == chips else chips
        rounds.append([(s, (s + shift) % chips) for s in range(senders)])
    return rounds


def solution(mesh):
    groups, members = mesh.shape["dp"], mesh.shape["grid"]
    assert groups == 4 and members % 2 == 0
    chips = members // 2

    def everywhere(target):
        return [
            (p * members + g, a * members + b)
            for p in range(groups)
            for g in range(members)
            for a, b in [target(p, g)]
        ]

    other_core = everywhere(lambda p, g: (p, g ^ 1))
    first = everywhere(lambda p, g: (p ^ (1 + g % 2), g))
    second = everywhere(lambda p, g: (p ^ (2 - g % 2), g))
    second_home = everywhere(lambda p, g: (p ^ (2 - g % 2), g ^ 1))

    rounds = line_rounds(chips)
    rounds += [[]] * (len(rounds) % 2)
    rounds = [
        [
            (p * members + 2 * s + c, p * members + 2 * t + c)
            for p in range(groups)
            for c in range(2)
            for s, t in rounds[at + c]
        ]
        for at in range(0, len(rounds), 2)
    ]

    def back(pairs):
        return [(target, source) for source, target in pairs]

    def shards(embeddings, cluster, order_key):
        rows = embeddings.shape[0]
        span = 256
        while span < rows * groups * members:
            span *= 2
        halves = (rows // 2, rows // 2 + EXTRA)
        names = (cluster.reshape(1, rows), order_key)
        raw = [lax.ppermute(embeddings, BOTH, pairs) for pairs in rounds]
        charge = [lax.ppermute(array, BOTH, other_core) for array in (embeddings, *names)]
        block, _, *parts = with_units(prepare_kernel, (rows + EXTRA, EXTRA, *halves), *charge)
        from_first = [lax.ppermute(part, BOTH, first) for part in parts]
        from_second = [lax.ppermute(block, BOTH, second)]
        own, own_codes = with_units(prepare_kernel, (rows + EXTRA, EXTRA), embeddings, *names)
        (both,) = with_units(complete_kernel, (rows + EXTRA,), block, own_codes)
        near_other = [lax.ppermute(both, BOTH, pairs) for pairs in rounds]
        from_corner = [lax.ppermute(part, BOTH, second) for part in from_first]
        near = [
            list(with_units(unit_kernel, (rows, rows // 2, rows // 2), rows_of))
            for rows_of in raw
        ]
        far = [[lax.ppermute(piece, BOTH, other_core) for piece in blocks[1:]] for blocks in near]

        in_charge, results, kept, sent = [], [], [], []
        best_two, mine = plane(block, own, [[block], from_first], rows, span)
        in_charge.append(mine)
        *from_corner, best_two = lax.optimization_barrier((*from_corner, best_two))
        blocks = [[block], from_first, from_second, from_corner]
        held, row, far_units = gather(blocks, far[0], rows, span)
        best_rest, mine = plane_rest(block, own, held, row, 2 * rows, rows, span)
        in_charge.append(mine)
        bests = [best_two, best_rest]
        far = [far_units] + [jnp.concatenate(pieces, axis=0) for pieces in far[1:]]
        whole, last = [tuple(range(groups))], [(0,), (1, 3), (2,)]
        for at, second_near in enumerate(near_other):
            second_near, *bests = lax.optimization_barrier((second_near, *bests))
            second_far = lax.ppermute(second_near, BOTH, other_core)
            bests, found = line(near[at][0], second_near, held, row, bests, rows, span, whole)
            kept.append(found)
            bests, found = line(
                far[at],
                second_far,
                held,
                row,
                bests,
                rows,
                span,
                last if at == len(rounds) - 1 else whole,
            )
            sent.append(found)
        sent = lax.ppermute(jnp.concatenate(sent, axis=1), BOTH, other_core)
        kept = jnp.maximum(jnp.concatenate(kept, axis=1), sent)
        for at, pairs in enumerate(rounds):
            found = lax.ppermute(kept[:, 2 * at * rows : 2 * (at + 1) * rows], BOTH, back(pairs))
            me = lax.axis_index(BOTH)
            sender = functools.reduce(jnp.logical_or, [me == source for source, _ in pairs])
            found = jnp.where(sender, found, -1.0)
            results += [found[:, :rows], lax.ppermute(found[:, rows:], BOTH, other_core)]
        from_x = lax.ppermute(bests[1], BOTH, first)
        in_charge += [bests[0], from_x[:, :rows]]
        onward = jnp.maximum(bests[2], from_x[:, rows:])
        results.append(lax.ppermute(onward, BOTH, second_home))
        home = functools.reduce(jnp.maximum, in_charge)
        results.append(lax.ppermute(home, BOTH, other_core))
        return functools.reduce(jnp.maximum, results).reshape(rows)

    placed = (P(BOTH, None), P(BOTH, None), P(BOTH))
    return jax.shard_map(
        shards, mesh=mesh, in_specs=placed, out_specs=P(BOTH), check_vma=False
    )
```

```python
import functools

import jax
import jax.numpy as jnp
from jax import lax
from jax.experimental import pallas as pl
from jax.experimental.pallas import tpu as pltpu
from jax.sharding import PartitionSpec as P

EPSILON = 1e-06
EXTRA = 16
CODES = 3
LANES = 128
TILE = 640
CHUNK = 32
BOTH = ("dp", "grid")


def up(value, multiple):
    return -(-value // multiple) * multiple


def turned_to_column(row, rows):
    return jnp.broadcast_to(row, (LANES, row.shape[1])).T[:rows]


def codes(block, rows, span, first=0):
    parts = block[block.shape[0] - EXTRA :, : up(rows, LANES)].astype(jnp.float32)
    parts = parts[first : first + CODES]
    return parts[2:3] * (4.0 * span) + parts[0:1] * 256.0 + parts[1:2]


def unit_rows(rows, out):
    values = rows[...].astype(jnp.float32)
    scale = lax.rsqrt(jnp.sum(values * values, axis=1, keepdims=True) + EPSILON)
    out[0 : rows.shape[0], :] = (values * scale).astype(jnp.bfloat16)


def give_parts(block, outs):
    for out, top in zip(outs, (0, block.shape[0] - outs[-1].shape[0])):
        out[...] = block[top : top + out.shape[0], :]


def prepare_kernel(embeddings, cluster, order_key, block, codes_out, *parts_out):
    rows, width = embeddings.shape
    unit_rows(embeddings, block)
    keys = order_key[...].reshape(1, rows)
    parts = [keys >> 8, keys & 255, cluster[...] + 1]
    parts = [part.astype(jnp.float32) for part in parts]
    parts = jnp.concatenate(parts + [jnp.zeros((EXTRA - CODES, rows), jnp.float32)], axis=0)
    parts = jnp.concatenate([parts, jnp.zeros((EXTRA, width - rows), jnp.float32)], axis=1)
    block[rows : rows + EXTRA, :] = parts.astype(jnp.bfloat16)
    codes_out[...] = block[rows : rows + EXTRA, :]
    if parts_out:
        give_parts(block, parts_out)


def complete_kernel(block, other_codes, out):
    rows = block.shape[0] - EXTRA
    out[0:rows, :] = block[0:rows, :]
    named = [part[...].astype(jnp.float32)[0:CODES] for part in (block.at[rows:, :], other_codes)]
    rest = jnp.zeros((EXTRA - 2 * CODES, block.shape[1]), jnp.float32)
    out[rows:, :] = jnp.concatenate(named + [rest], axis=0).astype(jnp.bfloat16)


def unit_kernel(rows_of, block, *parts_out):
    unit_rows(rows_of, block)
    give_parts(block, parts_out)


def with_units(kernel, heights, rows_of, *others):
    rows, width = rows_of.shape
    return pl.pallas_call(
        kernel,
        out_shape=[jax.ShapeDtypeStruct((height, width), jnp.bfloat16) for height in heights],
        compiler_params=pltpu.CompilerParams(vmem_limit_bytes=8 << 20),
        cost_estimate=pl.CostEstimate(flops=rows, bytes_accessed=rows, transcendentals=0),
    )(rows_of, *others)


def row_from_partial(partial, rows):
    padded = up(rows, LANES)
    if padded != rows:
        partial = jnp.concatenate(
            [partial, jnp.zeros((padded - rows, LANES), partial.dtype)], axis=0
        )
    return jnp.max(partial.T, axis=0, keepdims=True)[:, :rows]


def meet(units, parts, rows, span, held, held_codes):
    columns = [turned_to_column(row, rows) for row, _ in parts]
    starts = [(block, top) for block in range(len(parts)) for top in range(0, rows, CHUNK)]
    partial = {start: jnp.full((CHUNK, LANES), -1.0, jnp.float32) for start in starts}
    best_held = []
    for at in range(0, held.shape[0], TILE):
        tile = min(TILE, held.shape[0] - at)
        sims = lax.dot_general(
            units[...],
            held[at : at + tile, :],
            (((1,), (1,)), ((), ())),
            preferred_element_type=jnp.float32,
        )
        best = [jnp.full((CHUNK, LANES), -1.0, jnp.float32) for _ in range(0, tile, LANES)]
        for block, top in starts:
            to_block, to_held = parts[block][1]
            mine = columns[block][top : top + CHUNK]
            line = block * rows + top
            for lane in range(0, tile, LANES):
                part = sims[line : line + CHUNK, lane : lane + LANES]
                gap = mine - held_codes[:, at + lane : at + lane + LANES]
                if to_block and to_held:
                    part = jnp.where(jnp.abs(gap) < span, part, -1.0)
                    later = gap > 0.0
                    ours, theirs = jnp.where(later, part, -1.0), jnp.where(later, -1.0, part)
                elif to_block:
                    ours = jnp.where((gap > 0.0) & (gap < span), part, -1.0)
                else:
                    theirs = jnp.where((gap < 0.0) & (gap > -span), part, -1.0)
                if to_block:
                    partial[block, top] = jnp.maximum(partial[block, top], ours)
                if to_held:
                    best[lane // LANES] = jnp.maximum(best[lane // LANES], theirs)
        best_held += [jnp.max(some, axis=0, keepdims=True) for some in best]
    found = [
        row_from_partial(
            jnp.concatenate([partial[block, top] for top in range(0, rows, CHUNK)], axis=0), rows
        )
        for block, (_, (to_block, _)) in enumerate(parts)
        if to_block
    ]
    return found, jnp.concatenate(best_held, axis=1)


def assemble(whole, top, rows, pieces, extra):
    first, *others = pieces
    height = min(first.shape[0], rows)
    whole[top : top + height, :] = first[0:height, :]
    for last in others:
        height = last.shape[0] - extra
        whole[top + rows - height : top + rows, :] = last[0:height, :]


def hold(holds, held, rows, span):
    for at, block in enumerate(holds):
        assemble(held, at * rows, rows, block, EXTRA)
    row = [codes(block[-1], rows, span)[:, :rows] for block in holds]
    rest = held.shape[0] - len(holds) * rows
    if rest:
        held[len(holds) * rows :, :] = jnp.zeros((rest, held.shape[1]), held.dtype)
        row.append(jnp.zeros((1, rest), jnp.float32))
    return jnp.concatenate(row, axis=1)


def gather_kernel(rows, span, lengths, *refs):
    *pieces, held, row, joined = refs
    *holds, far = regrouped(pieces, lengths)
    row[...] = hold(holds, held, rows, span)
    assemble(joined, 0, rows, far, 0)


def gather(holds, far, rows, span):
    width = far[0].shape[1]
    total = len(holds) * rows
    parts = [*holds, far]
    return pl.pallas_call(
        functools.partial(gather_kernel, rows, span, [len(part) for part in parts]),
        out_shape=[
            jax.ShapeDtypeStruct((total, width), jnp.bfloat16),
            jax.ShapeDtypeStruct((1, total), jnp.float32),
            jax.ShapeDtypeStruct((rows, width), jnp.bfloat16),
        ],
        compiler_params=pltpu.CompilerParams(vmem_limit_bytes=8 << 20),
        cost_estimate=pl.CostEstimate(
            flops=rows * total * width // 4, bytes_accessed=rows, transcendentals=0
        ),
    )(*[piece for part in parts for piece in part])


def regrouped(flat, lengths):
    flat = iter(flat)
    return [[next(flat) for _ in range(length)] for length in lengths]


def pair(units, first, second, rows):
    units[0:rows, :] = first[0:rows, :]
    units[rows:, :] = second[0:rows, :]


def plane_kernel(rows, span, lengths, block, partner, *refs):
    *pieces, best, mine, held, units = refs
    row = hold(regrouped(pieces, lengths), held, rows, span)
    pair(units, block, partner, rows)
    parts = [(codes(block, rows, span), OWN), (codes(partner, rows, span), HELD)]
    (mine[...],), theirs = meet(units, parts, rows, span, held, row)
    best[...] = theirs[:, : best.shape[1]]


def rest_kernel(rows, span, block, partner, held, row, best, mine, units):
    count = best.shape[1]
    start = held.shape[0] - up(count, LANES)
    held, row = held.at[start:, :], row[:, start:]
    pair(units, block, partner, rows)
    parts = [(codes(block, rows, span), OWN), (codes(partner, rows, span), HELD)]
    (mine[...],), theirs = meet(units, parts, rows, span, held, row)
    best[...] = theirs[:, row.shape[1] - count :]


def line_kernel(rows, span, together, count, first, second, held, row, *refs):
    bests, outs, (found, units) = refs[:count], refs[count:-2], refs[-2:]
    pair(units, first, second, rows)
    parts = [(codes(second, rows, span, first=place), TWO) for place in (CODES, 0)]
    mine, theirs = meet(units, parts, rows, span, held, row[...])
    found[...] = jnp.concatenate(mine, axis=1)
    best = jnp.maximum(jnp.concatenate([best[...] for best in bests], axis=1), theirs)
    for out, places in zip(outs, together):
        out[...] = jnp.concatenate(
            [best[:, place * rows : (place + 1) * rows] for place in places], axis=1
        )


def plane(block, partner, holds, rows, span):
    width = block.shape[1]
    total = len(holds) * rows
    return pl.pallas_call(
        functools.partial(plane_kernel, rows, span, [len(part) for part in holds]),
        out_shape=[
            jax.ShapeDtypeStruct((1, total), jnp.float32),
            jax.ShapeDtypeStruct((1, rows), jnp.float32),
        ],
        scratch_shapes=[
            pltpu.VMEM((up(total, LANES), width), jnp.bfloat16),
            pltpu.VMEM((2 * rows, width), jnp.bfloat16),
        ],
        compiler_params=pltpu.CompilerParams(vmem_limit_bytes=12 << 20),
        cost_estimate=pl.CostEstimate(flops=rows, bytes_accessed=rows, transcendentals=0),
    )(block, partner, *[piece for part in holds for piece in part])


def plane_rest(block, partner, held, row, count, rows, span):
    return pl.pallas_call(
        functools.partial(rest_kernel, rows, span),
        out_shape=[
            jax.ShapeDtypeStruct((1, count), jnp.float32),
            jax.ShapeDtypeStruct((1, rows), jnp.float32),
        ],
        scratch_shapes=[pltpu.VMEM((2 * rows, block.shape[1]), jnp.bfloat16)],
        compiler_params=pltpu.CompilerParams(vmem_limit_bytes=12 << 20),
        cost_estimate=pl.CostEstimate(flops=rows, bytes_accessed=rows, transcendentals=0),
    )(block, partner, held, row)


def line(first, second, held, row, bests, rows, span, together):
    outs = [jax.ShapeDtypeStruct((1, rows * len(some)), jnp.float32) for some in together]
    *bests, found = pl.pallas_call(
        functools.partial(line_kernel, rows, span, together, len(bests)),
        out_shape=outs + [jax.ShapeDtypeStruct((1, 2 * rows), jnp.float32)],
        scratch_shapes=[pltpu.VMEM((2 * rows, second.shape[1]), jnp.bfloat16)],
        compiler_params=pltpu.CompilerParams(vmem_limit_bytes=12 << 20),
        cost_estimate=pl.CostEstimate(flops=rows, bytes_accessed=rows, transcendentals=0),
    )(first, second, held, row, *bests)
    return bests, found


OWN = (True, False)
HELD = (False, True)
TWO = (True, True)


def line_rounds(chips):
    if chips == 4:
        return [[(0, 2), (3, 1), (1, 0)], [(0, 3), (3, 2), (2, 1)]]
    rounds = []
    for shift in range(1, chips // 2 + 1):
        senders = chips // 2 if 2 * shift == chips else chips
        rounds.append([(s, (s + shift) % chips) for s in range(senders)])
    return rounds


def solution(mesh):
    groups, members = mesh.shape["dp"], mesh.shape["grid"]
    assert groups == 4 and members % 2 == 0
    chips = members // 2

    def everywhere(target):
        return [
            (p * members + g, a * members + b)
            for p in range(groups)
            for g in range(members)
            for a, b in [target(p, g)]
        ]

    other_core = everywhere(lambda p, g: (p, g ^ 1))
    first = everywhere(lambda p, g: (p ^ (1 + g % 2), g))
    second = everywhere(lambda p, g: (p ^ (2 - g % 2), g))
    second_home = everywhere(lambda p, g: (p ^ (2 - g % 2), g ^ 1))

    rounds = line_rounds(chips)
    rounds += [[]] * (len(rounds) % 2)
    rounds = [
        [
            (p * members + 2 * s + c, p * members + 2 * t + c)
            for p in range(groups)
            for c in range(2)
            for s, t in rounds[at + c]
        ]
        for at in range(0, len(rounds), 2)
    ]

    def back(pairs):
        return [(target, source) for source, target in pairs]

    def shards(embeddings, cluster, order_key):
        rows = embeddings.shape[0]
        span = 256
        while span < rows * groups * members:
            span *= 2
        halves = (rows // 2, rows // 2 + EXTRA)
        names = (cluster.reshape(1, rows), order_key)
        raw = [lax.ppermute(embeddings, BOTH, pairs) for pairs in rounds]
        charge = [lax.ppermute(array, BOTH, other_core) for array in (embeddings, *names)]
        block, _, *parts = with_units(prepare_kernel, (rows + EXTRA, EXTRA, *halves), *charge)
        from_first = [lax.ppermute(part, BOTH, first) for part in parts]
        from_second = [lax.ppermute(block, BOTH, second)]
        own, own_codes = with_units(prepare_kernel, (rows + EXTRA, EXTRA), embeddings, *names)
        (both,) = with_units(complete_kernel, (rows + EXTRA,), block, own_codes)
        near_other = [lax.ppermute(both, BOTH, pairs) for pairs in rounds]
        from_corner = [lax.ppermute(part, BOTH, second) for part in from_first]
        near = [
            list(with_units(unit_kernel, (rows, rows // 2, rows // 2), rows_of))
            for rows_of in raw
        ]
        far = [[lax.ppermute(piece, BOTH, other_core) for piece in blocks[1:]] for blocks in near]

        in_charge, results, kept, sent = [], [], [], []
        best_two, mine = plane(block, own, [[block], from_first], rows, span)
        in_charge.append(mine)
        *from_corner, best_two = lax.optimization_barrier((*from_corner, best_two))
        blocks = [[block], from_first, from_second, from_corner]
        held, row, far_units = gather(blocks, far[0], rows, span)
        best_rest, mine = plane_rest(block, own, held, row, 2 * rows, rows, span)
        in_charge.append(mine)
        bests = [best_two, best_rest]
        far = [far_units] + [jnp.concatenate(pieces, axis=0) for pieces in far[1:]]
        whole, last = [tuple(range(groups))], [(0,), (1, 3), (2,)]
        for at, second_near in enumerate(near_other):
            second_near, *bests = lax.optimization_barrier((second_near, *bests))
            second_far = lax.ppermute(second_near, BOTH, other_core)
            bests, found = line(near[at][0], second_near, held, row, bests, rows, span, whole)
            kept.append(found)
            bests, found = line(
                far[at],
                second_far,
                held,
                row,
                bests,
                rows,
                span,
                last if at == len(rounds) - 1 else whole,
            )
            sent.append(found)
        sent = lax.ppermute(jnp.concatenate(sent, axis=1), BOTH, other_core)
        kept = jnp.maximum(jnp.concatenate(kept, axis=1), sent)
        for at, pairs in enumerate(rounds):
            found = lax.ppermute(kept[:, 2 * at * rows : 2 * (at + 1) * rows], BOTH, back(pairs))
            me = lax.axis_index(BOTH)
            sender = functools.reduce(jnp.logical_or, [me == source for source, _ in pairs])
            found = jnp.where(sender, found, -1.0)
            results += [found[:, :rows], lax.ppermute(found[:, rows:], BOTH, other_core)]
        from_x = lax.ppermute(bests[1], BOTH, first)
        in_charge += [bests[0], from_x[:, :rows]]
        onward = jnp.maximum(bests[2], from_x[:, rows:])
        results.append(lax.ppermute(onward, BOTH, second_home))
        home = functools.reduce(jnp.maximum, in_charge)
        results.append(lax.ppermute(home, BOTH, other_core))
        return functools.reduce(jnp.maximum, results).reshape(rows)

    placed = (P(BOTH, None), P(BOTH, None), P(BOTH))
    return jax.shard_map(
        shards, mesh=mesh, in_specs=placed, out_specs=P(BOTH), check_vma=False
    )
```

```python
import functools

import jax
import jax.numpy as jnp
from jax import lax
from jax.experimental import pallas as pl
from jax.experimental.pallas import tpu as pltpu
from jax.sharding import PartitionSpec as P

EPSILON = 1e-06
EXTRA = 16
CODES = 3
LANES = 128
TILE = 256
CHUNK = 32
BOTH = ("dp", "grid")


def up(value, multiple):
    return -(-value // multiple) * multiple


def turned_to_column(row, rows):
    return jnp.broadcast_to(row, (LANES, row.shape[1])).T[:rows]


def codes(block, rows, span, first=0):
    parts = block[block.shape[0] - EXTRA :, : up(rows, LANES)].astype(jnp.float32)
    parts = parts[first : first + CODES]
    return parts[2:3] * (4.0 * span) + parts[0:1] * 256.0 + parts[1:2]


def unit_rows(rows, out):
    values = rows[...].astype(jnp.float32)
    scale = lax.rsqrt(jnp.sum(values * values, axis=1, keepdims=True) + EPSILON)
    out[0 : rows.shape[0], :] = (values * scale).astype(jnp.bfloat16)


def give_parts(block, outs):
    for out, top in zip(outs, (0, block.shape[0] - outs[-1].shape[0])):
        out[...] = block[top : top + out.shape[0], :]


def prepare_kernel(embeddings, cluster, order_key, block, codes_out, *parts_out):
    rows, width = embeddings.shape
    unit_rows(embeddings, block)
    keys = order_key[...].reshape(1, rows)
    parts = [keys >> 8, keys & 255, cluster[...] + 1]
    parts = [part.astype(jnp.float32) for part in parts]
    parts = jnp.concatenate(parts + [jnp.zeros((EXTRA - CODES, rows), jnp.float32)], axis=0)
    parts = jnp.concatenate([parts, jnp.zeros((EXTRA, width - rows), jnp.float32)], axis=1)
    block[rows : rows + EXTRA, :] = parts.astype(jnp.bfloat16)
    codes_out[...] = block[rows : rows + EXTRA, :]
    if parts_out:
        give_parts(block, parts_out)


def complete_kernel(block, other_codes, out):
    rows = block.shape[0] - EXTRA
    out[0:rows, :] = block[0:rows, :]
    named = [part[...].astype(jnp.float32)[0:CODES] for part in (block.at[rows:, :], other_codes)]
    rest = jnp.zeros((EXTRA - 2 * CODES, block.shape[1]), jnp.float32)
    out[rows:, :] = jnp.concatenate(named + [rest], axis=0).astype(jnp.bfloat16)


def unit_kernel(rows_of, block, *parts_out):
    unit_rows(rows_of, block)
    give_parts(block, parts_out)


def with_units(kernel, heights, rows_of, *others):
    rows, width = rows_of.shape
    return pl.pallas_call(
        kernel,
        out_shape=[jax.ShapeDtypeStruct((height, width), jnp.bfloat16) for height in heights],
        compiler_params=pltpu.CompilerParams(vmem_limit_bytes=8 << 20),
        cost_estimate=pl.CostEstimate(flops=rows, bytes_accessed=rows, transcendentals=0),
    )(rows_of, *others)


def row_from_partial(partial, rows):
    padded = up(rows, LANES)
    if padded != rows:
        partial = jnp.concatenate(
            [partial, jnp.zeros((padded - rows, LANES), partial.dtype)], axis=0
        )
    return jnp.max(partial.T, axis=0, keepdims=True)[:, :rows]


def meet(units, parts, rows, span, held, held_codes):
    columns = [turned_to_column(row, rows) for row, _ in parts]
    starts = [(block, top) for block in range(len(parts)) for top in range(0, rows, CHUNK)]
    partial = {start: jnp.full((CHUNK, LANES), -1.0, jnp.float32) for start in starts}
    best_held = []
    for at in range(0, held.shape[0], TILE):
        tile = min(TILE, held.shape[0] - at)
        sims = lax.dot_general(
            units[...],
            held[at : at + tile, :],
            (((1,), (1,)), ((), ())),
            preferred_element_type=jnp.float32,
        )
        best = [jnp.full((CHUNK, LANES), -1.0, jnp.float32) for _ in range(0, tile, LANES)]
        for block, top in starts:
            to_block, to_held = parts[block][1]
            mine = columns[block][top : top + CHUNK]
            line = block * rows + top
            for lane in range(0, tile, LANES):
                part = sims[line : line + CHUNK, lane : lane + LANES]
                gap = mine - held_codes[:, at + lane : at + lane + LANES]
                if to_block and to_held:
                    part = jnp.where(jnp.abs(gap) < span, part, -1.0)
                    later = gap > 0.0
                    ours, theirs = jnp.where(later, part, -1.0), jnp.where(later, -1.0, part)
                elif to_block:
                    ours = jnp.where((gap > 0.0) & (gap < span), part, -1.0)
                else:
                    theirs = jnp.where((gap < 0.0) & (gap > -span), part, -1.0)
                if to_block:
                    partial[block, top] = jnp.maximum(partial[block, top], ours)
                if to_held:
                    best[lane // LANES] = jnp.maximum(best[lane // LANES], theirs)
        best_held += [jnp.max(some, axis=0, keepdims=True) for some in best]
    found = [
        row_from_partial(
            jnp.concatenate([partial[block, top] for top in range(0, rows, CHUNK)], axis=0), rows
        )
        for block, (_, (to_block, _)) in enumerate(parts)
        if to_block
    ]
    return found, jnp.concatenate(best_held, axis=1)


def assemble(whole, top, rows, pieces, extra):
    first, *others = pieces
    height = min(first.shape[0], rows)
    whole[top : top + height, :] = first[0:height, :]
    for last in others:
        height = last.shape[0] - extra
        whole[top + rows - height : top + rows, :] = last[0:height, :]


def hold(holds, held, rows, span):
    for at, block in enumerate(holds):
        assemble(held, at * rows, rows, block, EXTRA)
    row = [codes(block[-1], rows, span)[:, :rows] for block in holds]
    rest = held.shape[0] - len(holds) * rows
    if rest:
        held[len(holds) * rows :, :] = jnp.zeros((rest, held.shape[1]), held.dtype)
        row.append(jnp.zeros((1, rest), jnp.float32))
    return jnp.concatenate(row, axis=1)


def gather_kernel(rows, span, lengths, *refs):
    *pieces, held, row, joined = refs
    *holds, far = regrouped(pieces, lengths)
    row[...] = hold(holds, held, rows, span)
    assemble(joined, 0, rows, far, 0)


def gather(holds, far, rows, span):
    width = far[0].shape[1]
    total = len(holds) * rows
    parts = [*holds, far]
    return pl.pallas_call(
        functools.partial(gather_kernel, rows, span, [len(part) for part in parts]),
        out_shape=[
            jax.ShapeDtypeStruct((total, width), jnp.bfloat16),
            jax.ShapeDtypeStruct((1, total), jnp.float32),
            jax.ShapeDtypeStruct((rows, width), jnp.bfloat16),
        ],
        compiler_params=pltpu.CompilerParams(vmem_limit_bytes=8 << 20),
        cost_estimate=pl.CostEstimate(
            flops=rows * total * width // 4, bytes_accessed=rows, transcendentals=0
        ),
    )(*[piece for part in parts for piece in part])


def regrouped(flat, lengths):
    flat = iter(flat)
    return [[next(flat) for _ in range(length)] for length in lengths]


def pair(units, first, second, rows):
    units[0:rows, :] = first[0:rows, :]
    units[rows:, :] = second[0:rows, :]


def plane_kernel(rows, span, lengths, block, partner, *refs):
    *pieces, best, mine, held, units = refs
    row = hold(regrouped(pieces, lengths), held, rows, span)
    pair(units, block, partner, rows)
    parts = [(codes(block, rows, span), OWN), (codes(partner, rows, span), HELD)]
    (mine[...],), theirs = meet(units, parts, rows, span, held, row)
    best[...] = theirs[:, : best.shape[1]]


def rest_kernel(rows, span, block, partner, held, row, best, mine, units):
    count = best.shape[1]
    start = held.shape[0] - up(count, LANES)
    held, row = held.at[start:, :], row[:, start:]
    pair(units, block, partner, rows)
    parts = [(codes(block, rows, span), OWN), (codes(partner, rows, span), HELD)]
    (mine[...],), theirs = meet(units, parts, rows, span, held, row)
    best[...] = theirs[:, row.shape[1] - count :]


def line_kernel(rows, span, together, count, first, second, held, row, *refs):
    bests, outs, (found, units) = refs[:count], refs[count:-2], refs[-2:]
    parts = [(codes(second, rows, span, first=place), TWO) for place in (CODES, 0)]

    def give(best):
        for out, places in zip(outs, together):
            out[...] = jnp.concatenate(
                [best[:, place * rows : (place + 1) * rows] for place in places], axis=1
            )

    arrived = jnp.max(parts[0][0]) > 0.0

    @pl.when(arrived)
    def _():
        pair(units, first, second, rows)
        mine, theirs = meet(units, parts, rows, span, held, row[...])
        found[...] = jnp.concatenate(mine, axis=1)
        give(jnp.maximum(jnp.concatenate([best[...] for best in bests], axis=1), theirs))

    @pl.when(jnp.logical_not(arrived))
    def _():
        found[...] = jnp.full(found.shape, -1.0, jnp.float32)
        give(jnp.concatenate([best[...] for best in bests], axis=1))


def plane(block, partner, holds, rows, span):
    width = block.shape[1]
    total = len(holds) * rows
    return pl.pallas_call(
        functools.partial(plane_kernel, rows, span, [len(part) for part in holds]),
        out_shape=[
            jax.ShapeDtypeStruct((1, total), jnp.float32),
            jax.ShapeDtypeStruct((1, rows), jnp.float32),
        ],
        scratch_shapes=[
            pltpu.VMEM((up(total, LANES), width), jnp.bfloat16),
            pltpu.VMEM((2 * rows, width), jnp.bfloat16),
        ],
        compiler_params=pltpu.CompilerParams(vmem_limit_bytes=12 << 20),
        cost_estimate=pl.CostEstimate(flops=rows, bytes_accessed=rows, transcendentals=0),
    )(block, partner, *[piece for part in holds for piece in part])


def plane_rest(block, partner, held, row, count, rows, span):
    return pl.pallas_call(
        functools.partial(rest_kernel, rows, span),
        out_shape=[
            jax.ShapeDtypeStruct((1, count), jnp.float32),
            jax.ShapeDtypeStruct((1, rows), jnp.float32),
        ],
        scratch_shapes=[pltpu.VMEM((2 * rows, block.shape[1]), jnp.bfloat16)],
        compiler_params=pltpu.CompilerParams(vmem_limit_bytes=12 << 20),
        cost_estimate=pl.CostEstimate(flops=rows, bytes_accessed=rows, transcendentals=0),
    )(block, partner, held, row)


def line(first, second, held, row, bests, rows, span, together):
    outs = [jax.ShapeDtypeStruct((1, rows * len(some)), jnp.float32) for some in together]
    *bests, found = pl.pallas_call(
        functools.partial(line_kernel, rows, span, together, len(bests)),
        out_shape=outs + [jax.ShapeDtypeStruct((1, 2 * rows), jnp.float32)],
        scratch_shapes=[pltpu.VMEM((2 * rows, second.shape[1]), jnp.bfloat16)],
        compiler_params=pltpu.CompilerParams(vmem_limit_bytes=12 << 20),
        cost_estimate=pl.CostEstimate(flops=rows, bytes_accessed=rows, transcendentals=0),
    )(first, second, held, row, *bests)
    return bests, found


OWN = (True, False)
HELD = (False, True)
TWO = (True, True)


def line_rounds(chips):
    if chips == 4:
        return [[(3, 1), (0, 2), (2, 3)], [(3, 0), (0, 1), (1, 2)]]
    rounds = []
    for shift in range(1, chips // 2 + 1):
        senders = chips // 2 if 2 * shift == chips else chips
        rounds.append([(s, (s + shift) % chips) for s in range(senders)])
    return rounds


def solution(mesh):
    groups, members = mesh.shape["dp"], mesh.shape["grid"]
    assert groups == 4 and members % 2 == 0
    chips = members // 2

    def everywhere(target):
        return [
            (p * members + g, a * members + b)
            for p in range(groups)
            for g in range(members)
            for a, b in [target(p, g)]
        ]

    other_core = everywhere(lambda p, g: (p, g ^ 1))
    first = everywhere(lambda p, g: (p ^ (1 + g % 2), g))
    second = everywhere(lambda p, g: (p ^ (2 - g % 2), g))
    second_home = everywhere(lambda p, g: (p ^ (2 - g % 2), g ^ 1))

    rounds = line_rounds(chips)
    rounds += [[]] * (len(rounds) % 2)
    rounds = [
        [
            (p * members + 2 * s + c, p * members + 2 * t + c)
            for p in range(groups)
            for c in range(2)
            for s, t in rounds[at + c]
        ]
        for at in range(0, len(rounds), 2)
    ]

    def back(pairs):
        return [(target, source) for source, target in pairs]

    def shards(embeddings, cluster, order_key):
        rows = embeddings.shape[0]
        span = 256
        while span < rows * groups * members:
            span *= 2
        halves = (rows // 2, rows // 2 + EXTRA)
        names = (cluster.reshape(1, rows), order_key)
        raw = [lax.ppermute(embeddings, BOTH, pairs) for pairs in rounds]
        charge = [lax.ppermute(array, BOTH, other_core) for array in (embeddings, *names)]
        block, _, *parts = with_units(prepare_kernel, (rows + EXTRA, EXTRA, *halves), *charge)
        from_first = [lax.ppermute(part, BOTH, first) for part in parts]
        from_second = [lax.ppermute(block, BOTH, second)]
        own, own_codes = with_units(prepare_kernel, (rows + EXTRA, EXTRA), embeddings, *names)
        (both,) = with_units(complete_kernel, (rows + EXTRA,), block, own_codes)
        near_other = [lax.ppermute(both, BOTH, pairs) for pairs in rounds]
        from_corner = [lax.ppermute(part, BOTH, second) for part in from_first]
        near = [
            list(with_units(unit_kernel, (rows, rows // 2, rows // 2), rows_of))
            for rows_of in raw
        ]
        far = [[lax.ppermute(piece, BOTH, other_core) for piece in blocks[1:]] for blocks in near]

        in_charge, results, kept, sent = [], [], [], []
        best_two, mine = plane(block, own, [[block], from_first], rows, span)
        in_charge.append(mine)
        *from_corner, best_two = lax.optimization_barrier((*from_corner, best_two))
        blocks = [[block], from_first, from_second, from_corner]
        held, row, far_units = gather(blocks, far[0], rows, span)
        best_rest, mine = plane_rest(block, own, held, row, 2 * rows, rows, span)
        in_charge.append(mine)
        bests = [best_two, best_rest]
        far = [far_units] + [jnp.concatenate(pieces, axis=0) for pieces in far[1:]]
        whole, last = [tuple(range(groups))], [(0,), (1, 3), (2,)]
        for at, second_near in enumerate(near_other):
            second_near, *bests = lax.optimization_barrier((second_near, *bests))
            second_far = lax.ppermute(second_near, BOTH, other_core)
            bests, found = line(near[at][0], second_near, held, row, bests, rows, span, whole)
            kept.append(found)
            bests, found = line(
                far[at],
                second_far,
                held,
                row,
                bests,
                rows,
                span,
                last if at == len(rounds) - 1 else whole,
            )
            sent.append(found)
        sent = lax.ppermute(jnp.concatenate(sent, axis=1), BOTH, other_core)
        kept = jnp.maximum(jnp.concatenate(kept, axis=1), sent)
        for at, pairs in enumerate(rounds):
            found = lax.ppermute(kept[:, 2 * at * rows : 2 * (at + 1) * rows], BOTH, back(pairs))
            me = lax.axis_index(BOTH)
            sender = functools.reduce(jnp.logical_or, [me == source for source, _ in pairs])
            found = jnp.where(sender, found, -1.0)
            results += [found[:, :rows], lax.ppermute(found[:, rows:], BOTH, other_core)]
        from_x = lax.ppermute(bests[1], BOTH, first)
        in_charge += [bests[0], from_x[:, :rows]]
        onward = jnp.maximum(bests[2], from_x[:, rows:])
        results.append(lax.ppermute(onward, BOTH, second_home))
        home = functools.reduce(jnp.maximum, in_charge)
        results.append(lax.ppermute(home, BOTH, other_core))
        return functools.reduce(jnp.maximum, results).reshape(rows)

    placed = (P(BOTH, None), P(BOTH, None), P(BOTH))
    return jax.shard_map(
        shards, mesh=mesh, in_specs=placed, out_specs=P(BOTH), check_vma=False
    )
```

```python
import functools

import jax
import jax.numpy as jnp
from jax import lax
from jax.experimental import pallas as pl
from jax.experimental.pallas import tpu as pltpu
from jax.sharding import PartitionSpec as P

EPSILON = 1e-06
EXTRA = 16
CODES = 3
LANES = 128
TILE = 256
CHUNK = 32
BOTH = ("dp", "grid")


def up(value, multiple):
    return -(-value // multiple) * multiple


def turned_to_column(row, rows):
    return jnp.broadcast_to(row, (LANES, row.shape[1])).T[:rows]


def codes(block, rows, span, first=0):
    parts = block[block.shape[0] - EXTRA :, : up(rows, LANES)].astype(jnp.float32)
    parts = parts[first : first + CODES]
    return parts[2:3] * (4.0 * span) + parts[0:1] * 256.0 + parts[1:2]


def unit_rows(rows, out):
    values = rows[...].astype(jnp.float32)
    scale = lax.rsqrt(jnp.sum(values * values, axis=1, keepdims=True) + EPSILON)
    out[0 : rows.shape[0], :] = (values * scale).astype(jnp.bfloat16)


def give_parts(block, outs):
    for out, top in zip(outs, (0, block.shape[0] - outs[-1].shape[0])):
        out[...] = block[top : top + out.shape[0], :]


def prepare_kernel(embeddings, cluster, order_key, block, codes_out, *parts_out):
    rows, width = embeddings.shape
    unit_rows(embeddings, block)
    keys = order_key[...].reshape(1, rows)
    parts = [keys >> 8, keys & 255, cluster[...] + 1]
    parts = [part.astype(jnp.float32) for part in parts]
    parts = jnp.concatenate(parts + [jnp.zeros((EXTRA - CODES, rows), jnp.float32)], axis=0)
    parts = jnp.concatenate([parts, jnp.zeros((EXTRA, width - rows), jnp.float32)], axis=1)
    block[rows : rows + EXTRA, :] = parts.astype(jnp.bfloat16)
    codes_out[...] = block[rows : rows + EXTRA, :]
    if parts_out:
        give_parts(block, parts_out)


def complete_kernel(block, other_codes, out):
    rows = block.shape[0] - EXTRA
    out[0:rows, :] = block[0:rows, :]
    named = [part[...].astype(jnp.float32)[0:CODES] for part in (block.at[rows:, :], other_codes)]
    rest = jnp.zeros((EXTRA - 2 * CODES, block.shape[1]), jnp.float32)
    out[rows:, :] = jnp.concatenate(named + [rest], axis=0).astype(jnp.bfloat16)


def unit_kernel(rows_of, block, *parts_out):
    unit_rows(rows_of, block)
    give_parts(block, parts_out)


def with_units(kernel, heights, rows_of, *others):
    rows, width = rows_of.shape
    return pl.pallas_call(
        kernel,
        out_shape=[jax.ShapeDtypeStruct((height, width), jnp.bfloat16) for height in heights],
        compiler_params=pltpu.CompilerParams(vmem_limit_bytes=8 << 20),
        cost_estimate=pl.CostEstimate(flops=rows, bytes_accessed=rows, transcendentals=0),
    )(rows_of, *others)


def row_from_partial(partial, rows):
    padded = up(rows, LANES)
    if padded != rows:
        partial = jnp.concatenate(
            [partial, jnp.zeros((padded - rows, LANES), partial.dtype)], axis=0
        )
    return jnp.max(partial.T, axis=0, keepdims=True)[:, :rows]


def meet(units, parts, rows, span, held, held_codes):
    columns = [turned_to_column(row, rows) for row, _ in parts]
    starts = [(block, top) for block in range(len(parts)) for top in range(0, rows, CHUNK)]
    partial = {start: jnp.full((CHUNK, LANES), -1.0, jnp.float32) for start in starts}
    best_held = []
    for at in range(0, held.shape[0], TILE):
        tile = min(TILE, held.shape[0] - at)
        sims = lax.dot_general(
            units[...],
            held[at : at + tile, :],
            (((1,), (1,)), ((), ())),
            preferred_element_type=jnp.float32,
        )
        best = [jnp.full((CHUNK, LANES), -1.0, jnp.float32) for _ in range(0, tile, LANES)]
        for block, top in starts:
            to_block, to_held = parts[block][1]
            mine = columns[block][top : top + CHUNK]
            line = block * rows + top
            for lane in range(0, tile, LANES):
                part = sims[line : line + CHUNK, lane : lane + LANES]
                gap = mine - held_codes[:, at + lane : at + lane + LANES]
                if to_block and to_held:
                    part = jnp.where(jnp.abs(gap) < span, part, -1.0)
                    later = gap > 0.0
                    ours, theirs = jnp.where(later, part, -1.0), jnp.where(later, -1.0, part)
                elif to_block:
                    ours = jnp.where((gap > 0.0) & (gap < span), part, -1.0)
                else:
                    theirs = jnp.where((gap < 0.0) & (gap > -span), part, -1.0)
                if to_block:
                    partial[block, top] = jnp.maximum(partial[block, top], ours)
                if to_held:
                    best[lane // LANES] = jnp.maximum(best[lane // LANES], theirs)
        best_held += [jnp.max(some, axis=0, keepdims=True) for some in best]
    found = [
        row_from_partial(
            jnp.concatenate([partial[block, top] for top in range(0, rows, CHUNK)], axis=0), rows
        )
        for block, (_, (to_block, _)) in enumerate(parts)
        if to_block
    ]
    return found, jnp.concatenate(best_held, axis=1)


def assemble(whole, top, rows, pieces, extra):
    first, *others = pieces
    height = min(first.shape[0], rows)
    whole[top : top + height, :] = first[0:height, :]
    for last in others:
        height = last.shape[0] - extra
        whole[top + rows - height : top + rows, :] = last[0:height, :]


def hold(holds, held, rows, span):
    for at, block in enumerate(holds):
        assemble(held, at * rows, rows, block, EXTRA)
    row = [codes(block[-1], rows, span)[:, :rows] for block in holds]
    rest = held.shape[0] - len(holds) * rows
    if rest:
        held[len(holds) * rows :, :] = jnp.zeros((rest, held.shape[1]), held.dtype)
        row.append(jnp.zeros((1, rest), jnp.float32))
    return jnp.concatenate(row, axis=1)


def gather_kernel(rows, span, lengths, *refs):
    *pieces, held, row, joined = refs
    *holds, far = regrouped(pieces, lengths)
    row[...] = hold(holds, held, rows, span)
    assemble(joined, 0, rows, far, 0)


def gather(holds, far, rows, span):
    width = far[0].shape[1]
    total = len(holds) * rows
    parts = [*holds, far]
    return pl.pallas_call(
        functools.partial(gather_kernel, rows, span, [len(part) for part in parts]),
        out_shape=[
            jax.ShapeDtypeStruct((total, width), jnp.bfloat16),
            jax.ShapeDtypeStruct((1, total), jnp.float32),
            jax.ShapeDtypeStruct((rows, width), jnp.bfloat16),
        ],
        compiler_params=pltpu.CompilerParams(vmem_limit_bytes=8 << 20),
        cost_estimate=pl.CostEstimate(
            flops=rows * total * width // 4, bytes_accessed=rows, transcendentals=0
        ),
    )(*[piece for part in parts for piece in part])


def regrouped(flat, lengths):
    flat = iter(flat)
    return [[next(flat) for _ in range(length)] for length in lengths]


def pair(units, first, second, rows):
    units[0:rows, :] = first[0:rows, :]
    units[rows:, :] = second[0:rows, :]


def plane_kernel(rows, span, lengths, block, partner, *refs):
    *pieces, best, mine, held, units = refs
    row = hold(regrouped(pieces, lengths), held, rows, span)
    pair(units, block, partner, rows)
    parts = [(codes(block, rows, span), OWN), (codes(partner, rows, span), HELD)]
    (mine[...],), theirs = meet(units, parts, rows, span, held, row)
    best[...] = theirs[:, : best.shape[1]]


def rest_kernel(rows, span, block, partner, held, row, best, mine, units):
    count = best.shape[1]
    start = held.shape[0] - up(count, LANES)
    held, row = held.at[start:, :], row[:, start:]
    pair(units, block, partner, rows)
    parts = [(codes(block, rows, span), OWN), (codes(partner, rows, span), HELD)]
    (mine[...],), theirs = meet(units, parts, rows, span, held, row)
    best[...] = theirs[:, row.shape[1] - count :]


def line_kernel(rows, span, together, count, first, second, held, row, *refs):
    bests, outs, (found, units) = refs[:count], refs[count:-2], refs[-2:]
    parts = [(codes(second, rows, span, first=place), TWO) for place in (CODES, 0)]

    def give(best):
        for out, places in zip(outs, together):
            out[...] = jnp.concatenate(
                [best[:, place * rows : (place + 1) * rows] for place in places], axis=1
            )

    arrived = jnp.max(parts[0][0]) > 0.0

    @pl.when(arrived)
    def _():
        pair(units, first, second, rows)
        mine, theirs = meet(units, parts, rows, span, held, row[...])
        found[...] = jnp.concatenate(mine, axis=1)
        give(jnp.maximum(jnp.concatenate([best[...] for best in bests], axis=1), theirs))

    @pl.when(jnp.logical_not(arrived))
    def _():
        found[...] = jnp.full(found.shape, -1.0, jnp.float32)
        give(jnp.concatenate([best[...] for best in bests], axis=1))


def plane(block, partner, holds, rows, span):
    width = block.shape[1]
    total = len(holds) * rows
    return pl.pallas_call(
        functools.partial(plane_kernel, rows, span, [len(part) for part in holds]),
        out_shape=[
            jax.ShapeDtypeStruct((1, total), jnp.float32),
            jax.ShapeDtypeStruct((1, rows), jnp.float32),
        ],
        scratch_shapes=[
            pltpu.VMEM((up(total, LANES), width), jnp.bfloat16),
            pltpu.VMEM((2 * rows, width), jnp.bfloat16),
        ],
        compiler_params=pltpu.CompilerParams(vmem_limit_bytes=12 << 20),
        cost_estimate=pl.CostEstimate(flops=rows, bytes_accessed=rows, transcendentals=0),
    )(block, partner, *[piece for part in holds for piece in part])


def plane_rest(block, partner, held, row, count, rows, span):
    return pl.pallas_call(
        functools.partial(rest_kernel, rows, span),
        out_shape=[
            jax.ShapeDtypeStruct((1, count), jnp.float32),
            jax.ShapeDtypeStruct((1, rows), jnp.float32),
        ],
        scratch_shapes=[pltpu.VMEM((2 * rows, block.shape[1]), jnp.bfloat16)],
        compiler_params=pltpu.CompilerParams(vmem_limit_bytes=12 << 20),
        cost_estimate=pl.CostEstimate(flops=rows, bytes_accessed=rows, transcendentals=0),
    )(block, partner, held, row)


def line(first, second, held, row, bests, rows, span, together):
    outs = [jax.ShapeDtypeStruct((1, rows * len(some)), jnp.float32) for some in together]
    *bests, found = pl.pallas_call(
        functools.partial(line_kernel, rows, span, together, len(bests)),
        out_shape=outs + [jax.ShapeDtypeStruct((1, 2 * rows), jnp.float32)],
        scratch_shapes=[pltpu.VMEM((2 * rows, second.shape[1]), jnp.bfloat16)],
        compiler_params=pltpu.CompilerParams(vmem_limit_bytes=12 << 20),
        cost_estimate=pl.CostEstimate(flops=rows, bytes_accessed=rows, transcendentals=0),
    )(first, second, held, row, *bests)
    return bests, found


OWN = (True, False)
HELD = (False, True)
TWO = (True, True)


def line_rounds(chips):
    if chips == 4:
        return [[(3, 1), (0, 2), (2, 3)], [(3, 0), (0, 1), (1, 2)]]
    rounds = []
    for shift in range(1, chips // 2 + 1):
        senders = chips // 2 if 2 * shift == chips else chips
        rounds.append([(s, (s + shift) % chips) for s in range(senders)])
    return rounds


def solution(mesh):
    groups, members = mesh.shape["dp"], mesh.shape["grid"]
    assert groups == 4 and members % 2 == 0
    chips = members // 2

    def everywhere(target):
        return [
            (p * members + g, a * members + b)
            for p in range(groups)
            for g in range(members)
            for a, b in [target(p, g)]
        ]

    other_core = everywhere(lambda p, g: (p, g ^ 1))
    first = everywhere(lambda p, g: (p ^ (1 + g % 2), g))
    second = everywhere(lambda p, g: (p ^ (2 - g % 2), g))
    homes = [
        everywhere(lambda p, g: (p ^ (1 + g % 2), g ^ 1)),
        everywhere(lambda p, g: (p ^ (2 - g % 2), g ^ 1)),
        everywhere(lambda p, g: (p ^ 3, g ^ 1)),
    ]

    rounds = line_rounds(chips)
    rounds += [[]] * (len(rounds) % 2)
    rounds = [
        [
            (p * members + 2 * s + c, p * members + 2 * t + c)
            for p in range(groups)
            for c in range(2)
            for s, t in rounds[at + c]
        ]
        for at in range(0, len(rounds), 2)
    ]

    def back(pairs):
        return [(target, source) for source, target in pairs]

    def shards(embeddings, cluster, order_key):
        rows = embeddings.shape[0]
        span = 256
        while span < rows * groups * members:
            span *= 2
        halves = (rows // 2, rows // 2 + EXTRA)
        names = (cluster.reshape(1, rows), order_key)
        raw = [lax.ppermute(embeddings, BOTH, pairs) for pairs in rounds]
        charge = [lax.ppermute(array, BOTH, other_core) for array in (embeddings, *names)]
        block, _, *parts = with_units(prepare_kernel, (rows + EXTRA, EXTRA, *halves), *charge)
        from_first = [lax.ppermute(part, BOTH, first) for part in parts]
        from_second = [lax.ppermute(block, BOTH, second)]
        own, own_codes = with_units(prepare_kernel, (rows + EXTRA, EXTRA), embeddings, *names)
        (both,) = with_units(complete_kernel, (rows + EXTRA,), block, own_codes)
        near_other = [lax.ppermute(both, BOTH, pairs) for pairs in rounds]
        from_corner = [lax.ppermute(part, BOTH, second) for part in from_first]
        near = [
            list(with_units(unit_kernel, (rows, rows // 2, rows // 2), rows_of))
            for rows_of in raw
        ]
        far = [[lax.ppermute(piece, BOTH, other_core) for piece in blocks[1:]] for blocks in near]

        in_charge, results, kept, sent = [], [], [], []
        best_two, mine = plane(block, own, [[block], from_first], rows, span)
        in_charge.append(mine)
        *from_corner, best_two = lax.optimization_barrier((*from_corner, best_two))
        blocks = [[block], from_first, from_second, from_corner]
        held, row, far_units = gather(blocks, far[0], rows, span)
        best_rest, mine = plane_rest(block, own, held, row, 2 * rows, rows, span)
        in_charge.append(mine)
        bests = [best_two, best_rest]
        far = [far_units] + [jnp.concatenate(pieces, axis=0) for pieces in far[1:]]
        whole, last = [tuple(range(groups))], [(at,) for at in range(groups)]
        for at, second_near in enumerate(near_other):
            second_near, *bests = lax.optimization_barrier((second_near, *bests))
            second_far = lax.ppermute(second_near, BOTH, other_core)
            bests, found = line(near[at][0], second_near, held, row, bests, rows, span, whole)
            kept.append(found)
            bests, found = line(
                far[at],
                second_far,
                held,
                row,
                bests,
                rows,
                span,
                last if at == len(rounds) - 1 else whole,
            )
            sent.append(found)
        sent = lax.ppermute(jnp.concatenate(sent, axis=1), BOTH, other_core)
        kept = jnp.maximum(jnp.concatenate(kept, axis=1), sent)
        kept, *bests = lax.optimization_barrier((kept, *bests))
        for at, pairs in enumerate(rounds):
            found = lax.ppermute(kept[:, 2 * at * rows : 2 * (at + 1) * rows], BOTH, back(pairs))
            me = lax.axis_index(BOTH)
            sender = functools.reduce(jnp.logical_or, [me == source for source, _ in pairs])
            found = jnp.where(sender, found, -1.0)
            results += [found[:, :rows], lax.ppermute(found[:, rows:], BOTH, other_core)]
        results += [
            lax.ppermute(best, BOTH, pairs) for best, pairs in zip(bests[1:], homes)
        ]
        in_charge.append(bests[0])
        home = functools.reduce(jnp.maximum, in_charge)
        results.append(lax.ppermute(home, BOTH, other_core))
        return functools.reduce(jnp.maximum, results).reshape(rows)

    placed = (P(BOTH, None), P(BOTH, None), P(BOTH))
    return jax.shard_map(
        shards, mesh=mesh, in_specs=placed, out_specs=P(BOTH), check_vma=False
    )
```

```python
import functools

import jax
import jax.numpy as jnp
from jax import lax
from jax.experimental import pallas as pl
from jax.experimental.pallas import tpu as pltpu
from jax.sharding import PartitionSpec as P

EPSILON = 1e-06
EXTRA = 16
CODES = 3
LANES = 128
TILE = 256
CHUNK = 32
BOTH = ("dp", "grid")


def up(value, multiple):
    return -(-value // multiple) * multiple


def turned_to_column(row, rows):
    return jnp.broadcast_to(row, (LANES, row.shape[1])).T[:rows]


def codes(block, rows, span, first=0):
    parts = block[block.shape[0] - EXTRA :, : up(rows, LANES)].astype(jnp.float32)
    parts = parts[first : first + CODES]
    return parts[2:3] * (4.0 * span) + parts[0:1] * 256.0 + parts[1:2]


def unit_rows(rows, out):
    values = rows[...].astype(jnp.float32)
    scale = lax.rsqrt(jnp.sum(values * values, axis=1, keepdims=True) + EPSILON)
    out[0 : rows.shape[0], :] = (values * scale).astype(jnp.bfloat16)


def give_parts(block, outs):
    for out, top in zip(outs, (0, block.shape[0] - outs[-1].shape[0])):
        out[...] = block[top : top + out.shape[0], :]


def code_rows(cluster, order_key, width):
    rows = order_key.shape[0]
    keys = order_key[...].reshape(1, rows)
    parts = [keys >> 8, keys & 255, cluster[...] + 1]
    parts = [part.astype(jnp.float32) for part in parts]
    parts = jnp.concatenate(parts + [jnp.zeros((EXTRA - CODES, rows), jnp.float32)], axis=0)
    parts = jnp.concatenate([parts, jnp.zeros((EXTRA, width - rows), jnp.float32)], axis=1)
    return parts.astype(jnp.bfloat16)


def prepare_kernel(embeddings, cluster, order_key, block, *parts_out):
    rows, width = embeddings.shape
    unit_rows(embeddings, block)
    block[rows : rows + EXTRA, :] = code_rows(cluster, order_key, width)
    give_parts(block, parts_out)


def codes_kernel(cluster, order_key, out):
    out[...] = code_rows(cluster, order_key, out.shape[1])


def own_kernel(embeddings, own_codes, block):
    unit_rows(embeddings, block)
    block[embeddings.shape[0] :, :] = own_codes[...]


def complete_kernel(block, other_codes, out):
    rows = block.shape[0] - EXTRA
    out[0:rows, :] = block[0:rows, :]
    named = [part[...].astype(jnp.float32)[0:CODES] for part in (block.at[rows:, :], other_codes)]
    rest = jnp.zeros((EXTRA - 2 * CODES, block.shape[1]), jnp.float32)
    out[rows:, :] = jnp.concatenate(named + [rest], axis=0).astype(jnp.bfloat16)


def unit_kernel(rows_of, block, *parts_out):
    unit_rows(rows_of, block)
    give_parts(block, parts_out)


def with_units(kernel, heights, width, *inputs):
    return pl.pallas_call(
        kernel,
        out_shape=[jax.ShapeDtypeStruct((height, width), jnp.bfloat16) for height in heights],
        compiler_params=pltpu.CompilerParams(vmem_limit_bytes=8 << 20),
        cost_estimate=pl.CostEstimate(flops=width, bytes_accessed=width, transcendentals=0),
    )(*inputs)


def row_from_partial(partial, rows):
    padded = up(rows, LANES)
    if padded != rows:
        partial = jnp.concatenate(
            [partial, jnp.zeros((padded - rows, LANES), partial.dtype)], axis=0
        )
    return jnp.max(partial.T, axis=0, keepdims=True)[:, :rows]


def meet(units, parts, rows, span, held, held_codes):
    columns = [turned_to_column(row, rows) for row, _ in parts]
    starts = [(block, top) for block in range(len(parts)) for top in range(0, rows, CHUNK)]
    partial = {start: jnp.full((CHUNK, LANES), -1.0, jnp.float32) for start in starts}
    best_held = []
    for at in range(0, held.shape[0], TILE):
        tile = min(TILE, held.shape[0] - at)
        sims = lax.dot_general(
            units[...],
            held[at : at + tile, :],
            (((1,), (1,)), ((), ())),
            preferred_element_type=jnp.float32,
        )
        best = [jnp.full((CHUNK, LANES), -1.0, jnp.float32) for _ in range(0, tile, LANES)]
        for block, top in starts:
            to_block, to_held = parts[block][1]
            mine = columns[block][top : top + CHUNK]
            line = block * rows + top
            for lane in range(0, tile, LANES):
                part = sims[line : line + CHUNK, lane : lane + LANES]
                gap = mine - held_codes[:, at + lane : at + lane + LANES]
                if to_block and to_held:
                    part = jnp.where(jnp.abs(gap) < span, part, -1.0)
                    later = gap > 0.0
                    ours, theirs = jnp.where(later, part, -1.0), jnp.where(later, -1.0, part)
                elif to_block:
                    ours = jnp.where((gap > 0.0) & (gap < span), part, -1.0)
                else:
                    theirs = jnp.where((gap < 0.0) & (gap > -span), part, -1.0)
                if to_block:
                    partial[block, top] = jnp.maximum(partial[block, top], ours)
                if to_held:
                    best[lane // LANES] = jnp.maximum(best[lane // LANES], theirs)
        best_held += [jnp.max(some, axis=0, keepdims=True) for some in best]
    found = [
        row_from_partial(
            jnp.concatenate([partial[block, top] for top in range(0, rows, CHUNK)], axis=0), rows
        )
        for block, (_, (to_block, _)) in enumerate(parts)
        if to_block
    ]
    return found, jnp.concatenate(best_held, axis=1)


def assemble(whole, top, rows, pieces, extra):
    first, *others = pieces
    height = min(first.shape[0], rows)
    whole[top : top + height, :] = first[0:height, :]
    for last in others:
        height = last.shape[0] - extra
        whole[top + rows - height : top + rows, :] = last[0:height, :]


def hold(holds, held, rows, span):
    for at, block in enumerate(holds):
        assemble(held, at * rows, rows, block, EXTRA)
    row = [codes(block[-1], rows, span)[:, :rows] for block in holds]
    rest = held.shape[0] - len(holds) * rows
    if rest:
        held[len(holds) * rows :, :] = jnp.zeros((rest, held.shape[1]), held.dtype)
        row.append(jnp.zeros((1, rest), jnp.float32))
    return jnp.concatenate(row, axis=1)


def gather_kernel(rows, span, lengths, *refs):
    *pieces, held, row, joined = refs
    *holds, far = regrouped(pieces, lengths)
    row[...] = hold(holds, held, rows, span)
    assemble(joined, 0, rows, far, 0)


def gather(holds, far, rows, span):
    width = far[0].shape[1]
    total = len(holds) * rows
    parts = [*holds, far]
    return pl.pallas_call(
        functools.partial(gather_kernel, rows, span, [len(part) for part in parts]),
        out_shape=[
            jax.ShapeDtypeStruct((total, width), jnp.bfloat16),
            jax.ShapeDtypeStruct((1, total), jnp.float32),
            jax.ShapeDtypeStruct((rows, width), jnp.bfloat16),
        ],
        compiler_params=pltpu.CompilerParams(vmem_limit_bytes=8 << 20),
        cost_estimate=pl.CostEstimate(
            flops=rows * total * width // 4, bytes_accessed=rows, transcendentals=0
        ),
    )(*[piece for part in parts for piece in part])


def regrouped(flat, lengths):
    flat = iter(flat)
    return [[next(flat) for _ in range(length)] for length in lengths]


def pair(units, first, second, rows):
    units[0:rows, :] = first[0:rows, :]
    units[rows:, :] = second[0:rows, :]


def plane_kernel(rows, span, lengths, block, partner, *refs):
    *pieces, best, mine, held, units = refs
    row = hold(regrouped(pieces, lengths), held, rows, span)
    pair(units, block, partner, rows)
    parts = [(codes(block, rows, span), OWN), (codes(partner, rows, span), HELD)]
    (mine[...],), theirs = meet(units, parts, rows, span, held, row)
    best[...] = theirs[:, : best.shape[1]]


def rest_kernel(rows, span, block, partner, held, row, best, mine, units):
    count = best.shape[1]
    start = held.shape[0] - up(count, LANES)
    held, row = held.at[start:, :], row[:, start:]
    pair(units, block, partner, rows)
    parts = [(codes(block, rows, span), OWN), (codes(partner, rows, span), HELD)]
    (mine[...],), theirs = meet(units, parts, rows, span, held, row)
    best[...] = theirs[:, row.shape[1] - count :]


def line_kernel(rows, span, together, count, first, second, held, row, *refs):
    bests, outs, (found, units) = refs[:count], refs[count:-2], refs[-2:]
    parts = [(codes(second, rows, span, first=place), TWO) for place in (CODES, 0)]

    def give(best):
        for out, places in zip(outs, together):
            out[...] = jnp.concatenate(
                [best[:, place * rows : (place + 1) * rows] for place in places], axis=1
            )

    arrived = jnp.max(parts[0][0]) > 0.0

    @pl.when(arrived)
    def _():
        pair(units, first, second, rows)
        mine, theirs = meet(units, parts, rows, span, held, row[...])
        found[...] = jnp.concatenate(mine, axis=1)
        give(jnp.maximum(jnp.concatenate([best[...] for best in bests], axis=1), theirs))

    @pl.when(jnp.logical_not(arrived))
    def _():
        found[...] = jnp.full(found.shape, -1.0, jnp.float32)
        give(jnp.concatenate([best[...] for best in bests], axis=1))


def plane(block, partner, holds, rows, span):
    width = block.shape[1]
    total = len(holds) * rows
    return pl.pallas_call(
        functools.partial(plane_kernel, rows, span, [len(part) for part in holds]),
        out_shape=[
            jax.ShapeDtypeStruct((1, total), jnp.float32),
            jax.ShapeDtypeStruct((1, rows), jnp.float32),
        ],
        scratch_shapes=[
            pltpu.VMEM((up(total, LANES), width), jnp.bfloat16),
            pltpu.VMEM((2 * rows, width), jnp.bfloat16),
        ],
        compiler_params=pltpu.CompilerParams(vmem_limit_bytes=12 << 20),
        cost_estimate=pl.CostEstimate(flops=rows, bytes_accessed=rows, transcendentals=0),
    )(block, partner, *[piece for part in holds for piece in part])


def plane_rest(block, partner, held, row, count, rows, span):
    return pl.pallas_call(
        functools.partial(rest_kernel, rows, span),
        out_shape=[
            jax.ShapeDtypeStruct((1, count), jnp.float32),
            jax.ShapeDtypeStruct((1, rows), jnp.float32),
        ],
        scratch_shapes=[pltpu.VMEM((2 * rows, block.shape[1]), jnp.bfloat16)],
        compiler_params=pltpu.CompilerParams(vmem_limit_bytes=12 << 20),
        cost_estimate=pl.CostEstimate(flops=rows, bytes_accessed=rows, transcendentals=0),
    )(block, partner, held, row)


def line(first, second, held, row, bests, rows, span, together):
    outs = [jax.ShapeDtypeStruct((1, rows * len(some)), jnp.float32) for some in together]
    *bests, found = pl.pallas_call(
        functools.partial(line_kernel, rows, span, together, len(bests)),
        out_shape=outs + [jax.ShapeDtypeStruct((1, 2 * rows), jnp.float32)],
        scratch_shapes=[pltpu.VMEM((2 * rows, second.shape[1]), jnp.bfloat16)],
        compiler_params=pltpu.CompilerParams(vmem_limit_bytes=12 << 20),
        cost_estimate=pl.CostEstimate(flops=rows, bytes_accessed=rows, transcendentals=0),
    )(first, second, held, row, *bests)
    return bests, found


OWN = (True, False)
HELD = (False, True)
TWO = (True, True)


def line_rounds(chips):
    if chips == 4:
        return [[(3, 1), (0, 2), (2, 3)], [(3, 0), (0, 1), (1, 2)]]
    rounds = []
    for shift in range(1, chips // 2 + 1):
        senders = chips // 2 if 2 * shift == chips else chips
        rounds.append([(s, (s + shift) % chips) for s in range(senders)])
    return rounds


def solution(mesh):
    groups, members = mesh.shape["dp"], mesh.shape["grid"]
    assert groups == 4 and members % 2 == 0
    chips = members // 2

    def everywhere(target):
        return [
            (p * members + g, a * members + b)
            for p in range(groups)
            for g in range(members)
            for a, b in [target(p, g)]
        ]

    other_core = everywhere(lambda p, g: (p, g ^ 1))
    first = everywhere(lambda p, g: (p ^ (1 + g % 2), g))
    second = everywhere(lambda p, g: (p ^ (2 - g % 2), g))
    second_home = everywhere(lambda p, g: (p ^ (2 - g % 2), g ^ 1))

    rounds = line_rounds(chips)
    rounds += [[]] * (len(rounds) % 2)
    rounds = [
        [
            (p * members + 2 * s + c, p * members + 2 * t + c)
            for p in range(groups)
            for c in range(2)
            for s, t in rounds[at + c]
        ]
        for at in range(0, len(rounds), 2)
    ]

    def back(pairs):
        return [(target, source) for source, target in pairs]

    def shards(embeddings, cluster, order_key):
        rows = embeddings.shape[0]
        span = 256
        while span < rows * groups * members:
            span *= 2
        halves = (rows // 2, rows // 2 + EXTRA)
        names = (cluster.reshape(1, rows), order_key)
        raw = [lax.ppermute(embeddings, BOTH, pairs) for pairs in rounds]
        charge = [lax.ppermute(array, BOTH, other_core) for array in (embeddings, *names)]
        width = embeddings.shape[1]
        block, *parts = with_units(prepare_kernel, (rows + EXTRA, *halves), width, *charge)
        from_first = [lax.ppermute(part, BOTH, first) for part in parts]
        (own_codes,) = with_units(codes_kernel, (EXTRA,), width, *names)
        later, own_codes = lax.optimization_barrier((block, own_codes))
        from_second = [lax.ppermute(later, BOTH, second)]
        (both,) = with_units(complete_kernel, (rows + EXTRA,), width, block, own_codes)
        (own,) = with_units(own_kernel, (rows + EXTRA,), width, embeddings, own_codes)
        near_other = [lax.ppermute(both, BOTH, pairs) for pairs in rounds]
        from_corner = [lax.ppermute(part, BOTH, second) for part in from_first]
        near = [
            list(with_units(unit_kernel, (rows, rows // 2, rows // 2), width, rows_of))
            for rows_of in raw
        ]
        far = [[lax.ppermute(piece, BOTH, other_core) for piece in blocks[1:]] for blocks in near]

        in_charge, results, kept, sent = [], [], [], []
        best_two, mine = plane(block, own, [[block], from_first], rows, span)
        in_charge.append(mine)
        *from_corner, best_two = lax.optimization_barrier((*from_corner, best_two))
        blocks = [[block], from_first, from_second, from_corner]
        held, row, far_units = gather(blocks, far[0], rows, span)
        best_rest, mine = plane_rest(block, own, held, row, 2 * rows, rows, span)
        in_charge.append(mine)
        bests = [best_two, best_rest]
        far = [far_units] + [jnp.concatenate(pieces, axis=0) for pieces in far[1:]]
        whole, last = [tuple(range(groups))], [(0,), (1, 3), (2,)]
        for at, second_near in enumerate(near_other):
            second_near, *bests = lax.optimization_barrier((second_near, *bests))
            second_far = lax.ppermute(second_near, BOTH, other_core)
            bests, found = line(near[at][0], second_near, held, row, bests, rows, span, whole)
            kept.append(found)
            bests, found = line(
                far[at],
                second_far,
                held,
                row,
                bests,
                rows,
                span,
                last if at == len(rounds) - 1 else whole,
            )
            sent.append(found)
        sent = lax.ppermute(jnp.concatenate(sent, axis=1), BOTH, other_core)
        kept = jnp.maximum(jnp.concatenate(kept, axis=1), sent)
        for at, pairs in enumerate(rounds):
            found = lax.ppermute(kept[:, 2 * at * rows : 2 * (at + 1) * rows], BOTH, back(pairs))
            me = lax.axis_index(BOTH)
            sender = functools.reduce(jnp.logical_or, [me == source for source, _ in pairs])
            found = jnp.where(sender, found, -1.0)
            results += [found[:, :rows], lax.ppermute(found[:, rows:], BOTH, other_core)]
        from_x = lax.ppermute(bests[1], BOTH, first)
        in_charge += [bests[0], from_x[:, :rows]]
        onward = jnp.maximum(bests[2], from_x[:, rows:])
        results.append(lax.ppermute(onward, BOTH, second_home))
        home = functools.reduce(jnp.maximum, in_charge)
        results.append(lax.ppermute(home, BOTH, other_core))
        return functools.reduce(jnp.maximum, results).reshape(rows)

    placed = (P(BOTH, None), P(BOTH, None), P(BOTH))
    return jax.shard_map(
        shards, mesh=mesh, in_specs=placed, out_specs=P(BOTH), check_vma=False
    )
```

```python
import functools

import jax
import jax.numpy as jnp
from jax import lax
from jax.experimental import pallas as pl
from jax.experimental.pallas import tpu as pltpu
from jax.sharding import PartitionSpec as P

EPSILON = 1e-06
EXTRA = 16
CODES = 3
LANES = 128
TILE = 256
CHUNK = 32
BOTH = ("dp", "grid")


def up(value, multiple):
    return -(-value // multiple) * multiple


def turned_to_column(row, rows):
    return jnp.broadcast_to(row, (LANES, row.shape[1])).T[:rows]


def codes(block, rows, span, first=0):
    parts = block[block.shape[0] - EXTRA :, : up(rows, LANES)].astype(jnp.float32)
    parts = parts[first : first + CODES]
    return parts[2:3] * (4.0 * span) + parts[0:1] * 256.0 + parts[1:2]


def unit_rows(rows, out):
    values = rows[...].astype(jnp.float32)
    scale = lax.rsqrt(jnp.sum(values * values, axis=1, keepdims=True) + EPSILON)
    out[0 : rows.shape[0], :] = (values * scale).astype(jnp.bfloat16)


def give_parts(block, outs):
    for out, top in zip(outs, (0, block.shape[0] - outs[-1].shape[0])):
        out[...] = block[top : top + out.shape[0], :]


def code_rows(cluster, order_key, width):
    rows = order_key.shape[0]
    keys = order_key[...].reshape(1, rows)
    parts = [keys >> 8, keys & 255, cluster[...] + 1]
    parts = [part.astype(jnp.float32) for part in parts]
    parts = jnp.concatenate(parts + [jnp.zeros((EXTRA - CODES, rows), jnp.float32)], axis=0)
    parts = jnp.concatenate([parts, jnp.zeros((EXTRA, width - rows), jnp.float32)], axis=1)
    return parts.astype(jnp.bfloat16)


def prepare_kernel(embeddings, cluster, order_key, block, *parts_out):
    rows, width = embeddings.shape
    unit_rows(embeddings, block)
    block[rows : rows + EXTRA, :] = code_rows(cluster, order_key, width)
    give_parts(block, parts_out)


def codes_kernel(cluster, order_key, out):
    out[...] = code_rows(cluster, order_key, out.shape[1])


def own_kernel(embeddings, own_codes, block):
    unit_rows(embeddings, block)
    block[embeddings.shape[0] :, :] = own_codes[...]


def complete_kernel(block, other_codes, out):
    rows = block.shape[0] - EXTRA
    out[0:rows, :] = block[0:rows, :]
    named = [part[...].astype(jnp.float32)[0:CODES] for part in (block.at[rows:, :], other_codes)]
    rest = jnp.zeros((EXTRA - 2 * CODES, block.shape[1]), jnp.float32)
    out[rows:, :] = jnp.concatenate(named + [rest], axis=0).astype(jnp.bfloat16)


def unit_kernel(rows_of, block, *parts_out):
    unit_rows(rows_of, block)
    give_parts(block, parts_out)


def with_units(kernel, heights, width, *inputs):
    return pl.pallas_call(
        kernel,
        out_shape=[jax.ShapeDtypeStruct((height, width), jnp.bfloat16) for height in heights],
        compiler_params=pltpu.CompilerParams(vmem_limit_bytes=8 << 20),
        cost_estimate=pl.CostEstimate(flops=width, bytes_accessed=width, transcendentals=0),
    )(*inputs)


def row_from_partial(partial, rows):
    padded = up(rows, LANES)
    if padded != rows:
        partial = jnp.concatenate(
            [partial, jnp.zeros((padded - rows, LANES), partial.dtype)], axis=0
        )
    return jnp.max(partial.T, axis=0, keepdims=True)[:, :rows]


def meet(units, parts, rows, span, held, held_codes):
    columns = [turned_to_column(row, rows) for row, _ in parts]
    starts = [(block, top) for block in range(len(parts)) for top in range(0, rows, CHUNK)]
    partial = {start: jnp.full((CHUNK, LANES), -1.0, jnp.float32) for start in starts}
    best_held = []
    for at in range(0, held.shape[0], TILE):
        tile = min(TILE, held.shape[0] - at)
        sims = lax.dot_general(
            units[...],
            held[at : at + tile, :],
            (((1,), (1,)), ((), ())),
            preferred_element_type=jnp.float32,
        )
        best = [jnp.full((CHUNK, LANES), -1.0, jnp.float32) for _ in range(0, tile, LANES)]
        for block, top in starts:
            to_block, to_held = parts[block][1]
            mine = columns[block][top : top + CHUNK]
            line = block * rows + top
            for lane in range(0, tile, LANES):
                part = sims[line : line + CHUNK, lane : lane + LANES]
                gap = mine - held_codes[:, at + lane : at + lane + LANES]
                if to_block and to_held:
                    part = jnp.where(jnp.abs(gap) < span, part, -1.0)
                    later = gap > 0.0
                    ours, theirs = jnp.where(later, part, -1.0), jnp.where(later, -1.0, part)
                elif to_block:
                    ours = jnp.where((gap > 0.0) & (gap < span), part, -1.0)
                else:
                    theirs = jnp.where((gap < 0.0) & (gap > -span), part, -1.0)
                if to_block:
                    partial[block, top] = jnp.maximum(partial[block, top], ours)
                if to_held:
                    best[lane // LANES] = jnp.maximum(best[lane // LANES], theirs)
        best_held += [jnp.max(some, axis=0, keepdims=True) for some in best]
    found = [
        row_from_partial(
            jnp.concatenate([partial[block, top] for top in range(0, rows, CHUNK)], axis=0), rows
        )
        for block, (_, (to_block, _)) in enumerate(parts)
        if to_block
    ]
    return found, jnp.concatenate(best_held, axis=1)


def assemble(whole, top, rows, pieces, extra):
    first, *others = pieces
    height = min(first.shape[0], rows)
    whole[top : top + height, :] = first[0:height, :]
    for last in others:
        height = last.shape[0] - extra
        whole[top + rows - height : top + rows, :] = last[0:height, :]


def hold(holds, held, rows, span):
    for at, block in enumerate(holds):
        assemble(held, at * rows, rows, block, EXTRA)
    row = [codes(block[-1], rows, span)[:, :rows] for block in holds]
    rest = held.shape[0] - len(holds) * rows
    if rest:
        held[len(holds) * rows :, :] = jnp.zeros((rest, held.shape[1]), held.dtype)
        row.append(jnp.zeros((1, rest), jnp.float32))
    return jnp.concatenate(row, axis=1)


def gather_kernel(rows, span, lengths, *refs):
    *pieces, held, row, joined = refs
    *holds, far = regrouped(pieces, lengths)
    row[...] = hold(holds, held, rows, span)
    assemble(joined, 0, rows, far, 0)


def gather(holds, far, rows, span):
    width = far[0].shape[1]
    total = len(holds) * rows
    parts = [*holds, far]
    return pl.pallas_call(
        functools.partial(gather_kernel, rows, span, [len(part) for part in parts]),
        out_shape=[
            jax.ShapeDtypeStruct((total, width), jnp.bfloat16),
            jax.ShapeDtypeStruct((1, total), jnp.float32),
            jax.ShapeDtypeStruct((rows, width), jnp.bfloat16),
        ],
        compiler_params=pltpu.CompilerParams(vmem_limit_bytes=8 << 20),
        cost_estimate=pl.CostEstimate(
            flops=rows * total * width // 4, bytes_accessed=rows, transcendentals=0
        ),
    )(*[piece for part in parts for piece in part])


def regrouped(flat, lengths):
    flat = iter(flat)
    return [[next(flat) for _ in range(length)] for length in lengths]


def pair(units, first, second, rows):
    units[0:rows, :] = first[0:rows, :]
    units[rows:, :] = second[0:rows, :]


def plane_kernel(rows, span, lengths, block, partner, *refs):
    *pieces, best, mine, held, units = refs
    row = hold(regrouped(pieces, lengths), held, rows, span)
    pair(units, block, partner, rows)
    parts = [(codes(block, rows, span), OWN), (codes(partner, rows, span), HELD)]
    (mine[...],), theirs = meet(units, parts, rows, span, held, row)
    best[...] = theirs[:, : best.shape[1]]


def rest_kernel(rows, span, block, partner, held, row, best, mine, units):
    count = best.shape[1]
    start = held.shape[0] - up(count, LANES)
    held, row = held.at[start:, :], row[:, start:]
    pair(units, block, partner, rows)
    parts = [(codes(block, rows, span), OWN), (codes(partner, rows, span), HELD)]
    (mine[...],), theirs = meet(units, parts, rows, span, held, row)
    best[...] = theirs[:, row.shape[1] - count :]


def line_kernel(rows, span, together, count, first, second, held, row, *refs):
    bests, outs, (found, units) = refs[:count], refs[count:-2], refs[-2:]
    parts = [(codes(second, rows, span, first=place), TWO) for place in (CODES, 0)]

    def give(best):
        for out, places in zip(outs, together):
            out[...] = jnp.concatenate(
                [best[:, place * rows : (place + 1) * rows] for place in places], axis=1
            )

    arrived = jnp.max(parts[0][0]) > 0.0

    @pl.when(arrived)
    def _():
        pair(units, first, second, rows)
        mine, theirs = meet(units, parts, rows, span, held, row[...])
        found[...] = jnp.concatenate(mine, axis=1)
        give(jnp.maximum(jnp.concatenate([best[...] for best in bests], axis=1), theirs))

    @pl.when(jnp.logical_not(arrived))
    def _():
        found[...] = jnp.full(found.shape, -1.0, jnp.float32)
        give(jnp.concatenate([best[...] for best in bests], axis=1))


def plane(block, partner, holds, rows, span):
    width = block.shape[1]
    total = len(holds) * rows
    return pl.pallas_call(
        functools.partial(plane_kernel, rows, span, [len(part) for part in holds]),
        out_shape=[
            jax.ShapeDtypeStruct((1, total), jnp.float32),
            jax.ShapeDtypeStruct((1, rows), jnp.float32),
        ],
        scratch_shapes=[
            pltpu.VMEM((up(total, LANES), width), jnp.bfloat16),
            pltpu.VMEM((2 * rows, width), jnp.bfloat16),
        ],
        compiler_params=pltpu.CompilerParams(vmem_limit_bytes=12 << 20),
        cost_estimate=pl.CostEstimate(flops=rows, bytes_accessed=rows, transcendentals=0),
    )(block, partner, *[piece for part in holds for piece in part])


def plane_rest(block, partner, held, row, count, rows, span):
    return pl.pallas_call(
        functools.partial(rest_kernel, rows, span),
        out_shape=[
            jax.ShapeDtypeStruct((1, count), jnp.float32),
            jax.ShapeDtypeStruct((1, rows), jnp.float32),
        ],
        scratch_shapes=[pltpu.VMEM((2 * rows, block.shape[1]), jnp.bfloat16)],
        compiler_params=pltpu.CompilerParams(vmem_limit_bytes=12 << 20),
        cost_estimate=pl.CostEstimate(flops=rows, bytes_accessed=rows, transcendentals=0),
    )(block, partner, held, row)


def line(first, second, held, row, bests, rows, span, together):
    outs = [jax.ShapeDtypeStruct((1, rows * len(some)), jnp.float32) for some in together]
    *bests, found = pl.pallas_call(
        functools.partial(line_kernel, rows, span, together, len(bests)),
        out_shape=outs + [jax.ShapeDtypeStruct((1, 2 * rows), jnp.float32)],
        scratch_shapes=[pltpu.VMEM((2 * rows, second.shape[1]), jnp.bfloat16)],
        compiler_params=pltpu.CompilerParams(vmem_limit_bytes=12 << 20),
        cost_estimate=pl.CostEstimate(flops=rows, bytes_accessed=rows, transcendentals=0),
    )(first, second, held, row, *bests)
    return bests, found


OWN = (True, False)
HELD = (False, True)
TWO = (True, True)


def line_rounds(chips):
    if chips == 4:
        return [[(3, 1), (0, 2), (2, 3)], [(3, 0), (0, 1), (1, 2)]]
    rounds = []
    for shift in range(1, chips // 2 + 1):
        senders = chips // 2 if 2 * shift == chips else chips
        rounds.append([(s, (s + shift) % chips) for s in range(senders)])
    return rounds


def solution(mesh):
    groups, members = mesh.shape["dp"], mesh.shape["grid"]
    assert groups == 4 and members % 2 == 0
    chips = members // 2

    def everywhere(target):
        return [
            (p * members + g, a * members + b)
            for p in range(groups)
            for g in range(members)
            for a, b in [target(p, g)]
        ]

    other_core = everywhere(lambda p, g: (p, g ^ 1))
    first = everywhere(lambda p, g: (p ^ (1 + g % 2), g))
    second = everywhere(lambda p, g: (p ^ (2 - g % 2), g))
    homes = [
        everywhere(lambda p, g: (p ^ (1 + g % 2), g ^ 1)),
        everywhere(lambda p, g: (p ^ (2 - g % 2), g ^ 1)),
        everywhere(lambda p, g: (p ^ 3, g ^ 1)),
    ]

    rounds = line_rounds(chips)
    rounds += [[]] * (len(rounds) % 2)
    rounds = [
        [
            (p * members + 2 * s + c, p * members + 2 * t + c)
            for p in range(groups)
            for c in range(2)
            for s, t in rounds[at + c]
        ]
        for at in range(0, len(rounds), 2)
    ]

    def back(pairs):
        return [(target, source) for source, target in pairs]

    def shards(embeddings, cluster, order_key):
        rows = embeddings.shape[0]
        span = 256
        while span < rows * groups * members:
            span *= 2
        halves = (rows // 2, rows // 2 + EXTRA)
        names = (cluster.reshape(1, rows), order_key)
        raw = [lax.ppermute(embeddings, BOTH, pairs) for pairs in rounds]
        charge = [lax.ppermute(array, BOTH, other_core) for array in (embeddings, *names)]
        width = embeddings.shape[1]
        block, *parts = with_units(prepare_kernel, (rows + EXTRA, *halves), width, *charge)
        from_first = [lax.ppermute(part, BOTH, first) for part in parts]
        (own_codes,) = with_units(codes_kernel, (EXTRA,), width, *names)
        later, own_codes = lax.optimization_barrier((block, own_codes))
        from_second = [lax.ppermute(later, BOTH, second)]
        (both,) = with_units(complete_kernel, (rows + EXTRA,), width, block, own_codes)
        (own,) = with_units(own_kernel, (rows + EXTRA,), width, embeddings, own_codes)
        near_other = [lax.ppermute(both, BOTH, pairs) for pairs in rounds]
        from_corner = [lax.ppermute(part, BOTH, second) for part in from_first]
        near = [
            list(with_units(unit_kernel, (rows, rows // 2, rows // 2), width, rows_of))
            for rows_of in raw
        ]
        far = [[lax.ppermute(piece, BOTH, other_core) for piece in blocks[1:]] for blocks in near]

        in_charge, results, kept, sent = [], [], [], []
        best_two, mine = plane(block, own, [[block], from_first], rows, span)
        in_charge.append(mine)
        *from_corner, best_two = lax.optimization_barrier((*from_corner, best_two))
        blocks = [[block], from_first, from_second, from_corner]
        held, row, far_units = gather(blocks, far[0], rows, span)
        best_rest, mine = plane_rest(block, own, held, row, 2 * rows, rows, span)
        in_charge.append(mine)
        bests = [best_two, best_rest]
        far = [far_units] + [jnp.concatenate(pieces, axis=0) for pieces in far[1:]]
        whole, last = [tuple(range(groups))], [(at,) for at in range(groups)]
        for at, second_near in enumerate(near_other):
            second_near, *bests = lax.optimization_barrier((second_near, *bests))
            second_far = lax.ppermute(second_near, BOTH, other_core)
            bests, found = line(near[at][0], second_near, held, row, bests, rows, span, whole)
            kept.append(found)
            bests, found = line(
                far[at],
                second_far,
                held,
                row,
                bests,
                rows,
                span,
                last if at == len(rounds) - 1 else whole,
            )
            sent.append(found)
        sent = lax.ppermute(jnp.concatenate(sent, axis=1), BOTH, other_core)
        kept = jnp.maximum(jnp.concatenate(kept, axis=1), sent)
        kept, *bests = lax.optimization_barrier((kept, *bests))
        for at, pairs in enumerate(rounds):
            found = lax.ppermute(kept[:, 2 * at * rows : 2 * (at + 1) * rows], BOTH, back(pairs))
            me = lax.axis_index(BOTH)
            sender = functools.reduce(jnp.logical_or, [me == source for source, _ in pairs])
            found = jnp.where(sender, found, -1.0)
            results.append(found[:, :rows])
            in_charge.append(found[:, rows:])
        results += [
            lax.ppermute(best, BOTH, pairs) for best, pairs in zip(bests[1:], homes)
        ]
        in_charge.append(bests[0])
        home = functools.reduce(jnp.maximum, in_charge)
        results.append(lax.ppermute(home, BOTH, other_core))
        return functools.reduce(jnp.maximum, results).reshape(rows)

    placed = (P(BOTH, None), P(BOTH, None), P(BOTH))
    return jax.shard_map(
        shards, mesh=mesh, in_specs=placed, out_specs=P(BOTH), check_vma=False
    )
```

```python
import functools

import jax
import jax.numpy as jnp
from jax import lax
from jax.experimental import pallas as pl
from jax.experimental.pallas import tpu as pltpu
from jax.sharding import PartitionSpec as P

EPSILON = 1e-06
EXTRA = 16
CODES = 3
LANES = 128
TILE = 256
CHUNK = 32
BOTH = ("dp", "grid")


def up(value, multiple):
    return -(-value // multiple) * multiple


def turned_to_column(row, rows):
    return jnp.broadcast_to(row, (LANES, row.shape[1])).T[:rows]


def codes(block, rows, span, first=0):
    parts = block[block.shape[0] - EXTRA :, : up(rows, LANES)].astype(jnp.float32)
    parts = parts[first : first + CODES]
    return parts[2:3] * (4.0 * span) + parts[0:1] * 256.0 + parts[1:2]


def unit_rows(rows, out):
    values = rows[...].astype(jnp.float32)
    scale = lax.rsqrt(jnp.sum(values * values, axis=1, keepdims=True) + EPSILON)
    out[0 : rows.shape[0], :] = (values * scale).astype(jnp.bfloat16)


def give_parts(block, outs):
    for out, top in zip(outs, (0, block.shape[0] - outs[-1].shape[0])):
        out[...] = block[top : top + out.shape[0], :]


def code_rows(cluster, order_key, width):
    rows = order_key.shape[0]
    keys = order_key[...].reshape(1, rows)
    parts = [keys >> 8, keys & 255, cluster[...] + 1]
    parts = [part.astype(jnp.float32) for part in parts]
    parts = jnp.concatenate(parts + [jnp.zeros((EXTRA - CODES, rows), jnp.float32)], axis=0)
    parts = jnp.concatenate([parts, jnp.zeros((EXTRA, width - rows), jnp.float32)], axis=1)
    return parts.astype(jnp.bfloat16)


def prepare_kernel(embeddings, cluster, order_key, block, *parts_out):
    rows, width = embeddings.shape
    unit_rows(embeddings, block)
    block[rows : rows + EXTRA, :] = code_rows(cluster, order_key, width)
    give_parts(block, parts_out)


def codes_kernel(cluster, order_key, out):
    out[...] = code_rows(cluster, order_key, out.shape[1])


def own_kernel(embeddings, own_codes, block):
    unit_rows(embeddings, block)
    block[embeddings.shape[0] :, :] = own_codes[...]


def complete_kernel(block, other_codes, out):
    rows = block.shape[0] - EXTRA
    out[0:rows, :] = block[0:rows, :]
    named = [part[...].astype(jnp.float32)[0:CODES] for part in (block.at[rows:, :], other_codes)]
    rest = jnp.zeros((EXTRA - 2 * CODES, block.shape[1]), jnp.float32)
    out[rows:, :] = jnp.concatenate(named + [rest], axis=0).astype(jnp.bfloat16)


def unit_kernel(rows_of, block, *parts_out):
    unit_rows(rows_of, block)
    give_parts(block, parts_out)


def with_units(kernel, heights, width, *inputs):
    return pl.pallas_call(
        kernel,
        out_shape=[jax.ShapeDtypeStruct((height, width), jnp.bfloat16) for height in heights],
        compiler_params=pltpu.CompilerParams(vmem_limit_bytes=8 << 20),
        cost_estimate=pl.CostEstimate(flops=width, bytes_accessed=width, transcendentals=0),
    )(*inputs)


def row_from_partial(partial, rows):
    padded = up(rows, LANES)
    if padded != rows:
        partial = jnp.concatenate(
            [partial, jnp.zeros((padded - rows, LANES), partial.dtype)], axis=0
        )
    return jnp.max(partial.T, axis=0, keepdims=True)[:, :rows]


def meet(units, parts, rows, span, held, held_codes):
    columns = [turned_to_column(row, rows) for row, _ in parts]
    starts = [(block, top) for block in range(len(parts)) for top in range(0, rows, CHUNK)]
    partial = {start: jnp.full((CHUNK, LANES), -1.0, jnp.float32) for start in starts}
    best_held = []
    for at in range(0, held.shape[0], TILE):
        tile = min(TILE, held.shape[0] - at)
        sims = lax.dot_general(
            units[...],
            held[at : at + tile, :],
            (((1,), (1,)), ((), ())),
            preferred_element_type=jnp.float32,
        )
        best = [jnp.full((CHUNK, LANES), -1.0, jnp.float32) for _ in range(0, tile, LANES)]
        for block, top in starts:
            to_block, to_held = parts[block][1]
            mine = columns[block][top : top + CHUNK]
            line = block * rows + top
            for lane in range(0, tile, LANES):
                part = sims[line : line + CHUNK, lane : lane + LANES]
                gap = mine - held_codes[:, at + lane : at + lane + LANES]
                if to_block and to_held:
                    part = jnp.where(jnp.abs(gap) < span, part, -1.0)
                    later = gap > 0.0
                    ours, theirs = jnp.where(later, part, -1.0), jnp.where(later, -1.0, part)
                elif to_block:
                    ours = jnp.where((gap > 0.0) & (gap < span), part, -1.0)
                else:
                    theirs = jnp.where((gap < 0.0) & (gap > -span), part, -1.0)
                if to_block:
                    partial[block, top] = jnp.maximum(partial[block, top], ours)
                if to_held:
                    best[lane // LANES] = jnp.maximum(best[lane // LANES], theirs)
        best_held += [jnp.max(some, axis=0, keepdims=True) for some in best]
    found = [
        row_from_partial(
            jnp.concatenate([partial[block, top] for top in range(0, rows, CHUNK)], axis=0), rows
        )
        for block, (_, (to_block, _)) in enumerate(parts)
        if to_block
    ]
    return found, jnp.concatenate(best_held, axis=1)


def assemble(whole, top, rows, pieces, extra):
    first, *others = pieces
    height = min(first.shape[0], rows)
    whole[top : top + height, :] = first[0:height, :]
    for last in others:
        height = last.shape[0] - extra
        whole[top + rows - height : top + rows, :] = last[0:height, :]


def hold(holds, held, rows, span):
    for at, block in enumerate(holds):
        assemble(held, at * rows, rows, block, EXTRA)
    row = [codes(block[-1], rows, span)[:, :rows] for block in holds]
    rest = held.shape[0] - len(holds) * rows
    if rest:
        held[len(holds) * rows :, :] = jnp.zeros((rest, held.shape[1]), held.dtype)
        row.append(jnp.zeros((1, rest), jnp.float32))
    return jnp.concatenate(row, axis=1)


def gather_kernel(rows, span, lengths, *refs):
    *pieces, held, row, joined = refs
    *holds, far = regrouped(pieces, lengths)
    row[...] = hold(holds, held, rows, span)
    assemble(joined, 0, rows, far, 0)


def gather(holds, far, rows, span):
    width = far[0].shape[1]
    total = len(holds) * rows
    parts = [*holds, far]
    return pl.pallas_call(
        functools.partial(gather_kernel, rows, span, [len(part) for part in parts]),
        out_shape=[
            jax.ShapeDtypeStruct((total, width), jnp.bfloat16),
            jax.ShapeDtypeStruct((1, total), jnp.float32),
            jax.ShapeDtypeStruct((rows, width), jnp.bfloat16),
        ],
        compiler_params=pltpu.CompilerParams(vmem_limit_bytes=8 << 20),
        cost_estimate=pl.CostEstimate(
            flops=rows * total * width // 4, bytes_accessed=rows, transcendentals=0
        ),
    )(*[piece for part in parts for piece in part])


def regrouped(flat, lengths):
    flat = iter(flat)
    return [[next(flat) for _ in range(length)] for length in lengths]


def pair(units, first, second, rows):
    units[0:rows, :] = first[0:rows, :]
    units[rows:, :] = second[0:rows, :]


def plane_kernel(rows, span, lengths, block, partner, *refs):
    *pieces, best, mine, held, units = refs
    row = hold(regrouped(pieces, lengths), held, rows, span)
    pair(units, block, partner, rows)
    parts = [(codes(block, rows, span), OWN), (codes(partner, rows, span), HELD)]
    (mine[...],), theirs = meet(units, parts, rows, span, held, row)
    best[...] = theirs[:, : best.shape[1]]


def rest_kernel(rows, span, block, partner, held, row, best, mine, units):
    count = best.shape[1]
    start = held.shape[0] - up(count, LANES)
    held, row = held.at[start:, :], row[:, start:]
    pair(units, block, partner, rows)
    parts = [(codes(block, rows, span), OWN), (codes(partner, rows, span), HELD)]
    (mine[...],), theirs = meet(units, parts, rows, span, held, row)
    best[...] = theirs[:, row.shape[1] - count :]


def line_kernel(rows, span, together, count, first, second, held, row, *refs):
    bests, outs, (found, units) = refs[:count], refs[count:-2], refs[-2:]
    parts = [(codes(second, rows, span, first=place), TWO) for place in (CODES, 0)]

    def give(best):
        for out, places in zip(outs, together):
            out[...] = jnp.concatenate(
                [best[:, place * rows : (place + 1) * rows] for place in places], axis=1
            )

    arrived = jnp.max(parts[0][0]) > 0.0

    @pl.when(arrived)
    def _():
        pair(units, first, second, rows)
        mine, theirs = meet(units, parts, rows, span, held, row[...])
        found[...] = jnp.concatenate(mine, axis=1)
        give(jnp.maximum(jnp.concatenate([best[...] for best in bests], axis=1), theirs))

    @pl.when(jnp.logical_not(arrived))
    def _():
        found[...] = jnp.full(found.shape, -1.0, jnp.float32)
        give(jnp.concatenate([best[...] for best in bests], axis=1))


def plane(block, partner, holds, rows, span):
    width = block.shape[1]
    total = len(holds) * rows
    return pl.pallas_call(
        functools.partial(plane_kernel, rows, span, [len(part) for part in holds]),
        out_shape=[
            jax.ShapeDtypeStruct((1, total), jnp.float32),
            jax.ShapeDtypeStruct((1, rows), jnp.float32),
        ],
        scratch_shapes=[
            pltpu.VMEM((up(total, LANES), width), jnp.bfloat16),
            pltpu.VMEM((2 * rows, width), jnp.bfloat16),
        ],
        compiler_params=pltpu.CompilerParams(vmem_limit_bytes=12 << 20),
        cost_estimate=pl.CostEstimate(flops=rows, bytes_accessed=rows, transcendentals=0),
    )(block, partner, *[piece for part in holds for piece in part])


def plane_rest(block, partner, held, row, count, rows, span):
    return pl.pallas_call(
        functools.partial(rest_kernel, rows, span),
        out_shape=[
            jax.ShapeDtypeStruct((1, count), jnp.float32),
            jax.ShapeDtypeStruct((1, rows), jnp.float32),
        ],
        scratch_shapes=[pltpu.VMEM((2 * rows, block.shape[1]), jnp.bfloat16)],
        compiler_params=pltpu.CompilerParams(vmem_limit_bytes=12 << 20),
        cost_estimate=pl.CostEstimate(flops=rows, bytes_accessed=rows, transcendentals=0),
    )(block, partner, held, row)


def line(first, second, held, row, bests, rows, span, together):
    outs = [jax.ShapeDtypeStruct((1, rows * len(some)), jnp.float32) for some in together]
    *bests, found = pl.pallas_call(
        functools.partial(line_kernel, rows, span, together, len(bests)),
        out_shape=outs + [jax.ShapeDtypeStruct((1, 2 * rows), jnp.float32)],
        scratch_shapes=[pltpu.VMEM((2 * rows, second.shape[1]), jnp.bfloat16)],
        compiler_params=pltpu.CompilerParams(vmem_limit_bytes=12 << 20),
        cost_estimate=pl.CostEstimate(flops=rows, bytes_accessed=rows, transcendentals=0),
    )(first, second, held, row, *bests)
    return bests, found


OWN = (True, False)
HELD = (False, True)
TWO = (True, True)


def line_rounds(chips):
    if chips == 4:
        return [[(3, 1), (0, 2), (2, 3)], [(3, 0), (0, 1), (1, 2)]]
    rounds = []
    for shift in range(1, chips // 2 + 1):
        senders = chips // 2 if 2 * shift == chips else chips
        rounds.append([(s, (s + shift) % chips) for s in range(senders)])
    return rounds


def solution(mesh):
    groups, members = mesh.shape["dp"], mesh.shape["grid"]
    assert groups == 4 and members % 2 == 0
    chips = members // 2

    def everywhere(target):
        return [
            (p * members + g, a * members + b)
            for p in range(groups)
            for g in range(members)
            for a, b in [target(p, g)]
        ]

    other_core = everywhere(lambda p, g: (p, g ^ 1))
    first = everywhere(lambda p, g: (p ^ (1 + g % 2), g))
    second = everywhere(lambda p, g: (p ^ (2 - g % 2), g))
    homes = [
        everywhere(lambda p, g: (p ^ (1 + g % 2), g ^ 1)),
        everywhere(lambda p, g: (p ^ (2 - g % 2), g ^ 1)),
        everywhere(lambda p, g: (p ^ 3, g ^ 1)),
    ]

    rounds = line_rounds(chips)
    rounds += [[]] * (len(rounds) % 2)
    rounds = [
        [
            (p * members + 2 * s + c, p * members + 2 * t + c)
            for p in range(groups)
            for c in range(2)
            for s, t in rounds[at + c]
        ]
        for at in range(0, len(rounds), 2)
    ]

    def back(pairs):
        return [(target, source) for source, target in pairs]

    def shards(embeddings, cluster, order_key):
        rows = embeddings.shape[0]
        span = 256
        while span < rows * groups * members:
            span *= 2
        halves = (rows // 2, rows // 2 + EXTRA)
        names = (cluster.reshape(1, rows), order_key)
        raw = [lax.ppermute(embeddings, BOTH, pairs) for pairs in rounds]
        charge = [lax.ppermute(array, BOTH, other_core) for array in (embeddings, *names)]
        width = embeddings.shape[1]
        block, *parts = with_units(prepare_kernel, (rows + EXTRA, *halves), width, *charge)
        from_first = [lax.ppermute(part, BOTH, first) for part in parts]
        (own_codes,) = with_units(codes_kernel, (EXTRA,), width, *names)
        later, own_codes = lax.optimization_barrier((block, own_codes))
        from_second = [lax.ppermute(later, BOTH, second)]
        (both,) = with_units(complete_kernel, (rows + EXTRA,), width, block, own_codes)
        (own,) = with_units(own_kernel, (rows + EXTRA,), width, embeddings, own_codes)
        near_other = [lax.ppermute(both, BOTH, pairs) for pairs in rounds]
        from_corner = [lax.ppermute(part, BOTH, second) for part in from_first]
        near = [
            list(with_units(unit_kernel, (rows, rows // 2, rows // 2), width, rows_of))
            for rows_of in raw
        ]
        far = [[lax.ppermute(piece, BOTH, other_core) for piece in blocks[1:]] for blocks in near]

        in_charge, results, kept, sent = [], [], [], []
        best_two, mine = plane(block, own, [[block], from_first], rows, span)
        in_charge.append(mine)
        *from_corner, best_two = lax.optimization_barrier((*from_corner, best_two))
        blocks = [[block], from_first, from_second, from_corner]
        held, row, far_units = gather(blocks, far[0], rows, span)
        best_rest, mine = plane_rest(block, own, held, row, 2 * rows, rows, span)
        in_charge.append(mine)
        bests = [best_two, best_rest]
        far = [far_units] + [jnp.concatenate(pieces, axis=0) for pieces in far[1:]]
        whole, last = [tuple(range(groups))], [(at,) for at in range(groups)]
        for at, second_near in enumerate(near_other):
            second_near, *bests = lax.optimization_barrier((second_near, *bests))
            second_far = lax.ppermute(second_near, BOTH, other_core)
            bests, found = line(near[at][0], second_near, held, row, bests, rows, span, whole)
            kept.append(found)
            bests, found = line(
                far[at],
                second_far,
                held,
                row,
                bests,
                rows,
                span,
                last if at == len(rounds) - 1 else whole,
            )
            sent.append(found)
        sent = lax.ppermute(jnp.concatenate(sent, axis=1), BOTH, other_core)
        kept = jnp.maximum(jnp.concatenate(kept, axis=1), sent)
        kept, *bests = lax.optimization_barrier((kept, *bests))
        for at, pairs in enumerate(rounds):
            found = lax.ppermute(kept[:, 2 * at * rows : 2 * (at + 1) * rows], BOTH, back(pairs))
            me = lax.axis_index(BOTH)
            sender = functools.reduce(jnp.logical_or, [me == source for source, _ in pairs])
            found = jnp.where(sender, found, -1.0)
            results.append(found[:, :rows])
            in_charge.append(found[:, rows:])
        results += [lax.ppermute(bests[at], BOTH, homes[at - 1]) for at in (3, 1, 2)]
        in_charge.append(bests[0])
        home = functools.reduce(jnp.maximum, in_charge)
        results.append(lax.ppermute(home, BOTH, other_core))
        return functools.reduce(jnp.maximum, results).reshape(rows)

    placed = (P(BOTH, None), P(BOTH, None), P(BOTH))
    return jax.shard_map(
        shards, mesh=mesh, in_specs=placed, out_specs=P(BOTH), check_vma=False
    )
```

```python
import functools

import jax
import jax.numpy as jnp
from jax import lax
from jax.experimental import pallas as pl
from jax.experimental.pallas import tpu as pltpu
from jax.sharding import PartitionSpec as P

EPSILON = 1e-06
EXTRA = 16
CODES = 3
LANES = 128
TILE = 256
CHUNK = 64
BOTH = ("dp", "grid")


def up(value, multiple):
    return -(-value // multiple) * multiple


def turned_to_column(row, rows):
    return jnp.broadcast_to(row, (LANES, row.shape[1])).T[:rows]


def codes(block, rows, span, first=0):
    parts = block[block.shape[0] - EXTRA :, : up(rows, LANES)].astype(jnp.float32)
    parts = parts[first : first + CODES]
    return parts[2:3] * (4.0 * span) + parts[0:1] * 256.0 + parts[1:2]


def unit_rows(rows, out):
    values = rows[...].astype(jnp.float32)
    scale = lax.rsqrt(jnp.sum(values * values, axis=1, keepdims=True) + EPSILON)
    out[0 : rows.shape[0], :] = (values * scale).astype(jnp.bfloat16)


def give_parts(block, outs):
    for out, top in zip(outs, (0, block.shape[0] - outs[-1].shape[0])):
        out[...] = block[top : top + out.shape[0], :]


def code_rows(cluster, order_key, width):
    rows = order_key.shape[0]
    keys = order_key[...].reshape(1, rows)
    parts = [keys >> 8, keys & 255, cluster[...] + 1]
    parts = [part.astype(jnp.float32) for part in parts]
    parts = jnp.concatenate(parts + [jnp.zeros((EXTRA - CODES, rows), jnp.float32)], axis=0)
    parts = jnp.concatenate([parts, jnp.zeros((EXTRA, width - rows), jnp.float32)], axis=1)
    return parts.astype(jnp.bfloat16)


def prepare_kernel(embeddings, cluster, order_key, block, *parts_out):
    rows, width = embeddings.shape
    unit_rows(embeddings, block)
    block[rows : rows + EXTRA, :] = code_rows(cluster, order_key, width)
    give_parts(block, parts_out)


def codes_kernel(cluster, order_key, out):
    out[...] = code_rows(cluster, order_key, out.shape[1])


def own_kernel(embeddings, own_codes, block):
    unit_rows(embeddings, block)
    block[embeddings.shape[0] :, :] = own_codes[...]


def complete_kernel(block, other_codes, out):
    rows = block.shape[0] - EXTRA
    out[0:rows, :] = block[0:rows, :]
    named = [part[...].astype(jnp.float32)[0:CODES] for part in (block.at[rows:, :], other_codes)]
    rest = jnp.zeros((EXTRA - 2 * CODES, block.shape[1]), jnp.float32)
    out[rows:, :] = jnp.concatenate(named + [rest], axis=0).astype(jnp.bfloat16)


def unit_kernel(rows_of, block, *parts_out):
    unit_rows(rows_of, block)
    give_parts(block, parts_out)


def with_units(kernel, heights, width, *inputs):
    return pl.pallas_call(
        kernel,
        out_shape=[jax.ShapeDtypeStruct((height, width), jnp.bfloat16) for height in heights],
        compiler_params=pltpu.CompilerParams(vmem_limit_bytes=8 << 20),
        cost_estimate=pl.CostEstimate(flops=width, bytes_accessed=width, transcendentals=0),
    )(*inputs)


def row_from_partial(partial, rows):
    padded = up(rows, LANES)
    if padded != rows:
        partial = jnp.concatenate(
            [partial, jnp.zeros((padded - rows, LANES), partial.dtype)], axis=0
        )
    return jnp.max(partial.T, axis=0, keepdims=True)[:, :rows]


def meet(units, parts, rows, span, held, held_codes):
    columns = [turned_to_column(row, rows) for row, _ in parts]
    starts = [(block, top) for block in range(len(parts)) for top in range(0, rows, CHUNK)]
    partial = {start: jnp.full((CHUNK, LANES), -1.0, jnp.float32) for start in starts}
    best_held = []
    for at in range(0, held.shape[0], TILE):
        tile = min(TILE, held.shape[0] - at)
        sims = lax.dot_general(
            units[...],
            held[at : at + tile, :],
            (((1,), (1,)), ((), ())),
            preferred_element_type=jnp.float32,
        )
        best = [jnp.full((CHUNK, LANES), -1.0, jnp.float32) for _ in range(0, tile, LANES)]
        for block, top in starts:
            to_block, to_held = parts[block][1]
            mine = columns[block][top : top + CHUNK]
            line = block * rows + top
            for lane in range(0, tile, LANES):
                part = sims[line : line + CHUNK, lane : lane + LANES]
                gap = mine - held_codes[:, at + lane : at + lane + LANES]
                if to_block and to_held:
                    part = jnp.where(jnp.abs(gap) < span, part, -1.0)
                    later = gap > 0.0
                    ours, theirs = jnp.where(later, part, -1.0), jnp.where(later, -1.0, part)
                elif to_block:
                    ours = jnp.where((gap > 0.0) & (gap < span), part, -1.0)
                else:
                    theirs = jnp.where((gap < 0.0) & (gap > -span), part, -1.0)
                if to_block:
                    partial[block, top] = jnp.maximum(partial[block, top], ours)
                if to_held:
                    best[lane // LANES] = jnp.maximum(best[lane // LANES], theirs)
        best_held += [jnp.max(some, axis=0, keepdims=True) for some in best]
    found = [
        row_from_partial(
            jnp.concatenate([partial[block, top] for top in range(0, rows, CHUNK)], axis=0), rows
        )
        for block, (_, (to_block, _)) in enumerate(parts)
        if to_block
    ]
    return found, jnp.concatenate(best_held, axis=1)


def assemble(whole, top, rows, pieces, extra):
    first, *others = pieces
    height = min(first.shape[0], rows)
    whole[top : top + height, :] = first[0:height, :]
    for last in others:
        height = last.shape[0] - extra
        whole[top + rows - height : top + rows, :] = last[0:height, :]


def hold(holds, held, rows, span):
    for at, block in enumerate(holds):
        assemble(held, at * rows, rows, block, EXTRA)
    row = [codes(block[-1], rows, span)[:, :rows] for block in holds]
    rest = held.shape[0] - len(holds) * rows
    if rest:
        held[len(holds) * rows :, :] = jnp.zeros((rest, held.shape[1]), held.dtype)
        row.append(jnp.zeros((1, rest), jnp.float32))
    return jnp.concatenate(row, axis=1)


def gather_kernel(rows, span, lengths, *refs):
    *pieces, held, row, joined = refs
    *holds, far = regrouped(pieces, lengths)
    row[...] = hold(holds, held, rows, span)
    assemble(joined, 0, rows, far, 0)


def gather(holds, far, rows, span):
    width = far[0].shape[1]
    total = len(holds) * rows
    parts = [*holds, far]
    return pl.pallas_call(
        functools.partial(gather_kernel, rows, span, [len(part) for part in parts]),
        out_shape=[
            jax.ShapeDtypeStruct((total, width), jnp.bfloat16),
            jax.ShapeDtypeStruct((1, total), jnp.float32),
            jax.ShapeDtypeStruct((rows, width), jnp.bfloat16),
        ],
        compiler_params=pltpu.CompilerParams(vmem_limit_bytes=8 << 20),
        cost_estimate=pl.CostEstimate(
            flops=rows * total * width // 4, bytes_accessed=rows, transcendentals=0
        ),
    )(*[piece for part in parts for piece in part])


def regrouped(flat, lengths):
    flat = iter(flat)
    return [[next(flat) for _ in range(length)] for length in lengths]


def pair(units, first, second, rows):
    units[0:rows, :] = first[0:rows, :]
    units[rows:, :] = second[0:rows, :]


def plane_kernel(rows, span, lengths, block, partner, *refs):
    *pieces, best, mine, held, units = refs
    row = hold(regrouped(pieces, lengths), held, rows, span)
    pair(units, block, partner, rows)
    parts = [(codes(block, rows, span), OWN), (codes(partner, rows, span), HELD)]
    (mine[...],), theirs = meet(units, parts, rows, span, held, row)
    best[...] = theirs[:, : best.shape[1]]


def rest_kernel(rows, span, block, partner, held, row, best, mine, units):
    count = best.shape[1]
    start = held.shape[0] - up(count, LANES)
    held, row = held.at[start:, :], row[:, start:]
    pair(units, block, partner, rows)
    parts = [(codes(block, rows, span), OWN), (codes(partner, rows, span), HELD)]
    (mine[...],), theirs = meet(units, parts, rows, span, held, row)
    best[...] = theirs[:, row.shape[1] - count :]


def line_kernel(rows, span, together, count, first, second, held, row, *refs):
    bests, outs, (found, units) = refs[:count], refs[count:-2], refs[-2:]
    parts = [(codes(second, rows, span, first=place), TWO) for place in (CODES, 0)]

    def give(best):
        for out, places in zip(outs, together):
            out[...] = jnp.concatenate(
                [best[:, place * rows : (place + 1) * rows] for place in places], axis=1
            )

    arrived = jnp.max(parts[0][0]) > 0.0

    @pl.when(arrived)
    def _():
        pair(units, first, second, rows)
        mine, theirs = meet(units, parts, rows, span, held, row[...])
        found[...] = jnp.concatenate(mine, axis=1)
        give(jnp.maximum(jnp.concatenate([best[...] for best in bests], axis=1), theirs))

    @pl.when(jnp.logical_not(arrived))
    def _():
        found[...] = jnp.full(found.shape, -1.0, jnp.float32)
        give(jnp.concatenate([best[...] for best in bests], axis=1))


def plane(block, partner, holds, rows, span):
    width = block.shape[1]
    total = len(holds) * rows
    return pl.pallas_call(
        functools.partial(plane_kernel, rows, span, [len(part) for part in holds]),
        out_shape=[
            jax.ShapeDtypeStruct((1, total), jnp.float32),
            jax.ShapeDtypeStruct((1, rows), jnp.float32),
        ],
        scratch_shapes=[
            pltpu.VMEM((up(total, LANES), width), jnp.bfloat16),
            pltpu.VMEM((2 * rows, width), jnp.bfloat16),
        ],
        compiler_params=pltpu.CompilerParams(vmem_limit_bytes=12 << 20),
        cost_estimate=pl.CostEstimate(flops=rows, bytes_accessed=rows, transcendentals=0),
    )(block, partner, *[piece for part in holds for piece in part])


def plane_rest(block, partner, held, row, count, rows, span):
    return pl.pallas_call(
        functools.partial(rest_kernel, rows, span),
        out_shape=[
            jax.ShapeDtypeStruct((1, count), jnp.float32),
            jax.ShapeDtypeStruct((1, rows), jnp.float32),
        ],
        scratch_shapes=[pltpu.VMEM((2 * rows, block.shape[1]), jnp.bfloat16)],
        compiler_params=pltpu.CompilerParams(vmem_limit_bytes=12 << 20),
        cost_estimate=pl.CostEstimate(flops=rows, bytes_accessed=rows, transcendentals=0),
    )(block, partner, held, row)


def line(first, second, held, row, bests, rows, span, together):
    outs = [jax.ShapeDtypeStruct((1, rows * len(some)), jnp.float32) for some in together]
    *bests, found = pl.pallas_call(
        functools.partial(line_kernel, rows, span, together, len(bests)),
        out_shape=outs + [jax.ShapeDtypeStruct((1, 2 * rows), jnp.float32)],
        scratch_shapes=[pltpu.VMEM((2 * rows, second.shape[1]), jnp.bfloat16)],
        compiler_params=pltpu.CompilerParams(vmem_limit_bytes=12 << 20),
        cost_estimate=pl.CostEstimate(flops=rows, bytes_accessed=rows, transcendentals=0),
    )(first, second, held, row, *bests)
    return bests, found


OWN = (True, False)
HELD = (False, True)
TWO = (True, True)


def line_rounds(chips):
    if chips == 4:
        return [[(3, 1), (0, 2), (2, 3)], [(3, 0), (0, 1), (1, 2)]]
    rounds = []
    for shift in range(1, chips // 2 + 1):
        senders = chips // 2 if 2 * shift == chips else chips
        rounds.append([(s, (s + shift) % chips) for s in range(senders)])
    return rounds


def solution(mesh):
    groups, members = mesh.shape["dp"], mesh.shape["grid"]
    assert groups == 4 and members % 2 == 0
    chips = members // 2

    def everywhere(target):
        return [
            (p * members + g, a * members + b)
            for p in range(groups)
            for g in range(members)
            for a, b in [target(p, g)]
        ]

    other_core = everywhere(lambda p, g: (p, g ^ 1))
    first = everywhere(lambda p, g: (p ^ (1 + g % 2), g))
    second = everywhere(lambda p, g: (p ^ (2 - g % 2), g))
    homes = [
        everywhere(lambda p, g: (p ^ (1 + g % 2), g ^ 1)),
        everywhere(lambda p, g: (p ^ (2 - g % 2), g ^ 1)),
        everywhere(lambda p, g: (p ^ 3, g ^ 1)),
    ]

    rounds = line_rounds(chips)
    rounds += [[]] * (len(rounds) % 2)
    rounds = [
        [
            (p * members + 2 * s + c, p * members + 2 * t + c)
            for p in range(groups)
            for c in range(2)
            for s, t in rounds[at + c]
        ]
        for at in range(0, len(rounds), 2)
    ]

    def back(pairs):
        return [(target, source) for source, target in pairs]

    def shards(embeddings, cluster, order_key):
        rows = embeddings.shape[0]
        span = 256
        while span < rows * groups * members:
            span *= 2
        halves = (rows // 2, rows // 2 + EXTRA)
        names = (cluster.reshape(1, rows), order_key)
        raw = [lax.ppermute(embeddings, BOTH, pairs) for pairs in rounds]
        charge = [lax.ppermute(array, BOTH, other_core) for array in (embeddings, *names)]
        width = embeddings.shape[1]
        block, *parts = with_units(prepare_kernel, (rows + EXTRA, *halves), width, *charge)
        from_first = [lax.ppermute(part, BOTH, first) for part in parts]
        (own_codes,) = with_units(codes_kernel, (EXTRA,), width, *names)
        later, own_codes = lax.optimization_barrier((block, own_codes))
        from_second = [lax.ppermute(later, BOTH, second)]
        (both,) = with_units(complete_kernel, (rows + EXTRA,), width, block, own_codes)
        (own,) = with_units(own_kernel, (rows + EXTRA,), width, embeddings, own_codes)
        near_other = [lax.ppermute(both, BOTH, pairs) for pairs in rounds]
        from_corner = [lax.ppermute(part, BOTH, second) for part in from_first]
        near = [
            list(with_units(unit_kernel, (rows, rows // 2, rows // 2), width, rows_of))
            for rows_of in raw
        ]
        far = [[lax.ppermute(piece, BOTH, other_core) for piece in blocks[1:]] for blocks in near]

        in_charge, results, kept, sent = [], [], [], []
        best_two, mine = plane(block, own, [[block], from_first], rows, span)
        in_charge.append(mine)
        *from_corner, best_two = lax.optimization_barrier((*from_corner, best_two))
        blocks = [[block], from_first, from_second, from_corner]
        held, row, far_units = gather(blocks, far[0], rows, span)
        best_rest, mine = plane_rest(block, own, held, row, 2 * rows, rows, span)
        in_charge.append(mine)
        bests = [best_two, best_rest]
        far = [far_units] + [jnp.concatenate(pieces, axis=0) for pieces in far[1:]]
        whole, last = [tuple(range(groups))], [(at,) for at in range(groups)]
        for at, second_near in enumerate(near_other):
            second_near, *bests = lax.optimization_barrier((second_near, *bests))
            second_far = lax.ppermute(second_near, BOTH, other_core)
            bests, found = line(near[at][0], second_near, held, row, bests, rows, span, whole)
            kept.append(found)
            bests, found = line(
                far[at],
                second_far,
                held,
                row,
                bests,
                rows,
                span,
                last if at == len(rounds) - 1 else whole,
            )
            sent.append(found)
        sent = lax.ppermute(jnp.concatenate(sent, axis=1), BOTH, other_core)
        kept = jnp.maximum(jnp.concatenate(kept, axis=1), sent)
        kept, *bests = lax.optimization_barrier((kept, *bests))
        for at, pairs in enumerate(rounds):
            found = lax.ppermute(kept[:, 2 * at * rows : 2 * (at + 1) * rows], BOTH, back(pairs))
            me = lax.axis_index(BOTH)
            sender = functools.reduce(jnp.logical_or, [me == source for source, _ in pairs])
            found = jnp.where(sender, found, -1.0)
            results.append(found[:, :rows])
            in_charge.append(found[:, rows:])
        results += [
            lax.ppermute(best, BOTH, pairs) for best, pairs in zip(bests[1:], homes)
        ]
        in_charge.append(bests[0])
        home = functools.reduce(jnp.maximum, in_charge)
        results.append(lax.ppermute(home, BOTH, other_core))
        return functools.reduce(jnp.maximum, results).reshape(rows)

    placed = (P(BOTH, None), P(BOTH, None), P(BOTH))
    return jax.shard_map(
        shards, mesh=mesh, in_specs=placed, out_specs=P(BOTH), check_vma=False
    )
```

```python
import functools

import jax
import jax.numpy as jnp
from jax import lax
from jax.experimental import pallas as pl
from jax.experimental.pallas import tpu as pltpu
from jax.sharding import PartitionSpec as P

EPSILON = 1e-06
EXTRA = 16
CODES = 3
LANES = 128
TILE = 256
CHUNK = 32
BOTH = ("dp", "grid")


def up(value, multiple):
    return -(-value // multiple) * multiple


def turned_to_column(row, rows):
    return jnp.broadcast_to(row, (LANES, row.shape[1])).T[:rows]


def codes(block, rows, span, first=0):
    parts = block[block.shape[0] - EXTRA :, : up(rows, LANES)].astype(jnp.float32)
    parts = parts[first : first + CODES]
    return parts[2:3] * (4.0 * span) + parts[0:1] * 256.0 + parts[1:2]


def unit_rows(rows, out):
    values = rows[...].astype(jnp.float32)
    scale = lax.rsqrt(jnp.sum(values * values, axis=1, keepdims=True) + EPSILON)
    out[0 : rows.shape[0], :] = (values * scale).astype(jnp.bfloat16)


def give_parts(block, outs):
    for out, top in zip(outs, (0, block.shape[0] - outs[-1].shape[0])):
        out[...] = block[top : top + out.shape[0], :]


def code_rows(cluster, order_key, width):
    rows = order_key.shape[0]
    keys = order_key[...].reshape(1, rows)
    parts = [keys >> 8, keys & 255, cluster[...] + 1]
    parts = [part.astype(jnp.float32) for part in parts]
    parts = jnp.concatenate(parts + [jnp.zeros((EXTRA - CODES, rows), jnp.float32)], axis=0)
    parts = jnp.concatenate([parts, jnp.zeros((EXTRA, width - rows), jnp.float32)], axis=1)
    return parts.astype(jnp.bfloat16)


def prepare_kernel(embeddings, cluster, order_key, block, *parts_out):
    rows, width = embeddings.shape
    unit_rows(embeddings, block)
    block[rows : rows + EXTRA, :] = code_rows(cluster, order_key, width)
    give_parts(block, parts_out)


def codes_kernel(cluster, order_key, out):
    out[...] = code_rows(cluster, order_key, out.shape[1])


def own_kernel(embeddings, own_codes, block):
    unit_rows(embeddings, block)
    block[embeddings.shape[0] :, :] = own_codes[...]


def complete_kernel(block, other_codes, out):
    rows = block.shape[0] - EXTRA
    out[0:rows, :] = block[0:rows, :]
    named = [part[...].astype(jnp.float32)[0:CODES] for part in (block.at[rows:, :], other_codes)]
    rest = jnp.zeros((EXTRA - 2 * CODES, block.shape[1]), jnp.float32)
    out[rows:, :] = jnp.concatenate(named + [rest], axis=0).astype(jnp.bfloat16)


def unit_kernel(rows_of, block, *parts_out):
    unit_rows(rows_of, block)
    give_parts(block, parts_out)


def with_units(kernel, heights, width, *inputs):
    return pl.pallas_call(
        kernel,
        out_shape=[jax.ShapeDtypeStruct((height, width), jnp.bfloat16) for height in heights],
        compiler_params=pltpu.CompilerParams(vmem_limit_bytes=8 << 20),
        cost_estimate=pl.CostEstimate(flops=width, bytes_accessed=width, transcendentals=0),
    )(*inputs)


def row_from_partial(partial, rows):
    padded = up(rows, LANES)
    if padded != rows:
        partial = jnp.concatenate(
            [partial, jnp.zeros((padded - rows, LANES), partial.dtype)], axis=0
        )
    return jnp.max(partial.T, axis=0, keepdims=True)[:, :rows]


def meet(units, parts, rows, span, held, held_codes):
    low = -(2**31)
    columns = [turned_to_column(row, rows).astype(jnp.int32) for row, _ in parts]
    after = [column + (2**31 - 1) for column in columns]
    before = [column + (low + 1) for column in columns]
    held_codes = held_codes.astype(jnp.int32)
    limit = low + span - 1
    starts = [(block, top) for block in range(len(parts)) for top in range(0, rows, CHUNK)]
    partial = {start: jnp.full((CHUNK, LANES), -1.0, jnp.float32) for start in starts}
    best_held = []
    for at in range(0, held.shape[0], TILE):
        tile = min(TILE, held.shape[0] - at)
        sims = [
            lax.dot_general(
                some[0:rows, :],
                held[at : at + tile, :],
                (((1,), (1,)), ((), ())),
                preferred_element_type=jnp.float32,
            )
            for some in units
        ]
        best = [jnp.full((CHUNK, LANES), -1.0, jnp.float32) for _ in range(0, tile, LANES)]
        for block, top in starts:
            to_block, to_held = parts[block][1]
            for lane in range(0, tile, LANES):
                part = sims[block][top : top + CHUNK, lane : lane + LANES]
                theirs = held_codes[:, at + lane : at + lane + LANES]
                if to_block:
                    earlier = after[block][top : top + CHUNK] - theirs < limit
                    ours = jnp.where(earlier, part, -1.0)
                    partial[block, top] = jnp.maximum(partial[block, top], ours)
                if to_held:
                    earlier = theirs - before[block][top : top + CHUNK] < limit
                    other = jnp.where(earlier, part, -1.0)
                    best[lane // LANES] = jnp.maximum(best[lane // LANES], other)
        best_held += [jnp.max(some, axis=0, keepdims=True) for some in best]
    found = [
        row_from_partial(
            jnp.concatenate([partial[block, top] for top in range(0, rows, CHUNK)], axis=0), rows
        )
        for block, (_, (to_block, _)) in enumerate(parts)
        if to_block
    ]
    return found, jnp.concatenate(best_held, axis=1)


def assemble(whole, top, rows, pieces, extra):
    first, *others = pieces
    height = min(first.shape[0], rows)
    whole[top : top + height, :] = first[0:height, :]
    for last in others:
        height = last.shape[0] - extra
        whole[top + rows - height : top + rows, :] = last[0:height, :]


def hold(holds, held, rows, span):
    for at, block in enumerate(holds):
        assemble(held, at * rows, rows, block, EXTRA)
    row = [codes(block[-1], rows, span)[:, :rows] for block in holds]
    rest = held.shape[0] - len(holds) * rows
    if rest:
        held[len(holds) * rows :, :] = jnp.zeros((rest, held.shape[1]), held.dtype)
        row.append(jnp.zeros((1, rest), jnp.float32))
    return jnp.concatenate(row, axis=1)


def gather_kernel(rows, span, lengths, *refs):
    *pieces, held, row, joined = refs
    *holds, far = regrouped(pieces, lengths)
    row[...] = hold(holds, held, rows, span)
    assemble(joined, 0, rows, far, 0)


def gather(holds, far, rows, span):
    width = far[0].shape[1]
    total = len(holds) * rows
    parts = [*holds, far]
    return pl.pallas_call(
        functools.partial(gather_kernel, rows, span, [len(part) for part in parts]),
        out_shape=[
            jax.ShapeDtypeStruct((total, width), jnp.bfloat16),
            jax.ShapeDtypeStruct((1, total), jnp.float32),
            jax.ShapeDtypeStruct((rows, width), jnp.bfloat16),
        ],
        compiler_params=pltpu.CompilerParams(vmem_limit_bytes=8 << 20),
        cost_estimate=pl.CostEstimate(
            flops=rows * total * width // 4, bytes_accessed=rows, transcendentals=0
        ),
    )(*[piece for part in parts for piece in part])


def regrouped(flat, lengths):
    flat = iter(flat)
    return [[next(flat) for _ in range(length)] for length in lengths]


def plane_kernel(rows, span, lengths, block, partner, *refs):
    *pieces, best, mine, held = refs
    row = hold(regrouped(pieces, lengths), held, rows, span)
    units = (block, partner)
    parts = [(codes(block, rows, span), OWN), (codes(partner, rows, span), HELD)]
    (mine[...],), theirs = meet(units, parts, rows, span, held, row)
    best[...] = theirs[:, : best.shape[1]]


def rest_kernel(rows, span, block, partner, held, row, best, mine):
    count = best.shape[1]
    start = held.shape[0] - up(count, LANES)
    held, row = held.at[start:, :], row[:, start:]
    units = (block, partner)
    parts = [(codes(block, rows, span), OWN), (codes(partner, rows, span), HELD)]
    (mine[...],), theirs = meet(units, parts, rows, span, held, row)
    best[...] = theirs[:, row.shape[1] - count :]


def line_kernel(rows, span, together, count, first, second, held, row, *refs):
    bests, outs, found = refs[:count], refs[count:-1], refs[-1]
    parts = [(codes(second, rows, span, first=place), TWO) for place in (CODES, 0)]

    def give(best):
        for out, places in zip(outs, together):
            out[...] = jnp.concatenate(
                [best[:, place * rows : (place + 1) * rows] for place in places], axis=1
            )

    arrived = jnp.max(parts[0][0]) > 0.0

    @pl.when(arrived)
    def _():
        units = (first, second)
        mine, theirs = meet(units, parts, rows, span, held, row[...])
        found[...] = jnp.concatenate(mine, axis=1)
        give(jnp.maximum(jnp.concatenate([best[...] for best in bests], axis=1), theirs))

    @pl.when(jnp.logical_not(arrived))
    def _():
        found[...] = jnp.full(found.shape, -1.0, jnp.float32)
        give(jnp.concatenate([best[...] for best in bests], axis=1))


def plane(block, partner, holds, rows, span):
    width = block.shape[1]
    total = len(holds) * rows
    return pl.pallas_call(
        functools.partial(plane_kernel, rows, span, [len(part) for part in holds]),
        out_shape=[
            jax.ShapeDtypeStruct((1, total), jnp.float32),
            jax.ShapeDtypeStruct((1, rows), jnp.float32),
        ],
        scratch_shapes=[
            pltpu.VMEM((up(total, LANES), width), jnp.bfloat16),
        ],
        compiler_params=pltpu.CompilerParams(vmem_limit_bytes=12 << 20),
        cost_estimate=pl.CostEstimate(flops=rows, bytes_accessed=rows, transcendentals=0),
    )(block, partner, *[piece for part in holds for piece in part])


def plane_rest(block, partner, held, row, count, rows, span):
    return pl.pallas_call(
        functools.partial(rest_kernel, rows, span),
        out_shape=[
            jax.ShapeDtypeStruct((1, count), jnp.float32),
            jax.ShapeDtypeStruct((1, rows), jnp.float32),
        ],
        compiler_params=pltpu.CompilerParams(vmem_limit_bytes=12 << 20),
        cost_estimate=pl.CostEstimate(flops=rows, bytes_accessed=rows, transcendentals=0),
    )(block, partner, held, row)


def line(first, second, held, row, bests, rows, span, together):
    outs = [jax.ShapeDtypeStruct((1, rows * len(some)), jnp.float32) for some in together]
    *bests, found = pl.pallas_call(
        functools.partial(line_kernel, rows, span, together, len(bests)),
        out_shape=outs + [jax.ShapeDtypeStruct((1, 2 * rows), jnp.float32)],
        compiler_params=pltpu.CompilerParams(vmem_limit_bytes=12 << 20),
        cost_estimate=pl.CostEstimate(flops=rows, bytes_accessed=rows, transcendentals=0),
    )(first, second, held, row, *bests)
    return bests, found


OWN = (True, False)
HELD = (False, True)
TWO = (True, True)


def line_rounds(chips):
    if chips == 4:
        return [[(3, 1), (0, 2), (2, 3)], [(3, 0), (0, 1), (1, 2)]]
    rounds = []
    for shift in range(1, chips // 2 + 1):
        senders = chips // 2 if 2 * shift == chips else chips
        rounds.append([(s, (s + shift) % chips) for s in range(senders)])
    return rounds


def solution(mesh):
    groups, members = mesh.shape["dp"], mesh.shape["grid"]
    assert groups == 4 and members % 2 == 0
    chips = members // 2

    def everywhere(target):
        return [
            (p * members + g, a * members + b)
            for p in range(groups)
            for g in range(members)
            for a, b in [target(p, g)]
        ]

    other_core = everywhere(lambda p, g: (p, g ^ 1))
    first = everywhere(lambda p, g: (p ^ (1 + g % 2), g))
    second = everywhere(lambda p, g: (p ^ (2 - g % 2), g))
    homes = [
        everywhere(lambda p, g: (p ^ (1 + g % 2), g ^ 1)),
        everywhere(lambda p, g: (p ^ (2 - g % 2), g ^ 1)),
        everywhere(lambda p, g: (p ^ 3, g ^ 1)),
    ]

    rounds = line_rounds(chips)
    rounds += [[]] * (len(rounds) % 2)
    rounds = [
        [
            (p * members + 2 * s + c, p * members + 2 * t + c)
            for p in range(groups)
            for c in range(2)
            for s, t in rounds[at + c]
        ]
        for at in range(0, len(rounds), 2)
    ]

    def back(pairs):
        return [(target, source) for source, target in pairs]

    def shards(embeddings, cluster, order_key):
        rows = embeddings.shape[0]
        span = 256
        while span < rows * groups * members:
            span *= 2
        halves = (rows // 2, rows // 2 + EXTRA)
        names = (cluster.reshape(1, rows), order_key)
        raw = [lax.ppermute(embeddings, BOTH, pairs) for pairs in rounds]
        charge = [lax.ppermute(array, BOTH, other_core) for array in (embeddings, *names)]
        width = embeddings.shape[1]
        block, *parts = with_units(prepare_kernel, (rows + EXTRA, *halves), width, *charge)
        from_first = [lax.ppermute(part, BOTH, first) for part in parts]
        (own_codes,) = with_units(codes_kernel, (EXTRA,), width, *names)
        later, own_codes = lax.optimization_barrier((block, own_codes))
        from_second = [lax.ppermute(later, BOTH, second)]
        (both,) = with_units(complete_kernel, (rows + EXTRA,), width, block, own_codes)
        (own,) = with_units(own_kernel, (rows + EXTRA,), width, embeddings, own_codes)
        near_other = [lax.ppermute(both, BOTH, pairs) for pairs in rounds]
        from_corner = [lax.ppermute(part, BOTH, second) for part in from_first]
        near = [
            list(with_units(unit_kernel, (rows, rows // 2, rows // 2), width, rows_of))
            for rows_of in raw
        ]
        far = [[lax.ppermute(piece, BOTH, other_core) for piece in blocks[1:]] for blocks in near]

        in_charge, results, kept, sent = [], [], [], []
        best_two, mine = plane(block, own, [[block], from_first], rows, span)
        in_charge.append(mine)
        *from_corner, best_two = lax.optimization_barrier((*from_corner, best_two))
        blocks = [[block], from_first, from_second, from_corner]
        held, row, far_units = gather(blocks, far[0], rows, span)
        best_rest, mine = plane_rest(block, own, held, row, 2 * rows, rows, span)
        in_charge.append(mine)
        bests = [best_two, best_rest]
        far = [far_units] + [jnp.concatenate(pieces, axis=0) for pieces in far[1:]]
        whole, last = [tuple(range(groups))], [(at,) for at in range(groups)]
        for at, second_near in enumerate(near_other):
            second_near, *bests = lax.optimization_barrier((second_near, *bests))
            second_far = lax.ppermute(second_near, BOTH, other_core)
            bests, found = line(near[at][0], second_near, held, row, bests, rows, span, whole)
            kept.append(found)
            bests, found = line(
                far[at],
                second_far,
                held,
                row,
                bests,
                rows,
                span,
                last if at == len(rounds) - 1 else whole,
            )
            sent.append(found)
        sent = lax.ppermute(jnp.concatenate(sent, axis=1), BOTH, other_core)
        kept = jnp.maximum(jnp.concatenate(kept, axis=1), sent)
        kept, *bests = lax.optimization_barrier((kept, *bests))
        for at, pairs in enumerate(rounds):
            found = lax.ppermute(kept[:, 2 * at * rows : 2 * (at + 1) * rows], BOTH, back(pairs))
            me = lax.axis_index(BOTH)
            sender = functools.reduce(jnp.logical_or, [me == source for source, _ in pairs])
            found = jnp.where(sender, found, -1.0)
            results.append(found[:, :rows])
            in_charge.append(found[:, rows:])
        results += [
            lax.ppermute(best, BOTH, pairs) for best, pairs in zip(bests[1:], homes)
        ]
        in_charge.append(bests[0])
        home = functools.reduce(jnp.maximum, in_charge)
        results.append(lax.ppermute(home, BOTH, other_core))
        return functools.reduce(jnp.maximum, results).reshape(rows)

    placed = (P(BOTH, None), P(BOTH, None), P(BOTH))
    return jax.shard_map(
        shards, mesh=mesh, in_specs=placed, out_specs=P(BOTH), check_vma=False
    )
```

```python
import functools

import jax
import jax.numpy as jnp
from jax import lax
from jax.experimental import pallas as pl
from jax.experimental.pallas import tpu as pltpu
from jax.sharding import PartitionSpec as P

EPSILON = 1e-06
EXTRA = 16
CODES = 3
LANES = 128
TILE = 256
CHUNK = 32
BOTH = ("dp", "grid")


def up(value, multiple):
    return -(-value // multiple) * multiple


def turned_to_column(row, rows):
    return jnp.broadcast_to(row, (LANES, row.shape[1])).T[:rows]


def codes(block, rows, span, first=0):
    parts = block[block.shape[0] - EXTRA :, : up(rows, LANES)].astype(jnp.float32)
    parts = parts[first : first + CODES]
    return parts[2:3] * (4.0 * span) + parts[0:1] * 256.0 + parts[1:2]


def unit_rows(rows, out):
    values = rows[...].astype(jnp.float32)
    scale = lax.rsqrt(jnp.sum(values * values, axis=1, keepdims=True) + EPSILON)
    out[0 : rows.shape[0], :] = (values * scale).astype(jnp.bfloat16)


def give_parts(block, outs):
    for out, top in zip(outs, (0, block.shape[0] - outs[-1].shape[0])):
        out[...] = block[top : top + out.shape[0], :]


def code_rows(cluster, order_key, width):
    rows = order_key.shape[0]
    keys = order_key[...].reshape(1, rows)
    parts = [keys >> 8, keys & 255, cluster[...] + 1]
    parts = [part.astype(jnp.float32) for part in parts]
    parts = jnp.concatenate(parts + [jnp.zeros((EXTRA - CODES, rows), jnp.float32)], axis=0)
    parts = jnp.concatenate([parts, jnp.zeros((EXTRA, width - rows), jnp.float32)], axis=1)
    return parts.astype(jnp.bfloat16)


def prepare_kernel(embeddings, cluster, order_key, block, *parts_out):
    rows, width = embeddings.shape
    unit_rows(embeddings, block)
    block[rows : rows + EXTRA, :] = code_rows(cluster, order_key, width)
    give_parts(block, parts_out)


def codes_kernel(cluster, order_key, out):
    out[...] = code_rows(cluster, order_key, out.shape[1])


def own_kernel(embeddings, own_codes, block):
    unit_rows(embeddings, block)
    block[embeddings.shape[0] :, :] = own_codes[...]


def complete_kernel(block, other_codes, out):
    rows = block.shape[0] - EXTRA
    out[0:rows, :] = block[0:rows, :]
    named = [part[...].astype(jnp.float32)[0:CODES] for part in (block.at[rows:, :], other_codes)]
    rest = jnp.zeros((EXTRA - 2 * CODES, block.shape[1]), jnp.float32)
    out[rows:, :] = jnp.concatenate(named + [rest], axis=0).astype(jnp.bfloat16)


def unit_kernel(rows_of, block, *parts_out):
    unit_rows(rows_of, block)
    give_parts(block, parts_out)


def with_units(kernel, heights, width, *inputs):
    return pl.pallas_call(
        kernel,
        out_shape=[jax.ShapeDtypeStruct((height, width), jnp.bfloat16) for height in heights],
        compiler_params=pltpu.CompilerParams(vmem_limit_bytes=8 << 20),
        cost_estimate=pl.CostEstimate(flops=width, bytes_accessed=width, transcendentals=0),
    )(*inputs)


def row_from_partial(partial, rows):
    padded = up(rows, LANES)
    if padded != rows:
        partial = jnp.concatenate(
            [partial, jnp.zeros((padded - rows, LANES), partial.dtype)], axis=0
        )
    return jnp.max(partial.T, axis=0, keepdims=True)[:, :rows]


def meet(units, parts, rows, span, held, held_codes):
    columns = [turned_to_column(row, rows) for row, _ in parts]
    starts = [(block, top) for block in range(len(parts)) for top in range(0, rows, CHUNK)]
    partial = {start: jnp.full((CHUNK, LANES), -1.0, jnp.float32) for start in starts}
    best_held = []
    for at in range(0, held.shape[0], TILE):
        tile = min(TILE, held.shape[0] - at)
        sims = [
            lax.dot_general(
                some[0:rows, :],
                held[at : at + tile, :],
                (((1,), (1,)), ((), ())),
                preferred_element_type=jnp.float32,
            )
            for some in units
        ]
        best = [jnp.full((CHUNK, LANES), -1.0, jnp.float32) for _ in range(0, tile, LANES)]
        for block, top in starts:
            to_block, to_held = parts[block][1]
            mine = columns[block][top : top + CHUNK]
            for lane in range(0, tile, LANES):
                part = sims[block][top : top + CHUNK, lane : lane + LANES]
                gap = mine - held_codes[:, at + lane : at + lane + LANES]
                if to_block and to_held:
                    part = jnp.where(jnp.abs(gap) < span, part, -1.0)
                    later = gap > 0.0
                    ours, theirs = jnp.where(later, part, -1.0), jnp.where(later, -1.0, part)
                elif to_block:
                    ours = jnp.where((gap > 0.0) & (gap < span), part, -1.0)
                else:
                    theirs = jnp.where((gap < 0.0) & (gap > -span), part, -1.0)
                if to_block:
                    partial[block, top] = jnp.maximum(partial[block, top], ours)
                if to_held:
                    best[lane // LANES] = jnp.maximum(best[lane // LANES], theirs)
        best_held += [jnp.max(some, axis=0, keepdims=True) for some in best]
    found = [
        row_from_partial(
            jnp.concatenate([partial[block, top] for top in range(0, rows, CHUNK)], axis=0), rows
        )
        for block, (_, (to_block, _)) in enumerate(parts)
        if to_block
    ]
    return found, jnp.concatenate(best_held, axis=1)


def assemble(whole, top, rows, pieces, extra):
    first, *others = pieces
    height = min(first.shape[0], rows)
    whole[top : top + height, :] = first[0:height, :]
    for last in others:
        height = last.shape[0] - extra
        whole[top + rows - height : top + rows, :] = last[0:height, :]


def hold(holds, held, rows, span):
    for at, block in enumerate(holds):
        assemble(held, at * rows, rows, block, EXTRA)
    row = [codes(block[-1], rows, span)[:, :rows] for block in holds]
    rest = held.shape[0] - len(holds) * rows
    if rest:
        held[len(holds) * rows :, :] = jnp.zeros((rest, held.shape[1]), held.dtype)
        row.append(jnp.zeros((1, rest), jnp.float32))
    return jnp.concatenate(row, axis=1)


def gather_kernel(rows, span, lengths, *refs):
    *pieces, held, row, joined = refs
    *holds, far = regrouped(pieces, lengths)
    row[...] = hold(holds, held, rows, span)
    assemble(joined, 0, rows, far, 0)


def gather(holds, far, rows, span):
    width = far[0].shape[1]
    total = len(holds) * rows
    parts = [*holds, far]
    return pl.pallas_call(
        functools.partial(gather_kernel, rows, span, [len(part) for part in parts]),
        out_shape=[
            jax.ShapeDtypeStruct((total, width), jnp.bfloat16),
            jax.ShapeDtypeStruct((1, total), jnp.float32),
            jax.ShapeDtypeStruct((rows, width), jnp.bfloat16),
        ],
        compiler_params=pltpu.CompilerParams(vmem_limit_bytes=8 << 20),
        cost_estimate=pl.CostEstimate(
            flops=rows * total * width // 4, bytes_accessed=rows, transcendentals=0
        ),
    )(*[piece for part in parts for piece in part])


def regrouped(flat, lengths):
    flat = iter(flat)
    return [[next(flat) for _ in range(length)] for length in lengths]


def plane_kernel(rows, span, lengths, block, partner, *refs):
    *pieces, best, mine, held = refs
    row = hold(regrouped(pieces, lengths), held, rows, span)
    units = (block, partner)
    parts = [(codes(block, rows, span), OWN), (codes(partner, rows, span), HELD)]
    (mine[...],), theirs = meet(units, parts, rows, span, held, row)
    best[...] = theirs[:, : best.shape[1]]


def rest_kernel(rows, span, block, partner, held, row, best, mine):
    count = best.shape[1]
    start = held.shape[0] - up(count, LANES)
    held, row = held.at[start:, :], row[:, start:]
    units = (block, partner)
    parts = [(codes(block, rows, span), OWN), (codes(partner, rows, span), HELD)]
    (mine[...],), theirs = meet(units, parts, rows, span, held, row)
    best[...] = theirs[:, row.shape[1] - count :]


def line_kernel(rows, span, together, count, first, second, held, row, *refs):
    bests, outs, found = refs[:count], refs[count:-1], refs[-1]
    parts = [(codes(second, rows, span, first=place), TWO) for place in (CODES, 0)]

    def give(best):
        for out, places in zip(outs, together):
            out[...] = jnp.concatenate(
                [best[:, place * rows : (place + 1) * rows] for place in places], axis=1
            )

    arrived = jnp.max(parts[0][0]) > 0.0

    @pl.when(arrived)
    def _():
        units = (first, second)
        mine, theirs = meet(units, parts, rows, span, held, row[...])
        found[...] = jnp.concatenate(mine, axis=1)
        give(jnp.maximum(jnp.concatenate([best[...] for best in bests], axis=1), theirs))

    @pl.when(jnp.logical_not(arrived))
    def _():
        found[...] = jnp.full(found.shape, -1.0, jnp.float32)
        give(jnp.concatenate([best[...] for best in bests], axis=1))


def plane(block, partner, holds, rows, span):
    width = block.shape[1]
    total = len(holds) * rows
    return pl.pallas_call(
        functools.partial(plane_kernel, rows, span, [len(part) for part in holds]),
        out_shape=[
            jax.ShapeDtypeStruct((1, total), jnp.float32),
            jax.ShapeDtypeStruct((1, rows), jnp.float32),
        ],
        scratch_shapes=[
            pltpu.VMEM((up(total, LANES), width), jnp.bfloat16),
        ],
        compiler_params=pltpu.CompilerParams(vmem_limit_bytes=12 << 20),
        cost_estimate=pl.CostEstimate(flops=rows, bytes_accessed=rows, transcendentals=0),
    )(block, partner, *[piece for part in holds for piece in part])


def plane_rest(block, partner, held, row, count, rows, span):
    return pl.pallas_call(
        functools.partial(rest_kernel, rows, span),
        out_shape=[
            jax.ShapeDtypeStruct((1, count), jnp.float32),
            jax.ShapeDtypeStruct((1, rows), jnp.float32),
        ],
        compiler_params=pltpu.CompilerParams(vmem_limit_bytes=12 << 20),
        cost_estimate=pl.CostEstimate(flops=rows, bytes_accessed=rows, transcendentals=0),
    )(block, partner, held, row)


def line(first, second, held, row, bests, rows, span, together):
    outs = [jax.ShapeDtypeStruct((1, rows * len(some)), jnp.float32) for some in together]
    *bests, found = pl.pallas_call(
        functools.partial(line_kernel, rows, span, together, len(bests)),
        out_shape=outs + [jax.ShapeDtypeStruct((1, 2 * rows), jnp.float32)],
        compiler_params=pltpu.CompilerParams(vmem_limit_bytes=12 << 20),
        cost_estimate=pl.CostEstimate(flops=rows, bytes_accessed=rows, transcendentals=0),
    )(first, second, held, row, *bests)
    return bests, found


OWN = (True, False)
HELD = (False, True)
TWO = (True, True)


def line_rounds(chips):
    if chips == 4:
        return [[(3, 1), (0, 2), (2, 3)], [(3, 0), (0, 1), (1, 2)]]
    rounds = []
    for shift in range(1, chips // 2 + 1):
        senders = chips // 2 if 2 * shift == chips else chips
        rounds.append([(s, (s + shift) % chips) for s in range(senders)])
    return rounds


def solution(mesh):
    groups, members = mesh.shape["dp"], mesh.shape["grid"]
    assert groups == 4 and members % 2 == 0
    chips = members // 2

    def everywhere(target):
        return [
            (p * members + g, a * members + b)
            for p in range(groups)
            for g in range(members)
            for a, b in [target(p, g)]
        ]

    other_core = everywhere(lambda p, g: (p, g ^ 1))
    first = everywhere(lambda p, g: (p ^ (1 + g % 2), g))
    second = everywhere(lambda p, g: (p ^ (2 - g % 2), g))
    homes = [
        everywhere(lambda p, g: (p ^ (1 + g % 2), g ^ 1)),
        everywhere(lambda p, g: (p ^ (2 - g % 2), g ^ 1)),
        everywhere(lambda p, g: (p ^ 3, g ^ 1)),
    ]

    rounds = line_rounds(chips)
    rounds += [[]] * (len(rounds) % 2)
    rounds = [
        [
            (p * members + 2 * s + c, p * members + 2 * t + c)
            for p in range(groups)
            for c in range(2)
            for s, t in rounds[at + c]
        ]
        for at in range(0, len(rounds), 2)
    ]

    def back(pairs):
        return [(target, source) for source, target in pairs]

    def shards(embeddings, cluster, order_key):
        rows = embeddings.shape[0]
        span = 256
        while span < rows * groups * members:
            span *= 2
        halves = (rows // 2, rows // 2 + EXTRA)
        names = (cluster.reshape(1, rows), order_key)
        raw = [lax.ppermute(embeddings, BOTH, pairs) for pairs in rounds]
        charge = [lax.ppermute(array, BOTH, other_core) for array in (embeddings, *names)]
        width = embeddings.shape[1]
        block, *parts = with_units(prepare_kernel, (rows + EXTRA, *halves), width, *charge)
        from_first = [lax.ppermute(part, BOTH, first) for part in parts]
        (own_codes,) = with_units(codes_kernel, (EXTRA,), width, *names)
        later, own_codes = lax.optimization_barrier((block, own_codes))
        from_second = [lax.ppermute(later, BOTH, second)]
        (both,) = with_units(complete_kernel, (rows + EXTRA,), width, block, own_codes)
        (own,) = with_units(own_kernel, (rows + EXTRA,), width, embeddings, own_codes)
        near_other = [lax.ppermute(both, BOTH, pairs) for pairs in rounds]
        from_corner = [lax.ppermute(part, BOTH, second) for part in from_first]
        near = [
            list(with_units(unit_kernel, (rows, rows // 2, rows // 2), width, rows_of))
            for rows_of in raw
        ]
        far = [[lax.ppermute(piece, BOTH, other_core) for piece in blocks[1:]] for blocks in near]

        in_charge, results, kept, sent = [], [], [], []
        best_two, mine = plane(block, own, [[block], from_first], rows, span)
        in_charge.append(mine)
        *from_corner, best_two = lax.optimization_barrier((*from_corner, best_two))
        blocks = [[block], from_first, from_second, from_corner]
        held, row, far_units = gather(blocks, far[0], rows, span)
        best_rest, mine = plane_rest(block, own, held, row, 2 * rows, rows, span)
        in_charge.append(mine)
        bests = [best_two, best_rest]
        far = [far_units] + [jnp.concatenate(pieces, axis=0) for pieces in far[1:]]
        whole, last = [tuple(range(groups))], [(at,) for at in range(groups)]
        for at, second_near in enumerate(near_other):
            second_near, *bests = lax.optimization_barrier((second_near, *bests))
            second_far = lax.ppermute(second_near, BOTH, other_core)
            bests, found = line(near[at][0], second_near, held, row, bests, rows, span, whole)
            kept.append(found)
            bests, found = line(
                far[at],
                second_far,
                held,
                row,
                bests,
                rows,
                span,
                last if at == len(rounds) - 1 else whole,
            )
            sent.append(found)
        sent = lax.ppermute(jnp.concatenate(sent, axis=1), BOTH, other_core)
        kept = jnp.maximum(jnp.concatenate(kept, axis=1), sent)
        kept, *bests = lax.optimization_barrier((kept, *bests))
        for at, pairs in enumerate(rounds):
            found = lax.ppermute(kept[:, 2 * at * rows : 2 * (at + 1) * rows], BOTH, back(pairs))
            me = lax.axis_index(BOTH)
            sender = functools.reduce(jnp.logical_or, [me == source for source, _ in pairs])
            found = jnp.where(sender, found, -1.0)
            results.append(found[:, :rows])
            in_charge.append(found[:, rows:])
        results += [
            lax.ppermute(best, BOTH, pairs) for best, pairs in zip(bests[1:], homes)
        ]
        in_charge.append(bests[0])
        home = functools.reduce(jnp.maximum, in_charge)
        results.append(lax.ppermute(home, BOTH, other_core))
        return functools.reduce(jnp.maximum, results).reshape(rows)

    placed = (P(BOTH, None), P(BOTH, None), P(BOTH))
    return jax.shard_map(
        shards, mesh=mesh, in_specs=placed, out_specs=P(BOTH), check_vma=False
    )
```
